32 devices in a mesh: dp: 2 (over core), row: 4 (over y, x), col: 4 (over z).
Axes of the slice: x: 2, y: 2, z: 4, core: 2. Of those that a mesh axis runs over, the one named last changes fastest.
Arguments:
- activations: bfloat16 [8192, 2048], P(('dp', 'col'), 'row'), may hold values from -6 to 6
- segments: int32 [8192], P(('dp', 'row')), may hold values from 0 to 127, as said below
- positions: int32 [8192], P(('dp', 'row')), may hold values from 0 to 2046, as said below
- first_gain: float32 [2048], P('row'), may hold values from 0.5 to 1.5
- query_weight: bfloat16 [2048, 2048], P('row', 'col'), may hold values from -0.125 to 0.125
- key_weight: bfloat16 [2048, 512], P('row', 'col'), may hold values from -0.125 to 0.125
- value_weight: bfloat16 [2048, 512], P('row', 'col'), may hold values from -0.125 to 0.125
- out_weight: bfloat16 [2048, 2048], P('col', 'row'), may hold values from -1 to 1
- second_gain: float32 [2048], P('row'), may hold values from 0.5 to 1.5
- gate_weight: bfloat16 [2048, 8192], P('row', 'col'), may hold values from -0.125 to 0.125
- up_weight: bfloat16 [2048, 8192], P('row', 'col'), may hold values from -0.125 to 0.125
- down_weight: bfloat16 [8192, 2048], P('col', 'row'), may hold values from -0.125 to 0.125
- cotangent: bfloat16 [8192, 2048], P(('dp', 'col'), 'row'), may hold values from -6 to 6
Outputs:
- block_out: bfloat16 [8192, 2048], P(('dp', 'col'), 'row')
- input_grad: float32 [8192, 2048], P(('dp', 'col'), 'row')
- first_gain_grad: float32 [2048], P('row')
- query_grad: float32 [2048, 2048], P('row', 'col')
- key_grad: float32 [2048, 512], P('row', 'col')
- value_grad: float32 [2048, 512], P('row', 'col')
- out_grad: float32 [2048, 2048], P('col', 'row')
- second_gain_grad: float32 [2048], P('row')
- gate_grad: float32 [2048, 8192], P('row', 'col')
- up_grad: float32 [2048, 8192], P('row', 'col')
- down_grad: float32 [8192, 2048], P('col', 'row')
The draws below stay inside these ranges and needn't reach their ends.
Inputs may be any that keep to these rules, and one draw needn't show every extreme that they name: `segments`: segment numbers never fall along the tokens; a document never crosses the end of a sequence of 1024 tokens. Within a document, positions rise by one from token to token; a document at the start of a sequence may begin at a position above 0.
All inputs are finite; a program needn't handle non-finite values.
Results may differ from the reference program's by a relative error of at most 0.017.
Values may be sent and summed in bfloat16 or wider, within the bound.
A program may use at most 512 MiB of HBM per device.

```python
import math
import jax
import jax.numpy as jnp
from jax import lax

D = 2048
FF = 8192
HEADS = 32
KV = 8
HEAD = 64
LENGTH = 1024
SEQS = 8
TOKENS = 8192


def doc_layout(key):
    sequences = TOKENS // LENGTH
    doc_total = 16
    shortest = LENGTH // 5 + 1
    first_key, second_key = jax.random.split(key)
    doc_lengths = jax.random.randint(first_key, (sequences, doc_total), shortest, 2 * LENGTH)
    doc_lengths = doc_lengths.at[sequences - 1, 0].set(2 * LENGTH - 1)
    offset = jax.random.randint(second_key, (sequences, 1), 0, doc_lengths[:, :1])
    offset = offset.at[0, 0].set(0)
    offset = offset.at[sequences - 1, 0].set(LENGTH - 1)
    doc_ends = jnp.cumsum(doc_lengths, axis=1) - offset
    doc_starts = jnp.concatenate([-offset, doc_ends[:, :-1]], axis=1)
    places = jnp.arange(LENGTH, dtype=jnp.int32)
    inside = (doc_ends[:, None, :] <= places[None, :, None]).astype(jnp.int32)
    local_doc = jnp.sum(inside, axis=2)
    chosen = (local_doc[:, :, None] == jnp.arange(doc_total)[None, None, :]).astype(jnp.int32)
    doc_begin = jnp.sum(chosen * doc_starts[:, None, :], axis=2)
    last_doc = local_doc[:, LENGTH - 1:LENGTH]
    numbered = jnp.where(local_doc == last_doc, doc_total - 1, local_doc)
    segment = numbered + doc_total * jnp.arange(sequences, dtype=jnp.int32)[:, None]
    position = places[None, :] - doc_begin
    return (segment.reshape(TOKENS).astype(jnp.int32), position.reshape(TOKENS).astype(jnp.int32))


def draw_segments(key, part):
    return doc_layout(key)[0]


def draw_positions(key, part):
    return doc_layout(key)[1]


def steps_of(rng, shape, cuts, smallest, high):
    def one(dim, parts):
        heights = jax.random.uniform(jax.random.fold_in(jax.random.fold_in(rng, 6), dim), (parts,), jnp.float32, smallest / len(cuts), high / len(cuts))
        return jnp.repeat(jnp.exp(heights), shape[dim] // parts).reshape((-1,) + (1,) * (len(shape) - dim - 1))

    level = one(*cuts[0])
    for cut in cuts[1:]:
        level = level * one(*cut)
    return level


def normal_values(rng, extent, width, bound, cuts=(), kind=jnp.bfloat16):
    entries = width * jax.random.normal(rng, extent, jnp.float32)
    if cuts:
        entries = entries * steps_of(rng, extent, cuts, -0.22, 0.18)
    return jnp.clip(entries, -bound, bound).astype(kind)


def setup_inputs(seed: int = 0) -> dict:
    arg_keys = jax.random.split(jax.random.key(seed), 14)
    return {
        "activations": normal_values(arg_keys[0], (TOKENS, D), 1.0, 6.0, ((0, 8), (1, 4))),
        "segments": draw_segments(jax.random.fold_in(arg_keys[13], 71), 0),
        "positions": draw_positions(jax.random.fold_in(arg_keys[13], 71), 0),
        "first_gain": jnp.clip(1.0 + 0.1 * jax.random.normal(arg_keys[3], (D,), jnp.float32), 0.5, 1.5),
        "query_weight": normal_values(arg_keys[4], (D, HEADS * HEAD), D ** -0.5, 0.125, ((0, 4), (1, 4))),
        "key_weight": normal_values(arg_keys[5], (D, KV * HEAD), D ** -0.5, 0.125, ((0, 4), (1, 4))),
        "value_weight": normal_values(arg_keys[6], (D, KV * HEAD), D ** -0.5, 0.125, ((0, 4), (1, 4))),
        "out_weight": normal_values(arg_keys[7], (HEADS * HEAD, D), (D // 64) ** -0.5, 1.0, ((0, 4), (1, 4))),
        "second_gain": jnp.clip(1.0 + 0.1 * jax.random.normal(arg_keys[8], (D,), jnp.float32), 0.5, 1.5),
        "gate_weight": normal_values(arg_keys[9], (D, FF), D ** -0.5, 0.125, ((0, 4), (1, 4))),
        "up_weight": normal_values(arg_keys[10], (D, FF), D ** -0.5, 0.125, ((0, 4), (1, 4))),
        "down_weight": normal_values(arg_keys[11], (FF, D), (FF // 4) ** -0.5, 0.125, ((0, 4), (1, 4))),
        "cotangent": normal_values(arg_keys[12], (TOKENS, D), 1.0, 6.0, ((0, 8), (1, 4))),
    }


EPSILON = 1e-05
THETA = 500000.0

@jax.custom_vjp
def low(v):
    return lax.optimization_barrier(v.astype(jnp.bfloat16)).astype(jnp.float32)

@jax.custom_vjp
def low_back(v):
    return v

def low_keep(v):
    return (low(v), None)

def low_pass(kept, grad):
    return (grad,)

def back_keep(v):
    return (v, None)

def back_low(kept, grad):
    return (low(grad),)
low.defvjp(low_keep, low_pass)
low_back.defvjp(back_keep, back_low)

def half_turn(values):
    middle_index = values.shape[-1] // 2
    return jnp.concatenate([-values[..., middle_index:], values[..., :middle_index]], axis=-1)

def rotary_tables(positions):
    exponent = jnp.arange(0, HEAD, 2).astype(jnp.float32) / HEAD
    inverse = jnp.power(jnp.float32(THETA), -exponent)
    phase = positions.astype(jnp.float32)[:, None] * inverse[None, :]
    phase = jnp.concatenate([phase, phase], axis=1)
    return (jnp.cos(phase), jnp.sin(phase))

def rotate(values, cosine, sine):
    return values * cosine[:, None, :] + half_turn(values) * sine[:, None, :]

def scaled_norm(values, gain):
    return values * lax.rsqrt(lax.optimization_barrier(jnp.mean(values * values, axis=-1, keepdims=True)) + EPSILON) * gain[None, :]

def one_sequence(pieces):
    query_rot, key_rot, value_low, segment_piece = pieces
    group_size = HEADS // KV
    key_full = jnp.repeat(key_rot, group_size, axis=1)
    value_full = jnp.repeat(value_low, group_size, axis=1)
    scores = low_back(jnp.einsum('qhd,shd->hqs', query_rot, key_full, precision=lax.Precision.HIGHEST) * HEAD ** (-0.5))
    places = jnp.arange(LENGTH)
    allowed = (segment_piece[:, None] == segment_piece[None, :]) & (places[:, None] >= places[None, :])
    scores = jnp.where(allowed[None], scores, -1e+30)
    softmax_weights = jax.nn.softmax(scores, axis=-1)
    return jnp.einsum('hqs,shd->qhd', low(softmax_weights), value_full, precision=lax.Precision.HIGHEST)

def layer(block_in, segment_piece, position_piece, first_gain, query_weight, key_weight, value_weight, out_weight, second_gain, gate_weight, up_weight, down_weight):
    highest = lax.Precision.HIGHEST
    row_count = block_in.shape[0]
    seq_count = row_count // LENGTH
    normed = low(scaled_norm(block_in, first_gain))
    query = low_back(jnp.dot(normed, query_weight, precision=highest))
    key_part = low_back(jnp.dot(normed, key_weight, precision=highest))
    value_part = low_back(jnp.dot(normed, value_weight, precision=highest))
    cosine, sine = rotary_tables(position_piece)
    query_rot = low(rotate(query.reshape(row_count, HEADS, HEAD), cosine, sine))
    key_rot = low(rotate(key_part.reshape(row_count, KV, HEAD), cosine, sine))
    value_low = low(value_part.reshape(row_count, KV, HEAD))
    attended = lax.map(jax.checkpoint(one_sequence), (query_rot.reshape(seq_count, LENGTH, HEADS, HEAD), key_rot.reshape(seq_count, LENGTH, KV, HEAD), value_low.reshape(seq_count, LENGTH, KV, HEAD), segment_piece.reshape(seq_count, LENGTH)))
    attn_mixed = low(low_back(attended.reshape(row_count, HEADS * HEAD)))
    middle = block_in + low_back(jnp.dot(attn_mixed, out_weight, precision=highest))
    second = low(scaled_norm(middle, second_gain))
    gate_part = low_back(jnp.dot(second, gate_weight, precision=highest))
    up_part = low_back(jnp.dot(second, up_weight, precision=highest))
    hidden = low(jax.nn.silu(gate_part) * up_part)
    return middle + low_back(jnp.dot(hidden, down_weight, precision=highest))

def reference(activations, segments, positions, first_gain, query_weight, key_weight, value_weight, out_weight, second_gain, gate_weight, up_weight, down_weight, cotangent):
    params = tuple((weight.astype(jnp.float32) for weight in (first_gain, query_weight, key_weight, value_weight, out_weight, second_gain, gate_weight, up_weight, down_weight)))
    group_size = math.gcd(SEQS, max(1, 4096 // LENGTH))
    steps_count = SEQS // group_size
    row_count = group_size * LENGTH
    inputs = activations.astype(jnp.float32).reshape(steps_count, row_count, D)
    seg_groups = segments.reshape(steps_count, row_count)
    pos_groups = positions.reshape(steps_count, row_count)
    cot_groups = cotangent.astype(jnp.float32).reshape(steps_count, row_count, D)

    def one_group(totals, batch_piece):
        block_in, segment_piece, position_piece, cot_piece = batch_piece

        def forward(block_value, *weights):
            return layer(block_value, segment_piece, position_piece, *weights)
        result, pullback = jax.vjp(forward, block_in, *params)
        gradients = pullback(cot_piece)
        totals = tuple((total + grad for total, grad in zip(totals, gradients[1:])))
        return (totals, (result.astype(jnp.bfloat16), gradients[0]))
    zeros_init = tuple((jnp.zeros_like(weight) for weight in params))
    totals, (outputs, input_grads) = lax.scan(one_group, zeros_init, (inputs, seg_groups, pos_groups, cot_groups))
    return (outputs.reshape(TOKENS, D), input_grads.reshape(TOKENS, D), totals[0], totals[1], totals[2], totals[3], totals[4], totals[5], totals[6], totals[7], totals[8])
```

```python
import jax
import jax.numpy as jnp
from jax import lax
from jax.sharding import PartitionSpec as P

HEAD = 64
EPSILON = 1e-05
THETA = 500000.0
F32 = jnp.float32
BF16 = jnp.bfloat16


def dot(left, right, dims):
    return lax.dot_general(left, right, (dims, ((), ())), preferred_element_type=F32)


def half_turn(values):
    middle_index = values.shape[-1] // 2
    return jnp.concatenate([-values[..., middle_index:], values[..., :middle_index]], axis=-1)


def rotary_tables(positions):
    exponent = jnp.arange(0, HEAD, 2).astype(F32) / HEAD
    inverse = jnp.power(F32(THETA), -exponent)
    phase = positions[:, None] * inverse[None, :]
    phase = jnp.concatenate([phase, phase], axis=1)
    return (jnp.cos(phase), jnp.sin(phase))


def rotate(values, cosine, sine):
    return values * cosine[:, None, :] + half_turn(values) * sine[:, None, :]


def rotate_back(gradients, cosine, sine):
    return gradients * cosine[:, None, :] - half_turn(gradients * sine[:, None, :])


def visible(segments):
    places = jnp.arange(segments.shape[0])
    return (segments[:, None] == segments[None, :]) & (places[:, None] >= places[None, :])


def attn_scores(query_rot, key_rot, allowed):
    scores = jnp.einsum("qhgd,shd->hgqs", query_rot, key_rot, preferred_element_type=F32) * HEAD ** (-0.5)
    return jnp.where(allowed[None, None], scores, -1e30)


def attend(query_rot, key_rot, value_low, allowed):
    scores = attn_scores(query_rot, key_rot, allowed)
    row_max = jnp.max(scores, axis=-1, keepdims=True)
    exponent = jnp.exp(scores - row_max)
    denominator = jnp.sum(exponent, axis=-1, keepdims=True)
    soft_weights = exponent / denominator
    logsum = row_max + jnp.log(denominator)
    output = jnp.einsum("hgqs,shd->qhgd", soft_weights.astype(BF16), value_low, preferred_element_type=F32)
    return (output, logsum)


def attend_back(query_rot, key_rot, value_low, allowed, logsum, out_grads):
    scores = attn_scores(query_rot, key_rot, allowed)
    soft_weights = jnp.where(allowed[None, None], jnp.exp(scores - logsum), 0.0)
    weight_grads = jnp.einsum("qhgd,shd->hgqs", out_grads, value_low, preferred_element_type=F32)
    value_back = jnp.einsum("hgqs,qhgd->shd", soft_weights.astype(BF16), out_grads, preferred_element_type=F32)
    score_grads = soft_weights * (weight_grads - jnp.sum(soft_weights * weight_grads, axis=-1, keepdims=True))
    score_low = score_grads.astype(BF16)
    query_back = jnp.einsum("hgqs,shd->qhgd", score_low, key_rot, preferred_element_type=F32) * HEAD ** (-0.5)
    key_back = jnp.einsum("hgqs,qhgd->shd", score_low, query_rot, preferred_element_type=F32) * HEAD ** (-0.5)
    return (query_back, key_back, value_back)


def gather(values, axis_name, axis=0):
    return lax.all_gather(values, axis_name, axis=axis, tiled=True)


def scatter(values, axis_name, axis=0):
    return lax.psum_scatter(values.astype(BF16), axis_name, scatter_dimension=axis, tiled=True)


def swap(values):
    rows, cols = lax.axis_size("row"), lax.axis_size("col")
    return lax.ppermute(values, ("row", "col"), [(r * cols + c, c * cols + r) for r in range(rows) for c in range(cols)])


def gather_shared(values):
    share = values.shape[0] // lax.axis_size("dp")
    part = lax.dynamic_slice_in_dim(values, lax.axis_index("dp") * share, share, 0)
    return lax.all_gather(part, ("row", "dp"), axis=0, tiled=True)


def scatter_shared(values):
    part = scatter(values, ("row", "dp"))
    return gather(part, "dp").astype(F32)


def local(
    activations, segments, positions, first_gain, query_weight, key_weight, value_weight, out_weight,
    second_gain, gate_weight, up_weight, down_weight, cotangent,
):
    rows = lax.axis_size("row")
    row, col = lax.axis_index("row"), lax.axis_index("col")
    length, width = activations.shape
    features = rows * width
    quarter = length // rows
    query_cols, key_cols = query_weight.shape[1], key_weight.shape[1]
    heads, kv_heads = query_cols // HEAD, key_cols // HEAD
    group_size = heads // kv_heads
    hidden_cols = gate_weight.shape[1]

    small = jnp.concatenate([segments.astype(F32), positions.astype(F32), first_gain, second_gain])
    small = gather(small[None], "row")
    own = lax.dynamic_slice_in_dim(small, col, 1, 0)[0]
    segment_own, position_own = own[:length], own[length : 2 * length]
    gain1 = small[:, 2 * length : 2 * length + width].reshape(features)
    gain2 = small[:, 2 * length + width :].reshape(features)

    x_all = gather(activations, "row", 1)
    qkv_weight = jnp.concatenate([query_weight, key_weight, value_weight], axis=1)
    qkv_all = gather(swap(qkv_weight), "col")
    out_all_w = gather(swap(out_weight), "col", 1)
    gate_all = gather_shared(gate_weight)
    up_all = gather_shared(up_weight)
    down_all = gather_shared(down_weight).reshape(rows, hidden_cols, width)

    cot_tok = lax.all_to_all(cotangent, "row", 0, 1, tiled=True)
    cot_all = gather(cot_tok, "col")

    x = x_all.astype(F32)
    inv1 = lax.rsqrt(jnp.mean(x * x, axis=1, keepdims=True) + EPSILON)
    first = (x * inv1 * gain1[None]).astype(BF16)
    projected = dot(first, qkv_all, ((1,), (0,)))
    cosine, sine = rotary_tables(position_own)
    query_rot = rotate(projected[:, :query_cols].reshape(length, heads, HEAD), cosine, sine)
    query_rot = query_rot.astype(BF16).reshape(length, kv_heads, group_size, HEAD)
    key_rot = rotate(projected[:, query_cols : query_cols + key_cols].reshape(length, kv_heads, HEAD), cosine, sine).astype(BF16)
    value_low = projected[:, query_cols + key_cols :].reshape(length, kv_heads, HEAD).astype(BF16)
    allowed = visible(segment_own)
    attended, logsum = attend(query_rot, key_rot, value_low, allowed)
    attn = attended.reshape(length, query_cols).astype(BF16)
    mixed = scatter(dot(attn, out_all_w, ((1,), (0,))), "row")
    x_tok = lax.dynamic_slice_in_dim(x_all, row * quarter, quarter, 0).astype(F32)
    middle = x_tok + mixed.astype(F32)
    inv2 = lax.rsqrt(jnp.mean(middle * middle, axis=1, keepdims=True) + EPSILON)
    second = (middle * inv2 * gain2[None]).astype(BF16)

    second_all = gather(second, "col")
    gate = dot(second_all, gate_all, ((1,), (0,)))
    up = dot(second_all, up_all, ((1,), (0,)))
    sigma = jax.nn.sigmoid(gate)
    swish = gate * sigma
    hidden = (swish * up).astype(BF16)
    tokens = hidden.shape[0]
    down_part = lax.dot_general(hidden, down_all, (((1,), (1,)), ((), ())), preferred_element_type=F32).reshape(tokens, features)
    out_tok = (middle + scatter(down_part, "col").astype(F32)).astype(BF16)
    block_out = lax.all_to_all(out_tok, "row", 1, 0, tiled=True)

    cot_split = cot_all.reshape(tokens, rows, width)
    dhidden = lax.dot_general(cot_split, down_all, (((1, 2), (0, 2)), ((), ())), preferred_element_type=F32)
    swish_grad = sigma * (1.0 + gate * (1.0 - sigma))
    dgate = (dhidden * up * swish_grad).astype(BF16)
    dup = (dhidden * swish).astype(BF16)
    dsecond = scatter(dot(dgate, gate_all, ((1,), (1,))) + dot(dup, up_all, ((1,), (1,))), "col").astype(F32)

    weighted = dsecond * gain2[None]
    inner = jnp.sum(middle * weighted, axis=1, keepdims=True) / features
    dmiddle = cot_tok.astype(F32) + inv2 * weighted - middle * (inv2 * inv2 * inv2 * inner)
    gain2_grad = jnp.sum(dsecond * middle * inv2, axis=0)
    dmid_all = gather(dmiddle.astype(BF16), "row")

    attn_grad = dot(dmid_all, out_all_w, ((1,), (1,))).astype(BF16).reshape(length, kv_heads, group_size, HEAD)
    query_back, key_back, value_back = attend_back(query_rot, key_rot, value_low, allowed, logsum, attn_grad)
    query_pre = rotate_back(query_back.reshape(length, heads, HEAD), cosine, sine).reshape(length, query_cols)
    key_pre = rotate_back(key_back, cosine, sine).reshape(length, key_cols)
    dqkv = jnp.concatenate([query_pre, key_pre, value_back.reshape(length, key_cols)], axis=1).astype(BF16)
    dfirst_part = dot(dqkv, qkv_all, ((1,), (1,)))
    inner1 = lax.psum(jnp.sum(x * gain1[None] * dfirst_part, axis=1), "row") / features
    dfirst = scatter(dfirst_part, "row", 1).astype(F32)
    own_x = activations.astype(F32)
    dmid_own = lax.dynamic_slice_in_dim(dmid_all, row * width, width, 1).astype(F32)
    input_grad = dmid_own + inv1 * first_gain[None] * dfirst - own_x * (inv1 * inv1 * inv1 * inner1[:, None])
    gain1_grad = lax.psum(jnp.sum(dfirst * own_x * inv1, axis=0), ("dp", "col"))
    gain2_grad = lax.psum(gain2_grad, ("dp", "row", "col"))
    gain2_grad = lax.dynamic_slice_in_dim(gain2_grad, row * width, width, 0)

    down_grad = lax.dot_general(hidden, cot_split, (((0,), (0,)), ((), ())), preferred_element_type=F32)
    down_grad = scatter_shared(down_grad.transpose(1, 0, 2).reshape(rows * hidden_cols, width))
    gate_grad = scatter_shared(dot(second_all, dgate, ((0,), (0,))))
    up_grad = scatter_shared(dot(second_all, dup, ((0,), (0,))))
    out_grad = swap(lax.psum(scatter(dot(attn, dmid_all, ((0,), (0,))), "col", 1), "dp")).astype(F32)
    qkv_grad = swap(lax.psum(scatter(dot(first, dqkv, ((0,), (0,))), "col"), "dp")).astype(F32)
    return (
        block_out,
        input_grad,
        gain1_grad,
        qkv_grad[:, :query_cols],
        qkv_grad[:, query_cols : query_cols + key_cols],
        qkv_grad[:, query_cols + key_cols :],
        out_grad,
        gain2_grad,
        gate_grad,
        up_grad,
        down_grad,
    )


def solution(mesh):
    tokens, block, swapped = P(("dp", "col"), "row"), P("row", "col"), P("col", "row")
    return jax.shard_map(
        local,
        mesh=mesh,
        in_specs=(
            tokens, P(("dp", "row")), P(("dp", "row")), P("row"), block, block, block, swapped,
            P("row"), block, block, swapped, tokens,
        ),
        out_specs=(tokens, tokens, P("row"), block, block, block, swapped, P("row"), block, block, swapped),
        check_vma=False,
    )
```

```python
import functools

import jax
import jax.numpy as jnp
from jax import lax
from jax.experimental import pallas as pl
from jax.experimental.pallas import tpu as pltpu
from jax.sharding import PartitionSpec as P

HEAD = 64
EPSILON = 1e-05
THETA = 500000.0
F32 = jnp.float32
BF16 = jnp.bfloat16


MESH = pl.DeviceIdType.MESH
VMEM_LIMIT = 60 * 1024 * 1024


def greet(row_size=0, col_size=0, dp_size=0):
    barrier = pltpu.get_barrier_semaphore()
    if row_size:
        row = lax.axis_index("row")
        for mask in range(1, row_size):
            pl.semaphore_signal(barrier, inc=1, device_id={"row": row ^ mask}, device_id_type=MESH)
    if col_size:
        col = lax.axis_index("col")

        @pl.when(col > 0)
        def _():
            pl.semaphore_signal(barrier, inc=1, device_id={"col": col - 1}, device_id_type=MESH)

        @pl.when(col < col_size - 1)
        def _():
            pl.semaphore_signal(barrier, inc=1, device_id={"col": col + 1}, device_id_type=MESH)

    if dp_size:
        pl.semaphore_signal(barrier, inc=1, device_id={"dp": 1 - lax.axis_index("dp")}, device_id_type=MESH)
    count = max(row_size - 1, 0) + (1 if dp_size else 0)
    if col_size:
        count = count + jnp.where(col > 0, 1, 0) + jnp.where(col < col_size - 1, 1, 0)
    pl.semaphore_wait(barrier, count)


def remote(src, dst, sends, recvs, place, device):
    return pltpu.make_async_remote_copy(
        src_ref=src, dst_ref=dst, send_sem=sends.at[place], recv_sem=recvs.at[place],
        device_id=device, device_id_type=MESH,
    )


class RowGather:
    def __init__(self, size, ref, sends, recvs):
        self.size, self.ref, self.sends, self.recvs = size, ref, sends, recvs
        self.bits = size.bit_length() - 1
        self.row = lax.axis_index("row")
        self.half = ref.shape[1] // 2

    @staticmethod
    def semaphores(size):
        return pltpu.SemaphoreType.DMA((2 * (size - 1),))

    def copies(self, step):
        out = []
        for part in range(2):
            order = list(range(self.bits)) if part == 0 else list(range(self.bits))[::-1]
            bit = 1 << order[step]
            for item in range(1 << step):
                mask = 0
                for j in range(step):
                    if item >> j & 1:
                        mask |= 1 << order[j]
                piece = self.ref.at[self.row ^ mask, pl.ds(part * self.half, self.half)]
                place = part * (self.size - 1) + (1 << step) - 1 + item
                out.append(remote(piece, piece, self.sends, self.recvs, place, {"row": self.row ^ bit}))
        return out

    def start(self):
        self.all = [self.copies(step) for step in range(self.bits)]
        for step in range(self.bits):
            count = 1 << step
            for part in range(2):
                self.all[step][part * count].start()

    def run(self):
        for step in range(self.bits):
            for copy in self.all[step]:
                copy.wait_recv()
            if step + 1 < self.bits:
                count = 1 << (step + 1)
                for part in range(2):
                    for item in range(1, count):
                        if item >> step & 1:
                            self.all[step + 1][part * count + item].start()
                for later in range(step + 2, self.bits):
                    count = 1 << later
                    for part in range(2):
                        for item in range(1, count):
                            if item >> (step + 1) == 0 and item >> step & 1:
                                self.all[later][part * count + item].start()
        for step in range(self.bits):
            for copy in self.all[step]:
                copy.wait_send()


def row_scatter_semaphores(size):
    return pltpu.SemaphoreType.DMA((2 * (size - 1),))


def row_scatter(size, part_ref, recv_ref, sends, recvs, finish):
    bits = size.bit_length() - 1
    row = lax.axis_index("row")
    half = part_ref.shape[1] // 2
    plans = []
    for part in range(2):
        order = list(range(bits)) if part == 0 else list(range(bits))[::-1]
        steps = []
        for step in range(bits):
            bit = 1 << order[step]
            rest = order[step + 1 :]
            copies = []
            count = 1 << len(rest)
            for item in range(count - 1, -1, -1):
                mask = bit
                for j, other in enumerate(rest):
                    if item >> j & 1:
                        mask |= 1 << other
                place = (size - 2 * count) + item
                copies.append((
                    item, mask ^ bit, place,
                    remote(
                        part_ref.at[row ^ mask, pl.ds(part * half, half)],
                        recv_ref.at[place, pl.ds(part * half, half)],
                        sends, recvs, part * (size - 1) + place, {"row": row ^ bit},
                    ),
                ))
            steps.append(copies)
        plans.append(steps)
    for part in range(2):
        for _, _, _, copy in plans[part][0]:
            copy.start()
    for step in range(bits):
        for part in range(2):
            rows = pl.ds(part * half, half)
            for item, mask, place, copy in plans[part][step]:
                copy.wait_recv()
                total = part_ref[row ^ mask, rows].astype(F32) + recv_ref[place, rows].astype(F32)
                if item:
                    part_ref[row ^ mask, rows] = total.astype(BF16)
                    if step + 1 < bits:
                        for item2, mask2, _, copy2 in plans[part][step + 1]:
                            sent = mask2 ^ (1 << (list(range(bits)) if part == 0 else list(range(bits))[::-1])[step + 1])
                            if sent == mask:
                                copy2.start()
                elif step + 1 < bits:
                    part_ref[row, rows] = total.astype(BF16)
                else:
                    finish(rows, total)
    for part in range(2):
        for step in range(bits):
            for _, _, _, copy in plans[part][step]:
                copy.wait_send()


def col_gather(size, ref, sends, recvs, seen=None):
    col = lax.axis_index("col")

    def right(step):
        piece = ref.at[lax.rem(col - step + size, size)]
        return remote(piece, piece, sends, recvs, step, {"col": lax.rem(col + 1, size)})

    def left(step):
        piece = ref.at[lax.rem(col + step, size)]
        return remote(piece, piece, sends, recvs, size - 1 + step, {"col": lax.rem(col + size - 1, size)})

    for step in range(size):
        for copy, has, goes in ((right, col >= step, col < size - 1), (left, col + step < size, col > 0)):
            if step:

                @pl.when(has)
                def _():
                    copy(step - 1).wait_recv()

            if step < size - 1:

                @pl.when(has & goes)
                def _():
                    copy(step).start()

            if seen is not None and (step or copy is right):

                @pl.when(has)
                def _():
                    seen(lax.rem(col - step + size, size) if copy is right else lax.rem(col + step, size))

    for step in range(size - 1):
        for copy, has, goes in ((right, col >= step, col < size - 1), (left, col + step < size, col > 0)):

            @pl.when(has & goes)
            def _():
                copy(step).wait_send()


def col_scatter(size, part_ref, recv_ref, sends, recvs, prepare):
    col = lax.axis_index("col")

    def right(target, source):
        return pltpu.make_async_remote_copy(
            src_ref=source.at[target], dst_ref=recv_ref.at[0, target], send_sem=sends.at[0], recv_sem=recvs.at[target],
            device_id={"col": lax.rem(col + 1, size)}, device_id_type=MESH,
        )

    def left(target, source):
        return pltpu.make_async_remote_copy(
            src_ref=source.at[target], dst_ref=recv_ref.at[1, target], send_sem=sends.at[1], recv_sem=recvs.at[size + target],
            device_id={"col": lax.rem(col + size - 1, size)}, device_id_type=MESH,
        )

    for time in range(2 * size - 1):
        for copy, side, first, step in ((right, 0, col == 0, time - col), (left, 1, col == size - 1, time - (size - 1 - col))):
            target = size - 1 - step if side == 0 else step
            valid = (step >= 0) & ((target >= col) if side == 0 else (target <= col))
            place = lax.rem(target + 4 * size, size)

            @pl.when(valid & ((target != col) | (side == 0)))
            def _():
                prepare(place)

            @pl.when(valid & jnp.logical_not(first))
            def _():
                copy(place, part_ref).wait_recv()

            @pl.when(valid & jnp.logical_not(first) & (target != col))
            def _():
                recv_ref[side, place] = (
                    recv_ref[side, place].astype(F32) + part_ref[place].astype(F32)
                ).astype(BF16)

            @pl.when(valid & (step > 0))
            def _():
                copy(place, part_ref).wait_send()

            @pl.when(valid & (target != col) & first)
            def _():
                copy(place, part_ref).start()

            @pl.when(valid & (target != col) & jnp.logical_not(first))
            def _():
                copy(place, recv_ref.at[side]).start()


VM = pl.BlockSpec(memory_space=pltpu.VMEM)


def params(ident):
    return pltpu.CompilerParams(collective_id=ident, has_side_effects=True, vmem_limit_bytes=VMEM_LIMIT)


def first_kernel(
    size, act_ref, cot_ref, small_ref, qkv_ref, out_ref,
    x_ref, first_ref, inv_ref, tok_ref, smalls_ref, qkvs_ref, outs_ref,
    got_ref, zq_ref, zo_ref, s1, r1, s2, r2, s3, r3, szq, rzq, szo, rzo, srow, rrow, score, rcore,
):
    row, col, core = lax.axis_index("row"), lax.axis_index("col"), lax.axis_index("dp")
    length, width = act_ref.shape
    quarter = length // size
    small_rows = small_ref.shape[0]
    gain_row = 2 * length // 128
    x_ref[row] = act_ref[...]
    smalls_ref[row] = small_ref[...]
    blocks = ((qkv_ref, zq_ref, qkvs_ref, szq, rzq), (out_ref, zo_ref, outs_ref, szo, rzo))
    for block, line, _, _, _ in blocks:
        share = block.shape[0] // 2
        line[col] = block[pl.ds(pl.multiple_of(core * share, 16), share)]
    greet(row_size=size, col_size=size, dp_size=2)
    gather = RowGather(size, x_ref, s1, r1)
    smalls = [
        remote(small_ref, smalls_ref.at[row], s3, r3, mask - 1, {"row": row ^ mask}) for mask in range(1, size)
    ]
    for move in smalls:
        move.start()
    gather.start()
    moves = [
        remote(cot_ref.at[pl.ds((row ^ mask) * quarter, quarter)], got_ref.at[row], s2, r2, mask - 1, {"row": row ^ mask})
        for mask in range(1, size)
    ]
    got_ref[row] = cot_ref[pl.ds(pl.multiple_of(row * quarter, 16), quarter)]

    def half(ref, place):
        share = ref.shape[1] // 2
        return ref.at[place, pl.ds(pl.multiple_of(core * share, 16), share)]

    def hand(which, mask):
        _, line, full, _, _ = blocks[which]
        return remote(line.at[row ^ mask], half(full, row), srow, rrow, which * (size - 1) + mask - 1, {"row": row ^ mask})

    def across(which, mask):
        full = blocks[which][2]
        piece = half(full, row ^ mask)
        return remote(piece, piece, score, rcore, which * size + mask, {"dp": 1 - core})

    def seen(which):
        def act(place):
            _, line, full, _, _ = blocks[which]

            @pl.when(place == row)
            def _():
                share = full.shape[1] // 2
                full[row, pl.ds(pl.multiple_of(core * share, 16), share)] = line[row]
                across(which, 0).start()

            for mask in range(1, size):

                @pl.when(place == row ^ mask)
                def _():
                    hand(which, mask).start()

        return act

    gather.run()
    for move in smalls:
        move.wait()

    for which, (_, line, _, sends, recvs) in enumerate(blocks):
        col_gather(size, line, sends, recvs, seen(which))
        if which == 0:
            for move in moves:
                move.start()

    @pl.loop(0, length // 128)
    def _(i):
        rows = pl.ds(pl.multiple_of(i * 128, 128), 128)
        total = jnp.zeros((128, 1), F32)
        for j in range(size):
            value = x_ref[j, rows].astype(F32)
            total += jnp.sum(value * value, axis=1, keepdims=True)
        inverse = lax.rsqrt(total / (size * width) + EPSILON)
        inv_ref[rows] = inverse
        for j in range(size):
            for k in range(width // 128):
                gain = smalls_ref[j, gain_row + k : gain_row + k + 1]
                value = x_ref[j, rows, k * 128 : (k + 1) * 128].astype(F32)
                first_ref[rows, j * width + k * 128 : j * width + (k + 1) * 128] = (value * inverse * gain).astype(BF16)

    for which in range(2):
        for mask in range(1, size):
            hand(which, mask).wait_recv()
            across(which, mask).start()
    for move in moves:
        move.wait()
    for j in range(size):
        tok_ref[:, j * width : (j + 1) * width] = got_ref[j]
    for which in range(2):
        for mask in range(1, size):
            hand(which, mask).wait_send()
        for mask in range(size):
            across(which, mask).wait()


def first_call(activations, cotangent, small, qkv_weight, out_weight):
    size = lax.axis_size("row")
    length, width = activations.shape
    quarter = length // size
    qkv_cols, heads_cols = qkv_weight.shape[1], out_weight.shape[0]
    dma = pltpu.SemaphoreType.DMA
    return pl.pallas_call(
        functools.partial(first_kernel, size),
        out_shape=(
            jax.ShapeDtypeStruct((size, length, width), BF16),
            jax.ShapeDtypeStruct((length, size * width), BF16),
            jax.ShapeDtypeStruct((length, 1), F32),
            jax.ShapeDtypeStruct((quarter, size * width), BF16),
            jax.ShapeDtypeStruct((size,) + small.shape, F32),
            jax.ShapeDtypeStruct((size,) + qkv_weight.shape, BF16),
            jax.ShapeDtypeStruct((size,) + out_weight.shape, BF16),
        ),
        in_specs=[VM] * 5,
        out_specs=(VM,) * 7,
        scratch_shapes=[
            pltpu.VMEM((size, quarter, width), BF16),
            pltpu.VMEM((size, width // 2, qkv_cols), BF16),
            pltpu.VMEM((size, heads_cols // 2, width), BF16),
        ]
        + [dma((2 * (size - 1),))] * 2
        + [dma((size - 1,))] * 4
        + [dma((2 * (size - 1),))] * 4
        + [dma((2 * (size - 1),))] * 2
        + [dma((2 * size,))] * 2,
        compiler_params=params(1),
    )(activations, cotangent, small, qkv_weight, out_weight)


def turn(values, low):
    return jnp.where(low, -pltpu.roll(values, 128 - HEAD // 2, 1), pltpu.roll(values, HEAD // 2, 1))


def low_columns(rows):
    return lax.broadcasted_iota(jnp.int32, (rows, 128), 1) % HEAD < HEAD // 2


def masked_scores(query, key, seg_col, seg_row, first_row):
    scores = lax.dot_general(query, key, (((1,), (1,)), ((), ())), preferred_element_type=F32)
    rows = lax.broadcasted_iota(jnp.int32, scores.shape, 0) + first_row
    columns = lax.broadcasted_iota(jnp.int32, scores.shape, 1)
    allowed = (seg_col == seg_row) & (rows >= columns)
    return jnp.where(allowed, scores, -1e30)


def attend_kernel(first_ref, weight_ref, cos_ref, sin_ref, segc_ref, segr_ref, q_ref, k_ref, v_ref, o_ref, oh_ref):
    heads, length, _ = q_ref.shape
    kvs = k_ref.shape[0]
    group = heads // kvs
    query_cols = heads * HEAD
    key_cols = (weight_ref.shape[1] - query_cols) // 2
    block = 256

    @pl.loop(0, length // block)
    def _(i):
        rows = pl.ds(pl.multiple_of(i * block, block), block)
        low = low_columns(block)
        cosine, sine = cos_ref[rows], sin_ref[rows]
        whole = jnp.dot(first_ref[rows], weight_ref[...], preferred_element_type=F32)
        for ref, count, start, factor in ((q_ref, heads, 0, HEAD ** (-0.5)), (k_ref, kvs, query_cols, 1.0)):
            for j in range((count + 1) // 2):
                part = whole[:, start + 128 * j : start + 128 * (j + 1)]
                part = ((part * cosine + turn(part, low) * sine) * factor).astype(BF16)
                for side in range(min(2, count - 2 * j)):
                    ref[2 * j + side, rows] = part[:, side * HEAD : (side + 1) * HEAD]
        for j in range(kvs):
            at = query_cols + key_cols + j * HEAD
            v_ref[j, rows] = whole[:, at : at + HEAD].astype(BF16)

    @pl.loop(0, heads)
    def _(head):
        kv = lax.div(head, group)
        for i in range(length // block):
            rows, extent = slice(i * block, (i + 1) * block), (i + 1) * block
            scores = masked_scores(q_ref[head, rows], k_ref[kv, :extent], segc_ref[rows], segr_ref[:, :extent], i * block)
            top = jnp.max(scores, axis=1, keepdims=True)
            weights = jnp.exp(scores - top)
            total = jnp.sum(weights, axis=1, keepdims=True)
            mixed = jnp.dot(weights.astype(BF16), v_ref[kv, :extent], preferred_element_type=F32)
            oh_ref[head, rows] = (mixed / total).astype(BF16)

    for head in range(heads):
        o_ref[:, head * HEAD : (head + 1) * HEAD] = oh_ref[head]


def attend_call(first, weight, cosine, sine, segc, segr, heads, kvs):
    length = first.shape[0]
    return pl.pallas_call(
        attend_kernel,
        out_shape=(
            jax.ShapeDtypeStruct((heads, length, HEAD), BF16),
            jax.ShapeDtypeStruct((kvs, length, HEAD), BF16),
            jax.ShapeDtypeStruct((kvs, length, HEAD), BF16),
            jax.ShapeDtypeStruct((length, heads * HEAD), BF16),
        ),
        in_specs=[VM] * 6,
        out_specs=(VM,) * 4,
        scratch_shapes=[pltpu.VMEM((heads, length, HEAD), BF16)],
        compiler_params=pltpu.CompilerParams(vmem_limit_bytes=VMEM_LIMIT),
    )(first, weight, cosine, sine, segc, segr)


def attend_back_kernel(
    dmid_ref, weight_ref, q_ref, k_ref, v_ref, cos_ref, sin_ref, segc_ref, segr_ref,
    dqkv_ref, inner_ref, do_ref, dq_ref, dk_ref, dv_ref,
):
    heads, length, _ = q_ref.shape
    kvs = k_ref.shape[0]
    group = heads // kvs
    query_cols = heads * HEAD
    key_cols = (dqkv_ref.shape[1] - query_cols) // 2
    block = 256
    parts, _, width = weight_ref.shape
    dk_ref[...] = jnp.zeros_like(dk_ref)
    dv_ref[...] = jnp.zeros_like(dv_ref)
    inner_ref[...] = jnp.zeros_like(inner_ref)

    @pl.loop(0, length // block)
    def _(i):
        rows = pl.ds(pl.multiple_of(i * block, block), block)
        total = jnp.zeros((block, query_cols), F32)
        for j in range(parts):
            total += lax.dot_general(
                dmid_ref[rows, j * width : (j + 1) * width], weight_ref[j], (((1,), (1,)), ((), ())), preferred_element_type=F32
            )
        for head in range(heads):
            do_ref[head, rows] = total[:, head * HEAD : (head + 1) * HEAD].astype(BF16)

    @pl.loop(0, heads)
    def _(head):
        kv = lax.div(head, group)
        for i in range(length // block):
            rows, extent = slice(i * block, (i + 1) * block), (i + 1) * block
            query, keys, grads = q_ref[head, rows], k_ref[kv, :extent], do_ref[head, rows]
            scores = masked_scores(query, keys, segc_ref[rows], segr_ref[:, :extent], i * block)
            top = jnp.max(scores, axis=1, keepdims=True)
            weights = jnp.exp(scores - top)
            weights = weights * (1.0 / jnp.sum(weights, axis=1, keepdims=True))
            back = lax.dot_general(grads, v_ref[kv, :extent], (((1,), (1,)), ((), ())), preferred_element_type=F32)
            dv_ref[kv, :extent] += lax.dot_general(
                weights.astype(BF16), grads, (((0,), (0,)), ((), ())), preferred_element_type=F32
            )
            ds = (weights * (back - jnp.sum(weights * back, axis=1, keepdims=True))).astype(BF16)
            dq = jnp.dot(ds, keys, preferred_element_type=F32)
            inner_ref[rows] += jnp.sum(dq * query.astype(F32), axis=1, keepdims=True)
            dq_ref[head, rows] = dq
            dk_ref[kv, :extent] += lax.dot_general(ds, query, (((0,), (0,)), ((), ())), preferred_element_type=F32)

    @pl.loop(0, length // block)
    def _(i):
        rows = pl.ds(pl.multiple_of(i * block, block), block)
        low = low_columns(block)
        cosine, sine = cos_ref[rows], sin_ref[rows]
        for ref, count, start, factor in ((dq_ref, heads, 0, HEAD ** (-0.5)), (dk_ref, kvs, query_cols, 1.0), (dv_ref, kvs, query_cols + key_cols, None)):
            for j in range((count + 1) // 2):
                sides = [ref[2 * j + side, rows] if 2 * j + side < count else jnp.zeros((block, HEAD), F32) for side in range(2)]
                part = jnp.concatenate(sides, axis=1)
                if factor is not None:
                    part = (part * cosine - turn(part * sine, low)) * factor
                dqkv_ref[rows, start + 128 * j : start + 128 * (j + 1)] = part.astype(BF16)
        more = jnp.zeros((block, 1), F32)
        for kv in range(kvs):
            more += jnp.sum(dk_ref[kv, rows] * k_ref[kv, rows].astype(F32) + dv_ref[kv, rows] * v_ref[kv, rows].astype(F32), axis=1, keepdims=True)
        inner_ref[rows] += more


def attend_back_call(dmid, weight, q, k, v, cosine, sine, segc, segr, columns):
    heads, length, _ = q.shape
    kvs = k.shape[0]
    return pl.pallas_call(
        attend_back_kernel,
        out_shape=(jax.ShapeDtypeStruct((length, columns), BF16), jax.ShapeDtypeStruct((length, 1), F32)),
        in_specs=[VM] * 9,
        out_specs=(VM,) * 2,
        scratch_shapes=[
            pltpu.VMEM((heads, length, HEAD), BF16),
            pltpu.VMEM((heads, length, HEAD), F32),
            pltpu.VMEM((kvs, length, HEAD), F32),
            pltpu.VMEM((kvs, length, HEAD), F32),
        ],
        compiler_params=pltpu.CompilerParams(vmem_limit_bytes=VMEM_LIMIT),
    )(dmid, weight, q, k, v, cosine, sine, segc, segr)


def middle_kernel(rows_n, cols_n, attn_ref, weight_ref, x_ref, gain_ref, mid_ref, second_ref, part_ref, recv_ref, s1, r1, s2, r2):
    row, col = lax.axis_index("row"), lax.axis_index("col")
    quarter, features = mid_ref.shape
    width = features // rows_n
    greet(row_size=rows_n, col_size=cols_n)

    @pl.loop(0, rows_n)
    def _(i):
        own = attn_ref[pl.ds(pl.multiple_of(i * quarter, 16), quarter)]
        for j in range(rows_n):
            part_ref[i, :, j * width : (j + 1) * width] = jnp.dot(own, weight_ref[j], preferred_element_type=F32).astype(BF16)

    def finish(rows, total):
        own = pl.ds(row * quarter + rows.start, rows.size)
        squares = jnp.zeros((rows.size, 1), F32)
        for j in range(rows_n):
            columns = slice(j * width, (j + 1) * width)
            value = total[:, columns] + x_ref[j, own].astype(F32)
            mid_ref[rows, columns] = value
            squares += jnp.sum(value * value, axis=1, keepdims=True)
        inverse = lax.rsqrt(squares / features + EPSILON)
        second_ref[col, rows] = (mid_ref[rows] * inverse * gain_ref[...]).astype(BF16)

    row_scatter(rows_n, part_ref, recv_ref, s1, r1, finish)
    col_gather(cols_n, second_ref, s2, r2)


def middle_call(attn, weight, x, gain):
    rows_n, cols_n = lax.axis_size("row"), lax.axis_size("col")
    length, features = attn.shape[0], weight.shape[0] * weight.shape[2]
    quarter = length // rows_n
    return pl.pallas_call(
        functools.partial(middle_kernel, rows_n, cols_n),
        out_shape=(
            jax.ShapeDtypeStruct((quarter, features), F32),
            jax.ShapeDtypeStruct((cols_n, quarter, features), BF16),
        ),
        in_specs=[VM] * 4,
        out_specs=(VM,) * 2,
        scratch_shapes=[
            pltpu.VMEM((rows_n, quarter, features), BF16),
            pltpu.VMEM((rows_n - 1, quarter, features), BF16),
        ]
        + [pltpu.SemaphoreType.DMA((2 * (rows_n - 1),))] * 2
        + [pltpu.SemaphoreType.DMA((2 * (cols_n - 1),))] * 2,
        compiler_params=params(2),
    )(attn, weight, x, gain)


def back_kernel(rows_n, cols_n, dgate_ref, dup_ref, gate_ref, up_ref, mid_ref, tok_ref, gain_ref, dmid_ref, grad_ref, part_ref, recv_ref, s1, r1, s2, r2):
    row, col = lax.axis_index("row"), lax.axis_index("col")
    quarter, features = mid_ref.shape
    greet(row_size=rows_n, col_size=cols_n)

    def prepare(target):
        tile = 512

        @pl.loop(0, features // tile)
        def _(i):
            columns = pl.ds(i * tile, tile)
            value = lax.dot_general(dgate_ref[target], gate_ref[columns], (((1,), (1,)), ((), ())), preferred_element_type=F32)
            value += lax.dot_general(dup_ref[target], up_ref[columns], (((1,), (1,)), ((), ())), preferred_element_type=F32)
            part_ref[target, :, columns] = value.astype(BF16)

    col_scatter(cols_n, part_ref, recv_ref, s1, r1, prepare)

    grad_ref[...] = jnp.zeros_like(grad_ref)

    @pl.loop(0, quarter // 64)
    def _(i):
        rows = pl.ds(i * 64, 64)
        got = part_ref[col, rows].astype(F32)
        got += jnp.where(col > 0, recv_ref[0, col, rows].astype(F32), 0.0)
        got += jnp.where(col < cols_n - 1, recv_ref[1, col, rows].astype(F32), 0.0)
        middle = mid_ref[rows]
        inverse = lax.rsqrt(jnp.sum(middle * middle, axis=1, keepdims=True) / features + EPSILON)
        weighted = got * gain_ref[...]
        inner = jnp.sum(middle * weighted, axis=1, keepdims=True) / features
        grad_ref[...] += jnp.sum(got * middle * inverse, axis=0, keepdims=True)
        value = tok_ref[rows].astype(F32) + inverse * weighted - middle * (inverse * inverse * inverse * inner)
        dmid_ref[row, rows] = value.astype(BF16)

    gather = RowGather(rows_n, dmid_ref, s2, r2)
    gather.start()
    gather.run()


def back_call(dgate, dup, gate, up, middle, tok, gain):
    rows_n, cols_n = lax.axis_size("row"), lax.axis_size("col")
    quarter, features = middle.shape
    hidden = gate.shape[1]
    return pl.pallas_call(
        functools.partial(back_kernel, rows_n, cols_n),
        out_shape=(
            jax.ShapeDtypeStruct((rows_n, quarter, features), BF16),
            jax.ShapeDtypeStruct((1, features), F32),
        ),
        in_specs=[VM] * 7,
        out_specs=(VM,) * 2,
        scratch_shapes=[
            pltpu.VMEM((cols_n, quarter, features), BF16),
            pltpu.VMEM((2, cols_n, quarter, features), BF16),
        ]
        + [pltpu.SemaphoreType.DMA((2,)), pltpu.SemaphoreType.DMA((2 * cols_n,))]
        + [pltpu.SemaphoreType.DMA((2 * (rows_n - 1),))] * 2,
        compiler_params=params(3),
    )(dgate.reshape(cols_n, quarter, hidden), dup.reshape(cols_n, quarter, hidden), gate, up, middle, tok, gain)


def last_kernel(size, dqkv_ref, weight_ref, out_ref, part_ref, recv_ref, s1, r1):
    greet(row_size=size)

    @pl.loop(0, size)
    def _(i):
        part_ref[i] = lax.dot_general(dqkv_ref[...], weight_ref[i], (((1,), (1,)), ((), ())), preferred_element_type=F32).astype(BF16)

    def finish(rows, total):
        out_ref[rows] = total

    row_scatter(size, part_ref, recv_ref, s1, r1, finish)


def last_call(dqkv, weight):
    size = lax.axis_size("row")
    length = dqkv.shape[0]
    width = weight.shape[0] // size
    return pl.pallas_call(
        functools.partial(last_kernel, size),
        out_shape=jax.ShapeDtypeStruct((length, width), F32),
        in_specs=[VM] * 2,
        out_specs=VM,
        scratch_shapes=[pltpu.VMEM((size, length, width), BF16), pltpu.VMEM((size - 1, length, width), BF16)]
        + [pltpu.SemaphoreType.DMA((2 * (size - 1),))] * 2,
        compiler_params=params(4),
    )(dqkv, weight.reshape(size, width, weight.shape[1]))


def dot(left, right, dims):
    return lax.dot_general(left, right, (dims, ((), ())), preferred_element_type=F32)


def rotary_tables(positions):
    exponent = jnp.arange(0, HEAD, 2).astype(F32) / HEAD
    inverse = jnp.power(F32(THETA), -exponent)
    phase = positions[:, None] * inverse[None, :]
    phase = jnp.concatenate([phase] * (2 * 128 // HEAD), axis=1)
    return (jnp.cos(phase), jnp.sin(phase))


def gather(values, axis_name, axis=0):
    return lax.all_gather(values, axis_name, axis=axis, tiled=True)


def scatter(values, axis_name, axis=0):
    return lax.psum_scatter(values.astype(BF16), axis_name, scatter_dimension=axis, tiled=True)


def swap(values):
    rows, cols = lax.axis_size("row"), lax.axis_size("col")
    return lax.ppermute(values, ("row", "col"), [(r * cols + c, c * cols + r) for r in range(rows) for c in range(cols)])


def gather_shared(values):
    share = values.shape[0] // lax.axis_size("dp")
    part = lax.dynamic_slice_in_dim(values, lax.axis_index("dp") * share, share, 0)
    return lax.all_gather(part, ("row", "dp"), axis=0, tiled=True)


def scatter_shared(values):
    part = scatter(values, ("row", "dp"))
    return gather(part, "dp").astype(F32)


def local(
    activations, segments, positions, first_gain, query_weight, key_weight, value_weight, out_weight,
    second_gain, gate_weight, up_weight, down_weight, cotangent,
):
    rows = lax.axis_size("row")
    row, col = lax.axis_index("row"), lax.axis_index("col")
    length, width = activations.shape
    features = rows * width
    query_cols, key_cols = query_weight.shape[1], key_weight.shape[1]
    heads, kvs = query_cols // HEAD, key_cols // HEAD
    hidden_cols = gate_weight.shape[1]
    spare = jnp.zeros((width, -key_cols % 128), BF16)
    key_span = key_cols + spare.shape[1]
    qkv_cols = query_cols + 2 * key_span

    small = jnp.concatenate([segments.astype(F32), positions.astype(F32), first_gain, second_gain]).reshape(-1, 128)
    qkv_weight = jnp.concatenate([query_weight, key_weight, spare, value_weight, spare], axis=1)
    x_blocks, first, inv1, cot_tok, smalls, qkv_all, out_all_w = first_call(activations, cotangent, small, qkv_weight, out_weight)
    qkv_all = qkv_all.reshape(features, qkv_cols)
    smalls = smalls.reshape(rows, -1)
    own = lax.dynamic_slice_in_dim(smalls, col, 1, 0)[0]
    segment_own, position_own = own[:length], own[length : 2 * length]
    gain2 = smalls[:, 2 * length + width :].reshape(1, features)

    gate_all = gather_shared(gate_weight)
    up_all = gather_shared(up_weight)
    cot_all = gather(cot_tok, "col")
    down_all = gather_shared(down_weight).reshape(rows, hidden_cols, width)

    cosine, sine = rotary_tables(position_own)
    segc, segr = segment_own[:, None], segment_own[None]
    q, k, v, attn = attend_call(first, qkv_all, cosine, sine, segc, segr, heads, kvs)
    middle, second_all = middle_call(attn, out_all_w, x_blocks, gain2)
    second_all = second_all.reshape(-1, features)
    gate = dot(second_all, gate_all, ((1,), (0,)))
    up = dot(second_all, up_all, ((1,), (0,)))
    sigma = jax.nn.sigmoid(gate)
    swish = gate * sigma
    hidden = (swish * up).astype(BF16)
    tokens = hidden.shape[0]
    down_part = lax.dot_general(hidden, down_all, (((1,), (1,)), ((), ())), preferred_element_type=F32).reshape(tokens, features)
    out_tok = (middle + scatter(down_part, "col").astype(F32)).astype(BF16)
    block_out = lax.all_to_all(out_tok, "row", 1, 0, tiled=True)

    cot_split = cot_all.reshape(tokens, rows, width)
    dhidden = lax.dot_general(cot_split, down_all, (((1, 2), (0, 2)), ((), ())), preferred_element_type=F32)
    swish_grad = sigma * (1.0 + gate * (1.0 - sigma))
    dgate = (dhidden * up * swish_grad).astype(BF16)
    dup = (dhidden * swish).astype(BF16)
    dmid_all, gain2_grad = back_call(dgate, dup, gate_all, up_all, middle, cot_tok, gain2)
    dmid_all, gain2_grad = dmid_all.reshape(length, features), gain2_grad[0]

    dqkv, inner1 = attend_back_call(dmid_all, out_all_w, q, k, v, cosine, sine, segc, segr, qkv_cols)
    inner1 = lax.psum(inner1, "row") / (inv1 * features)
    dfirst = last_call(dqkv, qkv_all)
    own_x = activations.astype(F32)
    dmid_own = lax.dynamic_slice_in_dim(dmid_all, row * width, width, 1).astype(F32)
    input_grad = dmid_own + inv1 * first_gain[None] * dfirst - own_x * (inv1 * inv1 * inv1 * inner1)
    gain1_grad = lax.psum(jnp.sum(dfirst * own_x * inv1, axis=0), ("dp", "col"))
    gain2_grad = lax.psum(gain2_grad, ("dp", "row", "col"))
    gain2_grad = lax.dynamic_slice_in_dim(gain2_grad, row * width, width, 0)

    down_grad = lax.dot_general(hidden, cot_split, (((0,), (0,)), ((), ())), preferred_element_type=F32)
    down_grad = scatter_shared(down_grad.transpose(1, 0, 2).reshape(rows * hidden_cols, width))
    gate_grad = scatter_shared(dot(second_all, dgate, ((0,), (0,))))
    up_grad = scatter_shared(dot(second_all, dup, ((0,), (0,))))
    out_grad = swap(lax.psum(scatter(dot(attn, dmid_all, ((0,), (0,))), "col", 1), "dp")).astype(F32)
    qkv_grad = swap(lax.psum(scatter(dot(first, dqkv, ((0,), (0,))), "col"), "dp")).astype(F32)
    return (
        block_out,
        input_grad,
        gain1_grad,
        qkv_grad[:, :query_cols],
        qkv_grad[:, query_cols : query_cols + key_cols],
        qkv_grad[:, query_cols + key_span : query_cols + key_span + key_cols],
        out_grad,
        gain2_grad,
        gate_grad,
        up_grad,
        down_grad,
    )


def solution(mesh):
    tokens, block, swapped = P(("dp", "col"), "row"), P("row", "col"), P("col", "row")
    return jax.shard_map(
        local,
        mesh=mesh,
        in_specs=(
            tokens, P(("dp", "row")), P(("dp", "row")), P("row"), block, block, block, swapped,
            P("row"), block, block, swapped, tokens,
        ),
        out_specs=(tokens, tokens, P("row"), block, block, block, swapped, P("row"), block, block, swapped),
        check_vma=False,
    )
```

```python
import functools

import jax
import jax.numpy as jnp
from jax import lax
from jax.experimental import pallas as pl
from jax.experimental.pallas import tpu as pltpu
from jax.sharding import PartitionSpec as P

HEAD = 64
EPSILON = 1e-05
THETA = 500000.0
F32 = jnp.float32
BF16 = jnp.bfloat16


MESH = pl.DeviceIdType.MESH
VMEM_LIMIT = 60 * 1024 * 1024


def greet(row_size=0, col_size=0, dp_size=0):
    barrier = pltpu.get_barrier_semaphore()
    if row_size:
        row = lax.axis_index("row")
        for mask in range(1, row_size):
            pl.semaphore_signal(barrier, inc=1, device_id={"row": row ^ mask}, device_id_type=MESH)
    if col_size:
        col = lax.axis_index("col")

        @pl.when(col > 0)
        def _():
            pl.semaphore_signal(barrier, inc=1, device_id={"col": col - 1}, device_id_type=MESH)

        @pl.when(col < col_size - 1)
        def _():
            pl.semaphore_signal(barrier, inc=1, device_id={"col": col + 1}, device_id_type=MESH)

    if dp_size:
        pl.semaphore_signal(barrier, inc=1, device_id={"dp": 1 - lax.axis_index("dp")}, device_id_type=MESH)
    count = max(row_size - 1, 0) + (1 if dp_size else 0)
    if col_size:
        count = count + jnp.where(col > 0, 1, 0) + jnp.where(col < col_size - 1, 1, 0)
    pl.semaphore_wait(barrier, count)


def remote(src, dst, sends, recvs, place, device):
    return pltpu.make_async_remote_copy(
        src_ref=src, dst_ref=dst, send_sem=sends.at[place], recv_sem=recvs.at[place],
        device_id=device, device_id_type=MESH,
    )


class RowGather:
    def __init__(self, size, ref, sends, recvs, begin=0, count=None, first=0):
        self.size, self.ref, self.sends, self.recvs = size, ref, sends, recvs
        self.bits = size.bit_length() - 1
        self.row = lax.axis_index("row")
        self.begin, self.first = begin, first
        self.half = (count or ref.shape[1]) // 2
        self.all = [self.copies(step) for step in range(self.bits)]

    def rows(self, part):
        return pl.ds(pl.multiple_of(self.begin + part * self.half, 16), self.half)

    def order(self, part):
        return list(range(self.bits)) if part == 0 else list(range(self.bits))[::-1]

    def copies(self, step):
        out = []
        for part in range(2):
            order = self.order(part)
            for item in range(1 << step):
                mask = 0
                for j in range(step):
                    if item >> j & 1:
                        mask |= 1 << order[j]
                piece = self.ref.at[self.row ^ mask, self.rows(part)]
                place = self.first + part * (self.size - 1) + (1 << step) - 1 + item
                out.append(remote(piece, piece, self.sends, self.recvs, place, {"row": self.row ^ (1 << order[step])}))
        return out

    def start(self):
        for step in range(self.bits):
            for part in range(2):
                self.all[step][part << step].start()

    def event(self, step, seen=None):
        for part in range(2):
            order = self.order(part)
            for item in range(1 << step):
                self.all[step][(part << step) + item].wait_recv()
                got = item | 1 << step
                for later in range(step + 1, self.bits):
                    self.all[later][(part << later) + got].start()
                if seen is not None:
                    mask = 0
                    for j in range(step + 1):
                        if got >> j & 1:
                            mask |= 1 << order[j]
                    seen(mask, part)

    def finish(self):
        for step in range(self.bits):
            for copy in self.all[step]:
                copy.wait_send()

    def run(self):
        for step in range(self.bits):
            self.event(step)
        self.finish()


class SharedGather:
    def __init__(self, size, shard, full, copied, sends, recvs, score, rcore, first):
        self.core, self.row = lax.axis_index("dp"), lax.axis_index("row")
        self.size, self.full, self.score, self.rcore, self.first = size, full, score, rcore, first * 2 * (size - 1)
        share = full.shape[1] // 2
        self.own = pltpu.make_async_copy(shard, full.at[self.row], copied.at[first])
        self.gather = RowGather(size, full, sends, recvs, self.core * share, share, self.first)

    def across(self, mask, part):
        piece = self.full.at[self.row ^ mask, self.gather.rows(part)]
        return remote(piece, piece, self.score, self.rcore, self.first + part * (self.size - 1) + mask - 1, {"dp": 1 - self.core})

    def load(self):
        self.own.start()

    def start(self):
        self.own.wait()
        self.gather.start()

    def event(self, step):
        self.gather.event(step, lambda mask, part: self.across(mask, part).start())

    def finish(self):
        self.gather.finish()
        for mask in range(1, self.size):
            for part in range(2):
                self.across(mask, part).wait()

    @staticmethod
    def scratch(size, count):
        dma = pltpu.SemaphoreType.DMA
        return [dma((count,))] + [dma((count * 2 * (size - 1),))] * 4


class RowScatter:
    def __init__(self, size, part_ref, recv_ref, sends, recvs):
        self.size, self.part, self.recv = size, part_ref, recv_ref
        self.bits = size.bit_length() - 1
        self.row = lax.axis_index("row")
        half = part_ref.shape[1] // 2
        self.rows = [pl.ds(part * half, half) for part in range(2)]
        self.plans = []
        for part in range(2):
            order = self.order(part)
            steps = []
            for step in range(self.bits):
                bit, rest = 1 << order[step], order[step + 1 :]
                count = 1 << len(rest)
                copies = []
                for item in range(count - 1, -1, -1):
                    mask = sum(1 << other for j, other in enumerate(rest) if item >> j & 1)
                    place = size - 2 * count + item
                    copies.append((
                        item, mask, place,
                        remote(
                            part_ref.at[self.row ^ mask ^ bit, self.rows[part]], recv_ref.at[place, self.rows[part]],
                            sends, recvs, part * (size - 1) + place, {"row": self.row ^ bit},
                        ),
                    ))
                steps.append(copies)
            self.plans.append(steps)

    def order(self, part):
        return list(range(self.bits)) if part == 0 else list(range(self.bits))[::-1]

    def start(self):
        for part in range(2):
            for _, _, _, copy in self.plans[part][0]:
                copy.start()

    def event(self, step, finish):
        last = step + 1 == self.bits
        for part in range(2):
            rows = self.rows[part]
            for item, mask, place, copy in self.plans[part][step]:
                copy.wait_recv()
                total = self.part[self.row ^ mask, rows].astype(F32) + self.recv[place, rows].astype(F32)
                if last:
                    finish(rows, total)
                    continue
                self.part[self.row ^ mask, rows] = total.astype(BF16)
                for _, mask2, _, copy2 in self.plans[part][step + 1]:
                    if mask2 ^ 1 << self.order(part)[step + 1] == mask:
                        copy2.start()

    def close(self):
        for part in range(2):
            for step in self.plans[part]:
                for _, _, _, copy in step:
                    copy.wait_send()

    def run(self, finish):
        self.start()
        for step in range(self.bits):
            self.event(step, finish)
        self.close()


class ColGather:
    def __init__(self, size, ref, sends, recvs, begin=0, end=None):
        self.size, self.ref, self.sends, self.recvs = size, ref, sends, recvs
        self.begin, self.end = begin, size - 1 if end is None else end
        self.col = lax.axis_index("col")

    def sides(self, step):
        size, col = self.size, self.col
        return (
            (0, lax.rem(col - step + size, size), col >= step, col < size - 1),
            (1, lax.rem(col + step, size), col + step < size, col > 0),
        )

    def copy(self, side, step):
        size, col = self.size, self.col
        piece = self.ref.at[self.sides(step)[side][1]]
        target = lax.rem(col + (1 if side == 0 else size - 1), size)
        return remote(piece, piece, self.sends, self.recvs, side * (size - 1) + step, {"col": target})

    def event(self, step, seen=None):
        for side, place, has, goes in self.sides(step):
            if step > self.begin:

                @pl.when(has)
                def _():
                    self.copy(side, step - 1).wait_recv()

            if step < self.end:

                @pl.when(has & goes)
                def _():
                    self.copy(side, step).start()

            if seen is not None and (step or side == 0):

                @pl.when(has)
                def _():
                    seen(place)

    def finish(self):
        for step in range(self.begin, self.end):
            for side, place, has, goes in self.sides(step):

                @pl.when(has & goes)
                def _():
                    self.copy(side, step).wait_send()

    def run(self):
        for step in range(self.begin, self.end + 1):
            self.event(step)
        self.finish()


class ColScatter:
    def __init__(self, size, part, recv, sends, recvs):
        self.size, self.part, self.recv, self.sends, self.recvs = size, part, recv, sends, recvs
        self.col = lax.axis_index("col")
        self.times = 2 * size - 1

    def copy(self, side, target, source):
        step = 1 if side == 0 else self.size - 1
        return pltpu.make_async_remote_copy(
            src_ref=source.at[target], dst_ref=self.recv.at[side, target], send_sem=self.sends.at[side],
            recv_sem=self.recvs.at[side * self.size + target],
            device_id={"col": lax.rem(self.col + step, self.size)}, device_id_type=MESH,
        )

    def event(self, time, prepare=None):
        size, col = self.size, self.col
        for side, first, step in ((0, col == 0, time - col), (1, col == size - 1, time - (size - 1 - col))):
            target = size - 1 - step if side == 0 else step
            valid = (step >= 0) & ((target >= col) if side == 0 else (target <= col))
            place = lax.rem(target + 4 * size, size)

            if prepare is not None:

                @pl.when(valid & ((target != col) | (side == 0)))
                def _():
                    prepare(place)

            @pl.when(valid & jnp.logical_not(first))
            def _():
                self.copy(side, place, self.part).wait_recv()

            @pl.when(valid & jnp.logical_not(first) & (target != col))
            def _():
                self.recv[side, place] = (self.recv[side, place].astype(F32) + self.part[place].astype(F32)).astype(BF16)

            @pl.when(valid & (step > 0))
            def _():
                self.copy(side, place, self.part).wait_send()

            @pl.when(valid & (target != col) & first)
            def _():
                self.copy(side, place, self.part).start()

            @pl.when(valid & (target != col) & jnp.logical_not(first))
            def _():
                self.copy(side, place, self.recv.at[side]).start()

    def total(self, rows):
        got = self.part[self.col, rows].astype(F32)
        got += jnp.where(self.col > 0, self.recv[0, self.col, rows].astype(F32), 0.0)
        got += jnp.where(self.col < self.size - 1, self.recv[1, self.col, rows].astype(F32), 0.0)
        return got


VM = pl.BlockSpec(memory_space=pltpu.VMEM)


def params(ident):
    return pltpu.CompilerParams(collective_id=ident, has_side_effects=True, vmem_limit_bytes=VMEM_LIMIT)


def keep_near(size, line, near, step):
    col = lax.axis_index("col")
    for side, place, has in ((0, col - step, col >= step), (1, col + step, col + step < size)):

        @pl.when(has)
        def _():
            near[side] = line[lax.rem(place + size, size)]


def take_near(size, line, near, step):
    col = lax.axis_index("col")
    for side, place, has in ((0, col - step, col >= step), (1, col + step, col + step < size)):

        @pl.when(has)
        def _():
            line[lax.rem(place + size, size)] = near[side]


def first_kernel(
    size, act_ref, cot_ref, small_ref, qkv_ref, out_ref,
    x_ref, first_ref, inv_ref, tok_ref, smalls_ref, qkvs_ref, outs_ref,
    near_ref,
    got_ref, zq_ref, zo_ref, zc_ref, s1, r1, s2, r2, s3, r3, szq, rzq, szo, rzo, srow, rrow, score, rcore, szc, rzc,
):
    row, col, core = lax.axis_index("row"), lax.axis_index("col"), lax.axis_index("dp")
    length, width = act_ref.shape
    quarter = length // size
    small_rows = small_ref.shape[0]
    gain_row = 2 * length // 128
    x_ref[row] = act_ref[...]
    smalls_ref[row] = small_ref[...]
    blocks = ((qkv_ref, zq_ref, qkvs_ref, szq, rzq), (out_ref, zo_ref, outs_ref, szo, rzo))
    for block, line, _, _, _ in blocks:
        share = block.shape[0] // 2
        line[col] = block[pl.ds(pl.multiple_of(core * share, 16), share)]
    greet(row_size=size, col_size=size, dp_size=2)
    gather = RowGather(size, x_ref, s1, r1)
    smalls = [
        remote(small_ref, smalls_ref.at[row], s3, r3, mask - 1, {"row": row ^ mask}) for mask in range(1, size)
    ]
    lines = [ColGather(size, line, sends, recvs) for _, line, _, sends, recvs in blocks]
    lines[0].event(0)
    for move in smalls:
        move.start()
    gather.start()
    moves = [
        remote(cot_ref.at[pl.ds((row ^ mask) * quarter, quarter)], got_ref.at[row], s2, r2, mask - 1, {"row": row ^ mask})
        for mask in range(1, size)
    ]
    got_ref[row] = cot_ref[pl.ds(pl.multiple_of(row * quarter, 16), quarter)]

    def half(ref, place):
        share = ref.shape[1] // 2
        return ref.at[place, pl.ds(pl.multiple_of(core * share, 16), share)]

    def hand(which, mask):
        _, line, full, _, _ = blocks[which]
        return remote(line.at[row ^ mask], half(full, row), srow, rrow, which * (size - 1) + mask - 1, {"row": row ^ mask})

    def across(which, mask):
        full = blocks[which][2]
        piece = half(full, row ^ mask)
        return remote(piece, piece, score, rcore, which * size + mask, {"dp": 1 - core})

    def seen(which):
        def act(place):
            _, line, full, _, _ = blocks[which]

            @pl.when(place == row)
            def _():
                share = full.shape[1] // 2
                full[row, pl.ds(pl.multiple_of(core * share, 16), share)] = line[row]
                across(which, 0).start()

            for mask in range(1, size):

                @pl.when(place == row ^ mask)
                def _():
                    hand(which, mask).start()

        return act

    act = seen(0)
    act(col)
    for step in range(1, size - 1):
        lines[0].event(step, act)
    gather.event(0)
    lines[0].event(size - 1, act)
    lines[1].event(0)
    for move in moves:
        move.start()
    for step in range(1, gather.bits):
        gather.event(step)
    for move in smalls:
        move.wait()

    @pl.loop(0, length // 128)
    def _(i):
        rows = pl.ds(pl.multiple_of(i * 128, 128), 128)
        total = jnp.zeros((128, 1), F32)
        for j in range(size):
            value = x_ref[j, rows].astype(F32)
            total += jnp.sum(value * value, axis=1, keepdims=True)
        inverse = lax.rsqrt(total / (size * width) + EPSILON)
        inv_ref[rows] = inverse
        for j in range(size):
            for k in range(width // 128):
                gain = smalls_ref[j, gain_row + k : gain_row + k + 1]
                value = x_ref[j, rows, k * 128 : (k + 1) * 128].astype(F32)
                first_ref[rows, j * width + k * 128 : j * width + (k + 1) * 128] = (value * inverse * gain).astype(BF16)

    for mask in range(1, size):
        hand(0, mask).wait_recv()
        across(0, mask).start()
    act = seen(1)
    act(col)
    lines[1].event(1, act)
    for move in moves:
        move.wait()
    for j in range(size):
        zc_ref[col, :, j * width : (j + 1) * width] = got_ref[j]
    tok_ref[...] = zc_ref[col]
    near = ColGather(size, zc_ref, szc, rzc, 0, 1)
    near.event(0)
    for step in range(2, size):
        lines[1].event(step, act)
    for mask in range(1, size):
        hand(1, mask).wait_recv()
        across(1, mask).start()
    near.event(1)
    keep_near(size, zc_ref, near_ref, 1)
    near.finish()
    gather.finish()
    for line in lines:
        line.finish()
    for which in range(2):
        for mask in range(1, size):
            hand(which, mask).wait_send()
        for mask in range(size):
            across(which, mask).wait()


def first_call(activations, cotangent, small, qkv_weight, out_weight):
    size = lax.axis_size("row")
    length, width = activations.shape
    quarter = length // size
    qkv_cols, heads_cols = qkv_weight.shape[1], out_weight.shape[0]
    dma = pltpu.SemaphoreType.DMA
    return pl.pallas_call(
        functools.partial(first_kernel, size),
        out_shape=(
            jax.ShapeDtypeStruct((size, length, width), BF16),
            jax.ShapeDtypeStruct((length, size * width), BF16),
            jax.ShapeDtypeStruct((length, 1), F32),
            jax.ShapeDtypeStruct((quarter, size * width), BF16),
            jax.ShapeDtypeStruct((size,) + small.shape, F32),
            jax.ShapeDtypeStruct((size,) + qkv_weight.shape, BF16),
            jax.ShapeDtypeStruct((size,) + out_weight.shape, BF16),
            jax.ShapeDtypeStruct((2, quarter, size * width), BF16),
        ),
        in_specs=[VM] * 5,
        out_specs=(VM,) * 8,
        scratch_shapes=[
            pltpu.VMEM((size, quarter, width), BF16),
            pltpu.VMEM((size, width // 2, qkv_cols), BF16),
            pltpu.VMEM((size, heads_cols // 2, width), BF16),
            pltpu.VMEM((size, quarter, size * width), BF16),
        ]
        + [dma((2 * (size - 1),))] * 2
        + [dma((size - 1,))] * 4
        + [dma((2 * (size - 1),))] * 4
        + [dma((2 * (size - 1),))] * 2
        + [dma((2 * size,))] * 2
        + [dma((2 * (size - 1),))] * 2,
        compiler_params=params(1),
    )(activations, cotangent, small, qkv_weight, out_weight)


def turn(values, low):
    return jnp.where(low, -pltpu.roll(values, 128 - HEAD // 2, 1), pltpu.roll(values, HEAD // 2, 1))


def low_columns(rows):
    return lax.broadcasted_iota(jnp.int32, (rows, 128), 1) % HEAD < HEAD // 2


def masked_scores(query, key, seg_col, seg_row, first_row):
    scores = lax.dot_general(query, key, (((1,), (1,)), ((), ())), preferred_element_type=F32)
    rows = lax.broadcasted_iota(jnp.int32, scores.shape, 0) + first_row
    columns = lax.broadcasted_iota(jnp.int32, scores.shape, 1)
    allowed = (seg_col == seg_row) & (rows >= columns)
    return jnp.where(allowed, scores, -1e30)


def attend_kernel(
    size, first_ref, weight_ref, cos_ref, sin_ref, segc_ref, segr_ref, near_ref, gate_ref,
    q_ref, k_ref, v_ref, o_ref, next_ref, gates_ref, oh_ref, zc_ref, szc, rzc, *shared,
):
    bulk = SharedGather(size, gate_ref, gates_ref, *shared, 0)
    bulk.load()
    take_near(size, zc_ref, near_ref, 1)
    greet(row_size=size, col_size=size, dp_size=2)
    bulk.start()
    line = ColGather(size, zc_ref, szc, rzc, 1, 2)
    line.event(1)
    heads, length, _ = q_ref.shape
    kvs = k_ref.shape[0]
    group = heads // kvs
    query_cols = heads * HEAD
    key_cols = (weight_ref.shape[1] - query_cols) // 2
    block = 256

    @pl.loop(0, length // block)
    def _(i):
        rows = pl.ds(pl.multiple_of(i * block, block), block)
        low = low_columns(block)
        cosine, sine = cos_ref[rows], sin_ref[rows]
        whole = jnp.dot(first_ref[rows], weight_ref[...], preferred_element_type=F32)
        for ref, count, start, factor in ((q_ref, heads, 0, HEAD ** (-0.5)), (k_ref, kvs, query_cols, 1.0)):
            for j in range((count + 1) // 2):
                part = whole[:, start + 128 * j : start + 128 * (j + 1)]
                part = ((part * cosine + turn(part, low) * sine) * factor).astype(BF16)
                for side in range(min(2, count - 2 * j)):
                    ref[2 * j + side, rows] = part[:, side * HEAD : (side + 1) * HEAD]
        for j in range(kvs):
            at = query_cols + key_cols + j * HEAD
            v_ref[j, rows] = whole[:, at : at + HEAD].astype(BF16)

    @pl.loop(0, heads)
    def _(head):
        kv = lax.div(head, group)
        for i in range(length // block):
            rows, extent = slice(i * block, (i + 1) * block), (i + 1) * block
            scores = masked_scores(q_ref[head, rows], k_ref[kv, :extent], segc_ref[rows], segr_ref[:, :extent], i * block)
            top = jnp.max(scores, axis=1, keepdims=True)
            weights = jnp.exp(scores - top)
            total = jnp.sum(weights, axis=1, keepdims=True)
            mixed = jnp.dot(weights.astype(BF16), v_ref[kv, :extent], preferred_element_type=F32)
            oh_ref[head, rows] = (mixed / total).astype(BF16)

    for head in range(heads):
        o_ref[:, head * HEAD : (head + 1) * HEAD] = oh_ref[head]
    for step in range(bulk.gather.bits):
        bulk.event(step)
    line.event(2)
    keep_near(size, zc_ref, next_ref, 2)
    line.finish()
    bulk.finish()


def attend_call(first, weight, cosine, sine, segc, segr, near, gate, heads, kvs):
    size = lax.axis_size("row")
    length = first.shape[0]
    dma = pltpu.SemaphoreType.DMA
    return pl.pallas_call(
        functools.partial(attend_kernel, size),
        out_shape=(
            jax.ShapeDtypeStruct((heads, length, HEAD), BF16),
            jax.ShapeDtypeStruct((kvs, length, HEAD), BF16),
            jax.ShapeDtypeStruct((kvs, length, HEAD), BF16),
            jax.ShapeDtypeStruct((length, heads * HEAD), BF16),
            jax.ShapeDtypeStruct(near.shape, BF16),
            jax.ShapeDtypeStruct((size,) + gate.shape, BF16),
        ),
        in_specs=[VM] * 8,
        out_specs=(VM,) * 5 + (pl.BlockSpec(memory_space=pl.ANY),),
        scratch_shapes=[
            pltpu.VMEM((heads, length, HEAD), BF16),
            pltpu.VMEM((size,) + near.shape[1:], BF16),
            dma((2 * (size - 1),)), dma((2 * (size - 1),)),
        ]
        + SharedGather.scratch(size, 1),
        compiler_params=params(6),
        cost_estimate=cost(45),
    )(first, weight, cosine, sine, segc, segr, near, gate)


class swap_halves:
    def __init__(self, part, other, sends, recvs):
        core = lax.axis_index("dp")
        share = part.shape[1] // 2
        self.move = remote(
            part.at[:, pl.ds(pl.multiple_of((1 - core) * share, 16), share)], other, sends, recvs, 0, {"dp": 1 - core}
        )

    def start(self):
        self.move.start()

    def wait(self):
        self.move.wait()


def add_halves(part, other, share):
    rows = pl.ds(pl.multiple_of(lax.axis_index("dp") * share.shape[1], 16), share.shape[1])
    for j in range(part.shape[0]):
        share[j] = (part[j, rows].astype(F32) + other[j].astype(F32)).astype(BF16)


def row_moves(size, source, target, sends, recvs, first, begin):
    row = lax.axis_index("row")
    if begin:
        target[row] = source[row]
    for mask in range(1, size):
        move = remote(source.at[row ^ mask], target.at[row], sends, recvs, first + mask - 1, {"row": row ^ mask})
        if begin:
            move.start()
        else:
            move.wait()


def cost(micros):
    return pl.CostEstimate(flops=int(micros * 1e9), bytes_accessed=1 << 20, transcendentals=0)


def attend_back_kernel(
    dmid_ref, weight_ref, q_ref, k_ref, v_ref, cos_ref, sin_ref, segc_ref, segr_ref,
    attn_ref, down_ref, mid_ref,
    dqkv_ref, inner_ref, blk_ref, line_ref, do_ref, dq_ref, dk_ref, dv_ref,
    recv_ref, part_ref, other_ref, share_ref, s1, r1, score, rcore, srow, rrow,
):
    row, core = lax.axis_index("row"), lax.axis_index("dp")
    cols_n = down_ref.shape[0]
    heads, length, _ = q_ref.shape
    kvs = k_ref.shape[0]
    group = heads // kvs
    query_cols = heads * HEAD
    key_cols = (dqkv_ref.shape[1] - query_cols) // 2
    block = 256
    parts, _, width = weight_ref.shape
    greet(row_size=parts, col_size=cols_n, dp_size=2)
    line = ColScatter(cols_n, down_ref, recv_ref, s1, r1)
    line.event(0)
    for j in range(parts):
        part_ref[j] = lax.dot_general(
            attn_ref[...], dmid_ref[:, j * width : (j + 1) * width], (((0,), (0,)), ((), ())), preferred_element_type=F32
        ).astype(BF16)
    cross = swap_halves(part_ref, other_ref, score, rcore)
    cross.start()
    dk_ref[...] = jnp.zeros_like(dk_ref)
    dv_ref[...] = jnp.zeros_like(dv_ref)
    inner_ref[...] = jnp.zeros_like(inner_ref)

    @pl.loop(0, length // block)
    def _(i):
        rows = pl.ds(pl.multiple_of(i * block, block), block)
        total = jnp.zeros((block, query_cols), F32)
        for j in range(parts):
            total += lax.dot_general(
                dmid_ref[rows, j * width : (j + 1) * width], weight_ref[j], (((1,), (1,)), ((), ())), preferred_element_type=F32
            )
        for head in range(heads):
            do_ref[head, rows] = total[:, head * HEAD : (head + 1) * HEAD].astype(BF16)

    @pl.loop(0, heads)
    def _(head):
        @pl.when(head == min(1, heads - 1))
        def _():
            cross.wait()
            add_halves(part_ref, other_ref, share_ref)
            row_moves(parts, share_ref, line_ref, srow, rrow, 0, True)

        @pl.when(head == heads // 2)
        def _():
            line.event(1)

        kv = lax.div(head, group)
        for i in range(length // block):
            rows, extent = slice(i * block, (i + 1) * block), (i + 1) * block
            query, keys, grads = q_ref[head, rows], k_ref[kv, :extent], do_ref[head, rows]
            scores = masked_scores(query, keys, segc_ref[rows], segr_ref[:, :extent], i * block)
            top = jnp.max(scores, axis=1, keepdims=True)
            weights = jnp.exp(scores - top)
            weights = weights * (1.0 / jnp.sum(weights, axis=1, keepdims=True))
            back = lax.dot_general(grads, v_ref[kv, :extent], (((1,), (1,)), ((), ())), preferred_element_type=F32)
            dv_ref[kv, :extent] += lax.dot_general(
                weights.astype(BF16), grads, (((0,), (0,)), ((), ())), preferred_element_type=F32
            )
            ds = (weights * (back - jnp.sum(weights * back, axis=1, keepdims=True))).astype(BF16)
            dq = jnp.dot(ds, keys, preferred_element_type=F32)
            inner_ref[rows] += jnp.sum(dq * query.astype(F32), axis=1, keepdims=True)
            dq_ref[head, rows] = dq
            dk_ref[kv, :extent] += lax.dot_general(ds, query, (((0,), (0,)), ((), ())), preferred_element_type=F32)

    @pl.loop(0, length // block)
    def _(i):
        rows = pl.ds(pl.multiple_of(i * block, block), block)
        low = low_columns(block)
        cosine, sine = cos_ref[rows], sin_ref[rows]
        for ref, count, start, factor in ((dq_ref, heads, 0, HEAD ** (-0.5)), (dk_ref, kvs, query_cols, 1.0), (dv_ref, kvs, query_cols + key_cols, None)):
            for j in range((count + 1) // 2):
                sides = [ref[2 * j + side, rows] if 2 * j + side < count else jnp.zeros((block, HEAD), F32) for side in range(2)]
                part = jnp.concatenate(sides, axis=1)
                if factor is not None:
                    part = (part * cosine - turn(part * sine, low)) * factor
                dqkv_ref[rows, start + 128 * j : start + 128 * (j + 1)] = part.astype(BF16)
        more = jnp.zeros((block, 1), F32)
        for kv in range(kvs):
            more += jnp.sum(dk_ref[kv, rows] * k_ref[kv, rows].astype(F32) + dv_ref[kv, rows] * v_ref[kv, rows].astype(F32), axis=1, keepdims=True)
        inner_ref[rows] += more

    for time in range(2, line.times):
        line.event(time)
    for j in range(parts):
        columns = slice(j * width, (j + 1) * width)
        blk_ref[j] = (mid_ref[:, columns] + line.total(slice(None))[:, columns]).astype(BF16)
    row_moves(parts, share_ref, line_ref, srow, rrow, 0, False)


def attend_back_call(dmid, weight, q, k, v, cosine, sine, segc, segr, columns, attn, down, middle):
    rows_n, cols_n = lax.axis_size("row"), lax.axis_size("col")
    _, heads_cols, width = weight.shape
    quarter = middle.shape[0]
    dma = pltpu.SemaphoreType.DMA
    heads, length, _ = q.shape
    kvs = k.shape[0]
    return pl.pallas_call(
        attend_back_kernel,
        out_shape=(
            jax.ShapeDtypeStruct((length, columns), BF16),
            jax.ShapeDtypeStruct((length, 1), F32),
            jax.ShapeDtypeStruct((rows_n, quarter, width), BF16),
            jax.ShapeDtypeStruct((rows_n, heads_cols // 2, width), BF16),
        ),
        in_specs=[VM] * 12,
        out_specs=(VM,) * 4,
        scratch_shapes=[
            pltpu.VMEM((heads, length, HEAD), BF16),
            pltpu.VMEM((heads, length, HEAD), F32),
            pltpu.VMEM((kvs, length, HEAD), F32),
            pltpu.VMEM((kvs, length, HEAD), F32),
            pltpu.VMEM((2,) + down.shape, BF16),
            pltpu.VMEM(weight.shape, BF16),
            pltpu.VMEM((rows_n, heads_cols // 2, width), BF16),
            pltpu.VMEM((rows_n, heads_cols // 2, width), BF16),
            dma((2,)), dma((2 * cols_n,)), dma((1,)), dma((1,)), dma((rows_n - 1,)), dma((rows_n - 1,)),
        ],
        compiler_params=params(5),
        cost_estimate=cost(80),
    )(dmid, weight, q, k, v, cosine, sine, segc, segr, attn, down, middle)


def middle_kernel(
    rows_n, cols_n, attn_ref, weight_ref, x_ref, gain_ref, tok_ref, near_ref, next_ref, up_ref, down_ref,
    mid_ref, second_ref, cot_ref, ups_ref, downs_ref, part_ref, recv_ref, s1, r1, s2, r2, szc, rzc, *shared,
):
    row, col = lax.axis_index("row"), lax.axis_index("col")
    quarter, features = mid_ref.shape
    width = features // rows_n
    bulks = [SharedGather(rows_n, up_ref, ups_ref, *shared, 0), SharedGather(rows_n, down_ref, downs_ref, *shared, 1)]
    for bulk in bulks:
        bulk.load()
    cot_ref[col] = tok_ref[...]
    take_near(cols_n, cot_ref, near_ref, 1)
    take_near(cols_n, cot_ref, next_ref, 2)
    greet(row_size=rows_n, col_size=cols_n, dp_size=2)
    rest = ColGather(cols_n, cot_ref, szc, rzc, 2)
    rest.event(2)

    @pl.loop(0, rows_n)
    def _(i):
        own = attn_ref[pl.ds(pl.multiple_of(i * quarter, 16), quarter)]
        for j in range(rows_n):
            part_ref[i, :, j * width : (j + 1) * width] = jnp.dot(own, weight_ref[j], preferred_element_type=F32).astype(BF16)

    def finish(rows, total):
        own = pl.ds(row * quarter + rows.start, rows.size)
        squares = jnp.zeros((rows.size, 1), F32)
        for j in range(rows_n):
            columns = slice(j * width, (j + 1) * width)
            value = total[:, columns] + x_ref[j, own].astype(F32)
            mid_ref[rows, columns] = value
            squares += jnp.sum(value * value, axis=1, keepdims=True)
        inverse = lax.rsqrt(squares / features + EPSILON)
        second_ref[col, rows] = (mid_ref[rows] * inverse * gain_ref[...]).astype(BF16)

    RowScatter(rows_n, part_ref, recv_ref, s1, r1).run(finish)
    line = ColGather(cols_n, second_ref, s2, r2)
    line.event(0)
    for bulk in bulks:
        bulk.start()
    for step in range(3, cols_n):
        rest.event(step)
    rest.finish()
    line.event(1)
    bits = bulks[0].gather.bits
    for bulk in bulks:
        bulk.event(0)
    for step in range(2, cols_n):
        line.event(step)
    for step in range(1, bits):
        for bulk in bulks:
            bulk.event(step)
    for bulk in bulks:
        bulk.finish()
    line.finish()


def middle_call(attn, weight, x, gain, tok, near, following, up, down):
    rows_n, cols_n = lax.axis_size("row"), lax.axis_size("col")
    length, features = attn.shape[0], weight.shape[0] * weight.shape[2]
    quarter = length // rows_n
    dma = pltpu.SemaphoreType.DMA
    anywhere = pl.BlockSpec(memory_space=pl.ANY)
    return pl.pallas_call(
        functools.partial(middle_kernel, rows_n, cols_n),
        out_shape=(
            jax.ShapeDtypeStruct((quarter, features), F32),
            jax.ShapeDtypeStruct((cols_n, quarter, features), BF16),
            jax.ShapeDtypeStruct((cols_n, quarter, features), BF16),
            jax.ShapeDtypeStruct((rows_n,) + up.shape, BF16),
            jax.ShapeDtypeStruct((rows_n,) + down.shape, BF16),
        ),
        in_specs=[VM] * 9,
        out_specs=(VM, VM, VM, anywhere, anywhere),
        scratch_shapes=[
            pltpu.VMEM((rows_n, quarter, features), BF16),
            pltpu.VMEM((rows_n - 1, quarter, features), BF16),
        ]
        + [dma((2 * (rows_n - 1),))] * 2
        + [dma((2 * (cols_n - 1),))] * 4
        + SharedGather.scratch(rows_n, 2),
        compiler_params=params(2),
        cost_estimate=cost(130),
    )(attn, weight, x, gain, tok, near, following, up, down)


def back_kernel(rows_n, cols_n, dgate_ref, dup_ref, gate_ref, up_ref, mid_ref, tok_ref, gain_ref, dmid_ref, grad_ref, part_ref, recv_ref, s1, r1, s2, r2):
    row, col = lax.axis_index("row"), lax.axis_index("col")
    quarter, features = mid_ref.shape
    greet(row_size=rows_n, col_size=cols_n)

    def prepare(target):
        tile = 512

        @pl.loop(0, features // tile)
        def _(i):
            columns = pl.ds(i * tile, tile)
            value = lax.dot_general(dgate_ref[target], gate_ref[columns], (((1,), (1,)), ((), ())), preferred_element_type=F32)
            value += lax.dot_general(dup_ref[target], up_ref[columns], (((1,), (1,)), ((), ())), preferred_element_type=F32)
            part_ref[target, :, columns] = value.astype(BF16)

    line = ColScatter(cols_n, part_ref, recv_ref, s1, r1)
    for time in range(line.times):
        line.event(time, prepare)

    grad_ref[...] = jnp.zeros_like(grad_ref)

    @pl.loop(0, quarter // 64)
    def _(i):
        rows = pl.ds(i * 64, 64)
        got = line.total(rows)
        middle = mid_ref[rows]
        inverse = lax.rsqrt(jnp.sum(middle * middle, axis=1, keepdims=True) / features + EPSILON)
        weighted = got * gain_ref[...]
        inner = jnp.sum(middle * weighted, axis=1, keepdims=True) / features
        grad_ref[...] += jnp.sum(got * middle * inverse, axis=0, keepdims=True)
        value = tok_ref[rows].astype(F32) + inverse * weighted - middle * (inverse * inverse * inverse * inner)
        dmid_ref[row, rows] = value.astype(BF16)

    gather = RowGather(rows_n, dmid_ref, s2, r2)
    gather.start()
    gather.run()


def back_call(dgate, dup, gate, up, middle, tok, gain):
    rows_n, cols_n = lax.axis_size("row"), lax.axis_size("col")
    quarter, features = middle.shape
    hidden = gate.shape[1]
    return pl.pallas_call(
        functools.partial(back_kernel, rows_n, cols_n),
        out_shape=(
            jax.ShapeDtypeStruct((rows_n, quarter, features), BF16),
            jax.ShapeDtypeStruct((1, features), F32),
        ),
        in_specs=[VM] * 7,
        out_specs=(VM,) * 2,
        scratch_shapes=[
            pltpu.VMEM((cols_n, quarter, features), BF16),
            pltpu.VMEM((2, cols_n, quarter, features), BF16),
        ]
        + [pltpu.SemaphoreType.DMA((2,)), pltpu.SemaphoreType.DMA((2 * cols_n,))]
        + [pltpu.SemaphoreType.DMA((2 * (rows_n - 1),))] * 2,
        compiler_params=params(3),
    )(dgate.reshape(cols_n, quarter, hidden), dup.reshape(cols_n, quarter, hidden), gate, up, middle, tok, gain)


def last_kernel(
    size, dqkv_ref, weight_ref, first_ref, outline_ref, blk_ref, inner_ref, act_ref, inv_ref, grad2_ref,
    out_ref, block_ref, inners_ref, gains_ref, gqkv_ref, gout_ref,
    part_ref, recv_ref, qpart_ref, qother_ref, qshare_ref, qline_ref, qrecv_ref, orecv_ref, rgain_ref, pair_ref, pairs_ref,
    s1, r1, sblk, rblk, sinn, rinn, score, rcore, srow, rrow, so, ro, sq, rq, sg, rg, sp, rp, sf, rf,
):
    row, col, core = lax.axis_index("row"), lax.axis_index("col"), lax.axis_index("dp")
    length, width = act_ref.shape
    quarter = length // size
    barrier = pltpu.get_barrier_semaphore()
    peers = [{"row": row ^ mask} for mask in range(1, size)]
    others = [{"col": lax.rem(col + k, size)} for k in range(1, size)]
    others += [{"col": lax.rem(col + k, size), "dp": 1 - core} for k in range(size)]
    for peer in peers + others:
        pl.semaphore_signal(barrier, inc=1, device_id=peer, device_id_type=MESH)
    pl.semaphore_wait(barrier, len(peers) + len(others))

    scatter = RowScatter(size, part_ref, recv_ref, s1, r1)
    inners_ref[row] = inner_ref[...]
    rgain_ref[row] = grad2_ref[row]
    small = []
    for mask in range(1, size):
        small.append(remote(inner_ref, inners_ref.at[row], sinn, rinn, mask - 1, {"row": row ^ mask}))
        small.append(remote(grad2_ref.at[row ^ mask], rgain_ref.at[row], sg, rg, mask - 1, {"row": row ^ mask}))
    for move in small:
        move.start()
    oline = ColScatter(size, outline_ref, orecv_ref, so, ro)
    oline.event(0)

    @pl.loop(0, size)
    def _(j):
        columns = pl.ds(pl.multiple_of(j * width, 128), width)
        qpart_ref[j] = lax.dot_general(
            first_ref[:, columns], dqkv_ref[...], (((0,), (0,)), ((), ())), preferred_element_type=F32
        ).astype(BF16)

    cross = swap_halves(qpart_ref, qother_ref, score, rcore)
    cross.start()
    oline.event(1)

    @pl.loop(0, size)
    def _(j):
        part_ref[j] = lax.dot_general(dqkv_ref[...], weight_ref[j], (((1,), (1,)), ((), ())), preferred_element_type=F32).astype(BF16)

    cross.wait()
    add_halves(qpart_ref, qother_ref, qshare_ref)
    row_moves(size, qshare_ref, qline_ref, srow, rrow, 0, True)
    scatter.start()
    for time in range(2, oline.times):
        oline.event(time)
    share_o = outline_ref.shape[1]
    share_q = qline_ref.shape[1]

    def across(ref, share, which):
        piece = ref.at[pl.ds(pl.multiple_of(core * share, 8), share)]
        return remote(piece, piece, sf, rf, which, {"dp": 1 - core})

    gout_ref[pl.ds(pl.multiple_of(core * share_o, 8), share_o)] = oline.total(slice(None))
    across(gout_ref, share_o, 0).start()

    block_ref[pl.ds(pl.multiple_of(row * quarter, 16), quarter)] = blk_ref[row]
    for mask in range(1, size):
        remote(
            blk_ref.at[row ^ mask], block_ref.at[pl.ds(pl.multiple_of(row * quarter, 16), quarter)], sblk, rblk, mask - 1, {"row": row ^ mask}
        ).start()
    row_moves(size, qshare_ref, qline_ref, srow, rrow, 0, False)
    qline = ColScatter(size, qline_ref, qrecv_ref, sq, rq)
    qline.event(0)
    pair_ref[0] = jnp.zeros_like(pair_ref[0])

    def finish(rows, total):
        out_ref[rows] = total
        pair_ref[0] += jnp.sum(total * act_ref[rows].astype(F32) * inv_ref[rows], axis=0, keepdims=True)

    for step in range(scatter.bits - 1):
        scatter.event(step, finish)
    qline.event(1)
    qline.event(2)
    scatter.event(scatter.bits - 1, finish)
    scatter.close()
    for move in small:
        move.wait()
    pair_ref[1] = jnp.sum(rgain_ref[...], axis=0)
    own = core * size + col
    pairs_ref[own] = pair_ref[...]
    for k, peer in enumerate(others):
        remote(pair_ref, pairs_ref.at[own], sp, rp, k, peer).start()
    for time in range(3, qline.times):
        qline.event(time)
    gqkv_ref[pl.ds(pl.multiple_of(core * share_q, 8), share_q)] = qline.total(slice(None))
    across(gqkv_ref, share_q, 1).start()
    for k, peer in enumerate(others):
        remote(pair_ref, pairs_ref.at[own], sp, rp, k, peer).wait()
    gains_ref[...] = jnp.sum(pairs_ref[...], axis=0)
    for mask in range(1, size):
        remote(
            blk_ref.at[row ^ mask], block_ref.at[pl.ds(pl.multiple_of(row * quarter, 16), quarter)], sblk, rblk, mask - 1, {"row": row ^ mask}
        ).wait()
    across(gout_ref, share_o, 0).wait()
    across(gqkv_ref, share_q, 1).wait()


def last_call(dqkv, weight, first, outline, blk, inner, activations, inv1, grad2):
    size = lax.axis_size("row")
    length, width = activations.shape
    columns = weight.shape[1]
    heads_cols = 2 * outline.shape[1]
    dma = pltpu.SemaphoreType.DMA
    count = 2 * size - 1
    return pl.pallas_call(
        functools.partial(last_kernel, size),
        out_shape=(
            jax.ShapeDtypeStruct((length, width), F32),
            jax.ShapeDtypeStruct((length, width), BF16),
            jax.ShapeDtypeStruct((size,) + inner.shape, F32),
            jax.ShapeDtypeStruct((2, 1, width), F32),
            jax.ShapeDtypeStruct((width, columns), F32),
            jax.ShapeDtypeStruct((heads_cols, width), F32),
        ),
        in_specs=[VM] * 9,
        out_specs=(VM,) * 6,
        scratch_shapes=[
            pltpu.VMEM((size, length, width), BF16),
            pltpu.VMEM((size - 1, length, width), BF16),
            pltpu.VMEM((size, width, columns), BF16),
            pltpu.VMEM((size, width // 2, columns), BF16),
            pltpu.VMEM((size, width // 2, columns), BF16),
            pltpu.VMEM((size, width // 2, columns), BF16),
            pltpu.VMEM((2, size, width // 2, columns), BF16),
            pltpu.VMEM((2, size, heads_cols // 2, width), BF16),
            pltpu.VMEM((size, 1, width), F32),
            pltpu.VMEM((2, 1, width), F32),
            pltpu.VMEM((2 * size, 2, 1, width), F32),
        ]
        + [dma((2 * (size - 1),))] * 2
        + [dma((size - 1,))] * 2
        + [dma((size - 1,))] * 2
        + [dma((1,))] * 2
        + [dma((size - 1,))] * 2
        + [dma((2,)), dma((2 * size,))] * 2
        + [dma((size - 1,))] * 2
        + [dma((count,))] * 2
        + [dma((2,))] * 2,
        compiler_params=params(4),
        cost_estimate=cost(80),
    )(dqkv, weight.reshape(size, width, columns), first, outline, blk, inner, activations, inv1, grad2.reshape(size, 1, width))


def weight_grads_kernel(second_ref, cot_ref, dgate_ref, dup_ref, hidden_ref, out_ref):
    which, part = pl.program_id(0), pl.program_id(1)
    span = out_ref.shape[2]
    columns = pl.ds(pl.multiple_of(part * span, 128), span)
    for index, left, right in ((0, second_ref, dgate_ref), (1, second_ref, dup_ref), (2, cot_ref, hidden_ref)):

        @pl.when(which == index)
        def _():
            out_ref[0, 0] = lax.dot_general(
                left[:, columns], right[...], (((0,), (0,)), ((), ())), preferred_element_type=F32
            ).astype(BF16)


def weight_grads_call(second, cot, dgate, dup, hidden):
    parts = 2 * lax.axis_size("row")
    span, columns = second.shape[1] // parts, hidden.shape[1]
    return pl.pallas_call(
        weight_grads_kernel,
        grid=(3, parts),
        out_shape=jax.ShapeDtypeStruct((parts, 3, span, columns), BF16),
        in_specs=[VM] * 5,
        out_specs=pl.BlockSpec((1, 1, span, columns), lambda g, p: (p, g, 0, 0)),
        compiler_params=pltpu.CompilerParams(vmem_limit_bytes=VMEM_LIMIT),
        cost_estimate=cost(30),
    )(second, cot, dgate, dup, hidden)


def dot(left, right, dims):
    return lax.dot_general(left, right, (dims, ((), ())), preferred_element_type=F32)


def rotary_tables(positions):
    exponent = jnp.arange(0, HEAD, 2).astype(F32) / HEAD
    inverse = jnp.power(F32(THETA), -exponent)
    phase = positions[:, None] * inverse[None, :]
    phase = jnp.concatenate([phase] * (2 * 128 // HEAD), axis=1)
    return (jnp.cos(phase), jnp.sin(phase))


def gather(values, axis_name, axis=0):
    return lax.all_gather(values, axis_name, axis=axis, tiled=True)


def local(
    activations, segments, positions, first_gain, query_weight, key_weight, value_weight, out_weight,
    second_gain, gate_weight, up_weight, down_weight, cotangent,
):
    rows = lax.axis_size("row")
    row, col = lax.axis_index("row"), lax.axis_index("col")
    length, width = activations.shape
    features = rows * width
    query_cols, key_cols = query_weight.shape[1], key_weight.shape[1]
    heads, kvs = query_cols // HEAD, key_cols // HEAD
    hidden_cols = gate_weight.shape[1]
    spare = jnp.zeros((width, -key_cols % 128), BF16)
    key_span = key_cols + spare.shape[1]
    qkv_cols = query_cols + 2 * key_span

    small = jnp.concatenate([segments.astype(F32), positions.astype(F32), first_gain, second_gain]).reshape(-1, 128)
    qkv_weight = jnp.concatenate([query_weight, key_weight, spare, value_weight, spare], axis=1)
    x_blocks, first, inv1, cot_tok, smalls, qkv_all, out_all_w, near = first_call(activations, cotangent, small, qkv_weight, out_weight)
    qkv_all = qkv_all.reshape(features, qkv_cols)
    smalls = smalls.reshape(rows, -1)
    own = lax.dynamic_slice_in_dim(smalls, col, 1, 0)[0]
    segment_own, position_own = own[:length], own[length : 2 * length]
    gain2 = smalls[:, 2 * length + width :].reshape(1, features)

    cosine, sine = rotary_tables(position_own)
    segc, segr = segment_own[:, None], segment_own[None]
    q, k, v, attn, following, gate_all = attend_call(first, qkv_all, cosine, sine, segc, segr, near, gate_weight, heads, kvs)
    middle, second_all, cot_all, up_all, down_all = middle_call(
        attn, out_all_w, x_blocks, gain2, cot_tok, near, following, up_weight, down_weight
    )
    gate_all, up_all = gate_all.reshape(features, hidden_cols), up_all.reshape(features, hidden_cols)
    second_all, cot_all = second_all.reshape(-1, features), cot_all.reshape(-1, features)
    gate = dot(second_all, gate_all, ((1,), (0,)))
    up = dot(second_all, up_all, ((1,), (0,)))
    sigma = jax.nn.sigmoid(gate)
    swish = gate * sigma
    hidden = (swish * up).astype(BF16)
    tokens = hidden.shape[0]
    down_part = lax.dot_general(hidden, down_all, (((1,), (1,)), ((), ())), preferred_element_type=F32).reshape(tokens, features)
    down_part = down_part.astype(BF16).reshape(-1, middle.shape[0], features)

    cot_split = cot_all.reshape(tokens, rows, width)
    dhidden = lax.dot_general(cot_split, down_all, (((1, 2), (0, 2)), ((), ())), preferred_element_type=F32)
    swish_grad = sigma * (1.0 + gate * (1.0 - sigma))
    dgate = (dhidden * up * swish_grad).astype(BF16)
    dup = (dhidden * swish).astype(BF16)
    grads = weight_grads_call(second_all, cot_all, dgate, dup, hidden)
    grads, dgate, dup = lax.optimization_barrier((grads, dgate, dup))
    grads = lax.psum_scatter(grads.reshape(-1, hidden_cols), ("row", "dp"), scatter_dimension=0, tiled=True)
    dmid_all, gain2_grad = back_call(dgate, dup, gate_all, up_all, middle, cot_tok, gain2)
    dmid_all = dmid_all.reshape(length, features)

    dqkv, inner1, blk, outline = attend_back_call(
        dmid_all, out_all_w, q, k, v, cosine, sine, segc, segr, qkv_cols, attn, down_part, middle
    )
    dfirst, block_out, inner1, gains, qkv_grad, out_grad = last_call(
        dqkv, qkv_all, first, outline, blk, inner1.reshape(-1, 128), activations, inv1, gain2_grad
    )
    inner1 = jnp.sum(inner1, axis=0).reshape(length, 1) / (inv1 * features)
    own_x = activations.astype(F32)
    dmid_own = lax.dynamic_slice_in_dim(dmid_all, row * width, width, 1).astype(F32)
    input_grad = dmid_own + inv1 * first_gain[None] * dfirst - own_x * (inv1 * inv1 * inv1 * inner1)

    grads, dfirst = lax.optimization_barrier((grads, dfirst))
    grads = gather(grads.reshape(1, 3, -1, hidden_cols), "dp").astype(F32)
    return (
        block_out,
        input_grad,
        gains[0, 0],
        qkv_grad[:, :query_cols],
        qkv_grad[:, query_cols : query_cols + key_cols],
        qkv_grad[:, query_cols + key_span : query_cols + key_span + key_cols],
        out_grad,
        gains[1, 0],
        grads[:, 0].reshape(width, hidden_cols),
        grads[:, 1].reshape(width, hidden_cols),
        grads[:, 2].reshape(width, hidden_cols).T,
    )


def solution(mesh):
    tokens, block, swapped = P(("dp", "col"), "row"), P("row", "col"), P("col", "row")
    return jax.shard_map(
        local,
        mesh=mesh,
        in_specs=(
            tokens, P(("dp", "row")), P(("dp", "row")), P("row"), block, block, block, swapped,
            P("row"), block, block, swapped, tokens,
        ),
        out_specs=(tokens, tokens, P("row"), block, block, block, swapped, P("row"), block, block, swapped),
        check_vma=False,
    )
```

```python
import functools

import jax
import jax.numpy as jnp
from jax import lax
from jax.experimental import pallas as pl
from jax.experimental.pallas import tpu as pltpu
from jax.sharding import PartitionSpec as P

HEAD = 64
EPSILON = 1e-05
THETA = 500000.0
F32 = jnp.float32
BF16 = jnp.bfloat16


MESH = pl.DeviceIdType.MESH
VMEM_LIMIT = 60 * 1024 * 1024


def greet(row_size=0, col_size=0, dp_size=0):
    barrier = pltpu.get_barrier_semaphore()
    if row_size:
        row = lax.axis_index("row")
        for mask in range(1, row_size):
            pl.semaphore_signal(barrier, inc=1, device_id={"row": row ^ mask}, device_id_type=MESH)
    if col_size:
        col = lax.axis_index("col")

        @pl.when(col > 0)
        def _():
            pl.semaphore_signal(barrier, inc=1, device_id={"col": col - 1}, device_id_type=MESH)

        @pl.when(col < col_size - 1)
        def _():
            pl.semaphore_signal(barrier, inc=1, device_id={"col": col + 1}, device_id_type=MESH)

    if dp_size:
        pl.semaphore_signal(barrier, inc=1, device_id={"dp": 1 - lax.axis_index("dp")}, device_id_type=MESH)
    count = max(row_size - 1, 0) + (1 if dp_size else 0)
    if col_size:
        count = count + jnp.where(col > 0, 1, 0) + jnp.where(col < col_size - 1, 1, 0)
    pl.semaphore_wait(barrier, count)


def remote(src, dst, sends, recvs, place, device):
    return pltpu.make_async_remote_copy(
        src_ref=src, dst_ref=dst, send_sem=sends.at[place], recv_sem=recvs.at[place],
        device_id=device, device_id_type=MESH,
    )


class RowGather:
    def __init__(self, size, ref, sends, recvs, begin=0, count=None, first=0):
        self.size, self.ref, self.sends, self.recvs = size, ref, sends, recvs
        self.bits = size.bit_length() - 1
        self.row = lax.axis_index("row")
        self.begin, self.first = begin, first
        self.half = (count or ref.shape[1]) // 2
        self.all = [self.copies(step) for step in range(self.bits)]

    def rows(self, part):
        return pl.ds(pl.multiple_of(self.begin + part * self.half, 16), self.half)

    def order(self, part):
        return list(range(self.bits)) if part == 0 else list(range(self.bits))[::-1]

    def copies(self, step):
        out = []
        for part in range(2):
            order = self.order(part)
            for item in range(1 << step):
                mask = 0
                for j in range(step):
                    if item >> j & 1:
                        mask |= 1 << order[j]
                piece = self.ref.at[self.row ^ mask, self.rows(part)]
                place = self.first + part * (self.size - 1) + (1 << step) - 1 + item
                out.append(remote(piece, piece, self.sends, self.recvs, place, {"row": self.row ^ (1 << order[step])}))
        return out

    def start(self):
        for step in range(self.bits):
            for part in range(2):
                self.all[step][part << step].start()

    def event(self, step, seen=None):
        for part in range(2):
            order = self.order(part)
            for item in range(1 << step):
                self.all[step][(part << step) + item].wait_recv()
                got = item | 1 << step
                for later in range(step + 1, self.bits):
                    self.all[later][(part << later) + got].start()
                if seen is not None:
                    mask = 0
                    for j in range(step + 1):
                        if got >> j & 1:
                            mask |= 1 << order[j]
                    seen(mask, part)

    def finish(self):
        for step in range(self.bits):
            for copy in self.all[step]:
                copy.wait_send()

    def run(self):
        for step in range(self.bits):
            self.event(step)
        self.finish()


class SharedGather:
    def __init__(self, size, shard, full, copied, sends, recvs, score, rcore, first):
        self.core, self.row = lax.axis_index("dp"), lax.axis_index("row")
        self.size, self.full, self.score, self.rcore, self.first = size, full, score, rcore, first * 2 * (size - 1)
        share = full.shape[1] // 2
        self.own = pltpu.make_async_copy(shard, full.at[self.row], copied.at[first])
        self.gather = RowGather(size, full, sends, recvs, self.core * share, share, self.first)

    def across(self, mask, part):
        piece = self.full.at[self.row ^ mask, self.gather.rows(part)]
        return remote(piece, piece, self.score, self.rcore, self.first + part * (self.size - 1) + mask - 1, {"dp": 1 - self.core})

    def load(self):
        self.own.start()

    def start(self):
        self.own.wait()
        self.gather.start()

    def event(self, step):
        self.gather.event(step, lambda mask, part: self.across(mask, part).start())

    def finish(self):
        self.gather.finish()
        for mask in range(1, self.size):
            for part in range(2):
                self.across(mask, part).wait()

    @staticmethod
    def scratch(size, count):
        dma = pltpu.SemaphoreType.DMA
        return [dma((count,))] + [dma((count * 2 * (size - 1),))] * 4


class RowScatter:
    def __init__(self, size, part_ref, recv_ref, sends, recvs, begin=0):
        self.size, self.part, self.recv = size, part_ref, recv_ref
        self.bits = size.bit_length() - 1
        self.row = lax.axis_index("row")
        half = recv_ref.shape[1] // 2
        self.rows = [pl.ds(part * half, half) for part in range(2)]
        self.own = [pl.ds(pl.multiple_of(begin + part * half, 16), half) for part in range(2)]
        self.plans = []
        for part in range(2):
            order = self.order(part)
            steps, held = [], {}
            for step in range(self.bits):
                bit, rest = 1 << order[step], order[step + 1 :]
                count = 1 << len(rest)
                copies, sums = [], {}
                for item in range(count - 1, -1, -1):
                    mask = sum(1 << other for j, other in enumerate(rest) if item >> j & 1)
                    place = size - 2 * count + item
                    copy = remote(
                        self.spot(part, mask ^ bit, held), recv_ref.at[place, self.rows[part]],
                        sends, recvs, part * (size - 1) + place, {"row": self.row ^ bit},
                    )
                    copies.append((mask, place, held.get(mask), copy))
                    sums[mask] = place
                held = sums
                steps.append(copies)
            self.plans.append(steps)

    def spot(self, part, mask, held):
        if mask in held:
            return self.recv.at[held[mask], self.rows[part]]
        return self.part.at[self.row ^ mask, self.own[part]]

    def order(self, part):
        return list(range(self.bits)) if part == 0 else list(range(self.bits))[::-1]

    def start(self):
        for part in range(2):
            for copies in self.plans[part][0]:
                copies[3].start()

    def event(self, step, finish):
        last = step + 1 == self.bits
        for part in range(2):
            rows, own = self.rows[part], self.own[part]
            for mask, place, before, copy in self.plans[part][step]:
                copy.wait_recv()
                size, begin, start = min(64, rows.size), own.start, rows.start

                @pl.loop(0, rows.size // size)
                def _(i):
                    here = pl.ds(pl.multiple_of(start + i * size, 16), size)
                    if before is None:
                        had = self.part[self.row ^ mask, pl.ds(pl.multiple_of(begin + i * size, 16), size)]
                    else:
                        had = self.recv[before, here]
                    total = had.astype(F32) + self.recv[place, here].astype(F32)
                    if last:
                        finish(here, total)
                    else:
                        self.recv[place, here] = total.astype(BF16)

                if last:
                    continue
                for mask2, _, _, copy2 in self.plans[part][step + 1]:
                    if mask2 ^ 1 << self.order(part)[step + 1] == mask:
                        copy2.start()

    def close(self):
        for part in range(2):
            for step in self.plans[part]:
                for _, _, _, copy in step:
                    copy.wait_send()

    def run(self, finish):
        self.start()
        for step in range(self.bits):
            self.event(step, finish)
        self.close()


class ColGather:
    def __init__(self, size, ref, sends, recvs, begin=0, end=None):
        self.size, self.ref, self.sends, self.recvs = size, ref, sends, recvs
        self.begin, self.end = begin, size - 1 if end is None else end
        self.col = lax.axis_index("col")

    def sides(self, step):
        size, col = self.size, self.col
        return (
            (0, lax.rem(col - step + size, size), col >= step, col < size - 1),
            (1, lax.rem(col + step, size), col + step < size, col > 0),
        )

    def copy(self, side, step):
        size, col = self.size, self.col
        piece = self.ref.at[self.sides(step)[side][1]]
        target = lax.rem(col + (1 if side == 0 else size - 1), size)
        return remote(piece, piece, self.sends, self.recvs, side * (size - 1) + step, {"col": target})

    def event(self, step, seen=None):
        for side, place, has, goes in self.sides(step):
            if step > self.begin:

                @pl.when(has)
                def _():
                    self.copy(side, step - 1).wait_recv()

            if step < self.end:

                @pl.when(has & goes)
                def _():
                    self.copy(side, step).start()

            if seen is not None and (step or side == 0):

                @pl.when(has)
                def _():
                    seen(place)

    def finish(self):
        for step in range(self.begin, self.end):
            for side, place, has, goes in self.sides(step):

                @pl.when(has & goes)
                def _():
                    self.copy(side, step).wait_send()

    def run(self):
        for step in range(self.begin, self.end + 1):
            self.event(step)
        self.finish()


class ColScatter:
    def __init__(self, size, part, recv, sends, recvs):
        self.size, self.part, self.recv, self.sends, self.recvs = size, part, recv, sends, recvs
        self.col = lax.axis_index("col")
        self.times = size

    def copy(self, side, target, source):
        step = 1 if side == 0 else self.size - 1
        return pltpu.make_async_remote_copy(
            src_ref=self.recv.at[target + 1 - side] if source is None else source.at[target], dst_ref=self.recv.at[target + 1 - side], send_sem=self.sends.at[side],
            recv_sem=self.recvs.at[side * self.size + target],
            device_id={"col": lax.rem(self.col + step, self.size)}, device_id_type=MESH,
        )

    def event(self, time, prepare=None):
        size, col = self.size, self.col
        for side, first, step in ((0, col == 0, time - col), (1, col == size - 1, time - (size - 1 - col))):
            target = size - 1 - step if side == 0 else step
            valid = (step >= 0) & ((target >= col) if side == 0 else (target <= col))
            place = lax.rem(target + 4 * size, size)

            if prepare is not None:

                @pl.when(valid & ((target != col) | (side == 0)))
                def _():
                    prepare(place)

            @pl.when(valid & jnp.logical_not(first))
            def _():
                self.copy(side, place, self.part).wait_recv()

            @pl.when(valid & jnp.logical_not(first) & (target != col))
            def _():
                chunk = min(64, self.part.shape[1])

                @pl.loop(0, self.part.shape[1] // chunk)
                def _(i):
                    rows = pl.ds(pl.multiple_of(i * chunk, 16), chunk)
                    self.recv[place + 1 - side, rows] = (
                        self.recv[place + 1 - side, rows].astype(F32) + self.part[place, rows].astype(F32)
                    ).astype(BF16)

            @pl.when(valid & (step > 0))
            def _():
                self.copy(side, place, self.part).wait_send()

            @pl.when(valid & (target != col) & first)
            def _():
                self.copy(side, place, self.part).start()

            @pl.when(valid & (target != col) & jnp.logical_not(first))
            def _():
                self.copy(side, place, None).start()

    def total(self, rows):
        got = self.part[self.col, rows].astype(F32)
        got += jnp.where(self.col > 0, self.recv[self.col + 1, rows].astype(F32), 0.0)
        got += jnp.where(self.col < self.size - 1, self.recv[self.col, rows].astype(F32), 0.0)
        return got


VM = pl.BlockSpec(memory_space=pltpu.VMEM)


def params(ident):
    return pltpu.CompilerParams(collective_id=ident, has_side_effects=True, vmem_limit_bytes=VMEM_LIMIT)


def keep_near(size, line, near, step):
    col = lax.axis_index("col")
    for side, place, has in ((0, col - step, col >= step), (1, col + step, col + step < size)):

        @pl.when(has)
        def _():
            near[side] = line[lax.rem(place + size, size)]


def take_near(size, line, near, step):
    col = lax.axis_index("col")
    for side, place, has in ((0, col - step, col >= step), (1, col + step, col + step < size)):

        @pl.when(has)
        def _():
            line[lax.rem(place + size, size)] = near[side]


def first_kernel(
    size, act_ref, cot_ref, small_ref, qkv_ref, out_ref,
    x_ref, first_ref, inv_ref, tok_ref, smalls_ref, qkvs_ref, outs_ref,
    near_ref,
    got_ref, zq_ref, zo_ref, zc_ref, s1, r1, s2, r2, s3, r3, szq, rzq, szo, rzo, srow, rrow, score, rcore, szc, rzc,
):
    row, col, core = lax.axis_index("row"), lax.axis_index("col"), lax.axis_index("dp")
    length, width = act_ref.shape
    quarter = length // size
    small_rows = small_ref.shape[0]
    gain_row = 2 * length // 128
    x_ref[row] = act_ref[...]
    smalls_ref[row] = small_ref[...]
    blocks = ((qkv_ref, zq_ref, qkvs_ref, szq, rzq), (out_ref, zo_ref, outs_ref, szo, rzo))
    for block, line, _, _, _ in blocks:
        share = block.shape[0] // 2
        line[col] = block[pl.ds(pl.multiple_of(core * share, 16), share)]
    greet(row_size=size, col_size=size, dp_size=2)
    gather = RowGather(size, x_ref, s1, r1)
    smalls = [
        remote(small_ref, smalls_ref.at[row], s3, r3, mask - 1, {"row": row ^ mask}) for mask in range(1, size)
    ]
    lines = [ColGather(size, line, sends, recvs) for _, line, _, sends, recvs in blocks]
    lines[0].event(0)
    for move in smalls:
        move.start()
    moves = [
        remote(cot_ref.at[pl.ds((row ^ mask) * quarter, quarter)], got_ref.at[row], s2, r2, mask - 1, {"row": row ^ mask})
        for mask in range(1, size)
    ]
    for move in moves:
        move.start()
    gather.start()
    got_ref[row] = cot_ref[pl.ds(pl.multiple_of(row * quarter, 16), quarter)]

    def half(ref, place):
        share = ref.shape[1] // 2
        return ref.at[place, pl.ds(pl.multiple_of(core * share, 16), share)]

    def hand(which, mask):
        _, line, full, _, _ = blocks[which]
        return remote(line.at[row ^ mask], half(full, row), srow, rrow, which * (size - 1) + mask - 1, {"row": row ^ mask})

    def across(which, mask):
        full = blocks[which][2]
        piece = half(full, row ^ mask)
        return remote(piece, piece, score, rcore, which * size + mask, {"dp": 1 - core})

    def seen(which):
        def act(place):
            _, line, full, _, _ = blocks[which]

            @pl.when(place == row)
            def _():
                share = full.shape[1] // 2
                full[row, pl.ds(pl.multiple_of(core * share, 16), share)] = line[row]
                across(which, 0).start()

            for mask in range(1, size):

                @pl.when(place == row ^ mask)
                def _():
                    hand(which, mask).start()

        return act

    act, act1 = seen(0), seen(1)
    act(col)
    near = ColGather(size, zc_ref, szc, rzc, 0, 1)
    for step in range(1, size - 1):
        lines[0].event(step, act)
    for move in moves:
        move.wait()
    for j in range(size):
        zc_ref[col, :, j * width : (j + 1) * width] = got_ref[j]
    tok_ref[...] = zc_ref[col]
    near.event(0)
    lines[1].event(0)
    lines[0].event(size - 1, act)
    act1(col)
    gather.event(0)
    lines[1].event(1, act1)
    for step in range(1, gather.bits):
        gather.event(step)
    for move in smalls:
        move.wait()

    @pl.loop(0, length // 128)
    def _(i):
        rows = pl.ds(pl.multiple_of(i * 128, 128), 128)
        total = jnp.zeros((128, 1), F32)
        for j in range(size):
            value = x_ref[j, rows].astype(F32)
            total += jnp.sum(value * value, axis=1, keepdims=True)
        inverse = lax.rsqrt(total / (size * width) + EPSILON)
        inv_ref[rows] = inverse
        for j in range(size):
            for k in range(width // 128):
                gain = smalls_ref[j, gain_row + k : gain_row + k + 1]
                value = x_ref[j, rows, k * 128 : (k + 1) * 128].astype(F32)
                first_ref[rows, j * width + k * 128 : j * width + (k + 1) * 128] = (value * inverse * gain).astype(BF16)

    for mask in range(1, size):
        hand(0, mask).wait_recv()
        across(0, mask).start()
    for step in range(2, size):
        lines[1].event(step, act1)
    for mask in range(1, size):
        hand(1, mask).wait_recv()
        across(1, mask).start()
    near.event(1)
    keep_near(size, zc_ref, near_ref, 1)
    near.finish()
    gather.finish()
    for line in lines:
        line.finish()
    for which in range(2):
        for mask in range(1, size):
            hand(which, mask).wait_send()
        for mask in range(size):
            across(which, mask).wait()


def first_call(activations, cotangent, small, qkv_weight, out_weight):
    size = lax.axis_size("row")
    length, width = activations.shape
    quarter = length // size
    qkv_cols, heads_cols = qkv_weight.shape[1], out_weight.shape[0]
    dma = pltpu.SemaphoreType.DMA
    return pl.pallas_call(
        functools.partial(first_kernel, size),
        out_shape=(
            jax.ShapeDtypeStruct((size, length, width), BF16),
            jax.ShapeDtypeStruct((length, size * width), BF16),
            jax.ShapeDtypeStruct((length, 1), F32),
            jax.ShapeDtypeStruct((quarter, size * width), BF16),
            jax.ShapeDtypeStruct((size,) + small.shape, F32),
            jax.ShapeDtypeStruct((size,) + qkv_weight.shape, BF16),
            jax.ShapeDtypeStruct((size,) + out_weight.shape, BF16),
            jax.ShapeDtypeStruct((2, quarter, size * width), BF16),
        ),
        in_specs=[VM] * 5,
        out_specs=(VM,) * 8,
        scratch_shapes=[
            pltpu.VMEM((size, quarter, width), BF16),
            pltpu.VMEM((size, width // 2, qkv_cols), BF16),
            pltpu.VMEM((size, heads_cols // 2, width), BF16),
            pltpu.VMEM((size, quarter, size * width), BF16),
        ]
        + [dma((2 * (size - 1),))] * 2
        + [dma((size - 1,))] * 4
        + [dma((2 * (size - 1),))] * 4
        + [dma((2 * (size - 1),))] * 2
        + [dma((2 * size,))] * 2
        + [dma((2 * (size - 1),))] * 2,
        compiler_params=params(1),
    )(activations, cotangent, small, qkv_weight, out_weight)


def turn(values, low):
    return jnp.where(low, -pltpu.roll(values, 128 - HEAD // 2, 1), pltpu.roll(values, HEAD // 2, 1))


def low_columns(rows):
    return lax.broadcasted_iota(jnp.int32, (rows, 128), 1) % HEAD < HEAD // 2


def masked_scores(query, key, seg_col, seg_row, first_row):
    scores = lax.dot_general(query, key, (((1,), (1,)), ((), ())), preferred_element_type=F32)
    rows = lax.broadcasted_iota(jnp.int32, scores.shape, 0) + first_row
    columns = lax.broadcasted_iota(jnp.int32, scores.shape, 1)
    allowed = (seg_col == seg_row) & (rows >= columns)
    return jnp.where(allowed, scores, -1e30)


def attend_kernel(
    size, first_ref, weight_ref, cos_ref, sin_ref, segc_ref, segr_ref, near_ref, gate_ref,
    q_ref, k_ref, v_ref, o_ref, next_ref, gates_ref, oh_ref, zc_ref, szc, rzc, *shared,
):
    bulk = SharedGather(size, gate_ref, gates_ref, *shared, 0)
    bulk.load()
    take_near(size, zc_ref, near_ref, 1)
    greet(row_size=size, col_size=size, dp_size=2)
    bulk.start()
    line = ColGather(size, zc_ref, szc, rzc, 1, 2)
    line.event(1)
    heads, length, _ = q_ref.shape
    kvs = k_ref.shape[0]
    group = heads // kvs
    query_cols = heads * HEAD
    key_cols = (weight_ref.shape[1] - query_cols) // 2
    block = 256

    @pl.loop(0, length // block)
    def _(i):
        rows = pl.ds(pl.multiple_of(i * block, block), block)
        low = low_columns(block)
        cosine, sine = cos_ref[rows], sin_ref[rows]
        whole = jnp.dot(first_ref[rows], weight_ref[...], preferred_element_type=F32)
        for ref, count, start, factor in ((q_ref, heads, 0, HEAD ** (-0.5)), (k_ref, kvs, query_cols, 1.0)):
            for j in range((count + 1) // 2):
                part = whole[:, start + 128 * j : start + 128 * (j + 1)]
                part = ((part * cosine + turn(part, low) * sine) * factor).astype(BF16)
                for side in range(min(2, count - 2 * j)):
                    ref[2 * j + side, rows] = part[:, side * HEAD : (side + 1) * HEAD]
        for j in range(kvs):
            at = query_cols + key_cols + j * HEAD
            v_ref[j, rows] = whole[:, at : at + HEAD].astype(BF16)

    @pl.loop(0, heads)
    def _(head):
        kv = lax.div(head, group)
        for i in range(length // block):
            rows, extent = slice(i * block, (i + 1) * block), (i + 1) * block
            scores = masked_scores(q_ref[head, rows], k_ref[kv, :extent], segc_ref[rows], segr_ref[:, :extent], i * block)
            top = jnp.max(scores, axis=1, keepdims=True)
            weights = jnp.exp(scores - top)
            total = jnp.sum(weights, axis=1, keepdims=True)
            mixed = jnp.dot(weights.astype(BF16), v_ref[kv, :extent], preferred_element_type=F32)
            oh_ref[head, rows] = (mixed / total).astype(BF16)

    for head in range(heads):
        o_ref[:, head * HEAD : (head + 1) * HEAD] = oh_ref[head]
    for step in range(bulk.gather.bits):
        bulk.event(step)
    line.event(2)
    keep_near(size, zc_ref, next_ref, 2)
    line.finish()
    bulk.finish()


def attend_call(first, weight, cosine, sine, segc, segr, near, gate, heads, kvs):
    size = lax.axis_size("row")
    length = first.shape[0]
    dma = pltpu.SemaphoreType.DMA
    return pl.pallas_call(
        functools.partial(attend_kernel, size),
        out_shape=(
            jax.ShapeDtypeStruct((heads, length, HEAD), BF16),
            jax.ShapeDtypeStruct((kvs, length, HEAD), BF16),
            jax.ShapeDtypeStruct((kvs, length, HEAD), BF16),
            jax.ShapeDtypeStruct((length, heads * HEAD), BF16),
            jax.ShapeDtypeStruct(near.shape, BF16),
            jax.ShapeDtypeStruct((size,) + gate.shape, BF16),
        ),
        in_specs=[VM] * 8,
        out_specs=(VM,) * 5 + (pl.BlockSpec(memory_space=pl.ANY),),
        scratch_shapes=[
            pltpu.VMEM((heads, length, HEAD), BF16),
            pltpu.VMEM((size,) + near.shape[1:], BF16),
            dma((2 * (size - 1),)), dma((2 * (size - 1),)),
        ]
        + SharedGather.scratch(size, 1),
        compiler_params=params(6),
        cost_estimate=cost(45),
    )(first, weight, cosine, sine, segc, segr, near, gate)


class swap_halves:
    def __init__(self, part, other, sends, recvs):
        core = lax.axis_index("dp")
        share = part.shape[1] // 2
        self.move = remote(
            part.at[:, pl.ds(pl.multiple_of((1 - core) * share, 16), share)], other, sends, recvs, 0, {"dp": 1 - core}
        )

    def start(self):
        self.move.start()

    def wait(self):
        self.move.wait()


def add_halves(part, other, share):
    rows = pl.ds(pl.multiple_of(lax.axis_index("dp") * share.shape[1], 16), share.shape[1])
    for j in range(part.shape[0]):
        share[j] = (part[j, rows].astype(F32) + other[j].astype(F32)).astype(BF16)


def row_moves(size, source, target, sends, recvs, first, begin):
    row = lax.axis_index("row")
    if begin:
        target[row] = source[row]
    for mask in range(1, size):
        move = remote(source.at[row ^ mask], target.at[row], sends, recvs, first + mask - 1, {"row": row ^ mask})
        if begin:
            move.start()
        else:
            move.wait()


def cost(micros):
    return pl.CostEstimate(flops=int(micros * 1e9), bytes_accessed=1 << 20, transcendentals=0)


def attend_back_kernel(
    dmid_ref, weight_ref, q_ref, k_ref, v_ref, cos_ref, sin_ref, segc_ref, segr_ref,
    attn_ref, down_ref, mid_ref, upshare_ref, downshare_ref,
    dqkv_ref, inner_ref, blk_ref, line_ref, gup_ref, gdown_ref, do_ref, dq_ref, dk_ref, dv_ref,
    recv_ref, part_ref, other_ref, share_ref, urecv_ref, drecv_ref, ustage_ref, dstage_ref,
    s1, r1, score, rcore, srow, rrow, su, ru, sd, rd, copied, sf, rf,
):
    row, core = lax.axis_index("row"), lax.axis_index("dp")
    cols_n = down_ref.shape[0]
    heads, length, _ = q_ref.shape
    kvs = k_ref.shape[0]
    group = heads // kvs
    query_cols = heads * HEAD
    key_cols = (dqkv_ref.shape[1] - query_cols) // 2
    block = 256
    parts, _, width = weight_ref.shape
    greet(row_size=parts, col_size=cols_n, dp_size=2)
    line = ColScatter(cols_n, down_ref, recv_ref, s1, r1)
    line.event(0)
    sums = [
        (RowScatter(parts, upshare_ref, urecv_ref, su, ru), ustage_ref, gup_ref),
        (RowScatter(parts, downshare_ref, drecv_ref, sd, rd), dstage_ref, gdown_ref),
    ]
    for scatter, _, _ in sums:
        scatter.start()
    for j in range(parts):
        part_ref[j] = lax.dot_general(
            attn_ref[...], dmid_ref[:, j * width : (j + 1) * width], (((0,), (0,)), ((), ())), preferred_element_type=F32
        ).astype(BF16)
    cross = swap_halves(part_ref, other_ref, score, rcore)
    cross.start()
    dk_ref[...] = jnp.zeros_like(dk_ref)
    dv_ref[...] = jnp.zeros_like(dv_ref)
    inner_ref[...] = jnp.zeros_like(inner_ref)

    @pl.loop(0, length // block)
    def _(i):
        rows = pl.ds(pl.multiple_of(i * block, block), block)
        total = jnp.zeros((block, query_cols), F32)
        for j in range(parts):
            total += lax.dot_general(
                dmid_ref[rows, j * width : (j + 1) * width], weight_ref[j], (((1,), (1,)), ((), ())), preferred_element_type=F32
            )
        for head in range(heads):
            do_ref[head, rows] = total[:, head * HEAD : (head + 1) * HEAD].astype(BF16)

    @pl.loop(0, heads)
    def _(head):
        @pl.when(head == min(1, heads - 1))
        def _():
            cross.wait()
            add_halves(part_ref, other_ref, share_ref)
            row_moves(parts, share_ref, line_ref, srow, rrow, 0, True)

        @pl.when(head == heads // 2)
        def _():
            line.event(1)

        kv = lax.div(head, group)
        for i in range(length // block):
            rows, extent = slice(i * block, (i + 1) * block), (i + 1) * block
            query, keys, grads = q_ref[head, rows], k_ref[kv, :extent], do_ref[head, rows]
            scores = masked_scores(query, keys, segc_ref[rows], segr_ref[:, :extent], i * block)
            top = jnp.max(scores, axis=1, keepdims=True)
            weights = jnp.exp(scores - top)
            weights = weights * (1.0 / jnp.sum(weights, axis=1, keepdims=True))
            back = lax.dot_general(grads, v_ref[kv, :extent], (((1,), (1,)), ((), ())), preferred_element_type=F32)
            dv_ref[kv, :extent] += lax.dot_general(
                weights.astype(BF16), grads, (((0,), (0,)), ((), ())), preferred_element_type=F32
            )
            ds = (weights * (back - jnp.sum(weights * back, axis=1, keepdims=True))).astype(BF16)
            dq = jnp.dot(ds, keys, preferred_element_type=F32)
            inner_ref[rows] += jnp.sum(dq * query.astype(F32), axis=1, keepdims=True)
            for side in range(2):

                @pl.when(lax.rem(head, 2) == side)
                def _():
                    dq_ref[lax.div(head, 2), rows, side * HEAD : (side + 1) * HEAD] = dq

            dk_ref[kv, :extent] += lax.dot_general(ds, query, (((0,), (0,)), ((), ())), preferred_element_type=F32)

    @pl.loop(0, length // block)
    def _(i):
        rows = pl.ds(pl.multiple_of(i * block, block), block)
        low = low_columns(block)
        cosine, sine = cos_ref[rows], sin_ref[rows]
        for ref, count, start, factor in ((dq_ref, heads, 0, HEAD ** (-0.5)), (dk_ref, kvs, query_cols, 1.0), (dv_ref, kvs, query_cols + key_cols, None)):
            for j in range((count + 1) // 2):
                if ref is dq_ref:
                    part = dq_ref[j, rows]
                else:
                    sides = [ref[2 * j + side, rows] if 2 * j + side < count else jnp.zeros((block, HEAD), F32) for side in range(2)]
                    part = jnp.concatenate(sides, axis=1)
                if factor is not None:
                    part = (part * cosine - turn(part * sine, low)) * factor
                dqkv_ref[rows, start + 128 * j : start + 128 * (j + 1)] = part.astype(BF16)
        more = jnp.zeros((block, 1), F32)
        for kv in range(kvs):
            more += jnp.sum(dk_ref[kv, rows] * k_ref[kv, rows].astype(F32) + dv_ref[kv, rows] * v_ref[kv, rows].astype(F32), axis=1, keepdims=True)
        inner_ref[rows] += more

    def finish(stage):
        def act(rows, total):
            stage[rows] = total

        return act

    if cols_n > 2:
        line.event(2)
    bits = sums[0][0].bits
    for step in range(bits - 1):
        for scatter, stage, _ in sums:
            scatter.event(step, finish(stage))
    for time in range(3, line.times):
        line.event(time)
    results = []
    for k, (scatter, stage, out) in enumerate(sums):
        scatter.event(bits - 1, finish(stage))
        moves = settle(stage, out, core, copied, sf, rf, k)
        for move in moves:
            move.start()
        results += moves
        scatter.close()

    @pl.loop(0, mid_ref.shape[0] // 64)
    def _(i):
        rows = pl.ds(pl.multiple_of(i * 64, 16), 64)
        total = mid_ref[rows] + line.total(rows)
        for j in range(parts):
            blk_ref[j, rows] = total[:, j * width : (j + 1) * width].astype(BF16)

    row_moves(parts, share_ref, line_ref, srow, rrow, 0, False)
    for move in results:
        move.wait()


def attend_back_call(dmid, weight, q, k, v, cosine, sine, segc, segr, columns, attn, down, middle, upshare, downshare):
    rows_n, cols_n = lax.axis_size("row"), lax.axis_size("col")
    _, heads_cols, width = weight.shape
    quarter = middle.shape[0]
    dma = pltpu.SemaphoreType.DMA
    heads, length, _ = q.shape
    kvs = k.shape[0]
    return pl.pallas_call(
        attend_back_kernel,
        out_shape=(
            jax.ShapeDtypeStruct((length, columns), BF16),
            jax.ShapeDtypeStruct((length, 1), F32),
            jax.ShapeDtypeStruct((rows_n, quarter, width), BF16),
            jax.ShapeDtypeStruct((rows_n, heads_cols // 2, width), BF16),
            jax.ShapeDtypeStruct((2 * upshare.shape[1], upshare.shape[2]), F32),
            jax.ShapeDtypeStruct((2 * downshare.shape[1], downshare.shape[2]), F32),
        ),
        in_specs=[VM] * 14,
        out_specs=(VM,) * 4 + (pl.BlockSpec(memory_space=pl.ANY),) * 2,
        scratch_shapes=[
            pltpu.VMEM((heads, length, HEAD), BF16),
            pltpu.VMEM(((heads + 1) // 2, length, 2 * HEAD), F32),
            pltpu.VMEM((kvs, length, HEAD), F32),
            pltpu.VMEM((kvs, length, HEAD), F32),
            pltpu.VMEM((down.shape[0] + 1,) + down.shape[1:], BF16),
            pltpu.VMEM(weight.shape, BF16),
            pltpu.VMEM((rows_n, heads_cols // 2, width), BF16),
            pltpu.VMEM((rows_n, heads_cols // 2, width), BF16),
            pltpu.VMEM((rows_n - 1,) + upshare.shape[1:], BF16),
            pltpu.VMEM((rows_n - 1,) + downshare.shape[1:], BF16),
            pltpu.VMEM(upshare.shape[1:], F32),
            pltpu.VMEM(downshare.shape[1:], F32),
            dma((2,)), dma((2 * cols_n,)), dma((1,)), dma((1,)), dma((rows_n - 1,)), dma((rows_n - 1,)),
        ]
        + [dma((2 * (rows_n - 1),))] * 4
        + [dma((2,))] * 3
        + [
        ],
        compiler_params=params(5),
        cost_estimate=cost(80),
    )(dmid, weight, q, k, v, cosine, sine, segc, segr, attn, down, middle, upshare, downshare)


def middle_kernel(
    rows_n, cols_n, attn_ref, weight_ref, x_ref, gain_ref, tok_ref, near_ref, next_ref, up_ref, down_ref,
    mid_ref, second_ref, cot_ref, ups_ref, downs_ref, part_ref, recv_ref, s1, r1, s2, r2, szc, rzc, *shared,
):
    row, col = lax.axis_index("row"), lax.axis_index("col")
    quarter, features = mid_ref.shape
    width = features // rows_n
    bulks = [SharedGather(rows_n, up_ref, ups_ref, *shared, 0), SharedGather(rows_n, down_ref, downs_ref, *shared, 1)]
    for bulk in bulks:
        bulk.load()
    cot_ref[col] = tok_ref[...]
    take_near(cols_n, cot_ref, near_ref, 1)
    take_near(cols_n, cot_ref, next_ref, 2)
    greet(row_size=rows_n, col_size=cols_n, dp_size=2)
    rest = ColGather(cols_n, cot_ref, szc, rzc, 2)
    rest.event(2)

    @pl.loop(0, rows_n)
    def _(i):
        own = attn_ref[pl.ds(pl.multiple_of(i * quarter, 16), quarter)]
        for j in range(rows_n):
            part_ref[i, :, j * width : (j + 1) * width] = jnp.dot(own, weight_ref[j], preferred_element_type=F32).astype(BF16)

    def finish(rows, total):
        own = pl.ds(row * quarter + rows.start, rows.size)
        squares = jnp.zeros((rows.size, 1), F32)
        for j in range(rows_n):
            columns = slice(j * width, (j + 1) * width)
            value = total[:, columns] + x_ref[j, own].astype(F32)
            mid_ref[rows, columns] = value
            squares += jnp.sum(value * value, axis=1, keepdims=True)
        inverse = lax.rsqrt(squares / features + EPSILON)
        second_ref[col, rows] = (mid_ref[rows] * inverse * gain_ref[...]).astype(BF16)

    RowScatter(rows_n, part_ref, recv_ref, s1, r1).run(finish)
    line = ColGather(cols_n, second_ref, s2, r2)
    line.event(0)
    for bulk in bulks:
        bulk.start()
    for step in range(3, cols_n):
        rest.event(step)
    rest.finish()
    line.event(1)
    bits = bulks[0].gather.bits
    for bulk in bulks:
        bulk.event(0)
    for step in range(2, cols_n):
        line.event(step)
    for step in range(1, bits):
        for bulk in bulks:
            bulk.event(step)
    for bulk in bulks:
        bulk.finish()
    line.finish()


def middle_call(attn, weight, x, gain, tok, near, following, up, down):
    rows_n, cols_n = lax.axis_size("row"), lax.axis_size("col")
    length, features = attn.shape[0], weight.shape[0] * weight.shape[2]
    quarter = length // rows_n
    dma = pltpu.SemaphoreType.DMA
    anywhere = pl.BlockSpec(memory_space=pl.ANY)
    return pl.pallas_call(
        functools.partial(middle_kernel, rows_n, cols_n),
        out_shape=(
            jax.ShapeDtypeStruct((quarter, features), F32),
            jax.ShapeDtypeStruct((cols_n, quarter, features), BF16),
            jax.ShapeDtypeStruct((cols_n, quarter, features), BF16),
            jax.ShapeDtypeStruct((rows_n,) + up.shape, BF16),
            jax.ShapeDtypeStruct((rows_n,) + down.shape, BF16),
        ),
        in_specs=[VM] * 9,
        out_specs=(VM, VM, VM, anywhere, anywhere),
        scratch_shapes=[
            pltpu.VMEM((rows_n, quarter, features), BF16),
            pltpu.VMEM((rows_n - 1, quarter, features), BF16),
        ]
        + [dma((2 * (rows_n - 1),))] * 2
        + [dma((2 * (cols_n - 1),))] * 4
        + SharedGather.scratch(rows_n, 2),
        compiler_params=params(2),
        cost_estimate=cost(130),
    )(attn, weight, x, gain, tok, near, following, up, down)


def settle(stage, out, core, copied, sends, recvs, place):
    rows = pl.ds(pl.multiple_of(core * stage.shape[0], 8), stage.shape[0])
    return (
        pltpu.make_async_copy(stage, out.at[rows], copied.at[place]),
        remote(stage, out.at[rows], sends, recvs, place, {"dp": 1 - core}),
    )


def back_kernel(
    rows_n, cols_n, dgate_ref, dup_ref, gate_ref, up_ref, mid_ref, tok_ref, gain_ref, second_ref,
    dmid_ref, grad_ref, ggate_ref, share_ref,
    w0_ref, w1_ref, part_ref, recv_ref, other_ref, grecv_ref, stage_ref,
    loads, s1, r1, s2, r2, sg, rg, score, rcore, copied, sf, rf, free,
):
    row, col, core = lax.axis_index("row"), lax.axis_index("col"), lax.axis_index("dp")
    quarter, features = mid_ref.shape
    width = features // rows_n
    hidden = dgate_ref.shape[1]
    share = width // 2
    moves = [pltpu.make_async_copy(ref, kept, loads.at[k]) for k, (ref, kept) in enumerate(((gate_ref, w0_ref), (up_ref, w1_ref)))]
    for move in moves:
        move.start()
    greet(row_size=rows_n, col_size=cols_n, dp_size=2)
    for move in moves:
        move.wait()

    def prepare(target):
        rows = pl.ds(pl.multiple_of(target * quarter, 16), quarter)

        @pl.loop(0, rows_n)
        def _(i):
            columns = pl.ds(pl.multiple_of(i * width, 128), width)
            value = lax.dot_general(dgate_ref[rows], w0_ref[i], (((1,), (1,)), ((), ())), preferred_element_type=F32)
            value += lax.dot_general(dup_ref[rows], w1_ref[i], (((1,), (1,)), ((), ())), preferred_element_type=F32)
            part_ref[target, :, columns] = value.astype(BF16)

    tile = min(512, hidden)

    def product(right, kept):
        @pl.loop(0, rows_n)
        def _(i):
            for t in range(hidden // tile):
                columns = slice(t * tile, (t + 1) * tile)
                kept[i, :, columns] = lax.dot_general(
                    second_ref[:, pl.ds(pl.multiple_of(i * width, 128), width)], right[:, columns], (((0,), (0,)), ((), ())),
                    preferred_element_type=F32,
                ).astype(BF16)

    def add(kept):
        @pl.loop(0, rows_n)
        def _(i):
            rows = pl.ds(pl.multiple_of(core * share, 16), share)
            kept[i, rows] = (kept[i, rows].astype(F32) + other_ref[i].astype(F32)).astype(BF16)

    line = ColScatter(cols_n, part_ref, recv_ref, s1, r1)
    prepare(cols_n - 1)
    prepare(0)
    line.event(0)
    for target in range(1, cols_n - 1):
        prepare(target)
    cross = [
        remote(kept.at[:, pl.ds(pl.multiple_of((1 - core) * share, 16), share)], other_ref, score, rcore, k, {"dp": 1 - core})
        for k, kept in enumerate((w0_ref, w1_ref))
    ]
    product(dgate_ref, w0_ref)
    cross[0].start()
    line.event(1)
    product(dup_ref, w1_ref)
    cross[0].wait()
    add(w0_ref)
    pl.semaphore_signal(free, inc=1, device_id={"dp": 1 - core}, device_id_type=MESH)
    scatter = RowScatter(rows_n, w0_ref, grecv_ref, sg, rg, core * share)
    scatter.start()
    pl.semaphore_wait(free, 1)
    cross[1].start()
    if cols_n > 2:
        line.event(2)
    cross[1].wait()
    add(w1_ref)
    keep = pltpu.make_async_copy(w1_ref.at[:, pl.ds(pl.multiple_of(core * share, 16), share)], share_ref, copied.at[1])
    keep.start()

    def finish(rows, total):
        stage_ref[rows] = total

    for step in range(scatter.bits - 1):
        scatter.event(step, finish)
    for time in range(3, line.times):
        line.event(time)

    grad_ref[...] = jnp.zeros_like(grad_ref)

    @pl.loop(0, quarter // 64)
    def _(i):
        rows = pl.ds(i * 64, 64)
        got = line.total(rows)
        middle = mid_ref[rows]
        inverse = lax.rsqrt(jnp.sum(middle * middle, axis=1, keepdims=True) / features + EPSILON)
        weighted = got * gain_ref[...]
        inner = jnp.sum(middle * weighted, axis=1, keepdims=True) / features
        grad_ref[...] += jnp.sum(got * middle * inverse, axis=0, keepdims=True)
        value = tok_ref[rows].astype(F32) + inverse * weighted - middle * (inverse * inverse * inverse * inner)
        dmid_ref[row, rows] = value.astype(BF16)

    gather = RowGather(rows_n, dmid_ref, s2, r2)
    gather.start()
    scatter.event(scatter.bits - 1, finish)
    results = settle(stage_ref, ggate_ref, core, copied, sf, rf, 0)
    for move in results:
        move.start()
    gather.run()
    scatter.close()
    keep.wait()
    for move in results:
        move.wait()


def back_call(dgate, dup, gate, up, middle, tok, gain, second):
    rows_n, cols_n = lax.axis_size("row"), lax.axis_size("col")
    quarter, features = middle.shape
    hidden = dgate.shape[1]
    width = features // rows_n
    dma = pltpu.SemaphoreType.DMA
    anywhere = pl.BlockSpec(memory_space=pl.ANY)
    line = 2 * (rows_n - 1)
    half = (rows_n, width // 2, hidden)
    return pl.pallas_call(
        functools.partial(back_kernel, rows_n, cols_n),
        out_shape=(
            jax.ShapeDtypeStruct((rows_n, quarter, features), BF16),
            jax.ShapeDtypeStruct((1, features), F32),
            jax.ShapeDtypeStruct((width, hidden), F32),
            jax.ShapeDtypeStruct(half, BF16),
        ),
        in_specs=[VM, VM, anywhere, anywhere, VM, VM, VM, VM],
        out_specs=(VM, VM, anywhere, anywhere),
        scratch_shapes=[
            pltpu.VMEM((rows_n, width, hidden), BF16),
            pltpu.VMEM((rows_n, width, hidden), BF16),
            pltpu.VMEM((cols_n, quarter, features), BF16),
            pltpu.VMEM((cols_n + 1, quarter, features), BF16),
            pltpu.VMEM(half, BF16),
            pltpu.VMEM((rows_n - 1,) + half[1:], BF16),
            pltpu.VMEM(half[1:], F32),
            dma((2,)), dma((2,)), dma((2 * cols_n,)),
            dma((line,)), dma((line,)), dma((line,)), dma((line,)),
            dma((2,)), dma((2,)), dma((2,)), dma((1,)), dma((1,)), pltpu.SemaphoreType.REGULAR,
        ],
        compiler_params=params(3),
        cost_estimate=cost(130),
    )(dgate, dup, gate, up, middle, tok, gain, second)


def last_kernel(
    size, dqkv_ref, weight_ref, first_ref, outline_ref, blk_ref, inner_ref, act_ref, inv_ref, grad2_ref,
    out_ref, block_ref, inners_ref, gains_ref, gqkv_ref, gout_ref,
    part_ref, recv_ref, qpart_ref, qother_ref, qshare_ref, qline_ref, qrecv_ref, orecv_ref, rgain_ref, pair_ref, pairs_ref,
    s1, r1, sblk, rblk, sinn, rinn, score, rcore, srow, rrow, so, ro, sq, rq, sg, rg, sp, rp, sf, rf,
):
    row, col, core = lax.axis_index("row"), lax.axis_index("col"), lax.axis_index("dp")
    length, width = act_ref.shape
    quarter = length // size
    barrier = pltpu.get_barrier_semaphore()
    peers = [{"row": row ^ mask} for mask in range(1, size)]
    others = [{"col": lax.rem(col + k, size)} for k in range(1, size)]
    others += [{"col": lax.rem(col + k, size), "dp": 1 - core} for k in range(size)]
    for peer in peers + others:
        pl.semaphore_signal(barrier, inc=1, device_id=peer, device_id_type=MESH)
    pl.semaphore_wait(barrier, len(peers) + len(others))

    scatter = RowScatter(size, part_ref, recv_ref, s1, r1)
    inners_ref[row] = inner_ref[...]
    rgain_ref[row] = grad2_ref[row]
    small = []
    for mask in range(1, size):
        small.append(remote(inner_ref, inners_ref.at[row], sinn, rinn, mask - 1, {"row": row ^ mask}))
        small.append(remote(grad2_ref.at[row ^ mask], rgain_ref.at[row], sg, rg, mask - 1, {"row": row ^ mask}))
    for move in small:
        move.start()
    oline = ColScatter(size, outline_ref, orecv_ref, so, ro)
    oline.event(0)

    @pl.loop(0, size)
    def _(j):
        columns = pl.ds(pl.multiple_of(j * width, 128), width)
        qpart_ref[j] = lax.dot_general(
            first_ref[:, columns], dqkv_ref[...], (((0,), (0,)), ((), ())), preferred_element_type=F32
        ).astype(BF16)

    cross = swap_halves(qpart_ref, qother_ref, score, rcore)
    cross.start()
    oline.event(1)

    @pl.loop(0, size)
    def _(j):
        part_ref[j] = lax.dot_general(dqkv_ref[...], weight_ref[j], (((1,), (1,)), ((), ())), preferred_element_type=F32).astype(BF16)

    cross.wait()
    add_halves(qpart_ref, qother_ref, qshare_ref)
    row_moves(size, qshare_ref, qline_ref, srow, rrow, 0, True)
    scatter.start()
    for time in range(2, oline.times):
        oline.event(time)
    share_o = outline_ref.shape[1]
    share_q = qline_ref.shape[1]

    def across(ref, share, which):
        piece = ref.at[pl.ds(pl.multiple_of(core * share, 8), share)]
        return remote(piece, piece, sf, rf, which, {"dp": 1 - core})

    gout_ref[pl.ds(pl.multiple_of(core * share_o, 8), share_o)] = oline.total(slice(None))
    across(gout_ref, share_o, 0).start()

    block_ref[pl.ds(pl.multiple_of(row * quarter, 16), quarter)] = blk_ref[row]
    for mask in range(1, size):
        remote(
            blk_ref.at[row ^ mask], block_ref.at[pl.ds(pl.multiple_of(row * quarter, 16), quarter)], sblk, rblk, mask - 1, {"row": row ^ mask}
        ).start()
    row_moves(size, qshare_ref, qline_ref, srow, rrow, 0, False)
    qline = ColScatter(size, qline_ref, qrecv_ref, sq, rq)
    qline.event(0)
    pair_ref[0] = jnp.zeros_like(pair_ref[0])

    def finish(rows, total):
        out_ref[rows] = total
        pair_ref[0] += jnp.sum(total * act_ref[rows].astype(F32) * inv_ref[rows], axis=0, keepdims=True)

    for step in range(scatter.bits - 1):
        scatter.event(step, finish)
    for time in range(1, min(3, qline.times)):
        qline.event(time)
    scatter.event(scatter.bits - 1, finish)
    scatter.close()
    for move in small:
        move.wait()
    pair_ref[1] = jnp.sum(rgain_ref[...], axis=0)
    own = core * size + col
    pairs_ref[own] = pair_ref[...]
    for k, peer in enumerate(others):
        remote(pair_ref, pairs_ref.at[own], sp, rp, k, peer).start()
    for time in range(3, qline.times):
        qline.event(time)
    gqkv_ref[pl.ds(pl.multiple_of(core * share_q, 8), share_q)] = qline.total(slice(None))
    across(gqkv_ref, share_q, 1).start()
    for k, peer in enumerate(others):
        remote(pair_ref, pairs_ref.at[own], sp, rp, k, peer).wait()
    gains_ref[...] = jnp.sum(pairs_ref[...], axis=0)
    for mask in range(1, size):
        remote(
            blk_ref.at[row ^ mask], block_ref.at[pl.ds(pl.multiple_of(row * quarter, 16), quarter)], sblk, rblk, mask - 1, {"row": row ^ mask}
        ).wait()
    across(gout_ref, share_o, 0).wait()
    across(gqkv_ref, share_q, 1).wait()


def last_call(dqkv, weight, first, outline, blk, inner, activations, inv1, grad2):
    size = lax.axis_size("row")
    length, width = activations.shape
    columns = weight.shape[1]
    heads_cols = 2 * outline.shape[1]
    dma = pltpu.SemaphoreType.DMA
    count = 2 * size - 1
    return pl.pallas_call(
        functools.partial(last_kernel, size),
        out_shape=(
            jax.ShapeDtypeStruct((length, width), F32),
            jax.ShapeDtypeStruct((length, width), BF16),
            jax.ShapeDtypeStruct((size,) + inner.shape, F32),
            jax.ShapeDtypeStruct((2, 1, width), F32),
            jax.ShapeDtypeStruct((width, columns), F32),
            jax.ShapeDtypeStruct((heads_cols, width), F32),
        ),
        in_specs=[VM] * 9,
        out_specs=(VM,) * 6,
        scratch_shapes=[
            pltpu.VMEM((size, length, width), BF16),
            pltpu.VMEM((size - 1, length, width), BF16),
            pltpu.VMEM((size, width, columns), BF16),
            pltpu.VMEM((size, width // 2, columns), BF16),
            pltpu.VMEM((size, width // 2, columns), BF16),
            pltpu.VMEM((size, width // 2, columns), BF16),
            pltpu.VMEM((size + 1, width // 2, columns), BF16),
            pltpu.VMEM((size + 1, heads_cols // 2, width), BF16),
            pltpu.VMEM((size, 1, width), F32),
            pltpu.VMEM((2, 1, width), F32),
            pltpu.VMEM((2 * size, 2, 1, width), F32),
        ]
        + [dma((2 * (size - 1),))] * 2
        + [dma((size - 1,))] * 2
        + [dma((size - 1,))] * 2
        + [dma((1,))] * 2
        + [dma((size - 1,))] * 2
        + [dma((2,)), dma((2 * size,))] * 2
        + [dma((size - 1,))] * 2
        + [dma((count,))] * 2
        + [dma((2,))] * 2,
        compiler_params=params(4),
        cost_estimate=cost(80),
    )(dqkv, weight.reshape(size, width, columns), first, outline, blk, inner, activations, inv1, grad2.reshape(size, 1, width))


def feed_kernel(
    second_ref, cot_ref, gate_ref, up_ref, down_ref, dgate_ref, dup_ref, own_ref, part_ref,
    hidden_ref, keep_ref, send_ref, other_ref, sends, recvs,
):
    core = lax.axis_index("dp")
    step = pl.program_id(0)
    rows_n, tile, width = down_ref.shape
    tokens = second_ref.shape[0]
    tiles = hidden_ref.shape[0]
    block = min(512, tokens)
    mine = tiles // 2

    def place(t):
        return pl.ds(pl.multiple_of(lax.rem(t, mine) * tile, tile), tile)

    def give(t):
        return remote(send_ref.at[:, place(t)], other_ref.at[:, place(t)], sends, recvs, lax.rem(t, mine), {"dp": 1 - core})

    @pl.when(step == 0)
    def _():
        greet(dp_size=2)

    @pl.when(step < tiles)
    def _():
        keep_ref[step] = down_ref[...]

        @pl.loop(0, tokens // block)
        def _(i):
            rows = pl.ds(pl.multiple_of(i * block, block), block)
            gate = jnp.dot(second_ref[rows], gate_ref[...], preferred_element_type=F32)
            up = jnp.dot(second_ref[rows], up_ref[...], preferred_element_type=F32)
            back = jnp.zeros((block, tile), F32)
            for j in range(rows_n):
                back += lax.dot_general(
                    cot_ref[rows, j * width : (j + 1) * width], down_ref[j], (((1,), (1,)), ((), ())), preferred_element_type=F32
                )
            sigma = jax.nn.sigmoid(gate)
            swish = gate * sigma
            hidden_ref[step, rows] = (swish * up).astype(BF16)
            dgate_ref[rows] = (back * up * (sigma * (1.0 + gate * (1.0 - sigma)))).astype(BF16)
            dup_ref[rows] = (back * swish).astype(BF16)

        for j in range(rows_n):
            value = lax.dot_general(
                hidden_ref[step], cot_ref[:, j * width : (j + 1) * width], (((0,), (0,)), ((), ())), preferred_element_type=F32
            ).astype(BF16)

            @pl.when(lax.div(step, mine) == core)
            def _():
                own_ref[j, place(step)] = value

            @pl.when(lax.div(step, mine) != core)
            def _():
                send_ref[j, place(step)] = value

        @pl.when(lax.div(step, mine) != core)
        def _():
            give(step).start()

    @pl.when(step >= tiles)
    def _():
        quarter = part_ref.shape[1]
        rows = pl.ds(pl.multiple_of((step - tiles) * quarter, quarter), quarter)
        for j in range(rows_n):
            total = jnp.zeros((quarter, width), F32)
            for t in range(tiles):
                total += jnp.dot(hidden_ref[t, rows], keep_ref[t, j], preferred_element_type=F32)
            part_ref[0, :, j * width : (j + 1) * width] = total.astype(BF16)

    @pl.when(step == pl.num_programs(0) - 1)
    def _():
        for t in range(mine):
            give(t).wait()
            for j in range(rows_n):
                own_ref[j, place(t)] = (own_ref[j, place(t)].astype(F32) + other_ref[j, place(t)].astype(F32)).astype(BF16)


def feed_call(second, cot, gate, up, down):
    rows_n, hidden, width = down.shape
    cols_n = lax.axis_size("col")
    tokens, features = second.shape
    tile = 256
    tiles = hidden // tile
    half = (rows_n, hidden // 2, width)

    def place(i):
        return jnp.minimum(i, tiles - 1)

    return pl.pallas_call(
        feed_kernel,
        grid=(tiles + cols_n,),
        out_shape=(
            jax.ShapeDtypeStruct((tokens, hidden), BF16),
            jax.ShapeDtypeStruct((tokens, hidden), BF16),
            jax.ShapeDtypeStruct(half, BF16),
            jax.ShapeDtypeStruct((cols_n, tokens // cols_n, features), BF16),
        ),
        in_specs=[
            VM,
            VM,
            pl.BlockSpec((features, tile), lambda i: (0, place(i))),
            pl.BlockSpec((features, tile), lambda i: (0, place(i))),
            pl.BlockSpec((rows_n, tile, width), lambda i: (0, place(i), 0)),
        ],
        out_specs=(
            pl.BlockSpec((tokens, tile), lambda i: (0, place(i))),
            pl.BlockSpec((tokens, tile), lambda i: (0, place(i))),
            VM,
            pl.BlockSpec((1, tokens // cols_n, features), lambda i: (jnp.maximum(i - tiles, 0), 0, 0)),
        ),
        scratch_shapes=[
            pltpu.VMEM((tiles, tokens, tile), BF16),
            pltpu.VMEM((tiles, rows_n, tile, width), BF16),
            pltpu.VMEM(half, BF16),
            pltpu.VMEM(half, BF16),
            pltpu.SemaphoreType.DMA((tiles // 2,)),
            pltpu.SemaphoreType.DMA((tiles // 2,)),
        ],
        compiler_params=params(7),
        cost_estimate=cost(50),
    )(second, cot, gate, up, down)


def rotary_tables(positions):
    exponent = jnp.arange(0, HEAD, 2).astype(F32) / HEAD
    inverse = jnp.power(F32(THETA), -exponent)
    phase = positions[:, None] * inverse[None, :]
    phase = jnp.concatenate([phase] * (2 * 128 // HEAD), axis=1)
    return (jnp.cos(phase), jnp.sin(phase))


def local(
    activations, segments, positions, first_gain, query_weight, key_weight, value_weight, out_weight,
    second_gain, gate_weight, up_weight, down_weight, cotangent,
):
    rows = lax.axis_size("row")
    row, col = lax.axis_index("row"), lax.axis_index("col")
    length, width = activations.shape
    features = rows * width
    query_cols, key_cols = query_weight.shape[1], key_weight.shape[1]
    heads, kvs = query_cols // HEAD, key_cols // HEAD
    hidden_cols = gate_weight.shape[1]
    spare = jnp.zeros((width, -key_cols % 128), BF16)
    key_span = key_cols + spare.shape[1]
    qkv_cols = query_cols + 2 * key_span

    small = jnp.concatenate([segments.astype(F32), positions.astype(F32), first_gain, second_gain]).reshape(-1, 128)
    qkv_weight = jnp.concatenate([query_weight, key_weight, spare, value_weight, spare], axis=1)
    x_blocks, first, inv1, cot_tok, smalls, qkv_all, out_all_w, near = first_call(activations, cotangent, small, qkv_weight, out_weight)
    qkv_all = qkv_all.reshape(features, qkv_cols)
    smalls = smalls.reshape(rows, -1)
    own = lax.dynamic_slice_in_dim(smalls, col, 1, 0)[0]
    segment_own, position_own = own[:length], own[length : 2 * length]
    gain2 = smalls[:, 2 * length + width :].reshape(1, features)

    cosine, sine = rotary_tables(position_own)
    segc, segr = segment_own[:, None], segment_own[None]
    q, k, v, attn, following, gate_all = attend_call(first, qkv_all, cosine, sine, segc, segr, near, gate_weight, heads, kvs)
    middle, second_all, cot_all, up_all, down_all = middle_call(
        attn, out_all_w, x_blocks, gain2, cot_tok, near, following, up_weight, down_weight
    )
    gate_all, up_all = gate_all.reshape(features, hidden_cols), up_all.reshape(features, hidden_cols)
    second_all, cot_all = second_all.reshape(-1, features), cot_all.reshape(-1, features)
    dgate, dup, down_share, down_part = feed_call(second_all, cot_all, gate_all, up_all, down_all)
    dmid_all, gain2_grad, gate_grad, up_share = back_call(
        dgate, dup, gate_all.reshape(rows, width, hidden_cols), up_all.reshape(rows, width, hidden_cols), middle, cot_tok, gain2, second_all
    )
    dmid_all = dmid_all.reshape(length, features)

    dqkv, inner1, blk, outline, up_grad, down_grad = attend_back_call(
        dmid_all, out_all_w, q, k, v, cosine, sine, segc, segr, qkv_cols, attn, down_part, middle, up_share, down_share
    )
    dfirst, block_out, inner1, gains, qkv_grad, out_grad = last_call(
        dqkv, qkv_all, first, outline, blk, inner1.reshape(-1, 128), activations, inv1, gain2_grad
    )
    inner1 = jnp.sum(inner1, axis=0).reshape(length, 1) / (inv1 * features)
    own_x = activations.astype(F32)
    dmid_own = lax.dynamic_slice_in_dim(dmid_all, row * width, width, 1).astype(F32)
    input_grad = dmid_own + inv1 * first_gain[None] * dfirst - own_x * (inv1 * inv1 * inv1 * inner1)

    return (
        block_out,
        input_grad,
        gains[0, 0],
        qkv_grad[:, :query_cols],
        qkv_grad[:, query_cols : query_cols + key_cols],
        qkv_grad[:, query_cols + key_span : query_cols + key_span + key_cols],
        out_grad,
        gains[1, 0],
        gate_grad,
        up_grad,
        down_grad,
    )


def solution(mesh):
    tokens, block, swapped = P(("dp", "col"), "row"), P("row", "col"), P("col", "row")
    return jax.shard_map(
        local,
        mesh=mesh,
        in_specs=(
            tokens, P(("dp", "row")), P(("dp", "row")), P("row"), block, block, block, swapped,
            P("row"), block, block, swapped, tokens,
        ),
        out_specs=(tokens, tokens, P("row"), block, block, block, swapped, P("row"), block, block, swapped),
        check_vma=False,
    )
```

```python
import functools

import jax
import jax.numpy as jnp
from jax import lax
from jax.experimental import pallas as pl
from jax.experimental.pallas import tpu as pltpu
from jax.sharding import PartitionSpec as P

HEAD = 64
EPSILON = 1e-05
THETA = 500000.0
F32 = jnp.float32
BF16 = jnp.bfloat16


MESH = pl.DeviceIdType.MESH
VMEM_LIMIT = 60 * 1024 * 1024


def greet(row_size=0, col_size=0, dp_size=0):
    barrier = pltpu.get_barrier_semaphore()
    if row_size:
        row = lax.axis_index("row")
        for mask in range(1, row_size):
            pl.semaphore_signal(barrier, inc=1, device_id={"row": row ^ mask}, device_id_type=MESH)
    if col_size:
        col = lax.axis_index("col")

        @pl.when(col > 0)
        def _():
            pl.semaphore_signal(barrier, inc=1, device_id={"col": col - 1}, device_id_type=MESH)

        @pl.when(col < col_size - 1)
        def _():
            pl.semaphore_signal(barrier, inc=1, device_id={"col": col + 1}, device_id_type=MESH)

    if dp_size:
        pl.semaphore_signal(barrier, inc=1, device_id={"dp": 1 - lax.axis_index("dp")}, device_id_type=MESH)
    count = max(row_size - 1, 0) + (1 if dp_size else 0)
    if col_size:
        count = count + jnp.where(col > 0, 1, 0) + jnp.where(col < col_size - 1, 1, 0)
    pl.semaphore_wait(barrier, count)


def remote(src, dst, sends, recvs, place, device):
    return pltpu.make_async_remote_copy(
        src_ref=src, dst_ref=dst, send_sem=sends.at[place], recv_sem=recvs.at[place],
        device_id=device, device_id_type=MESH,
    )


class RowGather:
    def __init__(self, size, ref, sends, recvs, begin=0, count=None, first=0):
        self.size, self.ref, self.sends, self.recvs = size, ref, sends, recvs
        self.bits = size.bit_length() - 1
        self.row = lax.axis_index("row")
        self.begin, self.first = begin, first
        self.half = (count or ref.shape[1]) // 2
        self.all = [self.copies(step) for step in range(self.bits)]

    def rows(self, part):
        return pl.ds(pl.multiple_of(self.begin + part * self.half, 16), self.half)

    def order(self, part):
        return list(range(self.bits)) if part == 0 else list(range(self.bits))[::-1]

    def copies(self, step):
        out = []
        for part in range(2):
            order = self.order(part)
            for item in range(1 << step):
                mask = 0
                for j in range(step):
                    if item >> j & 1:
                        mask |= 1 << order[j]
                piece = self.ref.at[self.row ^ mask, self.rows(part)]
                place = self.first + part * (self.size - 1) + (1 << step) - 1 + item
                out.append(remote(piece, piece, self.sends, self.recvs, place, {"row": self.row ^ (1 << order[step])}))
        return out

    def start(self):
        for step in range(self.bits):
            for part in range(2):
                self.all[step][part << step].start()

    def event(self, step, seen=None):
        for part in range(2):
            order = self.order(part)
            for item in range(1 << step):
                self.all[step][(part << step) + item].wait_recv()
                got = item | 1 << step
                for later in range(step + 1, self.bits):
                    self.all[later][(part << later) + got].start()
                if seen is not None:
                    mask = 0
                    for j in range(step + 1):
                        if got >> j & 1:
                            mask |= 1 << order[j]
                    seen(mask, part)

    def finish(self):
        for step in range(self.bits):
            for copy in self.all[step]:
                copy.wait_send()

    def run(self):
        for step in range(self.bits):
            self.event(step)
        self.finish()


class SharedGather:
    def __init__(self, size, shard, full, copied, sends, recvs, score, rcore, first):
        self.core, self.row = lax.axis_index("dp"), lax.axis_index("row")
        self.size, self.full, self.score, self.rcore, self.first = size, full, score, rcore, first * 2 * (size - 1)
        share = full.shape[1] // 2
        self.own = pltpu.make_async_copy(shard, full.at[self.row], copied.at[first])
        self.gather = RowGather(size, full, sends, recvs, self.core * share, share, self.first)

    def across(self, mask, part):
        piece = self.full.at[self.row ^ mask, self.gather.rows(part)]
        return remote(piece, piece, self.score, self.rcore, self.first + part * (self.size - 1) + mask - 1, {"dp": 1 - self.core})

    def load(self):
        self.own.start()

    def start(self):
        self.own.wait()
        self.gather.start()

    def event(self, step):
        self.gather.event(step, lambda mask, part: self.across(mask, part).start())

    def finish(self):
        self.gather.finish()
        for mask in range(1, self.size):
            for part in range(2):
                self.across(mask, part).wait()

    @staticmethod
    def scratch(size, count):
        dma = pltpu.SemaphoreType.DMA
        return [dma((count,))] + [dma((count * 2 * (size - 1),))] * 4


class RowScatter:
    def __init__(self, size, part_ref, recv_ref, sends, recvs, begin=0):
        self.size, self.part, self.recv = size, part_ref, recv_ref
        self.bits = size.bit_length() - 1
        self.row = lax.axis_index("row")
        half = recv_ref.shape[1] // 2
        self.rows = [pl.ds(part * half, half) for part in range(2)]
        self.own = [pl.ds(pl.multiple_of(begin + part * half, 16), half) for part in range(2)]
        self.plans = []
        for part in range(2):
            order = self.order(part)
            steps, held = [], {}
            for step in range(self.bits):
                bit, rest = 1 << order[step], order[step + 1 :]
                count = 1 << len(rest)
                copies, sums = [], {}
                for item in range(count - 1, -1, -1):
                    mask = sum(1 << other for j, other in enumerate(rest) if item >> j & 1)
                    place = size - 2 * count + item
                    copy = remote(
                        self.spot(part, mask ^ bit, held), recv_ref.at[place, self.rows[part]],
                        sends, recvs, part * (size - 1) + place, {"row": self.row ^ bit},
                    )
                    copies.append((mask, place, held.get(mask), copy))
                    sums[mask] = place
                held = sums
                steps.append(copies)
            self.plans.append(steps)

    def spot(self, part, mask, held):
        if mask in held:
            return self.recv.at[held[mask], self.rows[part]]
        return self.part.at[self.row ^ mask, self.own[part]]

    def order(self, part):
        return list(range(self.bits)) if part == 0 else list(range(self.bits))[::-1]

    def start(self):
        for part in range(2):
            for copies in self.plans[part][0]:
                copies[3].start()

    def event(self, step, finish):
        last = step + 1 == self.bits
        for part in range(2):
            rows, own = self.rows[part], self.own[part]
            for mask, place, before, copy in self.plans[part][step]:
                copy.wait_recv()
                size, begin, start = min(64, rows.size), own.start, rows.start

                @pl.loop(0, rows.size // size)
                def _(i):
                    here = pl.ds(pl.multiple_of(start + i * size, 16), size)
                    if before is None:
                        had = self.part[self.row ^ mask, pl.ds(pl.multiple_of(begin + i * size, 16), size)]
                    else:
                        had = self.recv[before, here]
                    total = had.astype(F32) + self.recv[place, here].astype(F32)
                    if last:
                        finish(here, total)
                    else:
                        self.recv[place, here] = total.astype(BF16)

                if last:
                    continue
                for mask2, _, _, copy2 in self.plans[part][step + 1]:
                    if mask2 ^ 1 << self.order(part)[step + 1] == mask:
                        copy2.start()

    def close(self):
        for part in range(2):
            for step in self.plans[part]:
                for _, _, _, copy in step:
                    copy.wait_send()

    def run(self, finish):
        self.start()
        for step in range(self.bits):
            self.event(step, finish)
        self.close()


class ColGather:
    def __init__(self, size, ref, sends, recvs, begin=0, end=None):
        self.size, self.ref, self.sends, self.recvs = size, ref, sends, recvs
        self.begin, self.end = begin, size - 1 if end is None else end
        self.col = lax.axis_index("col")

    def sides(self, step):
        size, col = self.size, self.col
        return (
            (0, lax.rem(col - step + size, size), col >= step, col < size - 1),
            (1, lax.rem(col + step, size), col + step < size, col > 0),
        )

    def copy(self, side, step):
        size, col = self.size, self.col
        piece = self.ref.at[self.sides(step)[side][1]]
        target = lax.rem(col + (1 if side == 0 else size - 1), size)
        return remote(piece, piece, self.sends, self.recvs, side * (size - 1) + step, {"col": target})

    def event(self, step, seen=None):
        for side, place, has, goes in self.sides(step):
            if step > self.begin:

                @pl.when(has)
                def _():
                    self.copy(side, step - 1).wait_recv()

            if step < self.end:

                @pl.when(has & goes)
                def _():
                    self.copy(side, step).start()

            if seen is not None and (step or side == 0):

                @pl.when(has)
                def _():
                    seen(place)

    def finish(self):
        for step in range(self.begin, self.end):
            for side, place, has, goes in self.sides(step):

                @pl.when(has & goes)
                def _():
                    self.copy(side, step).wait_send()

    def run(self):
        for step in range(self.begin, self.end + 1):
            self.event(step)
        self.finish()


class ColScatter:
    def __init__(self, size, part, recv, sends, recvs, begin=0, count=None, first=0):
        self.size, self.part, self.recv, self.sends, self.recvs = size, part, recv, sends, recvs
        self.begin, self.count, self.first = begin, count or part.shape[1], first
        self.col = lax.axis_index("col")
        self.times = size

    def copy(self, side, target, source):
        step = 1 if side == 0 else self.size - 1
        rows = pl.ds(self.begin, self.count)
        return pltpu.make_async_remote_copy(
            src_ref=self.recv.at[target + 1 - side, rows] if source is None else source.at[target, rows],
            dst_ref=self.recv.at[target + 1 - side, rows], send_sem=self.sends.at[2 * self.first + side],
            recv_sem=self.recvs.at[(2 * self.first + side) * self.size + target],
            device_id={"col": lax.rem(self.col + step, self.size)}, device_id_type=MESH,
        )

    def event(self, time, prepare=None):
        size, col = self.size, self.col
        for side, first, step in ((0, col == 0, time - col), (1, col == size - 1, time - (size - 1 - col))):
            target = size - 1 - step if side == 0 else step
            valid = (step >= 0) & ((target >= col) if side == 0 else (target <= col))
            place = lax.rem(target + 4 * size, size)

            if prepare is not None:

                @pl.when(valid & ((target != col) | (side == 0)))
                def _():
                    prepare(place)

            @pl.when(valid & jnp.logical_not(first))
            def _():
                self.copy(side, place, self.part).wait_recv()

            @pl.when(valid & jnp.logical_not(first) & (target != col))
            def _():
                chunk = min(64, self.count)

                @pl.loop(0, self.count // chunk)
                def _(i):
                    rows = pl.ds(pl.multiple_of(self.begin + i * chunk, 16), chunk)
                    self.recv[place + 1 - side, rows] = (
                        self.recv[place + 1 - side, rows].astype(F32) + self.part[place, rows].astype(F32)
                    ).astype(BF16)

            @pl.when(valid & (step > 0))
            def _():
                self.copy(side, place, self.part).wait_send()

            @pl.when(valid & (target != col) & first)
            def _():
                self.copy(side, place, self.part).start()

            @pl.when(valid & (target != col) & jnp.logical_not(first))
            def _():
                self.copy(side, place, None).start()

    def total(self, rows):
        got = self.part[self.col, rows].astype(F32)
        got += jnp.where(self.col > 0, self.recv[self.col + 1, rows].astype(F32), 0.0)
        got += jnp.where(self.col < self.size - 1, self.recv[self.col, rows].astype(F32), 0.0)
        return got


VM = pl.BlockSpec(memory_space=pltpu.VMEM)


def params(ident):
    return pltpu.CompilerParams(collective_id=ident, has_side_effects=True, vmem_limit_bytes=VMEM_LIMIT)


def keep_near(size, line, near, step):
    col = lax.axis_index("col")
    for side, place, has in ((0, col - step, col >= step), (1, col + step, col + step < size)):

        @pl.when(has)
        def _():
            near[side] = line[lax.rem(place + size, size)]


def take_near(size, line, near, step):
    col = lax.axis_index("col")
    for side, place, has in ((0, col - step, col >= step), (1, col + step, col + step < size)):

        @pl.when(has)
        def _():
            line[lax.rem(place + size, size)] = near[side]


def first_kernel(
    size, act_ref, cot_ref, small_ref, qkv_ref, out_ref,
    x_ref, first_ref, inv_ref, tok_ref, smalls_ref, qkvs_ref, outs_ref,
    near_ref,
    got_ref, zq_ref, zo_ref, zc_ref, s1, r1, s2, r2, s3, r3, szq, rzq, szo, rzo, srow, rrow, score, rcore, szc, rzc,
):
    row, col, core = lax.axis_index("row"), lax.axis_index("col"), lax.axis_index("dp")
    length, width = act_ref.shape
    quarter = length // size
    small_rows = small_ref.shape[0]
    gain_row = 2 * length // 128
    x_ref[row] = act_ref[...]
    smalls_ref[row] = small_ref[...]
    blocks = ((qkv_ref, zq_ref, qkvs_ref, szq, rzq), (out_ref, zo_ref, outs_ref, szo, rzo))
    for block, line, _, _, _ in blocks:
        share = block.shape[0] // 2
        line[col] = block[pl.ds(pl.multiple_of(core * share, 16), share)]
    greet(row_size=size, col_size=size, dp_size=2)
    gather = RowGather(size, x_ref, s1, r1)
    smalls = [
        remote(small_ref, smalls_ref.at[row], s3, r3, mask - 1, {"row": row ^ mask}) for mask in range(1, size)
    ]
    lines = [ColGather(size, line, sends, recvs) for _, line, _, sends, recvs in blocks]
    lines[0].event(0)
    for move in smalls:
        move.start()
    moves = [
        remote(cot_ref.at[pl.ds((row ^ mask) * quarter, quarter)], got_ref.at[row], s2, r2, mask - 1, {"row": row ^ mask})
        for mask in range(1, size)
    ]
    for move in moves:
        move.start()
    gather.start()
    got_ref[row] = cot_ref[pl.ds(pl.multiple_of(row * quarter, 16), quarter)]

    def half(ref, place):
        share = ref.shape[1] // 2
        return ref.at[place, pl.ds(pl.multiple_of(core * share, 16), share)]

    def hand(which, mask):
        _, line, full, _, _ = blocks[which]
        return remote(line.at[row ^ mask], half(full, row), srow, rrow, which * (size - 1) + mask - 1, {"row": row ^ mask})

    def across(which, mask):
        full = blocks[which][2]
        piece = half(full, row ^ mask)
        return remote(piece, piece, score, rcore, which * size + mask, {"dp": 1 - core})

    def seen(which):
        def act(place):
            _, line, full, _, _ = blocks[which]

            @pl.when(place == row)
            def _():
                share = full.shape[1] // 2
                full[row, pl.ds(pl.multiple_of(core * share, 16), share)] = line[row]
                across(which, 0).start()

            for mask in range(1, size):

                @pl.when(place == row ^ mask)
                def _():
                    hand(which, mask).start()

        return act

    act, act1 = seen(0), seen(1)
    act(col)
    near = ColGather(size, zc_ref, szc, rzc, 0, 1)
    for step in range(1, size - 1):
        lines[0].event(step, act)
    for move in moves:
        move.wait()
    for j in range(size):
        zc_ref[col, :, j * width : (j + 1) * width] = got_ref[j]
    tok_ref[...] = zc_ref[col]
    near.event(0)
    lines[1].event(0)
    lines[0].event(size - 1, act)
    act1(col)
    gather.event(0)
    lines[1].event(1, act1)
    for step in range(1, gather.bits):
        gather.event(step)
    for move in smalls:
        move.wait()

    @pl.loop(0, length // 128)
    def _(i):
        rows = pl.ds(pl.multiple_of(i * 128, 128), 128)
        total = jnp.zeros((128, 1), F32)
        for j in range(size):
            value = x_ref[j, rows].astype(F32)
            total += jnp.sum(value * value, axis=1, keepdims=True)
        inverse = lax.rsqrt(total / (size * width) + EPSILON)
        inv_ref[rows] = inverse
        for j in range(size):
            for k in range(width // 128):
                gain = smalls_ref[j, gain_row + k : gain_row + k + 1]
                value = x_ref[j, rows, k * 128 : (k + 1) * 128].astype(F32)
                first_ref[rows, j * width + k * 128 : j * width + (k + 1) * 128] = (value * inverse * gain).astype(BF16)

    for mask in range(1, size):
        hand(0, mask).wait_recv()
        across(0, mask).start()
    for step in range(2, size):
        lines[1].event(step, act1)
    for mask in range(1, size):
        hand(1, mask).wait_recv()
        across(1, mask).start()
    near.event(1)
    keep_near(size, zc_ref, near_ref, 1)
    near.finish()
    gather.finish()
    for line in lines:
        line.finish()
    for which in range(2):
        for mask in range(1, size):
            hand(which, mask).wait_send()
        for mask in range(size):
            across(which, mask).wait()


def first_call(activations, cotangent, small, qkv_weight, out_weight):
    size = lax.axis_size("row")
    length, width = activations.shape
    quarter = length // size
    qkv_cols, heads_cols = qkv_weight.shape[1], out_weight.shape[0]
    dma = pltpu.SemaphoreType.DMA
    return pl.pallas_call(
        functools.partial(first_kernel, size),
        out_shape=(
            jax.ShapeDtypeStruct((size, length, width), BF16),
            jax.ShapeDtypeStruct((length, size * width), BF16),
            jax.ShapeDtypeStruct((length, 1), F32),
            jax.ShapeDtypeStruct((quarter, size * width), BF16),
            jax.ShapeDtypeStruct((size,) + small.shape, F32),
            jax.ShapeDtypeStruct((size,) + qkv_weight.shape, BF16),
            jax.ShapeDtypeStruct((size,) + out_weight.shape, BF16),
            jax.ShapeDtypeStruct((2, quarter, size * width), BF16),
        ),
        in_specs=[VM] * 5,
        out_specs=(VM,) * 8,
        scratch_shapes=[
            pltpu.VMEM((size, quarter, width), BF16),
            pltpu.VMEM((size, width // 2, qkv_cols), BF16),
            pltpu.VMEM((size, heads_cols // 2, width), BF16),
            pltpu.VMEM((size, quarter, size * width), BF16),
        ]
        + [dma((2 * (size - 1),))] * 2
        + [dma((size - 1,))] * 4
        + [dma((2 * (size - 1),))] * 4
        + [dma((2 * (size - 1),))] * 2
        + [dma((2 * size,))] * 2
        + [dma((2 * (size - 1),))] * 2,
        compiler_params=params(1),
    )(activations, cotangent, small, qkv_weight, out_weight)


def turn(values, low):
    return jnp.where(low, -pltpu.roll(values, 128 - HEAD // 2, 1), pltpu.roll(values, HEAD // 2, 1))


def low_columns(rows):
    return lax.broadcasted_iota(jnp.int32, (rows, 128), 1) % HEAD < HEAD // 2


def masked_scores(query, key, seg_col, seg_row, first_row):
    scores = lax.dot_general(query, key, (((1,), (1,)), ((), ())), preferred_element_type=F32)
    rows = lax.broadcasted_iota(jnp.int32, scores.shape, 0) + first_row
    columns = lax.broadcasted_iota(jnp.int32, scores.shape, 1)
    allowed = (seg_col == seg_row) & (rows >= columns)
    return jnp.where(allowed, scores, -1e30)


def attend_kernel(
    size, first_ref, weight_ref, cos_ref, sin_ref, segc_ref, segr_ref, near_ref, gate_ref,
    q_ref, k_ref, v_ref, o_ref, next_ref, gates_ref, oh_ref, zc_ref, szc, rzc, *shared,
):
    bulk = SharedGather(size, gate_ref, gates_ref, *shared, 0)
    bulk.load()
    take_near(size, zc_ref, near_ref, 1)
    greet(row_size=size, col_size=size, dp_size=2)
    bulk.start()
    line = ColGather(size, zc_ref, szc, rzc, 1, 2)
    line.event(1)
    heads, length, _ = q_ref.shape
    kvs = k_ref.shape[0]
    group = heads // kvs
    query_cols = heads * HEAD
    key_cols = (weight_ref.shape[1] - query_cols) // 2
    block = 256

    @pl.loop(0, length // block)
    def _(i):
        rows = pl.ds(pl.multiple_of(i * block, block), block)
        low = low_columns(block)
        cosine, sine = cos_ref[rows], sin_ref[rows]
        whole = jnp.dot(first_ref[rows], weight_ref[...], preferred_element_type=F32)
        for ref, count, start, factor in ((q_ref, heads, 0, HEAD ** (-0.5)), (k_ref, kvs, query_cols, 1.0)):
            for j in range((count + 1) // 2):
                part = whole[:, start + 128 * j : start + 128 * (j + 1)]
                part = ((part * cosine + turn(part, low) * sine) * factor).astype(BF16)
                for side in range(min(2, count - 2 * j)):
                    ref[2 * j + side, rows] = part[:, side * HEAD : (side + 1) * HEAD]
        for j in range(kvs):
            at = query_cols + key_cols + j * HEAD
            v_ref[j, rows] = whole[:, at : at + HEAD].astype(BF16)

    @pl.loop(0, heads)
    def _(head):
        kv = lax.div(head, group)
        for i in range(length // block):
            rows, extent = slice(i * block, (i + 1) * block), (i + 1) * block
            scores = masked_scores(q_ref[head, rows], k_ref[kv, :extent], segc_ref[rows], segr_ref[:, :extent], i * block)
            top = jnp.max(scores, axis=1, keepdims=True)
            weights = jnp.exp(scores - top)
            total = jnp.sum(weights, axis=1, keepdims=True)
            mixed = jnp.dot(weights.astype(BF16), v_ref[kv, :extent], preferred_element_type=F32)
            oh_ref[head, rows] = (mixed / total).astype(BF16)

    for head in range(heads):
        o_ref[:, head * HEAD : (head + 1) * HEAD] = oh_ref[head]
    for step in range(bulk.gather.bits):
        bulk.event(step)
    line.event(2)
    keep_near(size, zc_ref, next_ref, 2)
    line.finish()
    bulk.finish()


def attend_call(first, weight, cosine, sine, segc, segr, near, gate, heads, kvs):
    size = lax.axis_size("row")
    length = first.shape[0]
    dma = pltpu.SemaphoreType.DMA
    return pl.pallas_call(
        functools.partial(attend_kernel, size),
        out_shape=(
            jax.ShapeDtypeStruct((heads, length, HEAD), BF16),
            jax.ShapeDtypeStruct((kvs, length, HEAD), BF16),
            jax.ShapeDtypeStruct((kvs, length, HEAD), BF16),
            jax.ShapeDtypeStruct((length, heads * HEAD), BF16),
            jax.ShapeDtypeStruct(near.shape, BF16),
            jax.ShapeDtypeStruct((size,) + gate.shape, BF16),
        ),
        in_specs=[VM] * 8,
        out_specs=(VM,) * 5 + (pl.BlockSpec(memory_space=pl.ANY),),
        scratch_shapes=[
            pltpu.VMEM((heads, length, HEAD), BF16),
            pltpu.VMEM((size,) + near.shape[1:], BF16),
            dma((2 * (size - 1),)), dma((2 * (size - 1),)),
        ]
        + SharedGather.scratch(size, 1),
        compiler_params=params(6),
        cost_estimate=cost(45),
    )(first, weight, cosine, sine, segc, segr, near, gate)


class swap_halves:
    def __init__(self, part, other, sends, recvs):
        core = lax.axis_index("dp")
        share = part.shape[1] // 2
        self.move = remote(
            part.at[:, pl.ds(pl.multiple_of((1 - core) * share, 16), share)], other, sends, recvs, 0, {"dp": 1 - core}
        )

    def start(self):
        self.move.start()

    def wait(self):
        self.move.wait()


def add_halves(part, other, share):
    rows = pl.ds(pl.multiple_of(lax.axis_index("dp") * share.shape[1], 16), share.shape[1])
    for j in range(part.shape[0]):
        share[j] = (part[j, rows].astype(F32) + other[j].astype(F32)).astype(BF16)


def row_moves(size, source, target, sends, recvs, first, begin):
    row = lax.axis_index("row")
    if begin:
        target[row] = source[row]
    for mask in range(1, size):
        move = remote(source.at[row ^ mask], target.at[row], sends, recvs, first + mask - 1, {"row": row ^ mask})
        if begin:
            move.start()
        else:
            move.wait()


def cost(micros):
    return pl.CostEstimate(flops=int(micros * 1e9), bytes_accessed=1 << 20, transcendentals=0)


def attend_back_kernel(
    dmid_ref, weight_ref, q_ref, k_ref, v_ref, cos_ref, sin_ref, segc_ref, segr_ref,
    attn_ref, down_ref, mid_ref, upshare_ref, gateshare_ref,
    dqkv_ref, inner_ref, blk_ref, line_ref, gup_ref, ggate_ref, do_ref, dq_ref, dk_ref, dv_ref,
    recv_ref, part_ref, other_ref, share_ref, urecv_ref, drecv_ref, ustage_ref, dstage_ref,
    s1, r1, score, rcore, srow, rrow, su, ru, sd, rd, copied, sf, rf,
):
    row, core = lax.axis_index("row"), lax.axis_index("dp")
    cols_n = down_ref.shape[0]
    heads, length, _ = q_ref.shape
    kvs = k_ref.shape[0]
    group = heads // kvs
    query_cols = heads * HEAD
    key_cols = (dqkv_ref.shape[1] - query_cols) // 2
    block = 256
    parts, _, width = weight_ref.shape
    greet(row_size=parts, col_size=cols_n, dp_size=2)
    line = ColScatter(cols_n, down_ref, recv_ref, s1, r1)
    line.event(0)
    sums = [
        (RowScatter(parts, upshare_ref, urecv_ref, su, ru), ustage_ref, gup_ref),
        (RowScatter(parts, gateshare_ref, drecv_ref, sd, rd), dstage_ref, ggate_ref),
    ]
    for scatter, _, _ in sums:
        scatter.start()
    for j in range(parts):
        part_ref[j] = lax.dot_general(
            attn_ref[...], dmid_ref[:, j * width : (j + 1) * width], (((0,), (0,)), ((), ())), preferred_element_type=F32
        ).astype(BF16)
    cross = swap_halves(part_ref, other_ref, score, rcore)
    cross.start()
    dk_ref[...] = jnp.zeros_like(dk_ref)
    dv_ref[...] = jnp.zeros_like(dv_ref)
    inner_ref[...] = jnp.zeros_like(inner_ref)

    @pl.loop(0, length // block)
    def _(i):
        rows = pl.ds(pl.multiple_of(i * block, block), block)
        total = jnp.zeros((block, query_cols), F32)
        for j in range(parts):
            total += lax.dot_general(
                dmid_ref[rows, j * width : (j + 1) * width], weight_ref[j], (((1,), (1,)), ((), ())), preferred_element_type=F32
            )
        for head in range(heads):
            do_ref[head, rows] = total[:, head * HEAD : (head + 1) * HEAD].astype(BF16)

    @pl.loop(0, heads)
    def _(head):
        @pl.when(head == min(1, heads - 1))
        def _():
            cross.wait()
            add_halves(part_ref, other_ref, share_ref)
            row_moves(parts, share_ref, line_ref, srow, rrow, 0, True)

        @pl.when(head == heads // 2)
        def _():
            line.event(1)

        kv = lax.div(head, group)
        for i in range(length // block):
            rows, extent = slice(i * block, (i + 1) * block), (i + 1) * block
            query, keys, grads = q_ref[head, rows], k_ref[kv, :extent], do_ref[head, rows]
            scores = masked_scores(query, keys, segc_ref[rows], segr_ref[:, :extent], i * block)
            top = jnp.max(scores, axis=1, keepdims=True)
            weights = jnp.exp(scores - top)
            weights = weights * (1.0 / jnp.sum(weights, axis=1, keepdims=True))
            back = lax.dot_general(grads, v_ref[kv, :extent], (((1,), (1,)), ((), ())), preferred_element_type=F32)
            dv_ref[kv, :extent] += lax.dot_general(
                weights.astype(BF16), grads, (((0,), (0,)), ((), ())), preferred_element_type=F32
            )
            ds = (weights * (back - jnp.sum(weights * back, axis=1, keepdims=True))).astype(BF16)
            dq = jnp.dot(ds, keys, preferred_element_type=F32)
            inner_ref[rows] += jnp.sum(dq * query.astype(F32), axis=1, keepdims=True)
            for side in range(2):

                @pl.when(lax.rem(head, 2) == side)
                def _():
                    dq_ref[lax.div(head, 2), rows, side * HEAD : (side + 1) * HEAD] = dq

            dk_ref[kv, :extent] += lax.dot_general(ds, query, (((0,), (0,)), ((), ())), preferred_element_type=F32)

    @pl.loop(0, length // block)
    def _(i):
        rows = pl.ds(pl.multiple_of(i * block, block), block)
        low = low_columns(block)
        cosine, sine = cos_ref[rows], sin_ref[rows]
        for ref, count, start, factor in ((dq_ref, heads, 0, HEAD ** (-0.5)), (dk_ref, kvs, query_cols, 1.0), (dv_ref, kvs, query_cols + key_cols, None)):
            for j in range((count + 1) // 2):
                if ref is dq_ref:
                    part = dq_ref[j, rows]
                else:
                    sides = [ref[2 * j + side, rows] if 2 * j + side < count else jnp.zeros((block, HEAD), F32) for side in range(2)]
                    part = jnp.concatenate(sides, axis=1)
                if factor is not None:
                    part = (part * cosine - turn(part * sine, low)) * factor
                dqkv_ref[rows, start + 128 * j : start + 128 * (j + 1)] = part.astype(BF16)
        more = jnp.zeros((block, 1), F32)
        for kv in range(kvs):
            more += jnp.sum(dk_ref[kv, rows] * k_ref[kv, rows].astype(F32) + dv_ref[kv, rows] * v_ref[kv, rows].astype(F32), axis=1, keepdims=True)
        inner_ref[rows] += more

    def finish(stage):
        def act(rows, total):
            stage[rows] = total

        return act

    if cols_n > 2:
        line.event(2)
    bits = sums[0][0].bits
    for step in range(bits - 1):
        for scatter, stage, _ in sums:
            scatter.event(step, finish(stage))
    for time in range(3, line.times):
        line.event(time)
    results = []
    for k, (scatter, stage, out) in enumerate(sums):
        scatter.event(bits - 1, finish(stage))
        moves = settle(stage, out, core, copied, sf, rf, k)
        for move in moves:
            move.start()
        results += moves
        scatter.close()

    @pl.loop(0, mid_ref.shape[0] // 64)
    def _(i):
        rows = pl.ds(pl.multiple_of(i * 64, 16), 64)
        total = mid_ref[rows] + line.total(rows)
        for j in range(parts):
            blk_ref[j, rows] = total[:, j * width : (j + 1) * width].astype(BF16)

    row_moves(parts, share_ref, line_ref, srow, rrow, 0, False)
    for move in results:
        move.wait()


def attend_back_call(dmid, weight, q, k, v, cosine, sine, segc, segr, columns, attn, down, middle, upshare, gateshare):
    rows_n, cols_n = lax.axis_size("row"), lax.axis_size("col")
    _, heads_cols, width = weight.shape
    quarter = middle.shape[0]
    dma = pltpu.SemaphoreType.DMA
    heads, length, _ = q.shape
    kvs = k.shape[0]
    return pl.pallas_call(
        attend_back_kernel,
        out_shape=(
            jax.ShapeDtypeStruct((length, columns), BF16),
            jax.ShapeDtypeStruct((length, 1), F32),
            jax.ShapeDtypeStruct((rows_n, quarter, width), BF16),
            jax.ShapeDtypeStruct((rows_n, heads_cols // 2, width), BF16),
            jax.ShapeDtypeStruct((2 * upshare.shape[1], upshare.shape[2]), F32),
            jax.ShapeDtypeStruct((2 * gateshare.shape[1], gateshare.shape[2]), F32),
        ),
        in_specs=[VM] * 14,
        out_specs=(VM,) * 4 + (pl.BlockSpec(memory_space=pl.ANY),) * 2,
        scratch_shapes=[
            pltpu.VMEM((heads, length, HEAD), BF16),
            pltpu.VMEM(((heads + 1) // 2, length, 2 * HEAD), F32),
            pltpu.VMEM((kvs, length, HEAD), F32),
            pltpu.VMEM((kvs, length, HEAD), F32),
            pltpu.VMEM((down.shape[0] + 1,) + down.shape[1:], BF16),
            pltpu.VMEM(weight.shape, BF16),
            pltpu.VMEM((rows_n, heads_cols // 2, width), BF16),
            pltpu.VMEM((rows_n, heads_cols // 2, width), BF16),
            pltpu.VMEM((rows_n - 1,) + upshare.shape[1:], BF16),
            pltpu.VMEM((rows_n - 1,) + gateshare.shape[1:], BF16),
            pltpu.VMEM(upshare.shape[1:], F32),
            pltpu.VMEM(gateshare.shape[1:], F32),
            dma((2,)), dma((2 * cols_n,)), dma((1,)), dma((1,)), dma((rows_n - 1,)), dma((rows_n - 1,)),
        ]
        + [dma((2 * (rows_n - 1),))] * 4
        + [dma((2,))] * 3
        + [
        ],
        compiler_params=params(5),
        cost_estimate=cost(80),
    )(dmid, weight, q, k, v, cosine, sine, segc, segr, attn, down, middle, upshare, gateshare)


def middle_kernel(
    rows_n, cols_n, attn_ref, weight_ref, x_ref, gain_ref, tok_ref, near_ref, next_ref, up_ref, down_ref,
    mid_ref, second_ref, cot_ref, ups_ref, downs_ref, part_ref, recv_ref, s1, r1, s2, r2, szc, rzc, *shared,
):
    row, col = lax.axis_index("row"), lax.axis_index("col")
    quarter, features = mid_ref.shape
    width = features // rows_n
    bulks = [SharedGather(rows_n, up_ref, ups_ref, *shared, 0), SharedGather(rows_n, down_ref, downs_ref, *shared, 1)]
    for bulk in bulks:
        bulk.load()
    cot_ref[col] = tok_ref[...]
    take_near(cols_n, cot_ref, near_ref, 1)
    take_near(cols_n, cot_ref, next_ref, 2)
    greet(row_size=rows_n, col_size=cols_n, dp_size=2)
    rest = ColGather(cols_n, cot_ref, szc, rzc, 2)
    rest.event(2)

    @pl.loop(0, rows_n)
    def _(i):
        own = attn_ref[pl.ds(pl.multiple_of(i * quarter, 16), quarter)]
        for j in range(rows_n):
            part_ref[i, :, j * width : (j + 1) * width] = jnp.dot(own, weight_ref[j], preferred_element_type=F32).astype(BF16)

    def finish(rows, total):
        own = pl.ds(row * quarter + rows.start, rows.size)
        squares = jnp.zeros((rows.size, 1), F32)
        for j in range(rows_n):
            columns = slice(j * width, (j + 1) * width)
            value = total[:, columns] + x_ref[j, own].astype(F32)
            mid_ref[rows, columns] = value
            squares += jnp.sum(value * value, axis=1, keepdims=True)
        inverse = lax.rsqrt(squares / features + EPSILON)
        second_ref[col, rows] = (mid_ref[rows] * inverse * gain_ref[...]).astype(BF16)

    RowScatter(rows_n, part_ref, recv_ref, s1, r1).run(finish)
    line = ColGather(cols_n, second_ref, s2, r2)
    line.event(0)
    for bulk in bulks:
        bulk.start()
    for step in range(3, cols_n):
        rest.event(step)
    rest.finish()
    line.event(1)
    bits = bulks[0].gather.bits
    for bulk in bulks:
        bulk.event(0)
    for step in range(2, cols_n):
        line.event(step)
    for step in range(1, bits):
        for bulk in bulks:
            bulk.event(step)
    for bulk in bulks:
        bulk.finish()
    line.finish()


def middle_call(attn, weight, x, gain, tok, near, following, up, down):
    rows_n, cols_n = lax.axis_size("row"), lax.axis_size("col")
    length, features = attn.shape[0], weight.shape[0] * weight.shape[2]
    quarter = length // rows_n
    dma = pltpu.SemaphoreType.DMA
    anywhere = pl.BlockSpec(memory_space=pl.ANY)
    return pl.pallas_call(
        functools.partial(middle_kernel, rows_n, cols_n),
        out_shape=(
            jax.ShapeDtypeStruct((quarter, features), F32),
            jax.ShapeDtypeStruct((cols_n, quarter, features), BF16),
            jax.ShapeDtypeStruct((cols_n, quarter, features), BF16),
            jax.ShapeDtypeStruct((rows_n,) + up.shape, BF16),
            jax.ShapeDtypeStruct((rows_n,) + down.shape, BF16),
        ),
        in_specs=[VM] * 9,
        out_specs=(VM, VM, VM, anywhere, anywhere),
        scratch_shapes=[
            pltpu.VMEM((rows_n, quarter, features), BF16),
            pltpu.VMEM((rows_n - 1, quarter, features), BF16),
        ]
        + [dma((2 * (rows_n - 1),))] * 2
        + [dma((2 * (cols_n - 1),))] * 4
        + SharedGather.scratch(rows_n, 2),
        compiler_params=params(2),
        cost_estimate=cost(130),
    )(attn, weight, x, gain, tok, near, following, up, down)


def settle(stage, out, core, copied, sends, recvs, place):
    rows = pl.ds(pl.multiple_of(core * stage.shape[0], 8), stage.shape[0])
    return (
        pltpu.make_async_copy(stage, out.at[rows], copied.at[place]),
        remote(stage, out.at[rows], sends, recvs, place, {"dp": 1 - core}),
    )


def back_kernel(
    rows_n, cols_n, dgate_ref, dup_ref, gate_ref, up_ref, mid_ref, tok_ref, gain_ref, second_ref, down_ref,
    dmid_ref, grad_ref, gdown_ref, share0_ref, share1_ref,
    w0_ref, w1_ref, part_ref, recv_ref, other_ref, drecv_ref, stage_ref,
    loads, s1, r1, s2, r2, sg, rg, score, rcore, copied, sf, rf, free,
):
    row, col, core = lax.axis_index("row"), lax.axis_index("col"), lax.axis_index("dp")
    quarter, features = mid_ref.shape
    width = features // rows_n
    hidden = dgate_ref.shape[1]
    share = width // 2
    moves = [pltpu.make_async_copy(ref, kept, loads.at[k]) for k, (ref, kept) in enumerate(((gate_ref, w0_ref), (up_ref, w1_ref)))]
    for move in moves:
        move.start()
    greet(row_size=rows_n, col_size=cols_n, dp_size=2)
    for move in moves:
        move.wait()

    def prepare(target):
        rows = pl.ds(pl.multiple_of(target * quarter, 16), quarter)

        @pl.loop(0, rows_n)
        def _(i):
            columns = pl.ds(pl.multiple_of(i * width, 128), width)
            value = lax.dot_general(dgate_ref[rows], w0_ref[i], (((1,), (1,)), ((), ())), preferred_element_type=F32)
            value += lax.dot_general(dup_ref[rows], w1_ref[i], (((1,), (1,)), ((), ())), preferred_element_type=F32)
            part_ref[target, :, columns] = value.astype(BF16)

    tile = min(512, hidden)

    def product(right, kept):
        @pl.loop(0, rows_n)
        def _(i):
            for t in range(hidden // tile):
                columns = slice(t * tile, (t + 1) * tile)
                kept[i, :, columns] = lax.dot_general(
                    second_ref[:, pl.ds(pl.multiple_of(i * width, 128), width)], right[:, columns], (((0,), (0,)), ((), ())),
                    preferred_element_type=F32,
                ).astype(BF16)

    def add(kept):
        chunk = min(64, share)
        chunks = share // chunk

        @pl.loop(0, rows_n * chunks)
        def _(i):
            block, start = lax.div(i, chunks), lax.rem(i, chunks) * chunk
            rows = pl.ds(pl.multiple_of(core * share + start, 16), chunk)
            other = other_ref[block, pl.ds(pl.multiple_of(start, 16), chunk)]
            kept[block, rows] = (kept[block, rows].astype(F32) + other.astype(F32)).astype(BF16)

    half = quarter // 2
    lines = [ColScatter(cols_n, part_ref, recv_ref, s1, r1, k * half, half, k) for k in range(2)]
    gathers = [RowGather(rows_n, dmid_ref, s2, r2, k * half, half, k * 2 * (rows_n - 1)) for k in range(2)]
    scatter = RowScatter(rows_n, down_ref, drecv_ref, sg, rg)
    cross = [
        remote(kept.at[:, pl.ds(pl.multiple_of((1 - core) * share, 16), share)], other_ref, score, rcore, k, {"dp": 1 - core})
        for k, kept in enumerate((w0_ref, w1_ref))
    ]
    keeps = [
        pltpu.make_async_copy(kept.at[:, pl.ds(pl.multiple_of(core * share, 16), share)], out, copied.at[1 + k])
        for k, (kept, out) in enumerate(((w0_ref, share0_ref), (w1_ref, share1_ref)))
    ]

    def finish(rows, total):
        stage_ref[rows] = total

    def norm_back(k):
        @pl.loop(0, half // 32)
        def _(i):
            rows = pl.ds(pl.multiple_of(k * half + i * 32, 32), 32)
            got = lines[k].total(rows)
            middle = mid_ref[rows]
            inverse = lax.rsqrt(jnp.sum(middle * middle, axis=1, keepdims=True) / features + EPSILON)
            weighted = got * gain_ref[...]
            inner = jnp.sum(middle * weighted, axis=1, keepdims=True) / features
            grad_ref[...] += jnp.sum(got * middle * inverse, axis=0, keepdims=True)
            value = tok_ref[rows].astype(F32) + inverse * weighted - middle * (inverse * inverse * inverse * inner)
            dmid_ref[row, rows] = value.astype(BF16)

    grad_ref[...] = jnp.zeros_like(grad_ref)
    scatter.start()
    for time in range(cols_n):
        lines[0].event(time, prepare)
        if time == cols_n - 2:
            for step in range(scatter.bits - 1):
                scatter.event(step, finish)
    lines[1].event(0)
    norm_back(0)
    gathers[0].start()
    scatter.event(scatter.bits - 1, finish)
    results = settle(stage_ref, gdown_ref, core, copied, sf, rf, 0)
    for move in results:
        move.start()
    product(dgate_ref, w0_ref)
    cross[0].start()
    lines[1].event(1)
    gathers[0].event(0)
    product(dup_ref, w1_ref)
    for time in range(2, cols_n - 1):
        lines[1].event(time)
    for step in range(1, gathers[0].bits):
        gathers[0].event(step)
    cross[0].wait()
    add(w0_ref)
    keeps[0].start()
    pl.semaphore_signal(free, inc=1, device_id={"dp": 1 - core}, device_id_type=MESH)
    pl.semaphore_wait(free, 1)
    cross[1].start()
    lines[1].event(cols_n - 1)
    norm_back(1)
    gathers[1].start()
    cross[1].wait()
    add(w1_ref)
    keeps[1].start()
    gathers[1].run()
    gathers[0].finish()
    scatter.close()
    for move in keeps:
        move.wait()
    for move in results:
        move.wait()


def back_call(dgate, dup, gate, up, middle, tok, gain, second, down_share):
    rows_n, cols_n = lax.axis_size("row"), lax.axis_size("col")
    quarter, features = middle.shape
    hidden = dgate.shape[1]
    width = features // rows_n
    dma = pltpu.SemaphoreType.DMA
    anywhere = pl.BlockSpec(memory_space=pl.ANY)
    line = 2 * (rows_n - 1)
    half = (rows_n, width // 2, hidden)
    return pl.pallas_call(
        functools.partial(back_kernel, rows_n, cols_n),
        out_shape=(
            jax.ShapeDtypeStruct((rows_n, quarter, features), BF16),
            jax.ShapeDtypeStruct((1, features), F32),
            jax.ShapeDtypeStruct((2 * down_share.shape[1], width), F32),
            jax.ShapeDtypeStruct(half, BF16),
            jax.ShapeDtypeStruct(half, BF16),
        ),
        in_specs=[VM, VM, anywhere, anywhere, VM, VM, VM, VM, VM],
        out_specs=(VM, VM, anywhere, anywhere, anywhere),
        scratch_shapes=[
            pltpu.VMEM((rows_n, width, hidden), BF16),
            pltpu.VMEM((rows_n, width, hidden), BF16),
            pltpu.VMEM((cols_n, quarter, features), BF16),
            pltpu.VMEM((cols_n + 1, quarter, features), BF16),
            pltpu.VMEM(half, BF16),
            pltpu.VMEM((rows_n - 1,) + down_share.shape[1:], BF16),
            pltpu.VMEM(down_share.shape[1:], F32),
            dma((2,)), dma((4,)), dma((4 * cols_n,)),
            dma((2 * line,)), dma((2 * line,)), dma((line,)), dma((line,)),
            dma((2,)), dma((2,)), dma((3,)), dma((1,)), dma((1,)), pltpu.SemaphoreType.REGULAR,
        ],
        compiler_params=params(3),
        cost_estimate=cost(130),
    )(dgate, dup, gate, up, middle, tok, gain, second, down_share)


def last_kernel(
    size, dqkv_ref, weight_ref, first_ref, outline_ref, blk_ref, inner_ref, act_ref, inv_ref, grad2_ref,
    out_ref, block_ref, inners_ref, gains_ref, gqkv_ref, gout_ref,
    part_ref, recv_ref, qpart_ref, qother_ref, qshare_ref, qline_ref, qrecv_ref, orecv_ref, rgain_ref, pair_ref, pairs_ref,
    s1, r1, sblk, rblk, sinn, rinn, score, rcore, srow, rrow, so, ro, sq, rq, sg, rg, sp, rp, sf, rf,
):
    row, col, core = lax.axis_index("row"), lax.axis_index("col"), lax.axis_index("dp")
    length, width = act_ref.shape
    quarter = length // size
    barrier = pltpu.get_barrier_semaphore()
    peers = [{"row": row ^ mask} for mask in range(1, size)]
    others = [{"col": lax.rem(col + k, size)} for k in range(1, size)]
    others += [{"col": lax.rem(col + k, size), "dp": 1 - core} for k in range(size)]
    for peer in peers + others:
        pl.semaphore_signal(barrier, inc=1, device_id=peer, device_id_type=MESH)
    pl.semaphore_wait(barrier, len(peers) + len(others))

    scatter = RowScatter(size, part_ref, recv_ref, s1, r1)
    inners_ref[row] = inner_ref[...]
    rgain_ref[row] = grad2_ref[row]
    small = []
    for mask in range(1, size):
        small.append(remote(inner_ref, inners_ref.at[row], sinn, rinn, mask - 1, {"row": row ^ mask}))
        small.append(remote(grad2_ref.at[row ^ mask], rgain_ref.at[row], sg, rg, mask - 1, {"row": row ^ mask}))
    for move in small:
        move.start()
    oline = ColScatter(size, outline_ref, orecv_ref, so, ro)
    oline.event(0)

    @pl.loop(0, size)
    def _(j):
        columns = pl.ds(pl.multiple_of(j * width, 128), width)
        qpart_ref[j] = lax.dot_general(
            first_ref[:, columns], dqkv_ref[...], (((0,), (0,)), ((), ())), preferred_element_type=F32
        ).astype(BF16)

    cross = swap_halves(qpart_ref, qother_ref, score, rcore)
    cross.start()
    oline.event(1)

    @pl.loop(0, size)
    def _(j):
        part_ref[j] = lax.dot_general(dqkv_ref[...], weight_ref[j], (((1,), (1,)), ((), ())), preferred_element_type=F32).astype(BF16)

    cross.wait()
    add_halves(qpart_ref, qother_ref, qshare_ref)
    row_moves(size, qshare_ref, qline_ref, srow, rrow, 0, True)
    scatter.start()
    for time in range(2, oline.times):
        oline.event(time)
    share_o = outline_ref.shape[1]
    share_q = qline_ref.shape[1]

    def across(ref, share, which):
        piece = ref.at[pl.ds(pl.multiple_of(core * share, 8), share)]
        return remote(piece, piece, sf, rf, which, {"dp": 1 - core})

    gout_ref[pl.ds(pl.multiple_of(core * share_o, 8), share_o)] = oline.total(slice(None))
    across(gout_ref, share_o, 0).start()

    block_ref[pl.ds(pl.multiple_of(row * quarter, 16), quarter)] = blk_ref[row]
    for mask in range(1, size):
        remote(
            blk_ref.at[row ^ mask], block_ref.at[pl.ds(pl.multiple_of(row * quarter, 16), quarter)], sblk, rblk, mask - 1, {"row": row ^ mask}
        ).start()
    row_moves(size, qshare_ref, qline_ref, srow, rrow, 0, False)
    qline = ColScatter(size, qline_ref, qrecv_ref, sq, rq)
    qline.event(0)
    pair_ref[0] = jnp.zeros_like(pair_ref[0])

    def finish(rows, total):
        out_ref[rows] = total
        pair_ref[0] += jnp.sum(total * act_ref[rows].astype(F32) * inv_ref[rows], axis=0, keepdims=True)

    for step in range(scatter.bits - 1):
        scatter.event(step, finish)
    for time in range(1, min(3, qline.times)):
        qline.event(time)
    scatter.event(scatter.bits - 1, finish)
    scatter.close()
    for move in small:
        move.wait()
    pair_ref[1] = jnp.sum(rgain_ref[...], axis=0)
    own = core * size + col
    pairs_ref[own] = pair_ref[...]
    for k, peer in enumerate(others):
        remote(pair_ref, pairs_ref.at[own], sp, rp, k, peer).start()
    for time in range(3, qline.times):
        qline.event(time)
    gqkv_ref[pl.ds(pl.multiple_of(core * share_q, 8), share_q)] = qline.total(slice(None))
    across(gqkv_ref, share_q, 1).start()
    for k, peer in enumerate(others):
        remote(pair_ref, pairs_ref.at[own], sp, rp, k, peer).wait()
    gains_ref[...] = jnp.sum(pairs_ref[...], axis=0)
    for mask in range(1, size):
        remote(
            blk_ref.at[row ^ mask], block_ref.at[pl.ds(pl.multiple_of(row * quarter, 16), quarter)], sblk, rblk, mask - 1, {"row": row ^ mask}
        ).wait()
    across(gout_ref, share_o, 0).wait()
    across(gqkv_ref, share_q, 1).wait()


def last_call(dqkv, weight, first, outline, blk, inner, activations, inv1, grad2):
    size = lax.axis_size("row")
    length, width = activations.shape
    columns = weight.shape[1]
    heads_cols = 2 * outline.shape[1]
    dma = pltpu.SemaphoreType.DMA
    count = 2 * size - 1
    return pl.pallas_call(
        functools.partial(last_kernel, size),
        out_shape=(
            jax.ShapeDtypeStruct((length, width), F32),
            jax.ShapeDtypeStruct((length, width), BF16),
            jax.ShapeDtypeStruct((size,) + inner.shape, F32),
            jax.ShapeDtypeStruct((2, 1, width), F32),
            jax.ShapeDtypeStruct((width, columns), F32),
            jax.ShapeDtypeStruct((heads_cols, width), F32),
        ),
        in_specs=[VM] * 9,
        out_specs=(VM,) * 6,
        scratch_shapes=[
            pltpu.VMEM((size, length, width), BF16),
            pltpu.VMEM((size - 1, length, width), BF16),
            pltpu.VMEM((size, width, columns), BF16),
            pltpu.VMEM((size, width // 2, columns), BF16),
            pltpu.VMEM((size, width // 2, columns), BF16),
            pltpu.VMEM((size, width // 2, columns), BF16),
            pltpu.VMEM((size + 1, width // 2, columns), BF16),
            pltpu.VMEM((size + 1, heads_cols // 2, width), BF16),
            pltpu.VMEM((size, 1, width), F32),
            pltpu.VMEM((2, 1, width), F32),
            pltpu.VMEM((2 * size, 2, 1, width), F32),
        ]
        + [dma((2 * (size - 1),))] * 2
        + [dma((size - 1,))] * 2
        + [dma((size - 1,))] * 2
        + [dma((1,))] * 2
        + [dma((size - 1,))] * 2
        + [dma((2,)), dma((2 * size,))] * 2
        + [dma((size - 1,))] * 2
        + [dma((count,))] * 2
        + [dma((2,))] * 2,
        compiler_params=params(4),
        cost_estimate=cost(80),
    )(dqkv, weight.reshape(size, width, columns), first, outline, blk, inner, activations, inv1, grad2.reshape(size, 1, width))


def feed_kernel(
    second_ref, cot_ref, gate_ref, up_ref, down_ref, dgate_ref, dup_ref, own_ref, part_ref,
    hidden_ref, keep_ref, send_ref, other_ref, sends, recvs,
):
    core = lax.axis_index("dp")
    step = pl.program_id(0)
    rows_n, tile, width = down_ref.shape
    tokens = second_ref.shape[0]
    tiles = hidden_ref.shape[0]
    block = min(512, tokens)
    mine = tiles // 2

    def place(t):
        return pl.ds(pl.multiple_of(lax.rem(t, mine) * tile, tile), tile)

    def give(t):
        return remote(send_ref.at[:, place(t)], other_ref.at[:, place(t)], sends, recvs, lax.rem(t, mine), {"dp": 1 - core})

    @pl.when(step == 0)
    def _():
        greet(dp_size=2)

    @pl.when(step < tiles)
    def _():
        keep_ref[step] = down_ref[...]

        @pl.loop(0, tokens // block)
        def _(i):
            rows = pl.ds(pl.multiple_of(i * block, block), block)
            gate = jnp.dot(second_ref[rows], gate_ref[...], preferred_element_type=F32)
            up = jnp.dot(second_ref[rows], up_ref[...], preferred_element_type=F32)
            back = jnp.zeros((block, tile), F32)
            for j in range(rows_n):
                back += lax.dot_general(
                    cot_ref[rows, j * width : (j + 1) * width], down_ref[j], (((1,), (1,)), ((), ())), preferred_element_type=F32
                )
            sigma = jax.nn.sigmoid(gate)
            swish = gate * sigma
            hidden_ref[step, rows] = (swish * up).astype(BF16)
            dgate_ref[rows] = (back * up * (sigma * (1.0 + gate * (1.0 - sigma)))).astype(BF16)
            dup_ref[rows] = (back * swish).astype(BF16)

        for j in range(rows_n):
            value = lax.dot_general(
                hidden_ref[step], cot_ref[:, j * width : (j + 1) * width], (((0,), (0,)), ((), ())), preferred_element_type=F32
            ).astype(BF16)

            @pl.when(lax.div(step, mine) == core)
            def _():
                own_ref[j, place(step)] = value

            @pl.when(lax.div(step, mine) != core)
            def _():
                send_ref[j, place(step)] = value

        @pl.when(lax.div(step, mine) != core)
        def _():
            give(step).start()

    @pl.when(step >= tiles)
    def _():
        quarter = part_ref.shape[1]
        rows = pl.ds(pl.multiple_of((step - tiles) * quarter, quarter), quarter)
        for j in range(rows_n):
            total = jnp.zeros((quarter, width), F32)
            for t in range(tiles):
                total += jnp.dot(hidden_ref[t, rows], keep_ref[t, j], preferred_element_type=F32)
            part_ref[0, :, j * width : (j + 1) * width] = total.astype(BF16)

    @pl.when(step == pl.num_programs(0) - 1)
    def _():
        for t in range(mine):
            give(t).wait()
            for j in range(rows_n):
                own_ref[j, place(t)] = (own_ref[j, place(t)].astype(F32) + other_ref[j, place(t)].astype(F32)).astype(BF16)


def feed_call(second, cot, gate, up, down):
    rows_n, hidden, width = down.shape
    cols_n = lax.axis_size("col")
    tokens, features = second.shape
    tile = 256
    tiles = hidden // tile
    half = (rows_n, hidden // 2, width)

    def place(i):
        return jnp.minimum(i, tiles - 1)

    return pl.pallas_call(
        feed_kernel,
        grid=(tiles + cols_n,),
        out_shape=(
            jax.ShapeDtypeStruct((tokens, hidden), BF16),
            jax.ShapeDtypeStruct((tokens, hidden), BF16),
            jax.ShapeDtypeStruct(half, BF16),
            jax.ShapeDtypeStruct((cols_n, tokens // cols_n, features), BF16),
        ),
        in_specs=[
            VM,
            VM,
            pl.BlockSpec((features, tile), lambda i: (0, place(i))),
            pl.BlockSpec((features, tile), lambda i: (0, place(i))),
            pl.BlockSpec((rows_n, tile, width), lambda i: (0, place(i), 0)),
        ],
        out_specs=(
            pl.BlockSpec((tokens, tile), lambda i: (0, place(i))),
            pl.BlockSpec((tokens, tile), lambda i: (0, place(i))),
            VM,
            pl.BlockSpec((1, tokens // cols_n, features), lambda i: (jnp.maximum(i - tiles, 0), 0, 0)),
        ),
        scratch_shapes=[
            pltpu.VMEM((tiles, tokens, tile), BF16),
            pltpu.VMEM((tiles, rows_n, tile, width), BF16),
            pltpu.VMEM(half, BF16),
            pltpu.VMEM(half, BF16),
            pltpu.SemaphoreType.DMA((tiles // 2,)),
            pltpu.SemaphoreType.DMA((tiles // 2,)),
        ],
        compiler_params=params(7),
        cost_estimate=cost(50),
    )(second, cot, gate, up, down)


def rotary_tables(positions):
    exponent = jnp.arange(0, HEAD, 2).astype(F32) / HEAD
    inverse = jnp.power(F32(THETA), -exponent)
    phase = positions[:, None] * inverse[None, :]
    phase = jnp.concatenate([phase] * (2 * 128 // HEAD), axis=1)
    return (jnp.cos(phase), jnp.sin(phase))


def local(
    activations, segments, positions, first_gain, query_weight, key_weight, value_weight, out_weight,
    second_gain, gate_weight, up_weight, down_weight, cotangent,
):
    rows = lax.axis_size("row")
    row, col = lax.axis_index("row"), lax.axis_index("col")
    length, width = activations.shape
    features = rows * width
    query_cols, key_cols = query_weight.shape[1], key_weight.shape[1]
    heads, kvs = query_cols // HEAD, key_cols // HEAD
    hidden_cols = gate_weight.shape[1]
    spare = jnp.zeros((width, -key_cols % 128), BF16)
    key_span = key_cols + spare.shape[1]
    qkv_cols = query_cols + 2 * key_span

    small = jnp.concatenate([segments.astype(F32), positions.astype(F32), first_gain, second_gain]).reshape(-1, 128)
    qkv_weight = jnp.concatenate([query_weight, key_weight, spare, value_weight, spare], axis=1)
    x_blocks, first, inv1, cot_tok, smalls, qkv_all, out_all_w, near = first_call(activations, cotangent, small, qkv_weight, out_weight)
    qkv_all = qkv_all.reshape(features, qkv_cols)
    smalls = smalls.reshape(rows, -1)
    own = lax.dynamic_slice_in_dim(smalls, col, 1, 0)[0]
    segment_own, position_own = own[:length], own[length : 2 * length]
    gain2 = smalls[:, 2 * length + width :].reshape(1, features)

    cosine, sine = rotary_tables(position_own)
    segc, segr = segment_own[:, None], segment_own[None]
    q, k, v, attn, following, gate_all = attend_call(first, qkv_all, cosine, sine, segc, segr, near, gate_weight, heads, kvs)
    middle, second_all, cot_all, up_all, down_all = middle_call(
        attn, out_all_w, x_blocks, gain2, cot_tok, near, following, up_weight, down_weight
    )
    gate_all, up_all = gate_all.reshape(features, hidden_cols), up_all.reshape(features, hidden_cols)
    second_all, cot_all = second_all.reshape(-1, features), cot_all.reshape(-1, features)
    dgate, dup, down_share, down_part = feed_call(second_all, cot_all, gate_all, up_all, down_all)
    dmid_all, gain2_grad, down_grad, gate_share, up_share = back_call(
        dgate, dup, gate_all.reshape(rows, width, hidden_cols), up_all.reshape(rows, width, hidden_cols), middle, cot_tok, gain2, second_all,
        down_share,
    )
    dmid_all = dmid_all.reshape(length, features)

    dqkv, inner1, blk, outline, up_grad, gate_grad = attend_back_call(
        dmid_all, out_all_w, q, k, v, cosine, sine, segc, segr, qkv_cols, attn, down_part, middle, up_share, gate_share
    )
    dfirst, block_out, inner1, gains, qkv_grad, out_grad = last_call(
        dqkv, qkv_all, first, outline, blk, inner1.reshape(-1, 128), activations, inv1, gain2_grad
    )
    inner1 = jnp.sum(inner1, axis=0).reshape(length, 1) / (inv1 * features)
    own_x = activations.astype(F32)
    dmid_own = lax.dynamic_slice_in_dim(dmid_all, row * width, width, 1).astype(F32)
    input_grad = dmid_own + inv1 * first_gain[None] * dfirst - own_x * (inv1 * inv1 * inv1 * inner1)

    return (
        block_out,
        input_grad,
        gains[0, 0],
        qkv_grad[:, :query_cols],
        qkv_grad[:, query_cols : query_cols + key_cols],
        qkv_grad[:, query_cols + key_span : query_cols + key_span + key_cols],
        out_grad,
        gains[1, 0],
        gate_grad,
        up_grad,
        down_grad,
    )


def solution(mesh):
    tokens, block, swapped = P(("dp", "col"), "row"), P("row", "col"), P("col", "row")
    return jax.shard_map(
        local,
        mesh=mesh,
        in_specs=(
            tokens, P(("dp", "row")), P(("dp", "row")), P("row"), block, block, block, swapped,
            P("row"), block, block, swapped, tokens,
        ),
        out_specs=(tokens, tokens, P("row"), block, block, block, swapped, P("row"), block, block, swapped),
        check_vma=False,
    )
```

```python
import functools

import jax
import jax.numpy as jnp
from jax import lax
from jax.experimental import pallas as pl
from jax.experimental.pallas import tpu as pltpu
from jax.sharding import PartitionSpec as P

HEAD = 64
EPSILON = 1e-05
THETA = 500000.0
F32 = jnp.float32
BF16 = jnp.bfloat16


MESH = pl.DeviceIdType.MESH
VMEM_LIMIT = 60 * 1024 * 1024


def greet(row_size=0, col_size=0, dp_size=0):
    barrier = pltpu.get_barrier_semaphore()
    if row_size:
        row = lax.axis_index("row")
        for mask in range(1, row_size):
            pl.semaphore_signal(barrier, inc=1, device_id={"row": row ^ mask}, device_id_type=MESH)
    if col_size:
        col = lax.axis_index("col")

        @pl.when(col > 0)
        def _():
            pl.semaphore_signal(barrier, inc=1, device_id={"col": col - 1}, device_id_type=MESH)

        @pl.when(col < col_size - 1)
        def _():
            pl.semaphore_signal(barrier, inc=1, device_id={"col": col + 1}, device_id_type=MESH)

    if dp_size:
        pl.semaphore_signal(barrier, inc=1, device_id={"dp": 1 - lax.axis_index("dp")}, device_id_type=MESH)
    count = max(row_size - 1, 0) + (1 if dp_size else 0)
    if col_size:
        count = count + jnp.where(col > 0, 1, 0) + jnp.where(col < col_size - 1, 1, 0)
    pl.semaphore_wait(barrier, count)


def remote(src, dst, sends, recvs, place, device):
    return pltpu.make_async_remote_copy(
        src_ref=src, dst_ref=dst, send_sem=sends.at[place], recv_sem=recvs.at[place],
        device_id=device, device_id_type=MESH,
    )


class RowGather:
    def __init__(self, size, ref, sends, recvs, begin=0, count=None, first=0):
        self.size, self.ref, self.sends, self.recvs = size, ref, sends, recvs
        self.bits = size.bit_length() - 1
        self.row = lax.axis_index("row")
        self.begin, self.first = begin, first
        self.half = (count or ref.shape[1]) // 2
        self.all = [self.copies(step) for step in range(self.bits)]

    def rows(self, part):
        return pl.ds(pl.multiple_of(self.begin + part * self.half, 16), self.half)

    def order(self, part):
        return list(range(self.bits)) if part == 0 else list(range(self.bits))[::-1]

    def copies(self, step):
        out = []
        for part in range(2):
            order = self.order(part)
            for item in range(1 << step):
                mask = 0
                for j in range(step):
                    if item >> j & 1:
                        mask |= 1 << order[j]
                piece = self.ref.at[self.row ^ mask, self.rows(part)]
                place = self.first + part * (self.size - 1) + (1 << step) - 1 + item
                out.append(remote(piece, piece, self.sends, self.recvs, place, {"row": self.row ^ (1 << order[step])}))
        return out

    def start(self):
        for step in range(self.bits):
            for part in range(2):
                self.all[step][part << step].start()

    def event(self, step, seen=None):
        for part in range(2):
            order = self.order(part)
            for item in range(1 << step):
                self.all[step][(part << step) + item].wait_recv()
                got = item | 1 << step
                for later in range(step + 1, self.bits):
                    self.all[later][(part << later) + got].start()
                if seen is not None:
                    mask = 0
                    for j in range(step + 1):
                        if got >> j & 1:
                            mask |= 1 << order[j]
                    seen(mask, part)

    def finish(self):
        for step in range(self.bits):
            for copy in self.all[step]:
                copy.wait_send()

    def run(self):
        for step in range(self.bits):
            self.event(step)
        self.finish()


class SharedGather:
    def __init__(self, size, shard, full, copied, sends, recvs, score, rcore, first):
        self.core, self.row = lax.axis_index("dp"), lax.axis_index("row")
        self.size, self.full, self.score, self.rcore, self.first = size, full, score, rcore, first * 2 * (size - 1)
        share = full.shape[1] // 2
        self.own = pltpu.make_async_copy(shard, full.at[self.row], copied.at[first])
        self.gather = RowGather(size, full, sends, recvs, self.core * share, share, self.first)

    def across(self, mask, part):
        piece = self.full.at[self.row ^ mask, self.gather.rows(part)]
        return remote(piece, piece, self.score, self.rcore, self.first + part * (self.size - 1) + mask - 1, {"dp": 1 - self.core})

    def load(self):
        self.own.start()

    def start(self):
        self.own.wait()
        self.gather.start()

    def event(self, step):
        self.gather.event(step, lambda mask, part: self.across(mask, part).start())

    def finish(self):
        self.gather.finish()
        for mask in range(1, self.size):
            for part in range(2):
                self.across(mask, part).wait()

    @staticmethod
    def scratch(size, count):
        dma = pltpu.SemaphoreType.DMA
        return [dma((count,))] + [dma((count * 2 * (size - 1),))] * 4


class RowScatter:
    def __init__(self, size, part_ref, recv_ref, sends, recvs, begin=0):
        self.size, self.part, self.recv = size, part_ref, recv_ref
        self.bits = size.bit_length() - 1
        self.row = lax.axis_index("row")
        half = recv_ref.shape[1] // 2
        self.rows = [pl.ds(part * half, half) for part in range(2)]
        self.own = [pl.ds(pl.multiple_of(begin + part * half, 16), half) for part in range(2)]
        self.plans = []
        for part in range(2):
            order = self.order(part)
            steps, held = [], {}
            for step in range(self.bits):
                bit, rest = 1 << order[step], order[step + 1 :]
                count = 1 << len(rest)
                copies, sums = [], {}
                for item in range(count - 1, -1, -1):
                    mask = sum(1 << other for j, other in enumerate(rest) if item >> j & 1)
                    place = size - 2 * count + item
                    copy = remote(
                        self.spot(part, mask ^ bit, held), recv_ref.at[place, self.rows[part]],
                        sends, recvs, part * (size - 1) + place, {"row": self.row ^ bit},
                    )
                    copies.append((mask, place, held.get(mask), copy))
                    sums[mask] = place
                held = sums
                steps.append(copies)
            self.plans.append(steps)

    def spot(self, part, mask, held):
        if mask in held:
            return self.recv.at[held[mask], self.rows[part]]
        return self.part.at[self.row ^ mask, self.own[part]]

    def order(self, part):
        return list(range(self.bits)) if part == 0 else list(range(self.bits))[::-1]

    def start(self):
        for part in range(2):
            for copies in self.plans[part][0]:
                copies[3].start()

    def event(self, step, finish):
        last = step + 1 == self.bits
        for part in range(2):
            rows, own = self.rows[part], self.own[part]
            for mask, place, before, copy in self.plans[part][step]:
                copy.wait_recv()
                size, begin, start = min(64, rows.size), own.start, rows.start

                @pl.loop(0, rows.size // size)
                def _(i):
                    here = pl.ds(pl.multiple_of(start + i * size, 16), size)
                    if before is None:
                        had = self.part[self.row ^ mask, pl.ds(pl.multiple_of(begin + i * size, 16), size)]
                    else:
                        had = self.recv[before, here]
                    total = had.astype(F32) + self.recv[place, here].astype(F32)
                    if last:
                        finish(here, total)
                    else:
                        self.recv[place, here] = total.astype(BF16)

                if last:
                    continue
                for mask2, _, _, copy2 in self.plans[part][step + 1]:
                    if mask2 ^ 1 << self.order(part)[step + 1] == mask:
                        copy2.start()

    def close(self):
        for part in range(2):
            for step in self.plans[part]:
                for _, _, _, copy in step:
                    copy.wait_send()

    def run(self, finish):
        self.start()
        for step in range(self.bits):
            self.event(step, finish)
        self.close()


class ColGather:
    def __init__(self, size, ref, sends, recvs, begin=0, end=None):
        self.size, self.ref, self.sends, self.recvs = size, ref, sends, recvs
        self.begin, self.end = begin, size - 1 if end is None else end
        self.col = lax.axis_index("col")

    def sides(self, step):
        size, col = self.size, self.col
        return (
            (0, lax.rem(col - step + size, size), col >= step, col < size - 1),
            (1, lax.rem(col + step, size), col + step < size, col > 0),
        )

    def copy(self, side, step):
        size, col = self.size, self.col
        piece = self.ref.at[self.sides(step)[side][1]]
        target = lax.rem(col + (1 if side == 0 else size - 1), size)
        return remote(piece, piece, self.sends, self.recvs, side * (size - 1) + step, {"col": target})

    def event(self, step, seen=None):
        for side, place, has, goes in self.sides(step):
            if step > self.begin:

                @pl.when(has)
                def _():
                    self.copy(side, step - 1).wait_recv()

            if step < self.end:

                @pl.when(has & goes)
                def _():
                    self.copy(side, step).start()

            if seen is not None and (step or side == 0):

                @pl.when(has)
                def _():
                    seen(place)

    def finish(self):
        for step in range(self.begin, self.end):
            for side, place, has, goes in self.sides(step):

                @pl.when(has & goes)
                def _():
                    self.copy(side, step).wait_send()

    def run(self):
        for step in range(self.begin, self.end + 1):
            self.event(step)
        self.finish()


class ColScatter:
    def __init__(self, size, part, recv, sends, recvs, begin=0, count=None, first=0):
        self.size, self.part, self.recv, self.sends, self.recvs = size, part, recv, sends, recvs
        self.begin, self.count, self.first = begin, count or part.shape[1], first
        self.col = lax.axis_index("col")
        self.times = size

    def copy(self, side, target, source):
        step = 1 if side == 0 else self.size - 1
        rows = pl.ds(self.begin, self.count)
        return pltpu.make_async_remote_copy(
            src_ref=self.recv.at[target + 1 - side, rows] if source is None else source.at[target, rows],
            dst_ref=self.recv.at[target + 1 - side, rows], send_sem=self.sends.at[2 * self.first + side],
            recv_sem=self.recvs.at[(2 * self.first + side) * self.size + target],
            device_id={"col": lax.rem(self.col + step, self.size)}, device_id_type=MESH,
        )

    def event(self, time, prepare=None):
        size, col = self.size, self.col
        for side, first, step in ((0, col == 0, time - col), (1, col == size - 1, time - (size - 1 - col))):
            target = size - 1 - step if side == 0 else step
            valid = (step >= 0) & ((target >= col) if side == 0 else (target <= col))
            place = lax.rem(target + 4 * size, size)

            if prepare is not None:

                @pl.when(valid & ((target != col) | (side == 0)))
                def _():
                    prepare(place)

            @pl.when(valid & jnp.logical_not(first))
            def _():
                self.copy(side, place, self.part).wait_recv()

            @pl.when(valid & jnp.logical_not(first) & (target != col))
            def _():
                chunk = min(64, self.count)

                @pl.loop(0, self.count // chunk)
                def _(i):
                    rows = pl.ds(pl.multiple_of(self.begin + i * chunk, 16), chunk)
                    self.recv[place + 1 - side, rows] = (
                        self.recv[place + 1 - side, rows].astype(F32) + self.part[place, rows].astype(F32)
                    ).astype(BF16)

            @pl.when(valid & (step > 0))
            def _():
                self.copy(side, place, self.part).wait_send()

            @pl.when(valid & (target != col) & first)
            def _():
                self.copy(side, place, self.part).start()

            @pl.when(valid & (target != col) & jnp.logical_not(first))
            def _():
                self.copy(side, place, None).start()

    def total(self, rows):
        got = self.part[self.col, rows].astype(F32)
        got += jnp.where(self.col > 0, self.recv[self.col + 1, rows].astype(F32), 0.0)
        got += jnp.where(self.col < self.size - 1, self.recv[self.col, rows].astype(F32), 0.0)
        return got


VM = pl.BlockSpec(memory_space=pltpu.VMEM)


def params(ident):
    return pltpu.CompilerParams(collective_id=ident, has_side_effects=True, vmem_limit_bytes=VMEM_LIMIT)


def keep_near(size, line, near, step):
    col = lax.axis_index("col")
    for side, place, has in ((0, col - step, col >= step), (1, col + step, col + step < size)):

        @pl.when(has)
        def _():
            near[side] = line[lax.rem(place + size, size)]


def take_near(size, line, near, step):
    col = lax.axis_index("col")
    for side, place, has in ((0, col - step, col >= step), (1, col + step, col + step < size)):

        @pl.when(has)
        def _():
            line[lax.rem(place + size, size)] = near[side]


def first_kernel(
    size, act_ref, cot_ref, small_ref, qkv_ref, out_ref,
    x_ref, first_ref, inv_ref, tok_ref, smalls_ref, qkvs_ref, outs_ref,
    near_ref,
    got_ref, zq_ref, zo_ref, zc_ref, s1, r1, s2, r2, s3, r3, szq, rzq, szo, rzo, srow, rrow, score, rcore, szc, rzc,
):
    row, col, core = lax.axis_index("row"), lax.axis_index("col"), lax.axis_index("dp")
    length, width = act_ref.shape
    quarter = length // size
    small_rows = small_ref.shape[0]
    gain_row = 2 * length // 128
    x_ref[row] = act_ref[...]
    smalls_ref[row] = small_ref[...]
    blocks = ((qkv_ref, zq_ref, qkvs_ref, szq, rzq), (out_ref, zo_ref, outs_ref, szo, rzo))
    for block, line, _, _, _ in blocks:
        share = block.shape[0] // 2
        line[col] = block[pl.ds(pl.multiple_of(core * share, 16), share)]
    greet(row_size=size, col_size=size, dp_size=2)
    gather = RowGather(size, x_ref, s1, r1)
    smalls = [
        remote(small_ref, smalls_ref.at[row], s3, r3, mask - 1, {"row": row ^ mask}) for mask in range(1, size)
    ]
    lines = [ColGather(size, line, sends, recvs) for _, line, _, sends, recvs in blocks]
    lines[0].event(0)
    for move in smalls:
        move.start()
    moves = [
        remote(cot_ref.at[pl.ds((row ^ mask) * quarter, quarter)], got_ref.at[row], s2, r2, mask - 1, {"row": row ^ mask})
        for mask in range(1, size)
    ]
    for move in moves:
        move.start()
    gather.start()
    got_ref[row] = cot_ref[pl.ds(pl.multiple_of(row * quarter, 16), quarter)]

    def half(ref, place):
        share = ref.shape[1] // 2
        return ref.at[place, pl.ds(pl.multiple_of(core * share, 16), share)]

    def hand(which, mask):
        _, line, full, _, _ = blocks[which]
        return remote(line.at[row ^ mask], half(full, row), srow, rrow, which * (size - 1) + mask - 1, {"row": row ^ mask})

    def across(which, mask):
        full = blocks[which][2]
        piece = half(full, row ^ mask)
        return remote(piece, piece, score, rcore, which * size + mask, {"dp": 1 - core})

    def seen(which):
        def act(place):
            _, line, full, _, _ = blocks[which]

            @pl.when(place == row)
            def _():
                share = full.shape[1] // 2
                full[row, pl.ds(pl.multiple_of(core * share, 16), share)] = line[row]
                across(which, 0).start()

            for mask in range(1, size):

                @pl.when(place == row ^ mask)
                def _():
                    hand(which, mask).start()

        return act

    act, act1 = seen(0), seen(1)
    act(col)
    near = ColGather(size, zc_ref, szc, rzc, 0, 1)
    for step in range(1, size - 1):
        lines[0].event(step, act)
    for move in moves:
        move.wait()
    for j in range(size):
        zc_ref[col, :, j * width : (j + 1) * width] = got_ref[j]
    tok_ref[...] = zc_ref[col]
    near.event(0)
    lines[1].event(0)
    lines[0].event(size - 1, act)
    act1(col)
    gather.event(0)
    lines[1].event(1, act1)
    for step in range(1, gather.bits):
        gather.event(step)
    for move in smalls:
        move.wait()

    @pl.loop(0, length // 128)
    def _(i):
        rows = pl.ds(pl.multiple_of(i * 128, 128), 128)
        total = jnp.zeros((128, 1), F32)
        for j in range(size):
            value = x_ref[j, rows].astype(F32)
            total += jnp.sum(value * value, axis=1, keepdims=True)
        inverse = lax.rsqrt(total / (size * width) + EPSILON)
        inv_ref[rows] = inverse
        for j in range(size):
            for k in range(width // 128):
                gain = smalls_ref[j, gain_row + k : gain_row + k + 1]
                value = x_ref[j, rows, k * 128 : (k + 1) * 128].astype(F32)
                first_ref[rows, j * width + k * 128 : j * width + (k + 1) * 128] = (value * inverse * gain).astype(BF16)

    for mask in range(1, size):
        hand(0, mask).wait_recv()
        across(0, mask).start()
    for step in range(2, size):
        lines[1].event(step, act1)
    for mask in range(1, size):
        hand(1, mask).wait_recv()
        across(1, mask).start()
    near.event(1)
    keep_near(size, zc_ref, near_ref, 1)
    near.finish()
    gather.finish()
    for line in lines:
        line.finish()
    for which in range(2):
        for mask in range(1, size):
            hand(which, mask).wait_send()
        for mask in range(size):
            across(which, mask).wait()


def first_call(activations, cotangent, small, qkv_weight, out_weight):
    size = lax.axis_size("row")
    length, width = activations.shape
    quarter = length // size
    qkv_cols, heads_cols = qkv_weight.shape[1], out_weight.shape[0]
    dma = pltpu.SemaphoreType.DMA
    return pl.pallas_call(
        functools.partial(first_kernel, size),
        out_shape=(
            jax.ShapeDtypeStruct((size, length, width), BF16),
            jax.ShapeDtypeStruct((length, size * width), BF16),
            jax.ShapeDtypeStruct((length, 1), F32),
            jax.ShapeDtypeStruct((quarter, size * width), BF16),
            jax.ShapeDtypeStruct((size,) + small.shape, F32),
            jax.ShapeDtypeStruct((size,) + qkv_weight.shape, BF16),
            jax.ShapeDtypeStruct((size,) + out_weight.shape, BF16),
            jax.ShapeDtypeStruct((2, quarter, size * width), BF16),
        ),
        in_specs=[VM] * 5,
        out_specs=(VM,) * 8,
        scratch_shapes=[
            pltpu.VMEM((size, quarter, width), BF16),
            pltpu.VMEM((size, width // 2, qkv_cols), BF16),
            pltpu.VMEM((size, heads_cols // 2, width), BF16),
            pltpu.VMEM((size, quarter, size * width), BF16),
        ]
        + [dma((2 * (size - 1),))] * 2
        + [dma((size - 1,))] * 4
        + [dma((2 * (size - 1),))] * 4
        + [dma((2 * (size - 1),))] * 2
        + [dma((2 * size,))] * 2
        + [dma((2 * (size - 1),))] * 2,
        compiler_params=params(1),
    )(activations, cotangent, small, qkv_weight, out_weight)


def turn(values, low):
    return jnp.where(low, -pltpu.roll(values, 128 - HEAD // 2, 1), pltpu.roll(values, HEAD // 2, 1))


def low_columns(rows):
    return lax.broadcasted_iota(jnp.int32, (rows, 128), 1) % HEAD < HEAD // 2


def masked_scores(query, key, seg_col, seg_row, first_row):
    scores = lax.dot_general(query, key, (((1,), (1,)), ((), ())), preferred_element_type=F32)
    rows = lax.broadcasted_iota(jnp.int32, scores.shape, 0) + first_row
    columns = lax.broadcasted_iota(jnp.int32, scores.shape, 1)
    allowed = (seg_col == seg_row) & (rows >= columns)
    return jnp.where(allowed, scores, -1e30)


def attend_kernel(
    size, first_ref, weight_ref, cos_ref, sin_ref, segc_ref, segr_ref, near_ref, gate_ref,
    q_ref, k_ref, v_ref, o_ref, next_ref, gates_ref, oh_ref, zc_ref, szc, rzc, *shared,
):
    bulk = SharedGather(size, gate_ref, gates_ref, *shared, 0)
    bulk.load()
    take_near(size, zc_ref, near_ref, 1)
    greet(row_size=size, col_size=size, dp_size=2)
    bulk.start()
    line = ColGather(size, zc_ref, szc, rzc, 1, 2)
    line.event(1)
    heads, length, _ = q_ref.shape
    kvs = k_ref.shape[0]
    group = heads // kvs
    query_cols = heads * HEAD
    key_cols = (weight_ref.shape[1] - query_cols) // 2
    block = 256

    @pl.loop(0, length // block)
    def _(i):
        rows = pl.ds(pl.multiple_of(i * block, block), block)
        low = low_columns(block)
        cosine, sine = cos_ref[rows], sin_ref[rows]
        whole = jnp.dot(first_ref[rows], weight_ref[...], preferred_element_type=F32)
        for ref, count, start, factor in ((q_ref, heads, 0, HEAD ** (-0.5)), (k_ref, kvs, query_cols, 1.0)):
            for j in range((count + 1) // 2):
                part = whole[:, start + 128 * j : start + 128 * (j + 1)]
                part = ((part * cosine + turn(part, low) * sine) * factor).astype(BF16)
                for side in range(min(2, count - 2 * j)):
                    ref[2 * j + side, rows] = part[:, side * HEAD : (side + 1) * HEAD]
        for j in range(kvs):
            at = query_cols + key_cols + j * HEAD
            v_ref[j, rows] = whole[:, at : at + HEAD].astype(BF16)

    @pl.loop(0, heads)
    def _(head):
        kv = lax.div(head, group)
        for i in range(length // block):
            rows, extent = slice(i * block, (i + 1) * block), (i + 1) * block
            scores = masked_scores(q_ref[head, rows], k_ref[kv, :extent], segc_ref[rows], segr_ref[:, :extent], i * block)
            top = jnp.max(scores, axis=1, keepdims=True)
            weights = jnp.exp(scores - top)
            total = jnp.sum(weights, axis=1, keepdims=True)
            mixed = jnp.dot(weights.astype(BF16), v_ref[kv, :extent], preferred_element_type=F32)
            oh_ref[head, rows] = (mixed / total).astype(BF16)

    for head in range(heads):
        o_ref[:, head * HEAD : (head + 1) * HEAD] = oh_ref[head]
    for step in range(bulk.gather.bits):
        bulk.event(step)
    line.event(2)
    keep_near(size, zc_ref, next_ref, 2)
    line.finish()
    bulk.finish()


def attend_call(first, weight, cosine, sine, segc, segr, near, gate, heads, kvs):
    size = lax.axis_size("row")
    length = first.shape[0]
    dma = pltpu.SemaphoreType.DMA
    return pl.pallas_call(
        functools.partial(attend_kernel, size),
        out_shape=(
            jax.ShapeDtypeStruct((heads, length, HEAD), BF16),
            jax.ShapeDtypeStruct((kvs, length, HEAD), BF16),
            jax.ShapeDtypeStruct((kvs, length, HEAD), BF16),
            jax.ShapeDtypeStruct((length, heads * HEAD), BF16),
            jax.ShapeDtypeStruct(near.shape, BF16),
            jax.ShapeDtypeStruct((size,) + gate.shape, BF16),
        ),
        in_specs=[VM] * 8,
        out_specs=(VM,) * 5 + (pl.BlockSpec(memory_space=pl.ANY),),
        scratch_shapes=[
            pltpu.VMEM((heads, length, HEAD), BF16),
            pltpu.VMEM((size,) + near.shape[1:], BF16),
            dma((2 * (size - 1),)), dma((2 * (size - 1),)),
        ]
        + SharedGather.scratch(size, 1),
        compiler_params=params(6),
        cost_estimate=cost(45),
    )(first, weight, cosine, sine, segc, segr, near, gate)


class swap_halves:
    def __init__(self, part, other, sends, recvs):
        core = lax.axis_index("dp")
        share = part.shape[1] // 2
        self.move = remote(
            part.at[:, pl.ds(pl.multiple_of((1 - core) * share, 16), share)], other, sends, recvs, 0, {"dp": 1 - core}
        )

    def start(self):
        self.move.start()

    def wait(self):
        self.move.wait()


def add_halves(part, other, share):
    rows = pl.ds(pl.multiple_of(lax.axis_index("dp") * share.shape[1], 16), share.shape[1])
    for j in range(part.shape[0]):
        share[j] = (part[j, rows].astype(F32) + other[j].astype(F32)).astype(BF16)


def row_moves(size, source, target, sends, recvs, first, begin):
    row = lax.axis_index("row")
    if begin:
        target[row] = source[row]
    for mask in range(1, size):
        move = remote(source.at[row ^ mask], target.at[row], sends, recvs, first + mask - 1, {"row": row ^ mask})
        if begin:
            move.start()
        else:
            move.wait()


def cost(micros):
    return pl.CostEstimate(flops=int(micros * 1e9), bytes_accessed=1 << 20, transcendentals=0)


def attend_back_kernel(
    dmid_ref, weight_ref, q_ref, k_ref, v_ref, cos_ref, sin_ref, segc_ref, segr_ref,
    attn_ref, down_ref, mid_ref, upshare_ref, gateshare_ref,
    dqkv_ref, inner_ref, blk_ref, line_ref, gup_ref, ggate_ref, do_ref, dq_ref, dk_ref, dv_ref,
    recv_ref, part_ref, other_ref, share_ref, urecv_ref, drecv_ref, ustage_ref, dstage_ref,
    s1, r1, score, rcore, srow, rrow, su, ru, sd, rd, copied, sf, rf,
):
    row, core = lax.axis_index("row"), lax.axis_index("dp")
    cols_n = down_ref.shape[0]
    heads, length, _ = q_ref.shape
    kvs = k_ref.shape[0]
    group = heads // kvs
    query_cols = heads * HEAD
    key_cols = (dqkv_ref.shape[1] - query_cols) // 2
    block = 256
    parts, _, width = weight_ref.shape
    greet(row_size=parts, col_size=cols_n, dp_size=2)
    line = ColScatter(cols_n, down_ref, recv_ref, s1, r1)
    line.event(0)
    sums = [
        (RowScatter(parts, upshare_ref, urecv_ref, su, ru), ustage_ref, gup_ref),
        (RowScatter(parts, gateshare_ref, drecv_ref, sd, rd), dstage_ref, ggate_ref),
    ]
    for scatter, _, _ in sums:
        scatter.start()
    for j in range(parts):
        part_ref[j] = lax.dot_general(
            attn_ref[...], dmid_ref[:, j * width : (j + 1) * width], (((0,), (0,)), ((), ())), preferred_element_type=F32
        ).astype(BF16)
    cross = swap_halves(part_ref, other_ref, score, rcore)
    cross.start()
    dk_ref[...] = jnp.zeros_like(dk_ref)
    dv_ref[...] = jnp.zeros_like(dv_ref)
    inner_ref[...] = jnp.zeros_like(inner_ref)

    @pl.loop(0, length // block)
    def _(i):
        rows = pl.ds(pl.multiple_of(i * block, block), block)
        total = jnp.zeros((block, query_cols), F32)
        for j in range(parts):
            total += lax.dot_general(
                dmid_ref[rows, j * width : (j + 1) * width], weight_ref[j], (((1,), (1,)), ((), ())), preferred_element_type=F32
            )
        for head in range(heads):
            do_ref[head, rows] = total[:, head * HEAD : (head + 1) * HEAD].astype(BF16)

    @pl.loop(0, heads)
    def _(head):
        @pl.when(head == min(1, heads - 1))
        def _():
            cross.wait()
            add_halves(part_ref, other_ref, share_ref)
            row_moves(parts, share_ref, line_ref, srow, rrow, 0, True)

        @pl.when(head == heads // 2)
        def _():
            line.event(1)

        kv = lax.div(head, group)
        for i in range(length // block):
            rows, extent = slice(i * block, (i + 1) * block), (i + 1) * block
            query, keys, grads = q_ref[head, rows], k_ref[kv, :extent], do_ref[head, rows]
            scores = masked_scores(query, keys, segc_ref[rows], segr_ref[:, :extent], i * block)
            top = jnp.max(scores, axis=1, keepdims=True)
            weights = jnp.exp(scores - top)
            weights = weights * (1.0 / jnp.sum(weights, axis=1, keepdims=True))
            back = lax.dot_general(grads, v_ref[kv, :extent], (((1,), (1,)), ((), ())), preferred_element_type=F32)
            dv_ref[kv, :extent] += lax.dot_general(
                weights.astype(BF16), grads, (((0,), (0,)), ((), ())), preferred_element_type=F32
            )
            ds = (weights * (back - jnp.sum(weights * back, axis=1, keepdims=True))).astype(BF16)
            dq = jnp.dot(ds, keys, preferred_element_type=F32)
            inner_ref[rows] += jnp.sum(dq * query.astype(F32), axis=1, keepdims=True)
            for side in range(2):

                @pl.when(lax.rem(head, 2) == side)
                def _():
                    dq_ref[lax.div(head, 2), rows, side * HEAD : (side + 1) * HEAD] = dq

            dk_ref[kv, :extent] += lax.dot_general(ds, query, (((0,), (0,)), ((), ())), preferred_element_type=F32)

    @pl.loop(0, length // block)
    def _(i):
        rows = pl.ds(pl.multiple_of(i * block, block), block)
        low = low_columns(block)
        cosine, sine = cos_ref[rows], sin_ref[rows]
        for ref, count, start, factor in ((dq_ref, heads, 0, HEAD ** (-0.5)), (dk_ref, kvs, query_cols, 1.0), (dv_ref, kvs, query_cols + key_cols, None)):
            for j in range((count + 1) // 2):
                if ref is dq_ref:
                    part = dq_ref[j, rows]
                else:
                    sides = [ref[2 * j + side, rows] if 2 * j + side < count else jnp.zeros((block, HEAD), F32) for side in range(2)]
                    part = jnp.concatenate(sides, axis=1)
                if factor is not None:
                    part = (part * cosine - turn(part * sine, low)) * factor
                dqkv_ref[rows, start + 128 * j : start + 128 * (j + 1)] = part.astype(BF16)
        more = jnp.zeros((block, 1), F32)
        for kv in range(kvs):
            more += jnp.sum(dk_ref[kv, rows] * k_ref[kv, rows].astype(F32) + dv_ref[kv, rows] * v_ref[kv, rows].astype(F32), axis=1, keepdims=True)
        inner_ref[rows] += more

    def finish(stage):
        def act(rows, total):
            stage[rows] = total

        return act

    if cols_n > 2:
        line.event(2)
    bits = sums[0][0].bits
    for step in range(bits - 1):
        for scatter, stage, _ in sums:
            scatter.event(step, finish(stage))
    for time in range(3, line.times):
        line.event(time)
    results = []
    for k, (scatter, stage, out) in enumerate(sums):
        scatter.event(bits - 1, finish(stage))
        moves = settle(stage, out, core, copied, sf, rf, k)
        for move in moves:
            move.start()
        results += moves
        scatter.close()

    @pl.loop(0, mid_ref.shape[0] // 64)
    def _(i):
        rows = pl.ds(pl.multiple_of(i * 64, 16), 64)
        total = mid_ref[rows] + line.total(rows)
        for j in range(parts):
            blk_ref[j, rows] = total[:, j * width : (j + 1) * width].astype(BF16)

    row_moves(parts, share_ref, line_ref, srow, rrow, 0, False)
    for move in results:
        move.wait()


def attend_back_call(dmid, weight, q, k, v, cosine, sine, segc, segr, columns, attn, down, middle, upshare, gateshare):
    rows_n, cols_n = lax.axis_size("row"), lax.axis_size("col")
    _, heads_cols, width = weight.shape
    quarter = middle.shape[0]
    dma = pltpu.SemaphoreType.DMA
    heads, length, _ = q.shape
    kvs = k.shape[0]
    return pl.pallas_call(
        attend_back_kernel,
        out_shape=(
            jax.ShapeDtypeStruct((length, columns), BF16),
            jax.ShapeDtypeStruct((length, 1), F32),
            jax.ShapeDtypeStruct((rows_n, quarter, width), BF16),
            jax.ShapeDtypeStruct((rows_n, heads_cols // 2, width), BF16),
            jax.ShapeDtypeStruct((2 * upshare.shape[1], upshare.shape[2]), F32),
            jax.ShapeDtypeStruct((2 * gateshare.shape[1], gateshare.shape[2]), F32),
        ),
        in_specs=[VM] * 14,
        out_specs=(VM,) * 4 + (pl.BlockSpec(memory_space=pl.ANY),) * 2,
        scratch_shapes=[
            pltpu.VMEM((heads, length, HEAD), BF16),
            pltpu.VMEM(((heads + 1) // 2, length, 2 * HEAD), F32),
            pltpu.VMEM((kvs, length, HEAD), F32),
            pltpu.VMEM((kvs, length, HEAD), F32),
            pltpu.VMEM((down.shape[0] + 1,) + down.shape[1:], BF16),
            pltpu.VMEM(weight.shape, BF16),
            pltpu.VMEM((rows_n, heads_cols // 2, width), BF16),
            pltpu.VMEM((rows_n, heads_cols // 2, width), BF16),
            pltpu.VMEM((rows_n - 1,) + upshare.shape[1:], BF16),
            pltpu.VMEM((rows_n - 1,) + gateshare.shape[1:], BF16),
            pltpu.VMEM(upshare.shape[1:], F32),
            pltpu.VMEM(gateshare.shape[1:], F32),
            dma((2,)), dma((2 * cols_n,)), dma((1,)), dma((1,)), dma((rows_n - 1,)), dma((rows_n - 1,)),
        ]
        + [dma((2 * (rows_n - 1),))] * 4
        + [dma((2,))] * 3
        + [
        ],
        compiler_params=params(5),
        cost_estimate=cost(80),
    )(dmid, weight, q, k, v, cosine, sine, segc, segr, attn, down, middle, upshare, gateshare)


def middle_kernel(
    rows_n, cols_n, attn_ref, weight_ref, x_ref, gain_ref, tok_ref, near_ref, next_ref, up_ref, down_ref,
    mid_ref, second_ref, cot_ref, ups_ref, downs_ref, part_ref, recv_ref, s1, r1, s2, r2, szc, rzc, *shared,
):
    row, col = lax.axis_index("row"), lax.axis_index("col")
    quarter, features = mid_ref.shape
    width = features // rows_n
    bulks = [SharedGather(rows_n, up_ref, ups_ref, *shared, 0), SharedGather(rows_n, down_ref, downs_ref, *shared, 1)]
    for bulk in bulks:
        bulk.load()
    cot_ref[col] = tok_ref[...]
    take_near(cols_n, cot_ref, near_ref, 1)
    take_near(cols_n, cot_ref, next_ref, 2)
    greet(row_size=rows_n, col_size=cols_n, dp_size=2)
    rest = ColGather(cols_n, cot_ref, szc, rzc, 2)
    rest.event(2)

    @pl.loop(0, rows_n)
    def _(i):
        own = attn_ref[pl.ds(pl.multiple_of(i * quarter, 16), quarter)]
        for j in range(rows_n):
            part_ref[i, :, j * width : (j + 1) * width] = jnp.dot(own, weight_ref[j], preferred_element_type=F32).astype(BF16)

    def finish(rows, total):
        own = pl.ds(row * quarter + rows.start, rows.size)
        squares = jnp.zeros((rows.size, 1), F32)
        for j in range(rows_n):
            columns = slice(j * width, (j + 1) * width)
            value = total[:, columns] + x_ref[j, own].astype(F32)
            mid_ref[rows, columns] = value
            squares += jnp.sum(value * value, axis=1, keepdims=True)
        inverse = lax.rsqrt(squares / features + EPSILON)
        second_ref[col, rows] = (mid_ref[rows] * inverse * gain_ref[...]).astype(BF16)

    scatter = RowScatter(rows_n, part_ref, recv_ref, s1, r1)
    scatter.start()
    for step in range(scatter.bits - 1):
        scatter.event(step, finish)
    for bulk in bulks:
        bulk.start()
    scatter.event(scatter.bits - 1, finish)
    line = ColGather(cols_n, second_ref, s2, r2)
    line.event(0)
    scatter.close()
    for step in range(3, cols_n):
        rest.event(step)
    rest.finish()
    line.event(1)
    bits = bulks[0].gather.bits
    for bulk in bulks:
        bulk.event(0)
    for step in range(2, cols_n):
        line.event(step)
    for step in range(1, bits):
        for bulk in bulks:
            bulk.event(step)
    for bulk in bulks:
        bulk.finish()
    line.finish()


def middle_call(attn, weight, x, gain, tok, near, following, up, down):
    rows_n, cols_n = lax.axis_size("row"), lax.axis_size("col")
    length, features = attn.shape[0], weight.shape[0] * weight.shape[2]
    quarter = length // rows_n
    dma = pltpu.SemaphoreType.DMA
    anywhere = pl.BlockSpec(memory_space=pl.ANY)
    return pl.pallas_call(
        functools.partial(middle_kernel, rows_n, cols_n),
        out_shape=(
            jax.ShapeDtypeStruct((quarter, features), F32),
            jax.ShapeDtypeStruct((cols_n, quarter, features), BF16),
            jax.ShapeDtypeStruct((cols_n, quarter, features), BF16),
            jax.ShapeDtypeStruct((rows_n,) + up.shape, BF16),
            jax.ShapeDtypeStruct((rows_n,) + down.shape, BF16),
        ),
        in_specs=[VM] * 9,
        out_specs=(VM, VM, VM, anywhere, anywhere),
        scratch_shapes=[
            pltpu.VMEM((rows_n, quarter, features), BF16),
            pltpu.VMEM((rows_n - 1, quarter, features), BF16),
        ]
        + [dma((2 * (rows_n - 1),))] * 2
        + [dma((2 * (cols_n - 1),))] * 4
        + SharedGather.scratch(rows_n, 2),
        compiler_params=params(2),
        cost_estimate=cost(130),
    )(attn, weight, x, gain, tok, near, following, up, down)


def settle(stage, out, core, copied, sends, recvs, place):
    rows = pl.ds(pl.multiple_of(core * stage.shape[0], 8), stage.shape[0])
    return (
        pltpu.make_async_copy(stage, out.at[rows], copied.at[place]),
        remote(stage, out.at[rows], sends, recvs, place, {"dp": 1 - core}),
    )


def back_kernel(
    rows_n, cols_n, dgate_ref, dup_ref, gate_ref, up_ref, mid_ref, tok_ref, gain_ref, second_ref, down_ref,
    dmid_ref, grad_ref, gdown_ref, share0_ref, share1_ref,
    w0_ref, w1_ref, part_ref, recv_ref, other_ref, drecv_ref, stage_ref,
    loads, s1, r1, s2, r2, sg, rg, score, rcore, copied, sf, rf, free,
):
    row, col, core = lax.axis_index("row"), lax.axis_index("col"), lax.axis_index("dp")
    quarter, features = mid_ref.shape
    width = features // rows_n
    hidden = dgate_ref.shape[1]
    share = width // 2
    moves = [pltpu.make_async_copy(ref, kept, loads.at[k]) for k, (ref, kept) in enumerate(((gate_ref, w0_ref), (up_ref, w1_ref)))]
    for move in moves:
        move.start()
    greet(row_size=rows_n, col_size=cols_n, dp_size=2)
    for move in moves:
        move.wait()

    def prepare(target):
        rows = pl.ds(pl.multiple_of(target * quarter, 16), quarter)

        @pl.loop(0, rows_n)
        def _(i):
            columns = pl.ds(pl.multiple_of(i * width, 128), width)
            value = lax.dot_general(dgate_ref[rows], w0_ref[i], (((1,), (1,)), ((), ())), preferred_element_type=F32)
            value += lax.dot_general(dup_ref[rows], w1_ref[i], (((1,), (1,)), ((), ())), preferred_element_type=F32)
            part_ref[target, :, columns] = value.astype(BF16)

    tile = min(512, hidden)

    def product(right, kept):
        @pl.loop(0, rows_n)
        def _(i):
            for t in range(hidden // tile):
                columns = slice(t * tile, (t + 1) * tile)
                kept[i, :, columns] = lax.dot_general(
                    second_ref[:, pl.ds(pl.multiple_of(i * width, 128), width)], right[:, columns], (((0,), (0,)), ((), ())),
                    preferred_element_type=F32,
                ).astype(BF16)

    def add(kept):
        chunk = min(64, share)
        chunks = share // chunk

        @pl.loop(0, rows_n * chunks)
        def _(i):
            block, start = lax.div(i, chunks), lax.rem(i, chunks) * chunk
            rows = pl.ds(pl.multiple_of(core * share + start, 16), chunk)
            other = other_ref[block, pl.ds(pl.multiple_of(start, 16), chunk)]
            kept[block, rows] = (kept[block, rows].astype(F32) + other.astype(F32)).astype(BF16)

    half = quarter // 2
    lines = [ColScatter(cols_n, part_ref, recv_ref, s1, r1, k * half, half, k) for k in range(2)]
    gathers = [RowGather(rows_n, dmid_ref, s2, r2, k * half, half, k * 2 * (rows_n - 1)) for k in range(2)]
    scatter = RowScatter(rows_n, down_ref, drecv_ref, sg, rg)
    cross = [
        remote(kept.at[:, pl.ds(pl.multiple_of((1 - core) * share, 16), share)], other_ref, score, rcore, k, {"dp": 1 - core})
        for k, kept in enumerate((w0_ref, w1_ref))
    ]
    keeps = [
        pltpu.make_async_copy(kept.at[:, pl.ds(pl.multiple_of(core * share, 16), share)], out, copied.at[1 + k])
        for k, (kept, out) in enumerate(((w0_ref, share0_ref), (w1_ref, share1_ref)))
    ]

    def finish(rows, total):
        stage_ref[rows] = total

    def norm_back(k):
        @pl.loop(0, half // 32)
        def _(i):
            rows = pl.ds(pl.multiple_of(k * half + i * 32, 32), 32)
            got = lines[k].total(rows)
            middle = mid_ref[rows]
            inverse = lax.rsqrt(jnp.sum(middle * middle, axis=1, keepdims=True) / features + EPSILON)
            weighted = got * gain_ref[...]
            inner = jnp.sum(middle * weighted, axis=1, keepdims=True) / features
            grad_ref[...] += jnp.sum(got * middle * inverse, axis=0, keepdims=True)
            value = tok_ref[rows].astype(F32) + inverse * weighted - middle * (inverse * inverse * inverse * inner)
            dmid_ref[row, rows] = value.astype(BF16)

    grad_ref[...] = jnp.zeros_like(grad_ref)
    scatter.start()
    for time in range(cols_n):
        lines[0].event(time, prepare)
        if time == cols_n - 2:
            for step in range(scatter.bits - 1):
                scatter.event(step, finish)
    lines[1].event(0)
    norm_back(0)
    gathers[0].start()
    scatter.event(scatter.bits - 1, finish)
    results = settle(stage_ref, gdown_ref, core, copied, sf, rf, 0)
    for move in results:
        move.start()
    product(dgate_ref, w0_ref)
    cross[0].start()
    lines[1].event(1)
    gathers[0].event(0)
    product(dup_ref, w1_ref)
    for time in range(2, cols_n - 1):
        lines[1].event(time)
    for step in range(1, gathers[0].bits):
        gathers[0].event(step)
    cross[0].wait()
    add(w0_ref)
    keeps[0].start()
    pl.semaphore_signal(free, inc=1, device_id={"dp": 1 - core}, device_id_type=MESH)
    pl.semaphore_wait(free, 1)
    cross[1].start()
    lines[1].event(cols_n - 1)
    norm_back(1)
    gathers[1].start()
    cross[1].wait()
    add(w1_ref)
    keeps[1].start()
    gathers[1].run()
    gathers[0].finish()
    scatter.close()
    for move in keeps:
        move.wait()
    for move in results:
        move.wait()


def back_call(dgate, dup, gate, up, middle, tok, gain, second, down_share):
    rows_n, cols_n = lax.axis_size("row"), lax.axis_size("col")
    quarter, features = middle.shape
    hidden = dgate.shape[1]
    width = features // rows_n
    dma = pltpu.SemaphoreType.DMA
    anywhere = pl.BlockSpec(memory_space=pl.ANY)
    line = 2 * (rows_n - 1)
    half = (rows_n, width // 2, hidden)
    return pl.pallas_call(
        functools.partial(back_kernel, rows_n, cols_n),
        out_shape=(
            jax.ShapeDtypeStruct((rows_n, quarter, features), BF16),
            jax.ShapeDtypeStruct((1, features), F32),
            jax.ShapeDtypeStruct((2 * down_share.shape[1], width), F32),
            jax.ShapeDtypeStruct(half, BF16),
            jax.ShapeDtypeStruct(half, BF16),
        ),
        in_specs=[VM, VM, anywhere, anywhere, VM, VM, VM, VM, VM],
        out_specs=(VM, VM, anywhere, anywhere, anywhere),
        scratch_shapes=[
            pltpu.VMEM((rows_n, width, hidden), BF16),
            pltpu.VMEM((rows_n, width, hidden), BF16),
            pltpu.VMEM((cols_n, quarter, features), BF16),
            pltpu.VMEM((cols_n + 1, quarter, features), BF16),
            pltpu.VMEM(half, BF16),
            pltpu.VMEM((rows_n - 1,) + down_share.shape[1:], BF16),
            pltpu.VMEM(down_share.shape[1:], F32),
            dma((2,)), dma((4,)), dma((4 * cols_n,)),
            dma((2 * line,)), dma((2 * line,)), dma((line,)), dma((line,)),
            dma((2,)), dma((2,)), dma((3,)), dma((1,)), dma((1,)), pltpu.SemaphoreType.REGULAR,
        ],
        compiler_params=params(3),
        cost_estimate=cost(130),
    )(dgate, dup, gate, up, middle, tok, gain, second, down_share)


def last_kernel(
    size, dqkv_ref, weight_ref, first_ref, outline_ref, blk_ref, inner_ref, act_ref, inv_ref, grad2_ref,
    out_ref, block_ref, inners_ref, gains_ref, gqkv_ref, gout_ref,
    part_ref, recv_ref, qpart_ref, qother_ref, qshare_ref, qline_ref, qrecv_ref, orecv_ref, rgain_ref, pair_ref, pairs_ref,
    s1, r1, sblk, rblk, sinn, rinn, score, rcore, srow, rrow, so, ro, sq, rq, sg, rg, sp, rp, sf, rf,
):
    row, col, core = lax.axis_index("row"), lax.axis_index("col"), lax.axis_index("dp")
    length, width = act_ref.shape
    quarter = length // size
    barrier = pltpu.get_barrier_semaphore()
    peers = [{"row": row ^ mask} for mask in range(1, size)]
    others = [{"col": lax.rem(col + k, size)} for k in range(1, size)]
    others += [{"col": lax.rem(col + k, size), "dp": 1 - core} for k in range(size)]
    for peer in peers + others:
        pl.semaphore_signal(barrier, inc=1, device_id=peer, device_id_type=MESH)
    pl.semaphore_wait(barrier, len(peers) + len(others))

    scatter = RowScatter(size, part_ref, recv_ref, s1, r1)
    inners_ref[row] = inner_ref[...]
    rgain_ref[row] = grad2_ref[row]
    small = []
    for mask in range(1, size):
        small.append(remote(inner_ref, inners_ref.at[row], sinn, rinn, mask - 1, {"row": row ^ mask}))
        small.append(remote(grad2_ref.at[row ^ mask], rgain_ref.at[row], sg, rg, mask - 1, {"row": row ^ mask}))
    for move in small:
        move.start()
    block_ref[pl.ds(pl.multiple_of(row * quarter, 16), quarter)] = blk_ref[row]
    for mask in range(1, size):
        remote(
            blk_ref.at[row ^ mask], block_ref.at[pl.ds(pl.multiple_of(row * quarter, 16), quarter)], sblk, rblk, mask - 1, {"row": row ^ mask}
        ).start()
    oline = ColScatter(size, outline_ref, orecv_ref, so, ro)
    oline.event(0)

    @pl.loop(0, size)
    def _(j):
        columns = pl.ds(pl.multiple_of(j * width, 128), width)
        qpart_ref[j] = lax.dot_general(
            first_ref[:, columns], dqkv_ref[...], (((0,), (0,)), ((), ())), preferred_element_type=F32
        ).astype(BF16)

    cross = swap_halves(qpart_ref, qother_ref, score, rcore)
    cross.start()
    oline.event(1)

    @pl.loop(0, size)
    def _(j):
        part_ref[j] = lax.dot_general(dqkv_ref[...], weight_ref[j], (((1,), (1,)), ((), ())), preferred_element_type=F32).astype(BF16)

    cross.wait()
    add_halves(qpart_ref, qother_ref, qshare_ref)
    row_moves(size, qshare_ref, qline_ref, srow, rrow, 0, True)
    for time in range(2, oline.times):
        oline.event(time)
    share_o = outline_ref.shape[1]
    share_q = qline_ref.shape[1]

    def across(ref, share, which):
        piece = ref.at[pl.ds(pl.multiple_of(core * share, 8), share)]
        return remote(piece, piece, sf, rf, which, {"dp": 1 - core})

    gout_ref[pl.ds(pl.multiple_of(core * share_o, 8), share_o)] = oline.total(slice(None))
    across(gout_ref, share_o, 0).start()

    row_moves(size, qshare_ref, qline_ref, srow, rrow, 0, False)
    scatter.start()
    qline = ColScatter(size, qline_ref, qrecv_ref, sq, rq)
    qline.event(0)
    pair_ref[0] = jnp.zeros_like(pair_ref[0])

    def finish(rows, total):
        out_ref[rows] = total
        pair_ref[0] += jnp.sum(total * act_ref[rows].astype(F32) * inv_ref[rows], axis=0, keepdims=True)

    for step in range(scatter.bits - 1):
        scatter.event(step, finish)
    for time in range(1, min(3, qline.times)):
        qline.event(time)
    scatter.event(scatter.bits - 1, finish)
    scatter.close()
    for move in small:
        move.wait()
    pair_ref[1] = jnp.sum(rgain_ref[...], axis=0)
    own = core * size + col
    pairs_ref[own] = pair_ref[...]
    for k, peer in enumerate(others):
        remote(pair_ref, pairs_ref.at[own], sp, rp, k, peer).start()
    for time in range(3, qline.times):
        qline.event(time)
    gqkv_ref[pl.ds(pl.multiple_of(core * share_q, 8), share_q)] = qline.total(slice(None))
    across(gqkv_ref, share_q, 1).start()
    for k, peer in enumerate(others):
        remote(pair_ref, pairs_ref.at[own], sp, rp, k, peer).wait()
    gains_ref[...] = jnp.sum(pairs_ref[...], axis=0)
    for mask in range(1, size):
        remote(
            blk_ref.at[row ^ mask], block_ref.at[pl.ds(pl.multiple_of(row * quarter, 16), quarter)], sblk, rblk, mask - 1, {"row": row ^ mask}
        ).wait()
    across(gout_ref, share_o, 0).wait()
    across(gqkv_ref, share_q, 1).wait()


def last_call(dqkv, weight, first, outline, blk, inner, activations, inv1, grad2):
    size = lax.axis_size("row")
    length, width = activations.shape
    columns = weight.shape[1]
    heads_cols = 2 * outline.shape[1]
    dma = pltpu.SemaphoreType.DMA
    count = 2 * size - 1
    return pl.pallas_call(
        functools.partial(last_kernel, size),
        out_shape=(
            jax.ShapeDtypeStruct((length, width), F32),
            jax.ShapeDtypeStruct((length, width), BF16),
            jax.ShapeDtypeStruct((size,) + inner.shape, F32),
            jax.ShapeDtypeStruct((2, 1, width), F32),
            jax.ShapeDtypeStruct((width, columns), F32),
            jax.ShapeDtypeStruct((heads_cols, width), F32),
        ),
        in_specs=[VM] * 9,
        out_specs=(VM,) * 6,
        scratch_shapes=[
            pltpu.VMEM((size, length, width), BF16),
            pltpu.VMEM((size - 1, length, width), BF16),
            pltpu.VMEM((size, width, columns), BF16),
            pltpu.VMEM((size, width // 2, columns), BF16),
            pltpu.VMEM((size, width // 2, columns), BF16),
            pltpu.VMEM((size, width // 2, columns), BF16),
            pltpu.VMEM((size + 1, width // 2, columns), BF16),
            pltpu.VMEM((size + 1, heads_cols // 2, width), BF16),
            pltpu.VMEM((size, 1, width), F32),
            pltpu.VMEM((2, 1, width), F32),
            pltpu.VMEM((2 * size, 2, 1, width), F32),
        ]
        + [dma((2 * (size - 1),))] * 2
        + [dma((size - 1,))] * 2
        + [dma((size - 1,))] * 2
        + [dma((1,))] * 2
        + [dma((size - 1,))] * 2
        + [dma((2,)), dma((2 * size,))] * 2
        + [dma((size - 1,))] * 2
        + [dma((count,))] * 2
        + [dma((2,))] * 2,
        compiler_params=params(4),
        cost_estimate=cost(80),
    )(dqkv, weight.reshape(size, width, columns), first, outline, blk, inner, activations, inv1, grad2.reshape(size, 1, width))


def feed_kernel(
    second_ref, cot_ref, gate_ref, up_ref, down_ref, dgate_ref, dup_ref, own_ref, part_ref,
    hidden_ref, keep_ref, send_ref, other_ref, sends, recvs,
):
    core = lax.axis_index("dp")
    step = pl.program_id(0)
    rows_n, tile, width = down_ref.shape
    tokens = second_ref.shape[0]
    tiles = hidden_ref.shape[0]
    block = tokens
    mine = tiles // 2

    def place(t):
        return pl.ds(pl.multiple_of(lax.rem(t, mine) * tile, tile), tile)

    def give(t):
        return remote(send_ref.at[:, place(t)], other_ref.at[:, place(t)], sends, recvs, lax.rem(t, mine), {"dp": 1 - core})

    @pl.when(step == 0)
    def _():
        greet(dp_size=2)

    @pl.when(step < tiles)
    def _():
        keep_ref[step] = down_ref[...]

        @pl.loop(0, tokens // block)
        def _(i):
            rows = pl.ds(pl.multiple_of(i * block, block), block)
            gate = jnp.dot(second_ref[rows], gate_ref[...], preferred_element_type=F32)
            up = jnp.dot(second_ref[rows], up_ref[...], preferred_element_type=F32)
            back = jnp.zeros((block, tile), F32)
            for j in range(rows_n):
                back += lax.dot_general(
                    cot_ref[rows, j * width : (j + 1) * width], down_ref[j], (((1,), (1,)), ((), ())), preferred_element_type=F32
                )
            sigma = jax.nn.sigmoid(gate)
            swish = gate * sigma
            hidden_ref[step, rows] = (swish * up).astype(BF16)
            dgate_ref[rows] = (back * up * (sigma * (1.0 + gate * (1.0 - sigma)))).astype(BF16)
            dup_ref[rows] = (back * swish).astype(BF16)

        for j in range(rows_n):
            value = lax.dot_general(
                hidden_ref[step], cot_ref[:, j * width : (j + 1) * width], (((0,), (0,)), ((), ())), preferred_element_type=F32
            ).astype(BF16)

            @pl.when(lax.div(step, mine) == core)
            def _():
                own_ref[j, place(step)] = value

            @pl.when(lax.div(step, mine) != core)
            def _():
                send_ref[j, place(step)] = value

        @pl.when(lax.div(step, mine) != core)
        def _():
            give(step).start()

    @pl.when(step >= tiles)
    def _():
        quarter = part_ref.shape[1]
        rows = pl.ds(pl.multiple_of((step - tiles) * quarter, quarter), quarter)
        for j in range(rows_n):
            total = jnp.zeros((quarter, width), F32)
            for t in range(tiles):
                total += jnp.dot(hidden_ref[t, rows], keep_ref[t, j], preferred_element_type=F32)
            part_ref[0, :, j * width : (j + 1) * width] = total.astype(BF16)

    @pl.when(step == pl.num_programs(0) - 1)
    def _():
        for t in range(mine):
            give(t).wait()
            for j in range(rows_n):
                own_ref[j, place(t)] = (own_ref[j, place(t)].astype(F32) + other_ref[j, place(t)].astype(F32)).astype(BF16)


def feed_call(second, cot, gate, up, down):
    rows_n, hidden, width = down.shape
    cols_n = lax.axis_size("col")
    tokens, features = second.shape
    tile = 256
    tiles = hidden // tile
    half = (rows_n, hidden // 2, width)

    def place(i):
        return jnp.minimum(i, tiles - 1)

    return pl.pallas_call(
        feed_kernel,
        grid=(tiles + cols_n,),
        out_shape=(
            jax.ShapeDtypeStruct((tokens, hidden), BF16),
            jax.ShapeDtypeStruct((tokens, hidden), BF16),
            jax.ShapeDtypeStruct(half, BF16),
            jax.ShapeDtypeStruct((cols_n, tokens // cols_n, features), BF16),
        ),
        in_specs=[
            VM,
            VM,
            pl.BlockSpec((features, tile), lambda i: (0, place(i))),
            pl.BlockSpec((features, tile), lambda i: (0, place(i))),
            pl.BlockSpec((rows_n, tile, width), lambda i: (0, place(i), 0)),
        ],
        out_specs=(
            pl.BlockSpec((tokens, tile), lambda i: (0, place(i))),
            pl.BlockSpec((tokens, tile), lambda i: (0, place(i))),
            VM,
            pl.BlockSpec((1, tokens // cols_n, features), lambda i: (jnp.maximum(i - tiles, 0), 0, 0)),
        ),
        scratch_shapes=[
            pltpu.VMEM((tiles, tokens, tile), BF16),
            pltpu.VMEM((tiles, rows_n, tile, width), BF16),
            pltpu.VMEM(half, BF16),
            pltpu.VMEM(half, BF16),
            pltpu.SemaphoreType.DMA((tiles // 2,)),
            pltpu.SemaphoreType.DMA((tiles // 2,)),
        ],
        compiler_params=params(7),
        cost_estimate=cost(50),
    )(second, cot, gate, up, down)


def rotary_tables(positions):
    exponent = jnp.arange(0, HEAD, 2).astype(F32) / HEAD
    inverse = jnp.power(F32(THETA), -exponent)
    phase = positions[:, None] * inverse[None, :]
    phase = jnp.concatenate([phase] * (2 * 128 // HEAD), axis=1)
    return (jnp.cos(phase), jnp.sin(phase))


def local(
    activations, segments, positions, first_gain, query_weight, key_weight, value_weight, out_weight,
    second_gain, gate_weight, up_weight, down_weight, cotangent,
):
    rows = lax.axis_size("row")
    row, col = lax.axis_index("row"), lax.axis_index("col")
    length, width = activations.shape
    features = rows * width
    query_cols, key_cols = query_weight.shape[1], key_weight.shape[1]
    heads, kvs = query_cols // HEAD, key_cols // HEAD
    hidden_cols = gate_weight.shape[1]
    spare = jnp.zeros((width, -key_cols % 128), BF16)
    key_span = key_cols + spare.shape[1]
    qkv_cols = query_cols + 2 * key_span

    small = jnp.concatenate([segments.astype(F32), positions.astype(F32), first_gain, second_gain]).reshape(-1, 128)
    qkv_weight = jnp.concatenate([query_weight, key_weight, spare, value_weight, spare], axis=1)
    x_blocks, first, inv1, cot_tok, smalls, qkv_all, out_all_w, near = first_call(activations, cotangent, small, qkv_weight, out_weight)
    qkv_all = qkv_all.reshape(features, qkv_cols)
    smalls = smalls.reshape(rows, -1)
    own = lax.dynamic_slice_in_dim(smalls, col, 1, 0)[0]
    segment_own, position_own = own[:length], own[length : 2 * length]
    gain2 = smalls[:, 2 * length + width :].reshape(1, features)

    cosine, sine = rotary_tables(position_own)
    segc, segr = segment_own[:, None], segment_own[None]
    q, k, v, attn, following, gate_all = attend_call(first, qkv_all, cosine, sine, segc, segr, near, gate_weight, heads, kvs)
    middle, second_all, cot_all, up_all, down_all = middle_call(
        attn, out_all_w, x_blocks, gain2, cot_tok, near, following, up_weight, down_weight
    )
    gate_all, up_all = gate_all.reshape(features, hidden_cols), up_all.reshape(features, hidden_cols)
    second_all, cot_all = second_all.reshape(-1, features), cot_all.reshape(-1, features)
    dgate, dup, down_share, down_part = feed_call(second_all, cot_all, gate_all, up_all, down_all)
    dmid_all, gain2_grad, down_grad, gate_share, up_share = back_call(
        dgate, dup, gate_all.reshape(rows, width, hidden_cols), up_all.reshape(rows, width, hidden_cols), middle, cot_tok, gain2, second_all,
        down_share,
    )
    dmid_all = dmid_all.reshape(length, features)

    dqkv, inner1, blk, outline, up_grad, gate_grad = attend_back_call(
        dmid_all, out_all_w, q, k, v, cosine, sine, segc, segr, qkv_cols, attn, down_part, middle, up_share, gate_share
    )
    dfirst, block_out, inner1, gains, qkv_grad, out_grad = last_call(
        dqkv, qkv_all, first, outline, blk, inner1.reshape(-1, 128), activations, inv1, gain2_grad
    )
    inner1 = jnp.sum(inner1, axis=0).reshape(length, 1) / (inv1 * features)
    own_x = activations.astype(F32)
    dmid_own = lax.dynamic_slice_in_dim(dmid_all, row * width, width, 1).astype(F32)
    input_grad = dmid_own + inv1 * first_gain[None] * dfirst - own_x * (inv1 * inv1 * inv1 * inner1)

    return (
        block_out,
        input_grad,
        gains[0, 0],
        qkv_grad[:, :query_cols],
        qkv_grad[:, query_cols : query_cols + key_cols],
        qkv_grad[:, query_cols + key_span : query_cols + key_span + key_cols],
        out_grad,
        gains[1, 0],
        gate_grad,
        up_grad,
        down_grad,
    )


def solution(mesh):
    tokens, block, swapped = P(("dp", "col"), "row"), P("row", "col"), P("col", "row")
    return jax.shard_map(
        local,
        mesh=mesh,
        in_specs=(
            tokens, P(("dp", "row")), P(("dp", "row")), P("row"), block, block, block, swapped,
            P("row"), block, block, swapped, tokens,
        ),
        out_specs=(tokens, tokens, P("row"), block, block, block, swapped, P("row"), block, block, swapped),
        check_vma=False,
    )
```

```python
import functools

import jax
import jax.numpy as jnp
from jax import lax
from jax.experimental import pallas as pl
from jax.experimental.pallas import tpu as pltpu
from jax.sharding import PartitionSpec as P

HEAD = 64
EPSILON = 1e-05
THETA = 500000.0
F32 = jnp.float32
BF16 = jnp.bfloat16


MESH = pl.DeviceIdType.MESH
VMEM_LIMIT = 60 * 1024 * 1024


def greet(row_size=0, col_size=0, dp_size=0):
    barrier = pltpu.get_barrier_semaphore()
    if row_size:
        row = lax.axis_index("row")
        for mask in range(1, row_size):
            pl.semaphore_signal(barrier, inc=1, device_id={"row": row ^ mask}, device_id_type=MESH)
    if col_size:
        col = lax.axis_index("col")

        @pl.when(col > 0)
        def _():
            pl.semaphore_signal(barrier, inc=1, device_id={"col": col - 1}, device_id_type=MESH)

        @pl.when(col < col_size - 1)
        def _():
            pl.semaphore_signal(barrier, inc=1, device_id={"col": col + 1}, device_id_type=MESH)

    if dp_size:
        pl.semaphore_signal(barrier, inc=1, device_id={"dp": 1 - lax.axis_index("dp")}, device_id_type=MESH)
    count = max(row_size - 1, 0) + (1 if dp_size else 0)
    if col_size:
        count = count + jnp.where(col > 0, 1, 0) + jnp.where(col < col_size - 1, 1, 0)
    pl.semaphore_wait(barrier, count)


def remote(src, dst, sends, recvs, place, device):
    return pltpu.make_async_remote_copy(
        src_ref=src, dst_ref=dst, send_sem=sends.at[place], recv_sem=recvs.at[place],
        device_id=device, device_id_type=MESH,
    )


class RowGather:
    def __init__(self, size, ref, sends, recvs, begin=0, count=None, first=0):
        self.size, self.ref, self.sends, self.recvs = size, ref, sends, recvs
        self.bits = size.bit_length() - 1
        self.row = lax.axis_index("row")
        self.begin, self.first = begin, first
        self.half = (count or ref.shape[1]) // 2
        self.all = [self.copies(step) for step in range(self.bits)]

    def rows(self, part):
        return pl.ds(pl.multiple_of(self.begin + part * self.half, 16), self.half)

    def order(self, part):
        return list(range(self.bits)) if part == 0 else list(range(self.bits))[::-1]

    def copies(self, step):
        out = []
        for part in range(2):
            order = self.order(part)
            for item in range(1 << step):
                mask = 0
                for j in range(step):
                    if item >> j & 1:
                        mask |= 1 << order[j]
                piece = self.ref.at[self.row ^ mask, self.rows(part)]
                place = self.first + part * (self.size - 1) + (1 << step) - 1 + item
                out.append(remote(piece, piece, self.sends, self.recvs, place, {"row": self.row ^ (1 << order[step])}))
        return out

    def start(self):
        for step in range(self.bits):
            for part in range(2):
                self.all[step][part << step].start()

    def event(self, step, seen=None):
        for part in range(2):
            order = self.order(part)
            for item in range(1 << step):
                self.all[step][(part << step) + item].wait_recv()
                got = item | 1 << step
                for later in range(step + 1, self.bits):
                    self.all[later][(part << later) + got].start()
                if seen is not None:
                    mask = 0
                    for j in range(step + 1):
                        if got >> j & 1:
                            mask |= 1 << order[j]
                    seen(mask, part)

    def finish(self):
        for step in range(self.bits):
            for copy in self.all[step]:
                copy.wait_send()

    def run(self):
        for step in range(self.bits):
            self.event(step)
        self.finish()


class SharedGather:
    def __init__(self, size, shard, full, copied, sends, recvs, score, rcore, first):
        self.core, self.row = lax.axis_index("dp"), lax.axis_index("row")
        self.size, self.full, self.score, self.rcore, self.first = size, full, score, rcore, first * 2 * (size - 1)
        share = full.shape[1] // 2
        self.own = pltpu.make_async_copy(shard, full.at[self.row], copied.at[first])
        self.gather = RowGather(size, full, sends, recvs, self.core * share, share, self.first)

    def across(self, mask, part):
        piece = self.full.at[self.row ^ mask, self.gather.rows(part)]
        return remote(piece, piece, self.score, self.rcore, self.first + part * (self.size - 1) + mask - 1, {"dp": 1 - self.core})

    def load(self):
        self.own.start()

    def start(self):
        self.own.wait()
        self.gather.start()

    def event(self, step):
        self.gather.event(step, lambda mask, part: self.across(mask, part).start())

    def finish(self):
        self.gather.finish()
        for mask in range(1, self.size):
            for part in range(2):
                self.across(mask, part).wait()

    @staticmethod
    def scratch(size, count):
        dma = pltpu.SemaphoreType.DMA
        return [dma((count,))] + [dma((count * 2 * (size - 1),))] * 4


class RowScatter:
    def __init__(self, size, part_ref, recv_ref, sends, recvs, begin=0):
        self.size, self.part, self.recv = size, part_ref, recv_ref
        self.bits = size.bit_length() - 1
        self.row = lax.axis_index("row")
        half = recv_ref.shape[1] // 2
        self.rows = [pl.ds(part * half, half) for part in range(2)]
        self.own = [pl.ds(pl.multiple_of(begin + part * half, 16), half) for part in range(2)]
        self.plans = []
        for part in range(2):
            order = self.order(part)
            steps, held = [], {}
            for step in range(self.bits):
                bit, rest = 1 << order[step], order[step + 1 :]
                count = 1 << len(rest)
                copies, sums = [], {}
                for item in range(count - 1, -1, -1):
                    mask = sum(1 << other for j, other in enumerate(rest) if item >> j & 1)
                    place = size - 2 * count + item
                    copy = remote(
                        self.spot(part, mask ^ bit, held), recv_ref.at[place, self.rows[part]],
                        sends, recvs, part * (size - 1) + place, {"row": self.row ^ bit},
                    )
                    copies.append((mask, place, held.get(mask), copy))
                    sums[mask] = place
                held = sums
                steps.append(copies)
            self.plans.append(steps)

    def spot(self, part, mask, held):
        if mask in held:
            return self.recv.at[held[mask], self.rows[part]]
        return self.part.at[self.row ^ mask, self.own[part]]

    def order(self, part):
        return list(range(self.bits)) if part == 0 else list(range(self.bits))[::-1]

    def start(self):
        for part in range(2):
            for copies in self.plans[part][0]:
                copies[3].start()

    def event(self, step, finish):
        last = step + 1 == self.bits
        for part in range(2):
            rows, own = self.rows[part], self.own[part]
            for mask, place, before, copy in self.plans[part][step]:
                copy.wait_recv()
                size, begin, start = min(64, rows.size), own.start, rows.start

                @pl.loop(0, rows.size // size)
                def _(i):
                    here = pl.ds(pl.multiple_of(start + i * size, 16), size)
                    if before is None:
                        had = self.part[self.row ^ mask, pl.ds(pl.multiple_of(begin + i * size, 16), size)]
                    else:
                        had = self.recv[before, here]
                    total = had.astype(F32) + self.recv[place, here].astype(F32)
                    if last:
                        finish(here, total)
                    else:
                        self.recv[place, here] = total.astype(BF16)

                if last:
                    continue
                for mask2, _, _, copy2 in self.plans[part][step + 1]:
                    if mask2 ^ 1 << self.order(part)[step + 1] == mask:
                        copy2.start()

    def close(self):
        for part in range(2):
            for step in self.plans[part]:
                for _, _, _, copy in step:
                    copy.wait_send()

    def run(self, finish):
        self.start()
        for step in range(self.bits):
            self.event(step, finish)
        self.close()


class ColGather:
    def __init__(self, size, ref, sends, recvs, begin=0, end=None, rows=None, first=0):
        self.size, self.ref, self.sends, self.recvs = size, ref, sends, recvs
        self.rows, self.first = rows or pl.ds(0, ref.shape[1]), first
        self.begin, self.end = begin, size - 1 if end is None else end
        self.col = lax.axis_index("col")

    def sides(self, step):
        size, col = self.size, self.col
        return (
            (0, lax.rem(col - step + size, size), col >= step, col < size - 1),
            (1, lax.rem(col + step, size), col + step < size, col > 0),
        )

    def copy(self, side, step):
        size, col = self.size, self.col
        piece = self.ref.at[self.sides(step)[side][1], self.rows]
        target = lax.rem(col + (1 if side == 0 else size - 1), size)
        return remote(piece, piece, self.sends, self.recvs, self.first + side * (size - 1) + step, {"col": target})

    def event(self, step, seen=None):
        for side, place, has, goes in self.sides(step):
            if step > self.begin:

                @pl.when(has)
                def _():
                    self.copy(side, step - 1).wait_recv()

            if step < self.end:

                @pl.when(has & goes)
                def _():
                    self.copy(side, step).start()

            if seen is not None and (step or side == 0):

                @pl.when(has)
                def _():
                    seen(place)

    def finish(self):
        for step in range(self.begin, self.end):
            for side, place, has, goes in self.sides(step):

                @pl.when(has & goes)
                def _():
                    self.copy(side, step).wait_send()

    def run(self):
        for step in range(self.begin, self.end + 1):
            self.event(step)
        self.finish()


class ColScatter:
    def __init__(self, size, part, recv, sends, recvs, begin=0, count=None, first=0):
        self.size, self.part, self.recv, self.sends, self.recvs = size, part, recv, sends, recvs
        self.begin, self.count, self.first = begin, count or part.shape[1], first
        self.col = lax.axis_index("col")
        self.times = size

    def copy(self, side, target, source):
        step = 1 if side == 0 else self.size - 1
        rows = pl.ds(self.begin, self.count)
        return pltpu.make_async_remote_copy(
            src_ref=self.recv.at[target + 1 - side, rows] if source is None else source.at[target, rows],
            dst_ref=self.recv.at[target + 1 - side, rows], send_sem=self.sends.at[2 * self.first + side],
            recv_sem=self.recvs.at[(2 * self.first + side) * self.size + target],
            device_id={"col": lax.rem(self.col + step, self.size)}, device_id_type=MESH,
        )

    def event(self, time, prepare=None):
        size, col = self.size, self.col
        for side, first, step in ((0, col == 0, time - col), (1, col == size - 1, time - (size - 1 - col))):
            target = size - 1 - step if side == 0 else step
            valid = (step >= 0) & ((target >= col) if side == 0 else (target <= col))
            place = lax.rem(target + 4 * size, size)

            if prepare is not None:

                @pl.when(valid & ((target != col) | (side == 0)))
                def _():
                    prepare(place)

            @pl.when(valid & jnp.logical_not(first))
            def _():
                self.copy(side, place, self.part).wait_recv()

            @pl.when(valid & jnp.logical_not(first) & (target != col))
            def _():
                chunk = min(64, self.count)

                @pl.loop(0, self.count // chunk)
                def _(i):
                    rows = pl.ds(pl.multiple_of(self.begin + i * chunk, 16), chunk)
                    self.recv[place + 1 - side, rows] = (
                        self.recv[place + 1 - side, rows].astype(F32) + self.part[place, rows].astype(F32)
                    ).astype(BF16)

            @pl.when(valid & (step > 0))
            def _():
                self.copy(side, place, self.part).wait_send()

            @pl.when(valid & (target != col) & first)
            def _():
                self.copy(side, place, self.part).start()

            @pl.when(valid & (target != col) & jnp.logical_not(first))
            def _():
                self.copy(side, place, None).start()

    def total(self, rows):
        got = self.part[self.col, rows].astype(F32)
        got += jnp.where(self.col > 0, self.recv[self.col + 1, rows].astype(F32), 0.0)
        got += jnp.where(self.col < self.size - 1, self.recv[self.col, rows].astype(F32), 0.0)
        return got


VM = pl.BlockSpec(memory_space=pltpu.VMEM)


def params(ident):
    return pltpu.CompilerParams(collective_id=ident, has_side_effects=True, vmem_limit_bytes=VMEM_LIMIT)


def keep_near(size, line, near, step):
    col = lax.axis_index("col")
    for side, place, has in ((0, col - step, col >= step), (1, col + step, col + step < size)):

        @pl.when(has)
        def _():
            near[side] = line[lax.rem(place + size, size)]


def take_near(size, line, near, step):
    col = lax.axis_index("col")
    for side, place, has in ((0, col - step, col >= step), (1, col + step, col + step < size)):

        @pl.when(has)
        def _():
            line[lax.rem(place + size, size)] = near[side]


def first_kernel(
    size, act_ref, cot_ref, small_ref, qkv_ref, out_ref,
    x_ref, first_ref, inv_ref, tok_ref, smalls_ref, qkvs_ref, outs_ref,
    near_ref,
    got_ref, zq_ref, zo_ref, zc_ref, s1, r1, s2, r2, s3, r3, szq, rzq, szo, rzo, srow, rrow, score, rcore, szc, rzc,
):
    row, col, core = lax.axis_index("row"), lax.axis_index("col"), lax.axis_index("dp")
    length, width = act_ref.shape
    quarter = length // size
    small_rows = small_ref.shape[0]
    gain_row = 2 * length // 128
    x_ref[row] = act_ref[...]
    smalls_ref[row] = small_ref[...]
    blocks = ((qkv_ref, zq_ref, qkvs_ref, szq, rzq), (out_ref, zo_ref, outs_ref, szo, rzo))
    for block, line, _, _, _ in blocks:
        share = block.shape[0] // 2
        line[col] = block[pl.ds(pl.multiple_of(core * share, 16), share)]
    greet(row_size=size, col_size=size, dp_size=2)
    gather = RowGather(size, x_ref, s1, r1)
    smalls = [
        remote(small_ref, smalls_ref.at[row], s3, r3, mask - 1, {"row": row ^ mask}) for mask in range(1, size)
    ]
    lines = [ColGather(size, line, sends, recvs) for _, line, _, sends, recvs in blocks]
    lines[0].event(0)
    for move in smalls:
        move.start()
    moves = [
        remote(cot_ref.at[pl.ds((row ^ mask) * quarter, quarter)], got_ref.at[row], s2, r2, mask - 1, {"row": row ^ mask})
        for mask in range(1, size)
    ]
    for move in moves:
        move.start()
    gather.start()
    got_ref[row] = cot_ref[pl.ds(pl.multiple_of(row * quarter, 16), quarter)]

    def half(ref, place):
        share = ref.shape[1] // 2
        return ref.at[place, pl.ds(pl.multiple_of(core * share, 16), share)]

    def hand(which, mask):
        _, line, full, _, _ = blocks[which]
        return remote(line.at[row ^ mask], half(full, row), srow, rrow, which * (size - 1) + mask - 1, {"row": row ^ mask})

    def across(which, mask):
        full = blocks[which][2]
        piece = half(full, row ^ mask)
        return remote(piece, piece, score, rcore, which * size + mask, {"dp": 1 - core})

    def seen(which):
        def act(place):
            _, line, full, _, _ = blocks[which]

            @pl.when(place == row)
            def _():
                share = full.shape[1] // 2
                full[row, pl.ds(pl.multiple_of(core * share, 16), share)] = line[row]
                across(which, 0).start()

            for mask in range(1, size):

                @pl.when(place == row ^ mask)
                def _():
                    hand(which, mask).start()

        return act

    act, act1 = seen(0), seen(1)
    act(col)
    near = ColGather(size, zc_ref, szc, rzc, 0, 1)
    for step in range(1, size - 1):
        lines[0].event(step, act)
    for move in moves:
        move.wait()
    for j in range(size):
        zc_ref[col, :, j * width : (j + 1) * width] = got_ref[j]
    tok_ref[...] = zc_ref[col]
    near.event(0)
    lines[1].event(0)
    lines[0].event(size - 1, act)
    act1(col)
    gather.event(0)
    lines[1].event(1, act1)
    for step in range(1, gather.bits):
        gather.event(step)
    for move in smalls:
        move.wait()

    @pl.loop(0, length // 128)
    def _(i):
        rows = pl.ds(pl.multiple_of(i * 128, 128), 128)
        total = jnp.zeros((128, 1), F32)
        for j in range(size):
            value = x_ref[j, rows].astype(F32)
            total += jnp.sum(value * value, axis=1, keepdims=True)
        inverse = lax.rsqrt(total / (size * width) + EPSILON)
        inv_ref[rows] = inverse
        for j in range(size):
            for k in range(width // 128):
                gain = smalls_ref[j, gain_row + k : gain_row + k + 1]
                value = x_ref[j, rows, k * 128 : (k + 1) * 128].astype(F32)
                first_ref[rows, j * width + k * 128 : j * width + (k + 1) * 128] = (value * inverse * gain).astype(BF16)

    for mask in range(1, size):
        hand(0, mask).wait_recv()
        across(0, mask).start()
    for step in range(2, size):
        lines[1].event(step, act1)
    for mask in range(1, size):
        hand(1, mask).wait_recv()
        across(1, mask).start()
    near.event(1)
    keep_near(size, zc_ref, near_ref, 1)
    near.finish()
    gather.finish()
    for line in lines:
        line.finish()
    for which in range(2):
        for mask in range(1, size):
            hand(which, mask).wait_send()
        for mask in range(size):
            across(which, mask).wait()


def first_call(activations, cotangent, small, qkv_weight, out_weight):
    size = lax.axis_size("row")
    length, width = activations.shape
    quarter = length // size
    qkv_cols, heads_cols = qkv_weight.shape[1], out_weight.shape[0]
    dma = pltpu.SemaphoreType.DMA
    return pl.pallas_call(
        functools.partial(first_kernel, size),
        out_shape=(
            jax.ShapeDtypeStruct((size, length, width), BF16),
            jax.ShapeDtypeStruct((length, size * width), BF16),
            jax.ShapeDtypeStruct((length, 1), F32),
            jax.ShapeDtypeStruct((quarter, size * width), BF16),
            jax.ShapeDtypeStruct((size,) + small.shape, F32),
            jax.ShapeDtypeStruct((size,) + qkv_weight.shape, BF16),
            jax.ShapeDtypeStruct((size,) + out_weight.shape, BF16),
            jax.ShapeDtypeStruct((2, quarter, size * width), BF16),
        ),
        in_specs=[VM] * 5,
        out_specs=(VM,) * 8,
        scratch_shapes=[
            pltpu.VMEM((size, quarter, width), BF16),
            pltpu.VMEM((size, width // 2, qkv_cols), BF16),
            pltpu.VMEM((size, heads_cols // 2, width), BF16),
            pltpu.VMEM((size, quarter, size * width), BF16),
        ]
        + [dma((2 * (size - 1),))] * 2
        + [dma((size - 1,))] * 4
        + [dma((2 * (size - 1),))] * 4
        + [dma((2 * (size - 1),))] * 2
        + [dma((2 * size,))] * 2
        + [dma((2 * (size - 1),))] * 2,
        compiler_params=params(1),
    )(activations, cotangent, small, qkv_weight, out_weight)


def turn(values, low):
    return jnp.where(low, -pltpu.roll(values, 128 - HEAD // 2, 1), pltpu.roll(values, HEAD // 2, 1))


def low_columns(rows):
    return lax.broadcasted_iota(jnp.int32, (rows, 128), 1) % HEAD < HEAD // 2


def masked_scores(query, key, seg_col, seg_row, first_row):
    scores = lax.dot_general(query, key, (((1,), (1,)), ((), ())), preferred_element_type=F32)
    rows = lax.broadcasted_iota(jnp.int32, scores.shape, 0) + first_row
    columns = lax.broadcasted_iota(jnp.int32, scores.shape, 1)
    allowed = (seg_col == seg_row) & (rows >= columns)
    return jnp.where(allowed, scores, -1e30)


def attend_kernel(
    size, first_ref, weight_ref, cos_ref, sin_ref, segc_ref, segr_ref, near_ref, gate_ref,
    q_ref, k_ref, v_ref, o_ref, next_ref, gates_ref, oh_ref, zc_ref, szc, rzc, *shared,
):
    bulk = SharedGather(size, gate_ref, gates_ref, *shared, 0)
    bulk.load()
    take_near(size, zc_ref, near_ref, 1)
    greet(row_size=size, col_size=size, dp_size=2)
    bulk.start()
    line = ColGather(size, zc_ref, szc, rzc, 1, 2)
    line.event(1)
    heads, length, _ = q_ref.shape
    kvs = k_ref.shape[0]
    group = heads // kvs
    query_cols = heads * HEAD
    key_cols = (weight_ref.shape[1] - query_cols) // 2
    block = 256

    @pl.loop(0, length // block)
    def _(i):
        rows = pl.ds(pl.multiple_of(i * block, block), block)
        low = low_columns(block)
        cosine, sine = cos_ref[rows], sin_ref[rows]
        whole = jnp.dot(first_ref[rows], weight_ref[...], preferred_element_type=F32)
        for ref, count, start, factor in ((q_ref, heads, 0, HEAD ** (-0.5)), (k_ref, kvs, query_cols, 1.0)):
            for j in range((count + 1) // 2):
                part = whole[:, start + 128 * j : start + 128 * (j + 1)]
                part = ((part * cosine + turn(part, low) * sine) * factor).astype(BF16)
                for side in range(min(2, count - 2 * j)):
                    ref[2 * j + side, rows] = part[:, side * HEAD : (side + 1) * HEAD]
        for j in range(kvs):
            at = query_cols + key_cols + j * HEAD
            v_ref[j, rows] = whole[:, at : at + HEAD].astype(BF16)

    @pl.loop(0, heads)
    def _(head):
        kv = lax.div(head, group)
        for i in range(length // block):
            rows, extent = slice(i * block, (i + 1) * block), (i + 1) * block
            scores = masked_scores(q_ref[head, rows], k_ref[kv, :extent], segc_ref[rows], segr_ref[:, :extent], i * block)
            top = jnp.max(scores, axis=1, keepdims=True)
            weights = jnp.exp(scores - top)
            total = jnp.sum(weights, axis=1, keepdims=True)
            mixed = jnp.dot(weights.astype(BF16), v_ref[kv, :extent], preferred_element_type=F32)
            oh_ref[head, rows] = (mixed / total).astype(BF16)

    for head in range(heads):
        o_ref[:, head * HEAD : (head + 1) * HEAD] = oh_ref[head]
    for step in range(bulk.gather.bits):
        bulk.event(step)
    line.event(2)
    keep_near(size, zc_ref, next_ref, 2)
    line.finish()
    bulk.finish()


def attend_call(first, weight, cosine, sine, segc, segr, near, gate, heads, kvs):
    size = lax.axis_size("row")
    length = first.shape[0]
    dma = pltpu.SemaphoreType.DMA
    return pl.pallas_call(
        functools.partial(attend_kernel, size),
        out_shape=(
            jax.ShapeDtypeStruct((heads, length, HEAD), BF16),
            jax.ShapeDtypeStruct((kvs, length, HEAD), BF16),
            jax.ShapeDtypeStruct((kvs, length, HEAD), BF16),
            jax.ShapeDtypeStruct((length, heads * HEAD), BF16),
            jax.ShapeDtypeStruct(near.shape, BF16),
            jax.ShapeDtypeStruct((size,) + gate.shape, BF16),
        ),
        in_specs=[VM] * 8,
        out_specs=(VM,) * 5 + (pl.BlockSpec(memory_space=pl.ANY),),
        scratch_shapes=[
            pltpu.VMEM((heads, length, HEAD), BF16),
            pltpu.VMEM((size,) + near.shape[1:], BF16),
            dma((2 * (size - 1),)), dma((2 * (size - 1),)),
        ]
        + SharedGather.scratch(size, 1),
        compiler_params=params(6),
        cost_estimate=cost(45),
    )(first, weight, cosine, sine, segc, segr, near, gate)


class swap_halves:
    def __init__(self, part, other, sends, recvs):
        core = lax.axis_index("dp")
        share = part.shape[1] // 2
        self.move = remote(
            part.at[:, pl.ds(pl.multiple_of((1 - core) * share, 16), share)], other, sends, recvs, 0, {"dp": 1 - core}
        )

    def start(self):
        self.move.start()

    def wait(self):
        self.move.wait()


def add_halves(part, other, share):
    rows = pl.ds(pl.multiple_of(lax.axis_index("dp") * share.shape[1], 16), share.shape[1])
    for j in range(part.shape[0]):
        share[j] = (part[j, rows].astype(F32) + other[j].astype(F32)).astype(BF16)


def row_moves(size, source, target, sends, recvs, first, begin):
    row = lax.axis_index("row")
    if begin:
        target[row] = source[row]
    for mask in range(1, size):
        move = remote(source.at[row ^ mask], target.at[row], sends, recvs, first + mask - 1, {"row": row ^ mask})
        if begin:
            move.start()
        else:
            move.wait()


def cost(micros):
    return pl.CostEstimate(flops=int(micros * 1e9), bytes_accessed=1 << 20, transcendentals=0)


def attend_back_kernel(
    dmid_ref, weight_ref, q_ref, k_ref, v_ref, cos_ref, sin_ref, segc_ref, segr_ref,
    attn_ref, down_ref, mid_ref, upshare_ref, gateshare_ref,
    dqkv_ref, inner_ref, blk_ref, line_ref, gup_ref, ggate_ref, do_ref, dq_ref, dk_ref, dv_ref,
    recv_ref, part_ref, other_ref, share_ref, urecv_ref, drecv_ref, ustage_ref, dstage_ref,
    s1, r1, score, rcore, srow, rrow, su, ru, sd, rd, copied, sf, rf,
):
    row, core = lax.axis_index("row"), lax.axis_index("dp")
    cols_n = down_ref.shape[0]
    heads, length, _ = q_ref.shape
    kvs = k_ref.shape[0]
    group = heads // kvs
    query_cols = heads * HEAD
    key_cols = (dqkv_ref.shape[1] - query_cols) // 2
    block = 256
    parts, _, width = weight_ref.shape
    greet(row_size=parts, col_size=cols_n, dp_size=2)
    line = ColScatter(cols_n, down_ref, recv_ref, s1, r1)
    line.event(0)
    sums = [
        (RowScatter(parts, upshare_ref, urecv_ref, su, ru), ustage_ref, gup_ref),
        (RowScatter(parts, gateshare_ref, drecv_ref, sd, rd), dstage_ref, ggate_ref),
    ]
    for scatter, _, _ in sums:
        scatter.start()
    for j in range(parts):
        part_ref[j] = lax.dot_general(
            attn_ref[...], dmid_ref[:, j * width : (j + 1) * width], (((0,), (0,)), ((), ())), preferred_element_type=F32
        ).astype(BF16)
    cross = swap_halves(part_ref, other_ref, score, rcore)
    cross.start()
    dk_ref[...] = jnp.zeros_like(dk_ref)
    dv_ref[...] = jnp.zeros_like(dv_ref)
    inner_ref[...] = jnp.zeros_like(inner_ref)

    @pl.loop(0, length // block)
    def _(i):
        rows = pl.ds(pl.multiple_of(i * block, block), block)
        total = jnp.zeros((block, query_cols), F32)
        for j in range(parts):
            total += lax.dot_general(
                dmid_ref[rows, j * width : (j + 1) * width], weight_ref[j], (((1,), (1,)), ((), ())), preferred_element_type=F32
            )
        for head in range(heads):
            do_ref[head, rows] = total[:, head * HEAD : (head + 1) * HEAD].astype(BF16)

    @pl.loop(0, heads)
    def _(head):
        @pl.when(head == min(1, heads - 1))
        def _():
            cross.wait()
            add_halves(part_ref, other_ref, share_ref)
            row_moves(parts, share_ref, line_ref, srow, rrow, 0, True)

        @pl.when(head == heads // 2)
        def _():
            line.event(1)

        kv = lax.div(head, group)
        for i in range(length // block):
            rows, extent = slice(i * block, (i + 1) * block), (i + 1) * block
            query, keys, grads = q_ref[head, rows], k_ref[kv, :extent], do_ref[head, rows]
            scores = masked_scores(query, keys, segc_ref[rows], segr_ref[:, :extent], i * block)
            top = jnp.max(scores, axis=1, keepdims=True)
            weights = jnp.exp(scores - top)
            weights = weights * (1.0 / jnp.sum(weights, axis=1, keepdims=True))
            back = lax.dot_general(grads, v_ref[kv, :extent], (((1,), (1,)), ((), ())), preferred_element_type=F32)
            dv_ref[kv, :extent] += lax.dot_general(
                weights.astype(BF16), grads, (((0,), (0,)), ((), ())), preferred_element_type=F32
            )
            ds = (weights * (back - jnp.sum(weights * back, axis=1, keepdims=True))).astype(BF16)
            dq = jnp.dot(ds, keys, preferred_element_type=F32)
            inner_ref[rows] += jnp.sum(dq * query.astype(F32), axis=1, keepdims=True)
            for side in range(2):

                @pl.when(lax.rem(head, 2) == side)
                def _():
                    dq_ref[lax.div(head, 2), rows, side * HEAD : (side + 1) * HEAD] = dq

            dk_ref[kv, :extent] += lax.dot_general(ds, query, (((0,), (0,)), ((), ())), preferred_element_type=F32)

    @pl.loop(0, length // block)
    def _(i):
        rows = pl.ds(pl.multiple_of(i * block, block), block)
        low = low_columns(block)
        cosine, sine = cos_ref[rows], sin_ref[rows]
        for ref, count, start, factor in ((dq_ref, heads, 0, HEAD ** (-0.5)), (dk_ref, kvs, query_cols, 1.0), (dv_ref, kvs, query_cols + key_cols, None)):
            for j in range((count + 1) // 2):
                if ref is dq_ref:
                    part = dq_ref[j, rows]
                else:
                    sides = [ref[2 * j + side, rows] if 2 * j + side < count else jnp.zeros((block, HEAD), F32) for side in range(2)]
                    part = jnp.concatenate(sides, axis=1)
                if factor is not None:
                    part = (part * cosine - turn(part * sine, low)) * factor
                dqkv_ref[rows, start + 128 * j : start + 128 * (j + 1)] = part.astype(BF16)
        more = jnp.zeros((block, 1), F32)
        for kv in range(kvs):
            more += jnp.sum(dk_ref[kv, rows] * k_ref[kv, rows].astype(F32) + dv_ref[kv, rows] * v_ref[kv, rows].astype(F32), axis=1, keepdims=True)
        inner_ref[rows] += more

    def finish(stage):
        def act(rows, total):
            stage[rows] = total

        return act

    if cols_n > 2:
        line.event(2)
    bits = sums[0][0].bits
    for step in range(bits - 1):
        for scatter, stage, _ in sums:
            scatter.event(step, finish(stage))
    for time in range(3, line.times):
        line.event(time)
    results = []
    for k, (scatter, stage, out) in enumerate(sums):
        scatter.event(bits - 1, finish(stage))
        moves = settle(stage, out, core, copied, sf, rf, k)
        for move in moves:
            move.start()
        results += moves
        scatter.close()

    @pl.loop(0, mid_ref.shape[0] // 64)
    def _(i):
        rows = pl.ds(pl.multiple_of(i * 64, 16), 64)
        total = mid_ref[rows] + line.total(rows)
        for j in range(parts):
            blk_ref[j, rows] = total[:, j * width : (j + 1) * width].astype(BF16)

    row_moves(parts, share_ref, line_ref, srow, rrow, 0, False)
    for move in results:
        move.wait()


def attend_back_call(dmid, weight, q, k, v, cosine, sine, segc, segr, columns, attn, down, middle, upshare, gateshare):
    rows_n, cols_n = lax.axis_size("row"), lax.axis_size("col")
    _, heads_cols, width = weight.shape
    quarter = middle.shape[0]
    dma = pltpu.SemaphoreType.DMA
    heads, length, _ = q.shape
    kvs = k.shape[0]
    return pl.pallas_call(
        attend_back_kernel,
        out_shape=(
            jax.ShapeDtypeStruct((length, columns), BF16),
            jax.ShapeDtypeStruct((length, 1), F32),
            jax.ShapeDtypeStruct((rows_n, quarter, width), BF16),
            jax.ShapeDtypeStruct((rows_n, heads_cols // 2, width), BF16),
            jax.ShapeDtypeStruct((2 * upshare.shape[1], upshare.shape[2]), F32),
            jax.ShapeDtypeStruct((2 * gateshare.shape[1], gateshare.shape[2]), F32),
        ),
        in_specs=[VM] * 14,
        out_specs=(VM,) * 4 + (pl.BlockSpec(memory_space=pl.ANY),) * 2,
        scratch_shapes=[
            pltpu.VMEM((heads, length, HEAD), BF16),
            pltpu.VMEM(((heads + 1) // 2, length, 2 * HEAD), F32),
            pltpu.VMEM((kvs, length, HEAD), F32),
            pltpu.VMEM((kvs, length, HEAD), F32),
            pltpu.VMEM((down.shape[0] + 1,) + down.shape[1:], BF16),
            pltpu.VMEM(weight.shape, BF16),
            pltpu.VMEM((rows_n, heads_cols // 2, width), BF16),
            pltpu.VMEM((rows_n, heads_cols // 2, width), BF16),
            pltpu.VMEM((rows_n - 1,) + upshare.shape[1:], BF16),
            pltpu.VMEM((rows_n - 1,) + gateshare.shape[1:], BF16),
            pltpu.VMEM(upshare.shape[1:], F32),
            pltpu.VMEM(gateshare.shape[1:], F32),
            dma((2,)), dma((2 * cols_n,)), dma((1,)), dma((1,)), dma((rows_n - 1,)), dma((rows_n - 1,)),
        ]
        + [dma((2 * (rows_n - 1),))] * 4
        + [dma((2,))] * 3
        + [
        ],
        compiler_params=params(5),
        cost_estimate=cost(80),
    )(dmid, weight, q, k, v, cosine, sine, segc, segr, attn, down, middle, upshare, gateshare)


def middle_kernel(
    rows_n, cols_n, attn_ref, weight_ref, x_ref, gain_ref, tok_ref, near_ref, next_ref, up_ref, down_ref,
    mid_ref, second_ref, cot_ref, ups_ref, downs_ref, part_ref, recv0_ref, recv1_ref, s0, r0, s1, r1, s2, r2, szc, rzc, *shared,
):
    row, col = lax.axis_index("row"), lax.axis_index("col")
    quarter, features = mid_ref.shape
    width = features // rows_n
    bulks = [SharedGather(rows_n, up_ref, ups_ref, *shared, 0), SharedGather(rows_n, down_ref, downs_ref, *shared, 1)]
    for bulk in bulks:
        bulk.load()
    cot_ref[col] = tok_ref[...]
    take_near(cols_n, cot_ref, near_ref, 1)
    take_near(cols_n, cot_ref, next_ref, 2)
    greet(row_size=rows_n, col_size=cols_n, dp_size=2)
    rest = ColGather(cols_n, cot_ref, szc, rzc, 2)
    rest.event(2)

    @pl.loop(0, rows_n)
    def _(i):
        own = attn_ref[pl.ds(pl.multiple_of(i * quarter, 16), quarter)]
        for j in range(rows_n):
            part_ref[i, :, j * width : (j + 1) * width] = jnp.dot(own, weight_ref[j], preferred_element_type=F32).astype(BF16)

    half = quarter // 2

    def finish(k):
        def act(rows, total):
            here = pl.ds(pl.multiple_of(k * half + rows.start, 16), rows.size)
            own = pl.ds(pl.multiple_of(row * quarter + k * half + rows.start, 16), rows.size)
            squares = jnp.zeros((rows.size, 1), F32)
            for j in range(rows_n):
                columns = slice(j * width, (j + 1) * width)
                value = total[:, columns] + x_ref[j, own].astype(F32)
                mid_ref[here, columns] = value
                squares += jnp.sum(value * value, axis=1, keepdims=True)
            inverse = lax.rsqrt(squares / features + EPSILON)
            second_ref[col, here] = (mid_ref[here] * inverse * gain_ref[...]).astype(BF16)

        return act

    scatters = [
        RowScatter(rows_n, part_ref, recv0_ref, s0, r0, 0),
        RowScatter(rows_n, part_ref, recv1_ref, s1, r1, half),
    ]
    lines = [
        ColGather(cols_n, second_ref, s2, r2, 0, None, pl.ds(k * half, half), k * 2 * (cols_n - 1)) for k in range(2)
    ]
    bits = scatters[0].bits
    scatters[0].start()
    scatters[0].event(0, finish(0))
    scatters[1].start()
    for step in range(1, bits):
        scatters[0].event(step, finish(0))
    lines[0].event(0)
    for step in range(bits - 1):
        scatters[1].event(step, finish(1))
    for bulk in bulks:
        bulk.start()
    scatters[1].event(bits - 1, finish(1))
    lines[1].event(0)
    for step in range(3, cols_n):
        rest.event(step)
    rest.finish()
    lines[0].event(1)
    lines[0].event(2)
    lines[1].event(1)
    for step in range(3, cols_n):
        lines[0].event(step)
        lines[1].event(step - 1)
    for bulk in bulks:
        bulk.event(0)
    lines[1].event(cols_n - 1)
    for step in range(1, bits):
        for bulk in bulks:
            bulk.event(step)
    for bulk in bulks:
        bulk.finish()
    for scatter in scatters:
        scatter.close()
    for line in lines:
        line.finish()


def middle_call(attn, weight, x, gain, tok, near, following, up, down):
    rows_n, cols_n = lax.axis_size("row"), lax.axis_size("col")
    length, features = attn.shape[0], weight.shape[0] * weight.shape[2]
    quarter = length // rows_n
    dma = pltpu.SemaphoreType.DMA
    anywhere = pl.BlockSpec(memory_space=pl.ANY)
    return pl.pallas_call(
        functools.partial(middle_kernel, rows_n, cols_n),
        out_shape=(
            jax.ShapeDtypeStruct((quarter, features), F32),
            jax.ShapeDtypeStruct((cols_n, quarter, features), BF16),
            jax.ShapeDtypeStruct((cols_n, quarter, features), BF16),
            jax.ShapeDtypeStruct((rows_n,) + up.shape, BF16),
            jax.ShapeDtypeStruct((rows_n,) + down.shape, BF16),
        ),
        in_specs=[VM] * 9,
        out_specs=(VM, VM, VM, anywhere, anywhere),
        scratch_shapes=[
            pltpu.VMEM((rows_n, quarter, features), BF16),
            pltpu.VMEM((rows_n - 1, quarter // 2, features), BF16),
            pltpu.VMEM((rows_n - 1, quarter // 2, features), BF16),
        ]
        + [dma((2 * (rows_n - 1),))] * 4
        + [dma((4 * (cols_n - 1),))] * 2
        + [dma((2 * (cols_n - 1),))] * 2
        + SharedGather.scratch(rows_n, 2),
        compiler_params=params(2),
        cost_estimate=cost(130),
    )(attn, weight, x, gain, tok, near, following, up, down)


def settle(stage, out, core, copied, sends, recvs, place):
    rows = pl.ds(pl.multiple_of(core * stage.shape[0], 8), stage.shape[0])
    return (
        pltpu.make_async_copy(stage, out.at[rows], copied.at[place]),
        remote(stage, out.at[rows], sends, recvs, place, {"dp": 1 - core}),
    )


def back_kernel(
    rows_n, cols_n, dgate_ref, dup_ref, gate_ref, up_ref, mid_ref, tok_ref, gain_ref, second_ref, down_ref,
    dmid_ref, grad_ref, gdown_ref, share0_ref, share1_ref,
    w0_ref, w1_ref, part_ref, recv_ref, other_ref, drecv_ref, stage_ref,
    loads, s1, r1, s2, r2, sg, rg, score, rcore, copied, sf, rf, free,
):
    row, col, core = lax.axis_index("row"), lax.axis_index("col"), lax.axis_index("dp")
    quarter, features = mid_ref.shape
    width = features // rows_n
    hidden = dgate_ref.shape[1]
    share = width // 2
    moves = [pltpu.make_async_copy(ref, kept, loads.at[k]) for k, (ref, kept) in enumerate(((gate_ref, w0_ref), (up_ref, w1_ref)))]
    for move in moves:
        move.start()
    greet(row_size=rows_n, col_size=cols_n, dp_size=2)
    for move in moves:
        move.wait()

    def prepare(target):
        rows = pl.ds(pl.multiple_of(target * quarter, 16), quarter)

        @pl.loop(0, rows_n)
        def _(i):
            columns = pl.ds(pl.multiple_of(i * width, 128), width)
            value = lax.dot_general(dgate_ref[rows], w0_ref[i], (((1,), (1,)), ((), ())), preferred_element_type=F32)
            value += lax.dot_general(dup_ref[rows], w1_ref[i], (((1,), (1,)), ((), ())), preferred_element_type=F32)
            part_ref[target, :, columns] = value.astype(BF16)

    tile = min(512, hidden)

    def product(right, kept):
        @pl.loop(0, rows_n)
        def _(i):
            for t in range(hidden // tile):
                columns = slice(t * tile, (t + 1) * tile)
                kept[i, :, columns] = lax.dot_general(
                    second_ref[:, pl.ds(pl.multiple_of(i * width, 128), width)], right[:, columns], (((0,), (0,)), ((), ())),
                    preferred_element_type=F32,
                ).astype(BF16)

    def add(kept):
        chunk = min(64, share)
        chunks = share // chunk

        @pl.loop(0, rows_n * chunks)
        def _(i):
            block, start = lax.div(i, chunks), lax.rem(i, chunks) * chunk
            rows = pl.ds(pl.multiple_of(core * share + start, 16), chunk)
            other = other_ref[block, pl.ds(pl.multiple_of(start, 16), chunk)]
            kept[block, rows] = (kept[block, rows].astype(F32) + other.astype(F32)).astype(BF16)

    half = quarter // 2
    lines = [ColScatter(cols_n, part_ref, recv_ref, s1, r1, k * half, half, k) for k in range(2)]
    gathers = [RowGather(rows_n, dmid_ref, s2, r2, k * half, half, k * 2 * (rows_n - 1)) for k in range(2)]
    scatter = RowScatter(rows_n, down_ref, drecv_ref, sg, rg)
    cross = [
        remote(kept.at[:, pl.ds(pl.multiple_of((1 - core) * share, 16), share)], other_ref, score, rcore, k, {"dp": 1 - core})
        for k, kept in enumerate((w0_ref, w1_ref))
    ]
    keeps = [
        pltpu.make_async_copy(kept.at[:, pl.ds(pl.multiple_of(core * share, 16), share)], out, copied.at[1 + k])
        for k, (kept, out) in enumerate(((w0_ref, share0_ref), (w1_ref, share1_ref)))
    ]

    def finish(rows, total):
        stage_ref[rows] = total

    def norm_back(k):
        @pl.loop(0, half // 32)
        def _(i):
            rows = pl.ds(pl.multiple_of(k * half + i * 32, 32), 32)
            got = lines[k].total(rows)
            middle = mid_ref[rows]
            inverse = lax.rsqrt(jnp.sum(middle * middle, axis=1, keepdims=True) / features + EPSILON)
            weighted = got * gain_ref[...]
            inner = jnp.sum(middle * weighted, axis=1, keepdims=True) / features
            grad_ref[...] += jnp.sum(got * middle * inverse, axis=0, keepdims=True)
            value = tok_ref[rows].astype(F32) + inverse * weighted - middle * (inverse * inverse * inverse * inner)
            dmid_ref[row, rows] = value.astype(BF16)

    grad_ref[...] = jnp.zeros_like(grad_ref)
    scatter.start()
    for time in range(cols_n):
        lines[0].event(time, prepare)
        if time == cols_n - 2:
            for step in range(scatter.bits - 1):
                scatter.event(step, finish)
    lines[1].event(0)
    norm_back(0)
    gathers[0].start()
    scatter.event(scatter.bits - 1, finish)
    results = settle(stage_ref, gdown_ref, core, copied, sf, rf, 0)
    for move in results:
        move.start()
    product(dgate_ref, w0_ref)
    cross[0].start()
    lines[1].event(1)
    gathers[0].event(0)
    product(dup_ref, w1_ref)
    for time in range(2, cols_n - 1):
        lines[1].event(time)
    for step in range(1, gathers[0].bits):
        gathers[0].event(step)
    cross[0].wait()
    add(w0_ref)
    keeps[0].start()
    pl.semaphore_signal(free, inc=1, device_id={"dp": 1 - core}, device_id_type=MESH)
    pl.semaphore_wait(free, 1)
    cross[1].start()
    lines[1].event(cols_n - 1)
    norm_back(1)
    gathers[1].start()
    cross[1].wait()
    add(w1_ref)
    keeps[1].start()
    gathers[1].run()
    gathers[0].finish()
    scatter.close()
    for move in keeps:
        move.wait()
    for move in results:
        move.wait()


def back_call(dgate, dup, gate, up, middle, tok, gain, second, down_share):
    rows_n, cols_n = lax.axis_size("row"), lax.axis_size("col")
    quarter, features = middle.shape
    hidden = dgate.shape[1]
    width = features // rows_n
    dma = pltpu.SemaphoreType.DMA
    anywhere = pl.BlockSpec(memory_space=pl.ANY)
    line = 2 * (rows_n - 1)
    half = (rows_n, width // 2, hidden)
    return pl.pallas_call(
        functools.partial(back_kernel, rows_n, cols_n),
        out_shape=(
            jax.ShapeDtypeStruct((rows_n, quarter, features), BF16),
            jax.ShapeDtypeStruct((1, features), F32),
            jax.ShapeDtypeStruct((2 * down_share.shape[1], width), F32),
            jax.ShapeDtypeStruct(half, BF16),
            jax.ShapeDtypeStruct(half, BF16),
        ),
        in_specs=[VM, VM, anywhere, anywhere, VM, VM, VM, VM, VM],
        out_specs=(VM, VM, anywhere, anywhere, anywhere),
        scratch_shapes=[
            pltpu.VMEM((rows_n, width, hidden), BF16),
            pltpu.VMEM((rows_n, width, hidden), BF16),
            pltpu.VMEM((cols_n, quarter, features), BF16),
            pltpu.VMEM((cols_n + 1, quarter, features), BF16),
            pltpu.VMEM(half, BF16),
            pltpu.VMEM((rows_n - 1,) + down_share.shape[1:], BF16),
            pltpu.VMEM(down_share.shape[1:], F32),
            dma((2,)), dma((4,)), dma((4 * cols_n,)),
            dma((2 * line,)), dma((2 * line,)), dma((line,)), dma((line,)),
            dma((2,)), dma((2,)), dma((3,)), dma((1,)), dma((1,)), pltpu.SemaphoreType.REGULAR,
        ],
        compiler_params=params(3),
        cost_estimate=cost(130),
    )(dgate, dup, gate, up, middle, tok, gain, second, down_share)


def last_kernel(
    size, dqkv_ref, weight_ref, first_ref, outline_ref, blk_ref, inner_ref, act_ref, inv_ref, grad2_ref,
    out_ref, block_ref, inners_ref, gains_ref, gqkv_ref, gout_ref,
    part_ref, recv_ref, qpart_ref, qother_ref, qshare_ref, qline_ref, qrecv_ref, orecv_ref, rgain_ref, pair_ref, pairs_ref,
    s1, r1, sblk, rblk, sinn, rinn, score, rcore, srow, rrow, so, ro, sq, rq, sg, rg, sp, rp, sf, rf,
):
    row, col, core = lax.axis_index("row"), lax.axis_index("col"), lax.axis_index("dp")
    length, width = act_ref.shape
    quarter = length // size
    barrier = pltpu.get_barrier_semaphore()
    peers = [{"row": row ^ mask} for mask in range(1, size)]
    others = [{"col": lax.rem(col + k, size)} for k in range(1, size)]
    others += [{"col": lax.rem(col + k, size), "dp": 1 - core} for k in range(size)]
    for peer in peers + others:
        pl.semaphore_signal(barrier, inc=1, device_id=peer, device_id_type=MESH)
    pl.semaphore_wait(barrier, len(peers) + len(others))

    scatter = RowScatter(size, part_ref, recv_ref, s1, r1)
    inners_ref[row] = inner_ref[...]
    rgain_ref[row] = grad2_ref[row]
    small = []
    for mask in range(1, size):
        small.append(remote(inner_ref, inners_ref.at[row], sinn, rinn, mask - 1, {"row": row ^ mask}))
        small.append(remote(grad2_ref.at[row ^ mask], rgain_ref.at[row], sg, rg, mask - 1, {"row": row ^ mask}))
    for move in small:
        move.start()
    block_ref[pl.ds(pl.multiple_of(row * quarter, 16), quarter)] = blk_ref[row]
    for mask in range(1, size):
        remote(
            blk_ref.at[row ^ mask], block_ref.at[pl.ds(pl.multiple_of(row * quarter, 16), quarter)], sblk, rblk, mask - 1, {"row": row ^ mask}
        ).start()
    oline = ColScatter(size, outline_ref, orecv_ref, so, ro)
    oline.event(0)

    @pl.loop(0, size)
    def _(j):
        columns = pl.ds(pl.multiple_of(j * width, 128), width)
        qpart_ref[j] = lax.dot_general(
            first_ref[:, columns], dqkv_ref[...], (((0,), (0,)), ((), ())), preferred_element_type=F32
        ).astype(BF16)

    cross = swap_halves(qpart_ref, qother_ref, score, rcore)
    cross.start()
    oline.event(1)

    @pl.loop(0, size)
    def _(j):
        part_ref[j] = lax.dot_general(dqkv_ref[...], weight_ref[j], (((1,), (1,)), ((), ())), preferred_element_type=F32).astype(BF16)

    cross.wait()
    add_halves(qpart_ref, qother_ref, qshare_ref)
    row_moves(size, qshare_ref, qline_ref, srow, rrow, 0, True)
    for time in range(2, oline.times):
        oline.event(time)
    share_o = outline_ref.shape[1]
    share_q = qline_ref.shape[1]

    def across(ref, share, which):
        piece = ref.at[pl.ds(pl.multiple_of(core * share, 8), share)]
        return remote(piece, piece, sf, rf, which, {"dp": 1 - core})

    gout_ref[pl.ds(pl.multiple_of(core * share_o, 8), share_o)] = oline.total(slice(None))
    across(gout_ref, share_o, 0).start()

    row_moves(size, qshare_ref, qline_ref, srow, rrow, 0, False)
    scatter.start()
    qline = ColScatter(size, qline_ref, qrecv_ref, sq, rq)
    qline.event(0)
    pair_ref[0] = jnp.zeros_like(pair_ref[0])

    def finish(rows, total):
        out_ref[rows] = total
        pair_ref[0] += jnp.sum(total * act_ref[rows].astype(F32) * inv_ref[rows], axis=0, keepdims=True)

    for step in range(scatter.bits - 1):
        scatter.event(step, finish)
    for time in range(1, min(3, qline.times)):
        qline.event(time)
    scatter.event(scatter.bits - 1, finish)
    scatter.close()
    for move in small:
        move.wait()
    pair_ref[1] = jnp.sum(rgain_ref[...], axis=0)
    own = core * size + col
    pairs_ref[own] = pair_ref[...]
    for k, peer in enumerate(others):
        remote(pair_ref, pairs_ref.at[own], sp, rp, k, peer).start()
    for time in range(3, qline.times):
        qline.event(time)
    gqkv_ref[pl.ds(pl.multiple_of(core * share_q, 8), share_q)] = qline.total(slice(None))
    across(gqkv_ref, share_q, 1).start()
    for k, peer in enumerate(others):
        remote(pair_ref, pairs_ref.at[own], sp, rp, k, peer).wait()
    gains_ref[...] = jnp.sum(pairs_ref[...], axis=0)
    for mask in range(1, size):
        remote(
            blk_ref.at[row ^ mask], block_ref.at[pl.ds(pl.multiple_of(row * quarter, 16), quarter)], sblk, rblk, mask - 1, {"row": row ^ mask}
        ).wait()
    across(gout_ref, share_o, 0).wait()
    across(gqkv_ref, share_q, 1).wait()


def last_call(dqkv, weight, first, outline, blk, inner, activations, inv1, grad2):
    size = lax.axis_size("row")
    length, width = activations.shape
    columns = weight.shape[1]
    heads_cols = 2 * outline.shape[1]
    dma = pltpu.SemaphoreType.DMA
    count = 2 * size - 1
    return pl.pallas_call(
        functools.partial(last_kernel, size),
        out_shape=(
            jax.ShapeDtypeStruct((length, width), F32),
            jax.ShapeDtypeStruct((length, width), BF16),
            jax.ShapeDtypeStruct((size,) + inner.shape, F32),
            jax.ShapeDtypeStruct((2, 1, width), F32),
            jax.ShapeDtypeStruct((width, columns), F32),
            jax.ShapeDtypeStruct((heads_cols, width), F32),
        ),
        in_specs=[VM] * 9,
        out_specs=(VM,) * 6,
        scratch_shapes=[
            pltpu.VMEM((size, length, width), BF16),
            pltpu.VMEM((size - 1, length, width), BF16),
            pltpu.VMEM((size, width, columns), BF16),
            pltpu.VMEM((size, width // 2, columns), BF16),
            pltpu.VMEM((size, width // 2, columns), BF16),
            pltpu.VMEM((size, width // 2, columns), BF16),
            pltpu.VMEM((size + 1, width // 2, columns), BF16),
            pltpu.VMEM((size + 1, heads_cols // 2, width), BF16),
            pltpu.VMEM((size, 1, width), F32),
            pltpu.VMEM((2, 1, width), F32),
            pltpu.VMEM((2 * size, 2, 1, width), F32),
        ]
        + [dma((2 * (size - 1),))] * 2
        + [dma((size - 1,))] * 2
        + [dma((size - 1,))] * 2
        + [dma((1,))] * 2
        + [dma((size - 1,))] * 2
        + [dma((2,)), dma((2 * size,))] * 2
        + [dma((size - 1,))] * 2
        + [dma((count,))] * 2
        + [dma((2,))] * 2,
        compiler_params=params(4),
        cost_estimate=cost(80),
    )(dqkv, weight.reshape(size, width, columns), first, outline, blk, inner, activations, inv1, grad2.reshape(size, 1, width))


def feed_kernel(
    second_ref, cot_ref, gate_ref, up_ref, down_ref, dgate_ref, dup_ref, own_ref, part_ref,
    hidden_ref, keep_ref, send_ref, other_ref, sends, recvs,
):
    core = lax.axis_index("dp")
    step = pl.program_id(0)
    rows_n, tile, width = down_ref.shape
    tokens = second_ref.shape[0]
    tiles = hidden_ref.shape[0]
    block = min(512, tokens)
    mine = tiles // 2

    def place(t):
        return pl.ds(pl.multiple_of(lax.rem(t, mine) * tile, tile), tile)

    def give(t):
        return remote(send_ref.at[:, place(t)], other_ref.at[:, place(t)], sends, recvs, lax.rem(t, mine), {"dp": 1 - core})

    @pl.when(step == 0)
    def _():
        greet(dp_size=2)

    @pl.when(step < tiles)
    def _():
        keep_ref[step] = down_ref[...]

        @pl.loop(0, tokens // block)
        def _(i):
            rows = pl.ds(pl.multiple_of(i * block, block), block)
            gate = jnp.dot(second_ref[rows], gate_ref[...], preferred_element_type=F32)
            up = jnp.dot(second_ref[rows], up_ref[...], preferred_element_type=F32)
            back = jnp.zeros((block, tile), F32)
            for j in range(rows_n):
                back += lax.dot_general(
                    cot_ref[rows, j * width : (j + 1) * width], down_ref[j], (((1,), (1,)), ((), ())), preferred_element_type=F32
                )
            sigma = jax.nn.sigmoid(gate)
            swish = gate * sigma
            hidden_ref[step, rows] = (swish * up).astype(BF16)
            dgate_ref[rows] = (back * up * (sigma * (1.0 + gate * (1.0 - sigma)))).astype(BF16)
            dup_ref[rows] = (back * swish).astype(BF16)

        for j in range(rows_n):
            value = lax.dot_general(
                hidden_ref[step], cot_ref[:, j * width : (j + 1) * width], (((0,), (0,)), ((), ())), preferred_element_type=F32
            ).astype(BF16)

            @pl.when(lax.div(step, mine) == core)
            def _():
                own_ref[j, place(step)] = value

            @pl.when(lax.div(step, mine) != core)
            def _():
                send_ref[j, place(step)] = value

        @pl.when(lax.div(step, mine) != core)
        def _():
            give(step).start()

    @pl.when(step >= tiles)
    def _():
        quarter = part_ref.shape[1]
        rows = pl.ds(pl.multiple_of((step - tiles) * quarter, quarter), quarter)
        for j in range(rows_n):
            total = jnp.zeros((quarter, width), F32)
            for t in range(tiles):
                total += jnp.dot(hidden_ref[t, rows], keep_ref[t, j], preferred_element_type=F32)
            part_ref[0, :, j * width : (j + 1) * width] = total.astype(BF16)

    @pl.when(step == pl.num_programs(0) - 1)
    def _():
        for t in range(mine):
            give(t).wait()
            for j in range(rows_n):
                own_ref[j, place(t)] = (own_ref[j, place(t)].astype(F32) + other_ref[j, place(t)].astype(F32)).astype(BF16)


def feed_call(second, cot, gate, up, down):
    rows_n, hidden, width = down.shape
    cols_n = lax.axis_size("col")
    tokens, features = second.shape
    tile = 256
    tiles = hidden // tile
    half = (rows_n, hidden // 2, width)

    def place(i):
        return jnp.minimum(i, tiles - 1)

    return pl.pallas_call(
        feed_kernel,
        grid=(tiles + cols_n,),
        out_shape=(
            jax.ShapeDtypeStruct((tokens, hidden), BF16),
            jax.ShapeDtypeStruct((tokens, hidden), BF16),
            jax.ShapeDtypeStruct(half, BF16),
            jax.ShapeDtypeStruct((cols_n, tokens // cols_n, features), BF16),
        ),
        in_specs=[
            VM,
            VM,
            pl.BlockSpec((features, tile), lambda i: (0, place(i))),
            pl.BlockSpec((features, tile), lambda i: (0, place(i))),
            pl.BlockSpec((rows_n, tile, width), lambda i: (0, place(i), 0)),
        ],
        out_specs=(
            pl.BlockSpec((tokens, tile), lambda i: (0, place(i))),
            pl.BlockSpec((tokens, tile), lambda i: (0, place(i))),
            VM,
            pl.BlockSpec((1, tokens // cols_n, features), lambda i: (jnp.maximum(i - tiles, 0), 0, 0)),
        ),
        scratch_shapes=[
            pltpu.VMEM((tiles, tokens, tile), BF16),
            pltpu.VMEM((tiles, rows_n, tile, width), BF16),
            pltpu.VMEM(half, BF16),
            pltpu.VMEM(half, BF16),
            pltpu.SemaphoreType.DMA((tiles // 2,)),
            pltpu.SemaphoreType.DMA((tiles // 2,)),
        ],
        compiler_params=params(7),
        cost_estimate=cost(50),
    )(second, cot, gate, up, down)


def rotary_tables(positions):
    exponent = jnp.arange(0, HEAD, 2).astype(F32) / HEAD
    inverse = jnp.power(F32(THETA), -exponent)
    phase = positions[:, None] * inverse[None, :]
    phase = jnp.concatenate([phase] * (2 * 128 // HEAD), axis=1)
    return (jnp.cos(phase), jnp.sin(phase))


def local(
    activations, segments, positions, first_gain, query_weight, key_weight, value_weight, out_weight,
    second_gain, gate_weight, up_weight, down_weight, cotangent,
):
    rows = lax.axis_size("row")
    row, col = lax.axis_index("row"), lax.axis_index("col")
    length, width = activations.shape
    features = rows * width
    query_cols, key_cols = query_weight.shape[1], key_weight.shape[1]
    heads, kvs = query_cols // HEAD, key_cols // HEAD
    hidden_cols = gate_weight.shape[1]
    spare = jnp.zeros((width, -key_cols % 128), BF16)
    key_span = key_cols + spare.shape[1]
    qkv_cols = query_cols + 2 * key_span

    small = jnp.concatenate([segments.astype(F32), positions.astype(F32), first_gain, second_gain]).reshape(-1, 128)
    qkv_weight = jnp.concatenate([query_weight, key_weight, spare, value_weight, spare], axis=1)
    x_blocks, first, inv1, cot_tok, smalls, qkv_all, out_all_w, near = first_call(activations, cotangent, small, qkv_weight, out_weight)
    qkv_all = qkv_all.reshape(features, qkv_cols)
    smalls = smalls.reshape(rows, -1)
    own = lax.dynamic_slice_in_dim(smalls, col, 1, 0)[0]
    segment_own, position_own = own[:length], own[length : 2 * length]
    gain2 = smalls[:, 2 * length + width :].reshape(1, features)

    cosine, sine = rotary_tables(position_own)
    segc, segr = segment_own[:, None], segment_own[None]
    q, k, v, attn, following, gate_all = attend_call(first, qkv_all, cosine, sine, segc, segr, near, gate_weight, heads, kvs)
    middle, second_all, cot_all, up_all, down_all = middle_call(
        attn, out_all_w, x_blocks, gain2, cot_tok, near, following, up_weight, down_weight
    )
    gate_all, up_all = gate_all.reshape(features, hidden_cols), up_all.reshape(features, hidden_cols)
    second_all, cot_all = second_all.reshape(-1, features), cot_all.reshape(-1, features)
    dgate, dup, down_share, down_part = feed_call(second_all, cot_all, gate_all, up_all, down_all)
    dmid_all, gain2_grad, down_grad, gate_share, up_share = back_call(
        dgate, dup, gate_all.reshape(rows, width, hidden_cols), up_all.reshape(rows, width, hidden_cols), middle, cot_tok, gain2, second_all,
        down_share,
    )
    dmid_all = dmid_all.reshape(length, features)

    dqkv, inner1, blk, outline, up_grad, gate_grad = attend_back_call(
        dmid_all, out_all_w, q, k, v, cosine, sine, segc, segr, qkv_cols, attn, down_part, middle, up_share, gate_share
    )
    dfirst, block_out, inner1, gains, qkv_grad, out_grad = last_call(
        dqkv, qkv_all, first, outline, blk, inner1.reshape(-1, 128), activations, inv1, gain2_grad
    )
    inner1 = jnp.sum(inner1, axis=0).reshape(length, 1) / (inv1 * features)
    own_x = activations.astype(F32)
    dmid_own = lax.dynamic_slice_in_dim(dmid_all, row * width, width, 1).astype(F32)
    input_grad = dmid_own + inv1 * first_gain[None] * dfirst - own_x * (inv1 * inv1 * inv1 * inner1)

    return (
        block_out,
        input_grad,
        gains[0, 0],
        qkv_grad[:, :query_cols],
        qkv_grad[:, query_cols : query_cols + key_cols],
        qkv_grad[:, query_cols + key_span : query_cols + key_span + key_cols],
        out_grad,
        gains[1, 0],
        gate_grad,
        up_grad,
        down_grad,
    )


def solution(mesh):
    tokens, block, swapped = P(("dp", "col"), "row"), P("row", "col"), P("col", "row")
    return jax.shard_map(
        local,
        mesh=mesh,
        in_specs=(
            tokens, P(("dp", "row")), P(("dp", "row")), P("row"), block, block, block, swapped,
            P("row"), block, block, swapped, tokens,
        ),
        out_specs=(tokens, tokens, P("row"), block, block, block, swapped, P("row"), block, block, swapped),
        check_vma=False,
    )
```

```python
import functools

import jax
import jax.numpy as jnp
from jax import lax
from jax.experimental import pallas as pl
from jax.experimental.pallas import tpu as pltpu
from jax.sharding import PartitionSpec as P

HEAD = 64
EPSILON = 1e-05
THETA = 500000.0
F32 = jnp.float32
BF16 = jnp.bfloat16


MESH = pl.DeviceIdType.MESH
VMEM_LIMIT = 60 * 1024 * 1024


def greet(row_size=0, col_size=0, dp_size=0):
    barrier = pltpu.get_barrier_semaphore()
    if row_size:
        row = lax.axis_index("row")
        for mask in range(1, row_size):
            pl.semaphore_signal(barrier, inc=1, device_id={"row": row ^ mask}, device_id_type=MESH)
    if col_size:
        col = lax.axis_index("col")

        @pl.when(col > 0)
        def _():
            pl.semaphore_signal(barrier, inc=1, device_id={"col": col - 1}, device_id_type=MESH)

        @pl.when(col < col_size - 1)
        def _():
            pl.semaphore_signal(barrier, inc=1, device_id={"col": col + 1}, device_id_type=MESH)

    if dp_size:
        pl.semaphore_signal(barrier, inc=1, device_id={"dp": 1 - lax.axis_index("dp")}, device_id_type=MESH)
    count = max(row_size - 1, 0) + (1 if dp_size else 0)
    if col_size:
        count = count + jnp.where(col > 0, 1, 0) + jnp.where(col < col_size - 1, 1, 0)
    pl.semaphore_wait(barrier, count)


def remote(src, dst, sends, recvs, place, device):
    return pltpu.make_async_remote_copy(
        src_ref=src, dst_ref=dst, send_sem=sends.at[place], recv_sem=recvs.at[place],
        device_id=device, device_id_type=MESH,
    )


class RowGather:
    def __init__(self, size, ref, sends, recvs, begin=0, count=None, first=0):
        self.size, self.ref, self.sends, self.recvs = size, ref, sends, recvs
        self.bits = size.bit_length() - 1
        self.row = lax.axis_index("row")
        self.begin, self.first = begin, first
        self.half = (count or ref.shape[1]) // 2
        self.all = [self.copies(step) for step in range(self.bits)]

    def rows(self, part):
        return pl.ds(pl.multiple_of(self.begin + part * self.half, 16), self.half)

    def order(self, part):
        return list(range(self.bits)) if part == 0 else list(range(self.bits))[::-1]

    def copies(self, step):
        out = []
        for part in range(2):
            order = self.order(part)
            for item in range(1 << step):
                mask = 0
                for j in range(step):
                    if item >> j & 1:
                        mask |= 1 << order[j]
                piece = self.ref.at[self.row ^ mask, self.rows(part)]
                place = self.first + part * (self.size - 1) + (1 << step) - 1 + item
                out.append(remote(piece, piece, self.sends, self.recvs, place, {"row": self.row ^ (1 << order[step])}))
        return out

    def start(self):
        for step in range(self.bits):
            for part in range(2):
                self.all[step][part << step].start()

    def event(self, step, seen=None):
        for part in range(2):
            order = self.order(part)
            for item in range(1 << step):
                self.all[step][(part << step) + item].wait_recv()
                got = item | 1 << step
                for later in range(step + 1, self.bits):
                    self.all[later][(part << later) + got].start()
                if seen is not None:
                    mask = 0
                    for j in range(step + 1):
                        if got >> j & 1:
                            mask |= 1 << order[j]
                    seen(mask, part)

    def finish(self):
        for step in range(self.bits):
            for copy in self.all[step]:
                copy.wait_send()

    def run(self):
        for step in range(self.bits):
            self.event(step)
        self.finish()


class SharedGather:
    def __init__(self, size, shard, full, copied, sends, recvs, score, rcore, first):
        self.core, self.row = lax.axis_index("dp"), lax.axis_index("row")
        self.size, self.full, self.score, self.rcore, self.first = size, full, score, rcore, first * 2 * (size - 1)
        share = full.shape[1] // 2
        self.own = pltpu.make_async_copy(shard, full.at[self.row], copied.at[first])
        self.gather = RowGather(size, full, sends, recvs, self.core * share, share, self.first)

    def across(self, mask, part):
        piece = self.full.at[self.row ^ mask, self.gather.rows(part)]
        return remote(piece, piece, self.score, self.rcore, self.first + part * (self.size - 1) + mask - 1, {"dp": 1 - self.core})

    def load(self):
        self.own.start()

    def start(self):
        self.own.wait()
        self.gather.start()

    def event(self, step):
        self.gather.event(step, lambda mask, part: self.across(mask, part).start())

    def finish(self):
        self.gather.finish()
        for mask in range(1, self.size):
            for part in range(2):
                self.across(mask, part).wait()

    @staticmethod
    def scratch(size, count):
        dma = pltpu.SemaphoreType.DMA
        return [dma((count,))] + [dma((count * 2 * (size - 1),))] * 4


class RowScatter:
    def __init__(self, size, part_ref, recv_ref, sends, recvs, begin=0):
        self.size, self.part, self.recv = size, part_ref, recv_ref
        self.bits = size.bit_length() - 1
        self.row = lax.axis_index("row")
        half = recv_ref.shape[1] // 2
        self.rows = [pl.ds(part * half, half) for part in range(2)]
        self.own = [pl.ds(pl.multiple_of(begin + part * half, 16), half) for part in range(2)]
        self.plans = []
        for part in range(2):
            order = self.order(part)
            steps, held = [], {}
            for step in range(self.bits):
                bit, rest = 1 << order[step], order[step + 1 :]
                count = 1 << len(rest)
                copies, sums = [], {}
                for item in range(count - 1, -1, -1):
                    mask = sum(1 << other for j, other in enumerate(rest) if item >> j & 1)
                    place = size - 2 * count + item
                    copy = remote(
                        self.spot(part, mask ^ bit, held), recv_ref.at[place, self.rows[part]],
                        sends, recvs, part * (size - 1) + place, {"row": self.row ^ bit},
                    )
                    copies.append((mask, place, held.get(mask), copy))
                    sums[mask] = place
                held = sums
                steps.append(copies)
            self.plans.append(steps)

    def spot(self, part, mask, held):
        if mask in held:
            return self.recv.at[held[mask], self.rows[part]]
        return self.part.at[self.row ^ mask, self.own[part]]

    def order(self, part):
        return list(range(self.bits)) if part == 0 else list(range(self.bits))[::-1]

    def start(self):
        for part in range(2):
            for copies in self.plans[part][0]:
                copies[3].start()

    def event(self, step, finish):
        last = step + 1 == self.bits
        for part in range(2):
            rows, own = self.rows[part], self.own[part]
            for mask, place, before, copy in self.plans[part][step]:
                copy.wait_recv()
                size, begin, start = min(64, rows.size), own.start, rows.start

                @pl.loop(0, rows.size // size)
                def _(i):
                    here = pl.ds(pl.multiple_of(start + i * size, 16), size)
                    if before is None:
                        had = self.part[self.row ^ mask, pl.ds(pl.multiple_of(begin + i * size, 16), size)]
                    else:
                        had = self.recv[before, here]
                    total = had.astype(F32) + self.recv[place, here].astype(F32)
                    if last:
                        finish(here, total)
                    else:
                        self.recv[place, here] = total.astype(BF16)

                if last:
                    continue
                for mask2, _, _, copy2 in self.plans[part][step + 1]:
                    if mask2 ^ 1 << self.order(part)[step + 1] == mask:
                        copy2.start()

    def close(self):
        for part in range(2):
            for step in self.plans[part]:
                for _, _, _, copy in step:
                    copy.wait_send()

    def run(self, finish):
        self.start()
        for step in range(self.bits):
            self.event(step, finish)
        self.close()


class ColGather:
    def __init__(self, size, ref, sends, recvs, begin=0, end=None, rows=None, first=0):
        self.size, self.ref, self.sends, self.recvs = size, ref, sends, recvs
        self.rows, self.first = rows or pl.ds(0, ref.shape[1]), first
        self.begin, self.end = begin, size - 1 if end is None else end
        self.col = lax.axis_index("col")

    def sides(self, step):
        size, col = self.size, self.col
        return (
            (0, lax.rem(col - step + size, size), col >= step, col < size - 1),
            (1, lax.rem(col + step, size), col + step < size, col > 0),
        )

    def copy(self, side, step):
        size, col = self.size, self.col
        piece = self.ref.at[self.sides(step)[side][1], self.rows]
        target = lax.rem(col + (1 if side == 0 else size - 1), size)
        return remote(piece, piece, self.sends, self.recvs, self.first + side * (size - 1) + step, {"col": target})

    def event(self, step, seen=None):
        for side, place, has, goes in self.sides(step):
            if step > self.begin:

                @pl.when(has)
                def _():
                    self.copy(side, step - 1).wait_recv()

            if step < self.end:

                @pl.when(has & goes)
                def _():
                    self.copy(side, step).start()

            if seen is not None and (step or side == 0):

                @pl.when(has)
                def _():
                    seen(place)

    def finish(self):
        for step in range(self.begin, self.end):
            for side, place, has, goes in self.sides(step):

                @pl.when(has & goes)
                def _():
                    self.copy(side, step).wait_send()

    def run(self):
        for step in range(self.begin, self.end + 1):
            self.event(step)
        self.finish()


class ColScatter:
    def __init__(self, size, part, recv, sends, recvs, begin=0, count=None, first=0):
        self.size, self.part, self.recv, self.sends, self.recvs = size, part, recv, sends, recvs
        self.begin, self.count, self.first = begin, count or part.shape[1], first
        self.col = lax.axis_index("col")
        self.times = size

    def copy(self, side, target, source):
        step = 1 if side == 0 else self.size - 1
        rows = pl.ds(self.begin, self.count)
        return pltpu.make_async_remote_copy(
            src_ref=self.recv.at[target + 1 - side, rows] if source is None else source.at[target, rows],
            dst_ref=self.recv.at[target + 1 - side, rows], send_sem=self.sends.at[2 * self.first + side],
            recv_sem=self.recvs.at[(2 * self.first + side) * self.size + target],
            device_id={"col": lax.rem(self.col + step, self.size)}, device_id_type=MESH,
        )

    def event(self, time, prepare=None):
        size, col = self.size, self.col
        for side, first, step in ((0, col == 0, time - col), (1, col == size - 1, time - (size - 1 - col))):
            target = size - 1 - step if side == 0 else step
            valid = (step >= 0) & ((target >= col) if side == 0 else (target <= col))
            place = lax.rem(target + 4 * size, size)

            if prepare is not None:

                @pl.when(valid & ((target != col) | (side == 0)))
                def _():
                    prepare(place)

            @pl.when(valid & jnp.logical_not(first))
            def _():
                self.copy(side, place, self.part).wait_recv()

            @pl.when(valid & jnp.logical_not(first) & (target != col))
            def _():
                chunk = min(64, self.count)

                @pl.loop(0, self.count // chunk)
                def _(i):
                    rows = pl.ds(pl.multiple_of(self.begin + i * chunk, 16), chunk)
                    self.recv[place + 1 - side, rows] = (
                        self.recv[place + 1 - side, rows].astype(F32) + self.part[place, rows].astype(F32)
                    ).astype(BF16)

            @pl.when(valid & (step > 0))
            def _():
                self.copy(side, place, self.part).wait_send()

            @pl.when(valid & (target != col) & first)
            def _():
                self.copy(side, place, self.part).start()

            @pl.when(valid & (target != col) & jnp.logical_not(first))
            def _():
                self.copy(side, place, None).start()

    def total(self, rows):
        got = self.part[self.col, rows].astype(F32)
        got += jnp.where(self.col > 0, self.recv[self.col + 1, rows].astype(F32), 0.0)
        got += jnp.where(self.col < self.size - 1, self.recv[self.col, rows].astype(F32), 0.0)
        return got


VM = pl.BlockSpec(memory_space=pltpu.VMEM)


def params(ident):
    return pltpu.CompilerParams(collective_id=ident, has_side_effects=True, vmem_limit_bytes=VMEM_LIMIT)


def keep_near(size, line, near, step):
    col = lax.axis_index("col")
    for side, place, has in ((0, col - step, col >= step), (1, col + step, col + step < size)):

        @pl.when(has)
        def _():
            near[side] = line[lax.rem(place + size, size)]


def take_near(size, line, near, step):
    col = lax.axis_index("col")
    for side, place, has in ((0, col - step, col >= step), (1, col + step, col + step < size)):

        @pl.when(has)
        def _():
            line[lax.rem(place + size, size)] = near[side]


def first_kernel(
    size, act_ref, cot_ref, small_ref, qkv_ref, out_ref,
    x_ref, first_ref, inv_ref, tok_ref, smalls_ref, qkvs_ref, outs_ref,
    near_ref,
    got_ref, zq_ref, zo_ref, zc_ref, s1, r1, s2, r2, s3, r3, szq, rzq, szo, rzo, srow, rrow, score, rcore, szc, rzc,
):
    row, col, core = lax.axis_index("row"), lax.axis_index("col"), lax.axis_index("dp")
    length, width = act_ref.shape
    quarter = length // size
    small_rows = small_ref.shape[0]
    gain_row = 2 * length // 128
    x_ref[row] = act_ref[...]
    smalls_ref[row] = small_ref[...]
    blocks = ((qkv_ref, zq_ref, qkvs_ref, szq, rzq), (out_ref, zo_ref, outs_ref, szo, rzo))
    for block, line, _, _, _ in blocks:
        share = block.shape[0] // 2
        line[col] = block[pl.ds(pl.multiple_of(core * share, 16), share)]
    greet(row_size=size, col_size=size, dp_size=2)
    gather = RowGather(size, x_ref, s1, r1)
    smalls = [
        remote(small_ref, smalls_ref.at[row], s3, r3, mask - 1, {"row": row ^ mask}) for mask in range(1, size)
    ]
    lines = [ColGather(size, line, sends, recvs) for _, line, _, sends, recvs in blocks]
    lines[0].event(0)
    for move in smalls:
        move.start()
    moves = [
        remote(cot_ref.at[pl.ds((row ^ mask) * quarter, quarter)], got_ref.at[row], s2, r2, mask - 1, {"row": row ^ mask})
        for mask in range(1, size)
    ]
    for move in moves:
        move.start()
    gather.start()
    got_ref[row] = cot_ref[pl.ds(pl.multiple_of(row * quarter, 16), quarter)]

    def half(ref, place):
        share = ref.shape[1] // 2
        return ref.at[place, pl.ds(pl.multiple_of(core * share, 16), share)]

    def hand(which, mask):
        _, line, full, _, _ = blocks[which]
        return remote(line.at[row ^ mask], half(full, row), srow, rrow, which * (size - 1) + mask - 1, {"row": row ^ mask})

    def across(which, mask):
        full = blocks[which][2]
        piece = half(full, row ^ mask)
        return remote(piece, piece, score, rcore, which * size + mask, {"dp": 1 - core})

    def seen(which):
        def act(place):
            _, line, full, _, _ = blocks[which]

            @pl.when(place == row)
            def _():
                share = full.shape[1] // 2
                full[row, pl.ds(pl.multiple_of(core * share, 16), share)] = line[row]
                across(which, 0).start()

            for mask in range(1, size):

                @pl.when(place == row ^ mask)
                def _():
                    hand(which, mask).start()

        return act

    act, act1 = seen(0), seen(1)
    act(col)
    near = ColGather(size, zc_ref, szc, rzc, 0, 1)
    for step in range(1, size - 1):
        lines[0].event(step, act)
    for move in moves:
        move.wait()
    for j in range(size):
        zc_ref[col, :, j * width : (j + 1) * width] = got_ref[j]
    tok_ref[...] = zc_ref[col]
    near.event(0)
    lines[1].event(0)
    lines[0].event(size - 1, act)
    act1(col)
    gather.event(0)
    lines[1].event(1, act1)
    for step in range(1, gather.bits):
        gather.event(step)
    for move in smalls:
        move.wait()

    @pl.loop(0, length // 128)
    def _(i):
        rows = pl.ds(pl.multiple_of(i * 128, 128), 128)
        total = jnp.zeros((128, 1), F32)
        for j in range(size):
            value = x_ref[j, rows].astype(F32)
            total += jnp.sum(value * value, axis=1, keepdims=True)
        inverse = lax.rsqrt(total / (size * width) + EPSILON)
        inv_ref[rows] = inverse
        for j in range(size):
            for k in range(width // 128):
                gain = smalls_ref[j, gain_row + k : gain_row + k + 1]
                value = x_ref[j, rows, k * 128 : (k + 1) * 128].astype(F32)
                first_ref[rows, j * width + k * 128 : j * width + (k + 1) * 128] = (value * inverse * gain).astype(BF16)

    for mask in range(1, size):
        hand(0, mask).wait_recv()
        across(0, mask).start()
    for step in range(2, size):
        lines[1].event(step, act1)
    for mask in range(1, size):
        hand(1, mask).wait_recv()
        across(1, mask).start()
    near.event(1)
    keep_near(size, zc_ref, near_ref, 1)
    near.finish()
    gather.finish()
    for line in lines:
        line.finish()
    for which in range(2):
        for mask in range(1, size):
            hand(which, mask).wait_send()
        for mask in range(size):
            across(which, mask).wait()


def first_call(activations, cotangent, small, qkv_weight, out_weight):
    size = lax.axis_size("row")
    length, width = activations.shape
    quarter = length // size
    qkv_cols, heads_cols = qkv_weight.shape[1], out_weight.shape[0]
    dma = pltpu.SemaphoreType.DMA
    return pl.pallas_call(
        functools.partial(first_kernel, size),
        out_shape=(
            jax.ShapeDtypeStruct((size, length, width), BF16),
            jax.ShapeDtypeStruct((length, size * width), BF16),
            jax.ShapeDtypeStruct((length, 1), F32),
            jax.ShapeDtypeStruct((quarter, size * width), BF16),
            jax.ShapeDtypeStruct((size,) + small.shape, F32),
            jax.ShapeDtypeStruct((size,) + qkv_weight.shape, BF16),
            jax.ShapeDtypeStruct((size,) + out_weight.shape, BF16),
            jax.ShapeDtypeStruct((2, quarter, size * width), BF16),
        ),
        in_specs=[VM] * 5,
        out_specs=(VM,) * 8,
        scratch_shapes=[
            pltpu.VMEM((size, quarter, width), BF16),
            pltpu.VMEM((size, width // 2, qkv_cols), BF16),
            pltpu.VMEM((size, heads_cols // 2, width), BF16),
            pltpu.VMEM((size, quarter, size * width), BF16),
        ]
        + [dma((2 * (size - 1),))] * 2
        + [dma((size - 1,))] * 4
        + [dma((2 * (size - 1),))] * 4
        + [dma((2 * (size - 1),))] * 2
        + [dma((2 * size,))] * 2
        + [dma((2 * (size - 1),))] * 2,
        compiler_params=params(1),
    )(activations, cotangent, small, qkv_weight, out_weight)


def turn(values, low):
    return jnp.where(low, -pltpu.roll(values, 128 - HEAD // 2, 1), pltpu.roll(values, HEAD // 2, 1))


def low_columns(rows):
    return lax.broadcasted_iota(jnp.int32, (rows, 128), 1) % HEAD < HEAD // 2


def masked_scores(query, key, seg_col, seg_row, first_row):
    scores = lax.dot_general(query, key, (((1,), (1,)), ((), ())), preferred_element_type=F32)
    rows = lax.broadcasted_iota(jnp.int32, scores.shape, 0) + first_row
    columns = lax.broadcasted_iota(jnp.int32, scores.shape, 1)
    allowed = (seg_col == seg_row) & (rows >= columns)
    return jnp.where(allowed, scores, -1e30)


def attend_kernel(
    size, first_ref, weight_ref, cos_ref, sin_ref, segc_ref, segr_ref, near_ref, gate_ref,
    q_ref, k_ref, v_ref, o_ref, next_ref, gates_ref, oh_ref, zc_ref, szc, rzc, *shared,
):
    bulk = SharedGather(size, gate_ref, gates_ref, *shared, 0)
    bulk.load()
    take_near(size, zc_ref, near_ref, 1)
    greet(row_size=size, col_size=size, dp_size=2)
    bulk.start()
    line = ColGather(size, zc_ref, szc, rzc, 1, 2)
    line.event(1)
    heads, length, _ = q_ref.shape
    kvs = k_ref.shape[0]
    group = heads // kvs
    query_cols = heads * HEAD
    key_cols = (weight_ref.shape[1] - query_cols) // 2
    block = 256

    @pl.loop(0, length // block)
    def _(i):
        rows = pl.ds(pl.multiple_of(i * block, block), block)
        low = low_columns(block)
        cosine, sine = cos_ref[rows], sin_ref[rows]
        whole = jnp.dot(first_ref[rows], weight_ref[...], preferred_element_type=F32)
        for ref, count, start, factor in ((q_ref, heads, 0, HEAD ** (-0.5)), (k_ref, kvs, query_cols, 1.0)):
            for j in range((count + 1) // 2):
                part = whole[:, start + 128 * j : start + 128 * (j + 1)]
                part = ((part * cosine + turn(part, low) * sine) * factor).astype(BF16)
                for side in range(min(2, count - 2 * j)):
                    ref[2 * j + side, rows] = part[:, side * HEAD : (side + 1) * HEAD]
        for j in range(kvs):
            at = query_cols + key_cols + j * HEAD
            v_ref[j, rows] = whole[:, at : at + HEAD].astype(BF16)

    @pl.loop(0, heads)
    def _(head):
        kv = lax.div(head, group)
        for i in range(length // block):
            rows, extent = slice(i * block, (i + 1) * block), (i + 1) * block
            scores = masked_scores(q_ref[head, rows], k_ref[kv, :extent], segc_ref[rows], segr_ref[:, :extent], i * block)
            top = jnp.max(scores, axis=1, keepdims=True)
            weights = jnp.exp(scores - top)
            total = jnp.sum(weights, axis=1, keepdims=True)
            mixed = jnp.dot(weights.astype(BF16), v_ref[kv, :extent], preferred_element_type=F32)
            oh_ref[head, rows] = (mixed / total).astype(BF16)

    for head in range(heads):
        o_ref[:, head * HEAD : (head + 1) * HEAD] = oh_ref[head]
    for step in range(bulk.gather.bits):
        bulk.event(step)
    line.event(2)
    keep_near(size, zc_ref, next_ref, 2)
    line.finish()
    bulk.finish()


def attend_call(first, weight, cosine, sine, segc, segr, near, gate, heads, kvs):
    size = lax.axis_size("row")
    length = first.shape[0]
    dma = pltpu.SemaphoreType.DMA
    return pl.pallas_call(
        functools.partial(attend_kernel, size),
        out_shape=(
            jax.ShapeDtypeStruct((heads, length, HEAD), BF16),
            jax.ShapeDtypeStruct((kvs, length, HEAD), BF16),
            jax.ShapeDtypeStruct((kvs, length, HEAD), BF16),
            jax.ShapeDtypeStruct((length, heads * HEAD), BF16),
            jax.ShapeDtypeStruct(near.shape, BF16),
            jax.ShapeDtypeStruct((size,) + gate.shape, BF16),
        ),
        in_specs=[VM] * 8,
        out_specs=(VM,) * 5 + (pl.BlockSpec(memory_space=pl.ANY),),
        scratch_shapes=[
            pltpu.VMEM((heads, length, HEAD), BF16),
            pltpu.VMEM((size,) + near.shape[1:], BF16),
            dma((2 * (size - 1),)), dma((2 * (size - 1),)),
        ]
        + SharedGather.scratch(size, 1),
        compiler_params=params(6),
        cost_estimate=cost(45),
    )(first, weight, cosine, sine, segc, segr, near, gate)


class swap_halves:
    def __init__(self, part, other, sends, recvs):
        core = lax.axis_index("dp")
        share = part.shape[1] // 2
        self.move = remote(
            part.at[:, pl.ds(pl.multiple_of((1 - core) * share, 16), share)], other, sends, recvs, 0, {"dp": 1 - core}
        )

    def start(self):
        self.move.start()

    def wait(self):
        self.move.wait()


def add_halves(part, other, share):
    rows = pl.ds(pl.multiple_of(lax.axis_index("dp") * share.shape[1], 16), share.shape[1])
    for j in range(part.shape[0]):
        share[j] = (part[j, rows].astype(F32) + other[j].astype(F32)).astype(BF16)


def row_moves(size, source, target, sends, recvs, first, begin):
    row = lax.axis_index("row")
    if begin:
        target[row] = source[row]
    for mask in range(1, size):
        move = remote(source.at[row ^ mask], target.at[row], sends, recvs, first + mask - 1, {"row": row ^ mask})
        if begin:
            move.start()
        else:
            move.wait()


def cost(micros):
    return pl.CostEstimate(flops=int(micros * 1e9), bytes_accessed=1 << 20, transcendentals=0)


def attend_back_kernel(
    dmid_ref, weight_ref, q_ref, k_ref, v_ref, cos_ref, sin_ref, segc_ref, segr_ref,
    attn_ref, down_ref, mid_ref, upshare_ref, gateshare_ref,
    dqkv_ref, inner_ref, blk_ref, line_ref, gup_ref, ggate_ref, do_ref, dq_ref, dk_ref, dv_ref,
    recv_ref, part_ref, other_ref, share_ref, urecv_ref, drecv_ref, ustage_ref, dstage_ref,
    s1, r1, score, rcore, srow, rrow, su, ru, sd, rd, copied, sf, rf,
):
    row, core = lax.axis_index("row"), lax.axis_index("dp")
    cols_n = down_ref.shape[0]
    heads, length, _ = q_ref.shape
    kvs = k_ref.shape[0]
    group = heads // kvs
    query_cols = heads * HEAD
    key_cols = (dqkv_ref.shape[1] - query_cols) // 2
    block = 256
    parts, _, width = weight_ref.shape
    greet(row_size=parts, col_size=cols_n, dp_size=2)
    line = ColScatter(cols_n, down_ref, recv_ref, s1, r1)
    line.event(0)
    sums = [
        (RowScatter(parts, upshare_ref, urecv_ref, su, ru), ustage_ref, gup_ref),
        (RowScatter(parts, gateshare_ref, drecv_ref, sd, rd), dstage_ref, ggate_ref),
    ]
    for scatter, _, _ in sums:
        scatter.start()
    for j in range(parts):
        part_ref[j] = lax.dot_general(
            attn_ref[...], dmid_ref[:, j * width : (j + 1) * width], (((0,), (0,)), ((), ())), preferred_element_type=F32
        ).astype(BF16)
    cross = swap_halves(part_ref, other_ref, score, rcore)
    cross.start()
    dk_ref[...] = jnp.zeros_like(dk_ref)
    dv_ref[...] = jnp.zeros_like(dv_ref)
    inner_ref[...] = jnp.zeros_like(inner_ref)

    @pl.loop(0, length // block)
    def _(i):
        rows = pl.ds(pl.multiple_of(i * block, block), block)
        total = jnp.zeros((block, query_cols), F32)
        for j in range(parts):
            total += lax.dot_general(
                dmid_ref[rows, j * width : (j + 1) * width], weight_ref[j], (((1,), (1,)), ((), ())), preferred_element_type=F32
            )
        for head in range(heads):
            do_ref[head, rows] = total[:, head * HEAD : (head + 1) * HEAD].astype(BF16)

    @pl.loop(0, heads)
    def _(head):
        @pl.when(head == min(1, heads - 1))
        def _():
            cross.wait()
            add_halves(part_ref, other_ref, share_ref)
            row_moves(parts, share_ref, line_ref, srow, rrow, 0, True)

        @pl.when(head == max(heads // 2 - 1, 0))
        def _():
            line.event(1)

        kv = lax.div(head, group)
        for i in range(length // block):
            rows, extent = slice(i * block, (i + 1) * block), (i + 1) * block
            query, keys, grads = q_ref[head, rows], k_ref[kv, :extent], do_ref[head, rows]
            scores = masked_scores(query, keys, segc_ref[rows], segr_ref[:, :extent], i * block)
            top = jnp.max(scores, axis=1, keepdims=True)
            weights = jnp.exp(scores - top)
            weights = weights * (1.0 / jnp.sum(weights, axis=1, keepdims=True))
            back = lax.dot_general(grads, v_ref[kv, :extent], (((1,), (1,)), ((), ())), preferred_element_type=F32)
            dv_ref[kv, :extent] += lax.dot_general(
                weights.astype(BF16), grads, (((0,), (0,)), ((), ())), preferred_element_type=F32
            )
            ds = (weights * (back - jnp.sum(weights * back, axis=1, keepdims=True))).astype(BF16)
            dq = jnp.dot(ds, keys, preferred_element_type=F32)
            inner_ref[rows] += jnp.sum(dq * query.astype(F32), axis=1, keepdims=True)
            for side in range(2):

                @pl.when(lax.rem(head, 2) == side)
                def _():
                    dq_ref[lax.div(head, 2), rows, side * HEAD : (side + 1) * HEAD] = dq

            dk_ref[kv, :extent] += lax.dot_general(ds, query, (((0,), (0,)), ((), ())), preferred_element_type=F32)

    @pl.loop(0, length // block)
    def _(i):
        rows = pl.ds(pl.multiple_of(i * block, block), block)
        low = low_columns(block)
        cosine, sine = cos_ref[rows], sin_ref[rows]
        for ref, count, start, factor in ((dq_ref, heads, 0, HEAD ** (-0.5)), (dk_ref, kvs, query_cols, 1.0), (dv_ref, kvs, query_cols + key_cols, None)):
            for j in range((count + 1) // 2):
                if ref is dq_ref:
                    part = dq_ref[j, rows]
                else:
                    sides = [ref[2 * j + side, rows] if 2 * j + side < count else jnp.zeros((block, HEAD), F32) for side in range(2)]
                    part = jnp.concatenate(sides, axis=1)
                if factor is not None:
                    part = (part * cosine - turn(part * sine, low)) * factor
                dqkv_ref[rows, start + 128 * j : start + 128 * (j + 1)] = part.astype(BF16)
        more = jnp.zeros((block, 1), F32)
        for kv in range(kvs):
            more += jnp.sum(dk_ref[kv, rows] * k_ref[kv, rows].astype(F32) + dv_ref[kv, rows] * v_ref[kv, rows].astype(F32), axis=1, keepdims=True)
        inner_ref[rows] += more

    def finish(stage):
        def act(rows, total):
            stage[rows] = total

        return act

    if cols_n > 2:
        line.event(2)
    bits = sums[0][0].bits
    for step in range(bits - 1):
        for scatter, stage, _ in sums:
            scatter.event(step, finish(stage))
    for time in range(3, line.times):
        line.event(time)
    results = []
    for k, (scatter, stage, out) in enumerate(sums):
        scatter.event(bits - 1, finish(stage))
        moves = settle(stage, out, core, copied, sf, rf, k)
        for move in moves:
            move.start()
        results += moves
        scatter.close()

    @pl.loop(0, mid_ref.shape[0] // 64)
    def _(i):
        rows = pl.ds(pl.multiple_of(i * 64, 16), 64)
        total = mid_ref[rows] + line.total(rows)
        for j in range(parts):
            blk_ref[j, rows] = total[:, j * width : (j + 1) * width].astype(BF16)

    row_moves(parts, share_ref, line_ref, srow, rrow, 0, False)
    for move in results:
        move.wait()


def attend_back_call(dmid, weight, q, k, v, cosine, sine, segc, segr, columns, attn, down, middle, upshare, gateshare):
    rows_n, cols_n = lax.axis_size("row"), lax.axis_size("col")
    _, heads_cols, width = weight.shape
    quarter = middle.shape[0]
    dma = pltpu.SemaphoreType.DMA
    heads, length, _ = q.shape
    kvs = k.shape[0]
    return pl.pallas_call(
        attend_back_kernel,
        out_shape=(
            jax.ShapeDtypeStruct((length, columns), BF16),
            jax.ShapeDtypeStruct((length, 1), F32),
            jax.ShapeDtypeStruct((rows_n, quarter, width), BF16),
            jax.ShapeDtypeStruct((rows_n, heads_cols // 2, width), BF16),
            jax.ShapeDtypeStruct((2 * upshare.shape[1], upshare.shape[2]), F32),
            jax.ShapeDtypeStruct((2 * gateshare.shape[1], gateshare.shape[2]), F32),
        ),
        in_specs=[VM] * 14,
        out_specs=(VM,) * 4 + (pl.BlockSpec(memory_space=pl.ANY),) * 2,
        scratch_shapes=[
            pltpu.VMEM((heads, length, HEAD), BF16),
            pltpu.VMEM(((heads + 1) // 2, length, 2 * HEAD), F32),
            pltpu.VMEM((kvs, length, HEAD), F32),
            pltpu.VMEM((kvs, length, HEAD), F32),
            pltpu.VMEM((down.shape[0] + 1,) + down.shape[1:], BF16),
            pltpu.VMEM(weight.shape, BF16),
            pltpu.VMEM((rows_n, heads_cols // 2, width), BF16),
            pltpu.VMEM((rows_n, heads_cols // 2, width), BF16),
            pltpu.VMEM((rows_n - 1,) + upshare.shape[1:], BF16),
            pltpu.VMEM((rows_n - 1,) + gateshare.shape[1:], BF16),
            pltpu.VMEM(upshare.shape[1:], F32),
            pltpu.VMEM(gateshare.shape[1:], F32),
            dma((2,)), dma((2 * cols_n,)), dma((1,)), dma((1,)), dma((rows_n - 1,)), dma((rows_n - 1,)),
        ]
        + [dma((2 * (rows_n - 1),))] * 4
        + [dma((2,))] * 3
        + [
        ],
        compiler_params=params(5),
        cost_estimate=cost(80),
    )(dmid, weight, q, k, v, cosine, sine, segc, segr, attn, down, middle, upshare, gateshare)


def middle_kernel(
    rows_n, cols_n, attn_ref, weight_ref, x_ref, gain_ref, tok_ref, near_ref, next_ref, up_ref, down_ref,
    mid_ref, second_ref, cot_ref, ups_ref, downs_ref, part_ref, recv0_ref, recv1_ref, s0, r0, s1, r1, s2, r2, szc, rzc, *shared,
):
    row, col = lax.axis_index("row"), lax.axis_index("col")
    quarter, features = mid_ref.shape
    width = features // rows_n
    bulks = [SharedGather(rows_n, up_ref, ups_ref, *shared, 0), SharedGather(rows_n, down_ref, downs_ref, *shared, 1)]
    for bulk in bulks:
        bulk.load()
    cot_ref[col] = tok_ref[...]
    take_near(cols_n, cot_ref, near_ref, 1)
    take_near(cols_n, cot_ref, next_ref, 2)
    greet(row_size=rows_n, col_size=cols_n, dp_size=2)
    rest = ColGather(cols_n, cot_ref, szc, rzc, 2)
    rest.event(2)

    @pl.loop(0, rows_n)
    def _(i):
        own = attn_ref[pl.ds(pl.multiple_of(i * quarter, 16), quarter)]
        for j in range(rows_n):
            part_ref[i, :, j * width : (j + 1) * width] = jnp.dot(own, weight_ref[j], preferred_element_type=F32).astype(BF16)

    half = quarter // 2

    def finish(k):
        def act(rows, total):
            here = pl.ds(pl.multiple_of(k * half + rows.start, 16), rows.size)
            own = pl.ds(pl.multiple_of(row * quarter + k * half + rows.start, 16), rows.size)
            squares = jnp.zeros((rows.size, 1), F32)
            for j in range(rows_n):
                columns = slice(j * width, (j + 1) * width)
                value = total[:, columns] + x_ref[j, own].astype(F32)
                mid_ref[here, columns] = value
                squares += jnp.sum(value * value, axis=1, keepdims=True)
            inverse = lax.rsqrt(squares / features + EPSILON)
            second_ref[col, here] = (mid_ref[here] * inverse * gain_ref[...]).astype(BF16)

        return act

    scatters = [
        RowScatter(rows_n, part_ref, recv0_ref, s0, r0, 0),
        RowScatter(rows_n, part_ref, recv1_ref, s1, r1, half),
    ]
    lines = [
        ColGather(cols_n, second_ref, s2, r2, 0, None, pl.ds(k * half, half), k * 2 * (cols_n - 1)) for k in range(2)
    ]
    bits = scatters[0].bits
    scatters[0].start()
    scatters[0].event(0, finish(0))
    scatters[1].start()
    for step in range(1, bits):
        scatters[0].event(step, finish(0))
    lines[0].event(0)
    for step in range(bits - 1):
        scatters[1].event(step, finish(1))
    for bulk in bulks:
        bulk.start()
    scatters[1].event(bits - 1, finish(1))
    lines[1].event(0)
    for step in range(3, cols_n):
        rest.event(step)
    rest.finish()
    lines[0].event(1)
    lines[0].event(2)
    lines[1].event(1)
    for step in range(3, cols_n):
        lines[0].event(step)
        lines[1].event(step - 1)
    for bulk in bulks:
        bulk.event(0)
    lines[1].event(cols_n - 1)
    for step in range(1, bits):
        for bulk in bulks:
            bulk.event(step)
    for bulk in bulks:
        bulk.finish()
    for scatter in scatters:
        scatter.close()
    for line in lines:
        line.finish()


def middle_call(attn, weight, x, gain, tok, near, following, up, down):
    rows_n, cols_n = lax.axis_size("row"), lax.axis_size("col")
    length, features = attn.shape[0], weight.shape[0] * weight.shape[2]
    quarter = length // rows_n
    dma = pltpu.SemaphoreType.DMA
    anywhere = pl.BlockSpec(memory_space=pl.ANY)
    return pl.pallas_call(
        functools.partial(middle_kernel, rows_n, cols_n),
        out_shape=(
            jax.ShapeDtypeStruct((quarter, features), F32),
            jax.ShapeDtypeStruct((cols_n, quarter, features), BF16),
            jax.ShapeDtypeStruct((cols_n, quarter, features), BF16),
            jax.ShapeDtypeStruct((rows_n,) + up.shape, BF16),
            jax.ShapeDtypeStruct((rows_n,) + down.shape, BF16),
        ),
        in_specs=[VM] * 9,
        out_specs=(VM, VM, VM, anywhere, anywhere),
        scratch_shapes=[
            pltpu.VMEM((rows_n, quarter, features), BF16),
            pltpu.VMEM((rows_n - 1, quarter // 2, features), BF16),
            pltpu.VMEM((rows_n - 1, quarter // 2, features), BF16),
        ]
        + [dma((2 * (rows_n - 1),))] * 4
        + [dma((4 * (cols_n - 1),))] * 2
        + [dma((2 * (cols_n - 1),))] * 2
        + SharedGather.scratch(rows_n, 2),
        compiler_params=params(2),
        cost_estimate=cost(130),
    )(attn, weight, x, gain, tok, near, following, up, down)


def settle(stage, out, core, copied, sends, recvs, place):
    rows = pl.ds(pl.multiple_of(core * stage.shape[0], 8), stage.shape[0])
    return (
        pltpu.make_async_copy(stage, out.at[rows], copied.at[place]),
        remote(stage, out.at[rows], sends, recvs, place, {"dp": 1 - core}),
    )


def back_kernel(
    rows_n, cols_n, dgate_ref, dup_ref, gate_ref, up_ref, mid_ref, tok_ref, gain_ref, second_ref, down_ref,
    dmid_ref, grad_ref, gdown_ref, share0_ref, share1_ref,
    w0_ref, w1_ref, part_ref, recv_ref, other_ref, drecv_ref, stage_ref,
    loads, s1, r1, s2, r2, sg, rg, score, rcore, copied, sf, rf, free,
):
    row, col, core = lax.axis_index("row"), lax.axis_index("col"), lax.axis_index("dp")
    quarter, features = mid_ref.shape
    width = features // rows_n
    hidden = dgate_ref.shape[1]
    share = width // 2
    moves = [pltpu.make_async_copy(ref, kept, loads.at[k]) for k, (ref, kept) in enumerate(((gate_ref, w0_ref), (up_ref, w1_ref)))]
    for move in moves:
        move.start()
    greet(row_size=rows_n, col_size=cols_n, dp_size=2)
    for move in moves:
        move.wait()

    def prepare(target):
        rows = pl.ds(pl.multiple_of(target * quarter, 16), quarter)

        @pl.loop(0, rows_n)
        def _(i):
            columns = pl.ds(pl.multiple_of(i * width, 128), width)
            value = lax.dot_general(dgate_ref[rows], w0_ref[i], (((1,), (1,)), ((), ())), preferred_element_type=F32)
            value += lax.dot_general(dup_ref[rows], w1_ref[i], (((1,), (1,)), ((), ())), preferred_element_type=F32)
            part_ref[target, :, columns] = value.astype(BF16)

    tile = min(512, hidden)

    def product(right, kept):
        @pl.loop(0, rows_n)
        def _(i):
            for t in range(hidden // tile):
                columns = slice(t * tile, (t + 1) * tile)
                kept[i, :, columns] = lax.dot_general(
                    second_ref[:, pl.ds(pl.multiple_of(i * width, 128), width)], right[:, columns], (((0,), (0,)), ((), ())),
                    preferred_element_type=F32,
                ).astype(BF16)

    def add(kept):
        chunk = min(64, share)
        chunks = share // chunk

        @pl.loop(0, rows_n * chunks)
        def _(i):
            block, start = lax.div(i, chunks), lax.rem(i, chunks) * chunk
            rows = pl.ds(pl.multiple_of(core * share + start, 16), chunk)
            other = other_ref[block, pl.ds(pl.multiple_of(start, 16), chunk)]
            kept[block, rows] = (kept[block, rows].astype(F32) + other.astype(F32)).astype(BF16)

    half = quarter // 2
    lines = [ColScatter(cols_n, part_ref, recv_ref, s1, r1, k * half, half, k) for k in range(2)]
    gathers = [RowGather(rows_n, dmid_ref, s2, r2, k * half, half, k * 2 * (rows_n - 1)) for k in range(2)]
    scatter = RowScatter(rows_n, down_ref, drecv_ref, sg, rg)
    cross = [
        remote(kept.at[:, pl.ds(pl.multiple_of((1 - core) * share, 16), share)], other_ref, score, rcore, k, {"dp": 1 - core})
        for k, kept in enumerate((w0_ref, w1_ref))
    ]
    keeps = [
        pltpu.make_async_copy(kept.at[:, pl.ds(pl.multiple_of(core * share, 16), share)], out, copied.at[1 + k])
        for k, (kept, out) in enumerate(((w0_ref, share0_ref), (w1_ref, share1_ref)))
    ]

    def finish(rows, total):
        stage_ref[rows] = total

    def norm_back(k):
        @pl.loop(0, half // 32)
        def _(i):
            rows = pl.ds(pl.multiple_of(k * half + i * 32, 32), 32)
            got = lines[k].total(rows)
            middle = mid_ref[rows]
            inverse = lax.rsqrt(jnp.sum(middle * middle, axis=1, keepdims=True) / features + EPSILON)
            weighted = got * gain_ref[...]
            inner = jnp.sum(middle * weighted, axis=1, keepdims=True) / features
            grad_ref[...] += jnp.sum(got * middle * inverse, axis=0, keepdims=True)
            value = tok_ref[rows].astype(F32) + inverse * weighted - middle * (inverse * inverse * inverse * inner)
            dmid_ref[row, rows] = value.astype(BF16)

    grad_ref[...] = jnp.zeros_like(grad_ref)
    scatter.start()
    for time in range(cols_n):
        lines[0].event(time, prepare)
        if time == cols_n - 2:
            for step in range(scatter.bits - 1):
                scatter.event(step, finish)
    lines[1].event(0)
    norm_back(0)
    gathers[0].start()
    scatter.event(scatter.bits - 1, finish)
    results = settle(stage_ref, gdown_ref, core, copied, sf, rf, 0)
    for move in results:
        move.start()
    product(dgate_ref, w0_ref)
    cross[0].start()
    lines[1].event(1)
    gathers[0].event(0)
    product(dup_ref, w1_ref)
    for time in range(2, cols_n - 1):
        lines[1].event(time)
    for step in range(1, gathers[0].bits):
        gathers[0].event(step)
    cross[0].wait()
    add(w0_ref)
    keeps[0].start()
    pl.semaphore_signal(free, inc=1, device_id={"dp": 1 - core}, device_id_type=MESH)
    pl.semaphore_wait(free, 1)
    cross[1].start()
    lines[1].event(cols_n - 1)
    norm_back(1)
    gathers[1].start()
    cross[1].wait()
    add(w1_ref)
    keeps[1].start()
    gathers[1].run()
    gathers[0].finish()
    scatter.close()
    for move in keeps:
        move.wait()
    for move in results:
        move.wait()


def back_call(dgate, dup, gate, up, middle, tok, gain, second, down_share):
    rows_n, cols_n = lax.axis_size("row"), lax.axis_size("col")
    quarter, features = middle.shape
    hidden = dgate.shape[1]
    width = features // rows_n
    dma = pltpu.SemaphoreType.DMA
    anywhere = pl.BlockSpec(memory_space=pl.ANY)
    line = 2 * (rows_n - 1)
    half = (rows_n, width // 2, hidden)
    return pl.pallas_call(
        functools.partial(back_kernel, rows_n, cols_n),
        out_shape=(
            jax.ShapeDtypeStruct((rows_n, quarter, features), BF16),
            jax.ShapeDtypeStruct((1, features), F32),
            jax.ShapeDtypeStruct((2 * down_share.shape[1], width), F32),
            jax.ShapeDtypeStruct(half, BF16),
            jax.ShapeDtypeStruct(half, BF16),
        ),
        in_specs=[VM, VM, anywhere, anywhere, VM, VM, VM, VM, VM],
        out_specs=(VM, VM, anywhere, anywhere, anywhere),
        scratch_shapes=[
            pltpu.VMEM((rows_n, width, hidden), BF16),
            pltpu.VMEM((rows_n, width, hidden), BF16),
            pltpu.VMEM((cols_n, quarter, features), BF16),
            pltpu.VMEM((cols_n + 1, quarter, features), BF16),
            pltpu.VMEM(half, BF16),
            pltpu.VMEM((rows_n - 1,) + down_share.shape[1:], BF16),
            pltpu.VMEM(down_share.shape[1:], F32),
            dma((2,)), dma((4,)), dma((4 * cols_n,)),
            dma((2 * line,)), dma((2 * line,)), dma((line,)), dma((line,)),
            dma((2,)), dma((2,)), dma((3,)), dma((1,)), dma((1,)), pltpu.SemaphoreType.REGULAR,
        ],
        compiler_params=params(3),
        cost_estimate=cost(130),
    )(dgate, dup, gate, up, middle, tok, gain, second, down_share)


def last_kernel(
    size, dqkv_ref, weight_ref, first_ref, outline_ref, blk_ref, inner_ref, act_ref, inv_ref, grad2_ref,
    out_ref, block_ref, inners_ref, gains_ref, gqkv_ref, gout_ref,
    part_ref, recv_ref, qpart_ref, qother_ref, qshare_ref, qline_ref, qrecv_ref, orecv_ref, rgain_ref, pair_ref, pairs_ref,
    s1, r1, sblk, rblk, sinn, rinn, score, rcore, srow, rrow, so, ro, sq, rq, sg, rg, sp, rp, sf, rf,
):
    row, col, core = lax.axis_index("row"), lax.axis_index("col"), lax.axis_index("dp")
    length, width = act_ref.shape
    quarter = length // size
    barrier = pltpu.get_barrier_semaphore()
    peers = [{"row": row ^ mask} for mask in range(1, size)]
    others = [{"col": lax.rem(col + k, size)} for k in range(1, size)]
    others += [{"col": lax.rem(col + k, size), "dp": 1 - core} for k in range(size)]
    for peer in peers + others:
        pl.semaphore_signal(barrier, inc=1, device_id=peer, device_id_type=MESH)
    pl.semaphore_wait(barrier, len(peers) + len(others))

    scatter = RowScatter(size, part_ref, recv_ref, s1, r1)
    inners_ref[row] = inner_ref[...]
    rgain_ref[row] = grad2_ref[row]
    small = []
    for mask in range(1, size):
        small.append(remote(inner_ref, inners_ref.at[row], sinn, rinn, mask - 1, {"row": row ^ mask}))
        small.append(remote(grad2_ref.at[row ^ mask], rgain_ref.at[row], sg, rg, mask - 1, {"row": row ^ mask}))
    for move in small:
        move.start()
    block_ref[pl.ds(pl.multiple_of(row * quarter, 16), quarter)] = blk_ref[row]
    for mask in range(1, size):
        remote(
            blk_ref.at[row ^ mask], block_ref.at[pl.ds(pl.multiple_of(row * quarter, 16), quarter)], sblk, rblk, mask - 1, {"row": row ^ mask}
        ).start()
    oline = ColScatter(size, outline_ref, orecv_ref, so, ro)
    oline.event(0)

    @pl.loop(0, size)
    def _(j):
        columns = pl.ds(pl.multiple_of(j * width, 128), width)
        qpart_ref[j] = lax.dot_general(
            first_ref[:, columns], dqkv_ref[...], (((0,), (0,)), ((), ())), preferred_element_type=F32
        ).astype(BF16)

    cross = swap_halves(qpart_ref, qother_ref, score, rcore)
    cross.start()
    oline.event(1)

    @pl.loop(0, size)
    def _(j):
        part_ref[j] = lax.dot_general(dqkv_ref[...], weight_ref[j], (((1,), (1,)), ((), ())), preferred_element_type=F32).astype(BF16)

    cross.wait()
    add_halves(qpart_ref, qother_ref, qshare_ref)
    row_moves(size, qshare_ref, qline_ref, srow, rrow, 0, True)
    for time in range(2, oline.times):
        oline.event(time)
    share_o = outline_ref.shape[1]
    share_q = qline_ref.shape[1]

    def across(ref, share, which):
        piece = ref.at[pl.ds(pl.multiple_of(core * share, 8), share)]
        return remote(piece, piece, sf, rf, which, {"dp": 1 - core})

    gout_ref[pl.ds(pl.multiple_of(core * share_o, 8), share_o)] = oline.total(slice(None))
    across(gout_ref, share_o, 0).start()

    row_moves(size, qshare_ref, qline_ref, srow, rrow, 0, False)
    scatter.start()
    qline = ColScatter(size, qline_ref, qrecv_ref, sq, rq)
    qline.event(0)
    pair_ref[0] = jnp.zeros_like(pair_ref[0])

    def finish(rows, total):
        out_ref[rows] = total
        pair_ref[0] += jnp.sum(total * act_ref[rows].astype(F32) * inv_ref[rows], axis=0, keepdims=True)

    for step in range(scatter.bits - 1):
        scatter.event(step, finish)
    for time in range(1, min(3, qline.times)):
        qline.event(time)
    scatter.event(scatter.bits - 1, finish)
    scatter.close()
    for move in small:
        move.wait()
    pair_ref[1] = jnp.sum(rgain_ref[...], axis=0)
    own = core * size + col
    pairs_ref[own] = pair_ref[...]
    for k, peer in enumerate(others):
        remote(pair_ref, pairs_ref.at[own], sp, rp, k, peer).start()
    for time in range(3, qline.times):
        qline.event(time)
    gqkv_ref[pl.ds(pl.multiple_of(core * share_q, 8), share_q)] = qline.total(slice(None))
    across(gqkv_ref, share_q, 1).start()
    for k, peer in enumerate(others):
        remote(pair_ref, pairs_ref.at[own], sp, rp, k, peer).wait()
    gains_ref[...] = jnp.sum(pairs_ref[...], axis=0)
    for mask in range(1, size):
        remote(
            blk_ref.at[row ^ mask], block_ref.at[pl.ds(pl.multiple_of(row * quarter, 16), quarter)], sblk, rblk, mask - 1, {"row": row ^ mask}
        ).wait()
    across(gout_ref, share_o, 0).wait()
    across(gqkv_ref, share_q, 1).wait()


def last_call(dqkv, weight, first, outline, blk, inner, activations, inv1, grad2):
    size = lax.axis_size("row")
    length, width = activations.shape
    columns = weight.shape[1]
    heads_cols = 2 * outline.shape[1]
    dma = pltpu.SemaphoreType.DMA
    count = 2 * size - 1
    return pl.pallas_call(
        functools.partial(last_kernel, size),
        out_shape=(
            jax.ShapeDtypeStruct((length, width), F32),
            jax.ShapeDtypeStruct((length, width), BF16),
            jax.ShapeDtypeStruct((size,) + inner.shape, F32),
            jax.ShapeDtypeStruct((2, 1, width), F32),
            jax.ShapeDtypeStruct((width, columns), F32),
            jax.ShapeDtypeStruct((heads_cols, width), F32),
        ),
        in_specs=[VM] * 9,
        out_specs=(VM,) * 6,
        scratch_shapes=[
            pltpu.VMEM((size, length, width), BF16),
            pltpu.VMEM((size - 1, length, width), BF16),
            pltpu.VMEM((size, width, columns), BF16),
            pltpu.VMEM((size, width // 2, columns), BF16),
            pltpu.VMEM((size, width // 2, columns), BF16),
            pltpu.VMEM((size, width // 2, columns), BF16),
            pltpu.VMEM((size + 1, width // 2, columns), BF16),
            pltpu.VMEM((size + 1, heads_cols // 2, width), BF16),
            pltpu.VMEM((size, 1, width), F32),
            pltpu.VMEM((2, 1, width), F32),
            pltpu.VMEM((2 * size, 2, 1, width), F32),
        ]
        + [dma((2 * (size - 1),))] * 2
        + [dma((size - 1,))] * 2
        + [dma((size - 1,))] * 2
        + [dma((1,))] * 2
        + [dma((size - 1,))] * 2
        + [dma((2,)), dma((2 * size,))] * 2
        + [dma((size - 1,))] * 2
        + [dma((count,))] * 2
        + [dma((2,))] * 2,
        compiler_params=params(4),
        cost_estimate=cost(80),
    )(dqkv, weight.reshape(size, width, columns), first, outline, blk, inner, activations, inv1, grad2.reshape(size, 1, width))


def feed_kernel(
    second_ref, cot_ref, gate_ref, up_ref, down_ref, dgate_ref, dup_ref, own_ref, part_ref,
    hidden_ref, keep_ref, send_ref, other_ref, sends, recvs,
):
    core = lax.axis_index("dp")
    step = pl.program_id(0)
    rows_n, tile, width = down_ref.shape
    tokens = second_ref.shape[0]
    tiles = hidden_ref.shape[0]
    block = min(256, tokens)
    mine = tiles // 2

    def place(t):
        return pl.ds(pl.multiple_of(lax.rem(t, mine) * tile, tile), tile)

    def give(t):
        return remote(send_ref.at[:, place(t)], other_ref.at[:, place(t)], sends, recvs, lax.rem(t, mine), {"dp": 1 - core})

    @pl.when(step == 0)
    def _():
        greet(dp_size=2)

    @pl.when(step < tiles)
    def _():
        keep_ref[step] = down_ref[...]

        @pl.loop(0, tokens // block)
        def _(i):
            rows = pl.ds(pl.multiple_of(i * block, block), block)
            gate = jnp.dot(second_ref[rows], gate_ref[...], preferred_element_type=F32)
            up = jnp.dot(second_ref[rows], up_ref[...], preferred_element_type=F32)
            back = jnp.zeros((block, tile), F32)
            for j in range(rows_n):
                back += lax.dot_general(
                    cot_ref[rows, j * width : (j + 1) * width], down_ref[j], (((1,), (1,)), ((), ())), preferred_element_type=F32
                )
            sigma = jax.nn.sigmoid(gate)
            swish = gate * sigma
            hidden_ref[step, rows] = (swish * up).astype(BF16)
            dgate_ref[rows] = (back * up * (sigma * (1.0 + gate * (1.0 - sigma)))).astype(BF16)
            dup_ref[rows] = (back * swish).astype(BF16)

        for j in range(rows_n):
            value = lax.dot_general(
                hidden_ref[step], cot_ref[:, j * width : (j + 1) * width], (((0,), (0,)), ((), ())), preferred_element_type=F32
            ).astype(BF16)

            @pl.when(lax.div(step, mine) == core)
            def _():
                own_ref[j, place(step)] = value

            @pl.when(lax.div(step, mine) != core)
            def _():
                send_ref[j, place(step)] = value

        @pl.when(lax.div(step, mine) != core)
        def _():
            give(step).start()

    @pl.when(step >= tiles)
    def _():
        quarter = part_ref.shape[1]
        rows = pl.ds(pl.multiple_of((step - tiles) * quarter, quarter), quarter)
        for j in range(rows_n):
            total = jnp.zeros((quarter, width), F32)
            for t in range(tiles):
                total += jnp.dot(hidden_ref[t, rows], keep_ref[t, j], preferred_element_type=F32)
            part_ref[0, :, j * width : (j + 1) * width] = total.astype(BF16)

    @pl.when(step == pl.num_programs(0) - 1)
    def _():
        for t in range(mine):
            give(t).wait()
            for j in range(rows_n):
                own_ref[j, place(t)] = (own_ref[j, place(t)].astype(F32) + other_ref[j, place(t)].astype(F32)).astype(BF16)


def feed_call(second, cot, gate, up, down):
    rows_n, hidden, width = down.shape
    cols_n = lax.axis_size("col")
    tokens, features = second.shape
    tile = 256
    tiles = hidden // tile
    half = (rows_n, hidden // 2, width)

    def place(i):
        return jnp.minimum(i, tiles - 1)

    return pl.pallas_call(
        feed_kernel,
        grid=(tiles + cols_n,),
        out_shape=(
            jax.ShapeDtypeStruct((tokens, hidden), BF16),
            jax.ShapeDtypeStruct((tokens, hidden), BF16),
            jax.ShapeDtypeStruct(half, BF16),
            jax.ShapeDtypeStruct((cols_n, tokens // cols_n, features), BF16),
        ),
        in_specs=[
            VM,
            VM,
            pl.BlockSpec((features, tile), lambda i: (0, place(i))),
            pl.BlockSpec((features, tile), lambda i: (0, place(i))),
            pl.BlockSpec((rows_n, tile, width), lambda i: (0, place(i), 0)),
        ],
        out_specs=(
            pl.BlockSpec((tokens, tile), lambda i: (0, place(i))),
            pl.BlockSpec((tokens, tile), lambda i: (0, place(i))),
            VM,
            pl.BlockSpec((1, tokens // cols_n, features), lambda i: (jnp.maximum(i - tiles, 0), 0, 0)),
        ),
        scratch_shapes=[
            pltpu.VMEM((tiles, tokens, tile), BF16),
            pltpu.VMEM((tiles, rows_n, tile, width), BF16),
            pltpu.VMEM(half, BF16),
            pltpu.VMEM(half, BF16),
            pltpu.SemaphoreType.DMA((tiles // 2,)),
            pltpu.SemaphoreType.DMA((tiles // 2,)),
        ],
        compiler_params=params(7),
        cost_estimate=cost(50),
    )(second, cot, gate, up, down)


def rotary_tables(positions):
    exponent = jnp.arange(0, HEAD, 2).astype(F32) / HEAD
    inverse = jnp.power(F32(THETA), -exponent)
    phase = positions[:, None] * inverse[None, :]
    phase = jnp.concatenate([phase] * (2 * 128 // HEAD), axis=1)
    return (jnp.cos(phase), jnp.sin(phase))


def local(
    activations, segments, positions, first_gain, query_weight, key_weight, value_weight, out_weight,
    second_gain, gate_weight, up_weight, down_weight, cotangent,
):
    rows = lax.axis_size("row")
    row, col = lax.axis_index("row"), lax.axis_index("col")
    length, width = activations.shape
    features = rows * width
    query_cols, key_cols = query_weight.shape[1], key_weight.shape[1]
    heads, kvs = query_cols // HEAD, key_cols // HEAD
    hidden_cols = gate_weight.shape[1]
    spare = jnp.zeros((width, -key_cols % 128), BF16)
    key_span = key_cols + spare.shape[1]
    qkv_cols = query_cols + 2 * key_span

    small = jnp.concatenate([segments.astype(F32), positions.astype(F32), first_gain, second_gain]).reshape(-1, 128)
    qkv_weight = jnp.concatenate([query_weight, key_weight, spare, value_weight, spare], axis=1)
    x_blocks, first, inv1, cot_tok, smalls, qkv_all, out_all_w, near = first_call(activations, cotangent, small, qkv_weight, out_weight)
    qkv_all = qkv_all.reshape(features, qkv_cols)
    smalls = smalls.reshape(rows, -1)
    own = lax.dynamic_slice_in_dim(smalls, col, 1, 0)[0]
    segment_own, position_own = own[:length], own[length : 2 * length]
    gain2 = smalls[:, 2 * length + width :].reshape(1, features)

    cosine, sine = rotary_tables(position_own)
    segc, segr = segment_own[:, None], segment_own[None]
    q, k, v, attn, following, gate_all = attend_call(first, qkv_all, cosine, sine, segc, segr, near, gate_weight, heads, kvs)
    middle, second_all, cot_all, up_all, down_all = middle_call(
        attn, out_all_w, x_blocks, gain2, cot_tok, near, following, up_weight, down_weight
    )
    gate_all, up_all = gate_all.reshape(features, hidden_cols), up_all.reshape(features, hidden_cols)
    second_all, cot_all = second_all.reshape(-1, features), cot_all.reshape(-1, features)
    dgate, dup, down_share, down_part = feed_call(second_all, cot_all, gate_all, up_all, down_all)
    dmid_all, gain2_grad, down_grad, gate_share, up_share = back_call(
        dgate, dup, gate_all.reshape(rows, width, hidden_cols), up_all.reshape(rows, width, hidden_cols), middle, cot_tok, gain2, second_all,
        down_share,
    )
    dmid_all = dmid_all.reshape(length, features)

    dqkv, inner1, blk, outline, up_grad, gate_grad = attend_back_call(
        dmid_all, out_all_w, q, k, v, cosine, sine, segc, segr, qkv_cols, attn, down_part, middle, up_share, gate_share
    )
    dfirst, block_out, inner1, gains, qkv_grad, out_grad = last_call(
        dqkv, qkv_all, first, outline, blk, inner1.reshape(-1, 128), activations, inv1, gain2_grad
    )
    inner1 = jnp.sum(inner1, axis=0).reshape(length, 1) / (inv1 * features)
    own_x = activations.astype(F32)
    dmid_own = lax.dynamic_slice_in_dim(dmid_all, row * width, width, 1).astype(F32)
    input_grad = dmid_own + inv1 * first_gain[None] * dfirst - own_x * (inv1 * inv1 * inv1 * inner1)

    return (
        block_out,
        input_grad,
        gains[0, 0],
        qkv_grad[:, :query_cols],
        qkv_grad[:, query_cols : query_cols + key_cols],
        qkv_grad[:, query_cols + key_span : query_cols + key_span + key_cols],
        out_grad,
        gains[1, 0],
        gate_grad,
        up_grad,
        down_grad,
    )


def solution(mesh):
    tokens, block, swapped = P(("dp", "col"), "row"), P("row", "col"), P("col", "row")
    return jax.shard_map(
        local,
        mesh=mesh,
        in_specs=(
            tokens, P(("dp", "row")), P(("dp", "row")), P("row"), block, block, block, swapped,
            P("row"), block, block, swapped, tokens,
        ),
        out_specs=(tokens, tokens, P("row"), block, block, block, swapped, P("row"), block, block, swapped),
        check_vma=False,
    )
```

```python
import functools

import jax
import jax.numpy as jnp
from jax import lax
from jax.experimental import pallas as pl
from jax.experimental.pallas import tpu as pltpu
from jax.sharding import PartitionSpec as P

HEAD = 64
EPSILON = 1e-05
THETA = 500000.0
F32 = jnp.float32
BF16 = jnp.bfloat16


MESH = pl.DeviceIdType.MESH
VMEM_LIMIT = 60 * 1024 * 1024


def greet(row_size=0, col_size=0, dp_size=0):
    barrier = pltpu.get_barrier_semaphore()
    if row_size:
        row = lax.axis_index("row")
        for mask in range(1, row_size):
            pl.semaphore_signal(barrier, inc=1, device_id={"row": row ^ mask}, device_id_type=MESH)
    if col_size:
        col = lax.axis_index("col")

        @pl.when(col > 0)
        def _():
            pl.semaphore_signal(barrier, inc=1, device_id={"col": col - 1}, device_id_type=MESH)

        @pl.when(col < col_size - 1)
        def _():
            pl.semaphore_signal(barrier, inc=1, device_id={"col": col + 1}, device_id_type=MESH)

    if dp_size:
        pl.semaphore_signal(barrier, inc=1, device_id={"dp": 1 - lax.axis_index("dp")}, device_id_type=MESH)
    count = max(row_size - 1, 0) + (1 if dp_size else 0)
    if col_size:
        count = count + jnp.where(col > 0, 1, 0) + jnp.where(col < col_size - 1, 1, 0)
    pl.semaphore_wait(barrier, count)


def remote(src, dst, sends, recvs, place, device):
    return pltpu.make_async_remote_copy(
        src_ref=src, dst_ref=dst, send_sem=sends.at[place], recv_sem=recvs.at[place],
        device_id=device, device_id_type=MESH,
    )


class RowGather:
    def __init__(self, size, ref, sends, recvs, begin=0, count=None, first=0):
        self.size, self.ref, self.sends, self.recvs = size, ref, sends, recvs
        self.bits = size.bit_length() - 1
        self.row = lax.axis_index("row")
        self.begin, self.first = begin, first
        self.half = (count or ref.shape[1]) // 2
        self.all = [self.copies(step) for step in range(self.bits)]

    def rows(self, part):
        return pl.ds(pl.multiple_of(self.begin + part * self.half, 16), self.half)

    def order(self, part):
        return list(range(self.bits)) if part == 0 else list(range(self.bits))[::-1]

    def copies(self, step):
        out = []
        for part in range(2):
            order = self.order(part)
            for item in range(1 << step):
                mask = 0
                for j in range(step):
                    if item >> j & 1:
                        mask |= 1 << order[j]
                piece = self.ref.at[self.row ^ mask, self.rows(part)]
                place = self.first + part * (self.size - 1) + (1 << step) - 1 + item
                out.append(remote(piece, piece, self.sends, self.recvs, place, {"row": self.row ^ (1 << order[step])}))
        return out

    def start(self):
        for step in range(self.bits):
            for part in range(2):
                self.all[step][part << step].start()

    def event(self, step, seen=None):
        for part in range(2):
            order = self.order(part)
            for item in range(1 << step):
                self.all[step][(part << step) + item].wait_recv()
                got = item | 1 << step
                for later in range(step + 1, self.bits):
                    self.all[later][(part << later) + got].start()
                if seen is not None:
                    mask = 0
                    for j in range(step + 1):
                        if got >> j & 1:
                            mask |= 1 << order[j]
                    seen(mask, part)

    def finish(self):
        for step in range(self.bits):
            for copy in self.all[step]:
                copy.wait_send()

    def run(self):
        for step in range(self.bits):
            self.event(step)
        self.finish()


class SharedGather:
    def __init__(self, size, shard, full, copied, sends, recvs, score, rcore, first):
        self.core, self.row = lax.axis_index("dp"), lax.axis_index("row")
        self.size, self.full, self.score, self.rcore, self.first = size, full, score, rcore, first * 2 * (size - 1)
        share = full.shape[1] // 2
        self.own = pltpu.make_async_copy(shard, full.at[self.row], copied.at[first])
        self.gather = RowGather(size, full, sends, recvs, self.core * share, share, self.first)

    def across(self, mask, part):
        piece = self.full.at[self.row ^ mask, self.gather.rows(part)]
        return remote(piece, piece, self.score, self.rcore, self.first + part * (self.size - 1) + mask - 1, {"dp": 1 - self.core})

    def load(self):
        self.own.start()

    def start(self):
        self.own.wait()
        self.gather.start()

    def event(self, step):
        self.gather.event(step, lambda mask, part: self.across(mask, part).start())

    def finish(self):
        self.gather.finish()
        for mask in range(1, self.size):
            for part in range(2):
                self.across(mask, part).wait()

    @staticmethod
    def scratch(size, count):
        dma = pltpu.SemaphoreType.DMA
        return [dma((count,))] + [dma((count * 2 * (size - 1),))] * 4


class RowScatter:
    def __init__(self, size, part_ref, recv_ref, sends, recvs, begin=0):
        self.size, self.part, self.recv = size, part_ref, recv_ref
        self.bits = size.bit_length() - 1
        self.row = lax.axis_index("row")
        half = recv_ref.shape[1] // 2
        self.rows = [pl.ds(part * half, half) for part in range(2)]
        self.own = [pl.ds(pl.multiple_of(begin + part * half, 16), half) for part in range(2)]
        self.plans = []
        for part in range(2):
            order = self.order(part)
            steps, held = [], {}
            for step in range(self.bits):
                bit, rest = 1 << order[step], order[step + 1 :]
                count = 1 << len(rest)
                copies, sums = [], {}
                for item in range(count - 1, -1, -1):
                    mask = sum(1 << other for j, other in enumerate(rest) if item >> j & 1)
                    place = size - 2 * count + item
                    copy = remote(
                        self.spot(part, mask ^ bit, held), recv_ref.at[place, self.rows[part]],
                        sends, recvs, part * (size - 1) + place, {"row": self.row ^ bit},
                    )
                    copies.append((mask, place, held.get(mask), copy))
                    sums[mask] = place
                held = sums
                steps.append(copies)
            self.plans.append(steps)

    def spot(self, part, mask, held):
        if mask in held:
            return self.recv.at[held[mask], self.rows[part]]
        return self.part.at[self.row ^ mask, self.own[part]]

    def order(self, part):
        return list(range(self.bits)) if part == 0 else list(range(self.bits))[::-1]

    def start(self):
        for part in range(2):
            for copies in self.plans[part][0]:
                copies[3].start()

    def event(self, step, finish):
        last = step + 1 == self.bits
        for part in range(2):
            rows, own = self.rows[part], self.own[part]
            for mask, place, before, copy in self.plans[part][step]:
                copy.wait_recv()
                size, begin, start = min(64, rows.size), own.start, rows.start

                @pl.loop(0, rows.size // size)
                def _(i):
                    here = pl.ds(pl.multiple_of(start + i * size, 16), size)
                    if before is None:
                        had = self.part[self.row ^ mask, pl.ds(pl.multiple_of(begin + i * size, 16), size)]
                    else:
                        had = self.recv[before, here]
                    total = had.astype(F32) + self.recv[place, here].astype(F32)
                    if last:
                        finish(here, total)
                    else:
                        self.recv[place, here] = total.astype(BF16)

                if last:
                    continue
                for mask2, _, _, copy2 in self.plans[part][step + 1]:
                    if mask2 ^ 1 << self.order(part)[step + 1] == mask:
                        copy2.start()

    def close(self):
        for part in range(2):
            for step in self.plans[part]:
                for _, _, _, copy in step:
                    copy.wait_send()

    def run(self, finish):
        self.start()
        for step in range(self.bits):
            self.event(step, finish)
        self.close()


class ColGather:
    def __init__(self, size, ref, sends, recvs, begin=0, end=None, rows=None, first=0):
        self.size, self.ref, self.sends, self.recvs = size, ref, sends, recvs
        self.rows, self.first = rows or pl.ds(0, ref.shape[1]), first
        self.begin, self.end = begin, size - 1 if end is None else end
        self.col = lax.axis_index("col")

    def sides(self, step):
        size, col = self.size, self.col
        return (
            (0, lax.rem(col - step + size, size), col >= step, col < size - 1),
            (1, lax.rem(col + step, size), col + step < size, col > 0),
        )

    def copy(self, side, step):
        size, col = self.size, self.col
        piece = self.ref.at[self.sides(step)[side][1], self.rows]
        target = lax.rem(col + (1 if side == 0 else size - 1), size)
        return remote(piece, piece, self.sends, self.recvs, self.first + side * (size - 1) + step, {"col": target})

    def event(self, step, seen=None):
        for side, place, has, goes in self.sides(step):
            if step > self.begin:

                @pl.when(has)
                def _():
                    self.copy(side, step - 1).wait_recv()

            if step < self.end:

                @pl.when(has & goes)
                def _():
                    self.copy(side, step).start()

            if seen is not None and (step or side == 0):

                @pl.when(has)
                def _():
                    seen(place)

    def finish(self):
        for step in range(self.begin, self.end):
            for side, place, has, goes in self.sides(step):

                @pl.when(has & goes)
                def _():
                    self.copy(side, step).wait_send()

    def run(self):
        for step in range(self.begin, self.end + 1):
            self.event(step)
        self.finish()


class ColScatter:
    def __init__(self, size, part, recv, sends, recvs, begin=0, count=None, first=0):
        self.size, self.part, self.recv, self.sends, self.recvs = size, part, recv, sends, recvs
        self.begin, self.count, self.first = begin, count or part.shape[1], first
        self.col = lax.axis_index("col")
        self.times = size

    def copy(self, side, target, source):
        step = 1 if side == 0 else self.size - 1
        rows = pl.ds(self.begin, self.count)
        return pltpu.make_async_remote_copy(
            src_ref=self.recv.at[target + 1 - side, rows] if source is None else source.at[target, rows],
            dst_ref=self.recv.at[target + 1 - side, rows], send_sem=self.sends.at[2 * self.first + side],
            recv_sem=self.recvs.at[(2 * self.first + side) * self.size + target],
            device_id={"col": lax.rem(self.col + step, self.size)}, device_id_type=MESH,
        )

    def event(self, time, prepare=None):
        size, col = self.size, self.col
        for side, first, step in ((0, col == 0, time - col), (1, col == size - 1, time - (size - 1 - col))):
            target = size - 1 - step if side == 0 else step
            valid = (step >= 0) & ((target >= col) if side == 0 else (target <= col))
            place = lax.rem(target + 4 * size, size)

            if prepare is not None:

                @pl.when(valid & ((target != col) | (side == 0)))
                def _():
                    prepare(place)

            @pl.when(valid & jnp.logical_not(first))
            def _():
                self.copy(side, place, self.part).wait_recv()

            @pl.when(valid & jnp.logical_not(first) & (target != col))
            def _():
                chunk = min(64, self.count)

                @pl.loop(0, self.count // chunk)
                def _(i):
                    rows = pl.ds(pl.multiple_of(self.begin + i * chunk, 16), chunk)
                    self.recv[place + 1 - side, rows] = (
                        self.recv[place + 1 - side, rows].astype(F32) + self.part[place, rows].astype(F32)
                    ).astype(BF16)

            @pl.when(valid & (step > 0))
            def _():
                self.copy(side, place, self.part).wait_send()

            @pl.when(valid & (target != col) & first)
            def _():
                self.copy(side, place, self.part).start()

            @pl.when(valid & (target != col) & jnp.logical_not(first))
            def _():
                self.copy(side, place, None).start()

    def total(self, rows):
        got = self.part[self.col, rows].astype(F32)
        got += jnp.where(self.col > 0, self.recv[self.col + 1, rows].astype(F32), 0.0)
        got += jnp.where(self.col < self.size - 1, self.recv[self.col, rows].astype(F32), 0.0)
        return got


VM = pl.BlockSpec(memory_space=pltpu.VMEM)


def params(ident):
    return pltpu.CompilerParams(collective_id=ident, has_side_effects=True, vmem_limit_bytes=VMEM_LIMIT)


def keep_near(size, line, near, step):
    col = lax.axis_index("col")
    for side, place, has in ((0, col - step, col >= step), (1, col + step, col + step < size)):

        @pl.when(has)
        def _():
            near[side] = line[lax.rem(place + size, size)]


def take_near(size, line, near, step):
    col = lax.axis_index("col")
    for side, place, has in ((0, col - step, col >= step), (1, col + step, col + step < size)):

        @pl.when(has)
        def _():
            line[lax.rem(place + size, size)] = near[side]


def first_kernel(
    size, act_ref, cot_ref, small_ref, qkv_ref, out_ref,
    x_ref, first_ref, inv_ref, tok_ref, smalls_ref, qkvs_ref, outs_ref,
    near_ref,
    got_ref, zq_ref, zo_ref, zc_ref, s1, r1, s2, r2, s3, r3, szq, rzq, szo, rzo, srow, rrow, score, rcore, szc, rzc,
):
    row, col, core = lax.axis_index("row"), lax.axis_index("col"), lax.axis_index("dp")
    length, width = act_ref.shape
    quarter = length // size
    small_rows = small_ref.shape[0]
    gain_row = 2 * length // 128
    x_ref[row] = act_ref[...]
    smalls_ref[row] = small_ref[...]
    blocks = ((qkv_ref, zq_ref, qkvs_ref, szq, rzq), (out_ref, zo_ref, outs_ref, szo, rzo))
    for block, line, _, _, _ in blocks:
        share = block.shape[0] // 2
        line[col] = block[pl.ds(pl.multiple_of(core * share, 16), share)]
    greet(row_size=size, col_size=size, dp_size=2)
    gather = RowGather(size, x_ref, s1, r1)
    smalls = [
        remote(small_ref, smalls_ref.at[row], s3, r3, mask - 1, {"row": row ^ mask}) for mask in range(1, size)
    ]
    lines = [ColGather(size, line, sends, recvs) for _, line, _, sends, recvs in blocks]
    lines[0].event(0)
    for move in smalls:
        move.start()
    moves = [
        remote(cot_ref.at[pl.ds((row ^ mask) * quarter, quarter)], got_ref.at[row], s2, r2, mask - 1, {"row": row ^ mask})
        for mask in range(1, size)
    ]
    for move in moves:
        move.start()
    gather.start()
    got_ref[row] = cot_ref[pl.ds(pl.multiple_of(row * quarter, 16), quarter)]

    def half(ref, place):
        share = ref.shape[1] // 2
        return ref.at[place, pl.ds(pl.multiple_of(core * share, 16), share)]

    def hand(which, mask):
        _, line, full, _, _ = blocks[which]
        return remote(line.at[row ^ mask], half(full, row), srow, rrow, which * (size - 1) + mask - 1, {"row": row ^ mask})

    def across(which, mask):
        full = blocks[which][2]
        piece = half(full, row ^ mask)
        return remote(piece, piece, score, rcore, which * size + mask, {"dp": 1 - core})

    def seen(which):
        def act(place):
            _, line, full, _, _ = blocks[which]

            @pl.when(place == row)
            def _():
                share = full.shape[1] // 2
                full[row, pl.ds(pl.multiple_of(core * share, 16), share)] = line[row]
                across(which, 0).start()

            for mask in range(1, size):

                @pl.when(place == row ^ mask)
                def _():
                    hand(which, mask).start()

        return act

    act, act1 = seen(0), seen(1)
    act(col)
    near = ColGather(size, zc_ref, szc, rzc, 0, 1)
    for step in range(1, size - 1):
        lines[0].event(step, act)
    for move in moves:
        move.wait()
    for j in range(size):
        zc_ref[col, :, j * width : (j + 1) * width] = got_ref[j]
    tok_ref[...] = zc_ref[col]
    near.event(0)
    lines[1].event(0)
    lines[0].event(size - 1, act)
    act1(col)
    gather.event(0)
    lines[1].event(1, act1)
    for step in range(1, gather.bits):
        gather.event(step)
    for move in smalls:
        move.wait()

    @pl.loop(0, length // 128)
    def _(i):
        rows = pl.ds(pl.multiple_of(i * 128, 128), 128)
        total = jnp.zeros((128, 1), F32)
        for j in range(size):
            value = x_ref[j, rows].astype(F32)
            total += jnp.sum(value * value, axis=1, keepdims=True)
        inverse = lax.rsqrt(total / (size * width) + EPSILON)
        inv_ref[rows] = inverse
        for j in range(size):
            for k in range(width // 128):
                gain = smalls_ref[j, gain_row + k : gain_row + k + 1]
                value = x_ref[j, rows, k * 128 : (k + 1) * 128].astype(F32)
                first_ref[rows, j * width + k * 128 : j * width + (k + 1) * 128] = (value * inverse * gain).astype(BF16)

    for mask in range(1, size):
        hand(0, mask).wait_recv()
        across(0, mask).start()
    for step in range(2, size):
        lines[1].event(step, act1)
    for mask in range(1, size):
        hand(1, mask).wait_recv()
        across(1, mask).start()
    near.event(1)
    keep_near(size, zc_ref, near_ref, 1)
    near.finish()
    gather.finish()
    for line in lines:
        line.finish()
    for which in range(2):
        for mask in range(1, size):
            hand(which, mask).wait_send()
        for mask in range(size):
            across(which, mask).wait()


def first_call(activations, cotangent, small, qkv_weight, out_weight):
    size = lax.axis_size("row")
    length, width = activations.shape
    quarter = length // size
    qkv_cols, heads_cols = qkv_weight.shape[1], out_weight.shape[0]
    dma = pltpu.SemaphoreType.DMA
    return pl.pallas_call(
        functools.partial(first_kernel, size),
        out_shape=(
            jax.ShapeDtypeStruct((size, length, width), BF16),
            jax.ShapeDtypeStruct((length, size * width), BF16),
            jax.ShapeDtypeStruct((length, 1), F32),
            jax.ShapeDtypeStruct((quarter, size * width), BF16),
            jax.ShapeDtypeStruct((size,) + small.shape, F32),
            jax.ShapeDtypeStruct((size,) + qkv_weight.shape, BF16),
            jax.ShapeDtypeStruct((size,) + out_weight.shape, BF16),
            jax.ShapeDtypeStruct((2, quarter, size * width), BF16),
        ),
        in_specs=[VM] * 5,
        out_specs=(VM,) * 8,
        scratch_shapes=[
            pltpu.VMEM((size, quarter, width), BF16),
            pltpu.VMEM((size, width // 2, qkv_cols), BF16),
            pltpu.VMEM((size, heads_cols // 2, width), BF16),
            pltpu.VMEM((size, quarter, size * width), BF16),
        ]
        + [dma((2 * (size - 1),))] * 2
        + [dma((size - 1,))] * 4
        + [dma((2 * (size - 1),))] * 4
        + [dma((2 * (size - 1),))] * 2
        + [dma((2 * size,))] * 2
        + [dma((2 * (size - 1),))] * 2,
        compiler_params=params(1),
    )(activations, cotangent, small, qkv_weight, out_weight)


def turn(values, low):
    return jnp.where(low, -pltpu.roll(values, 128 - HEAD // 2, 1), pltpu.roll(values, HEAD // 2, 1))


def low_columns(rows):
    return lax.broadcasted_iota(jnp.int32, (rows, 128), 1) % HEAD < HEAD // 2


def masked_scores(query, key, seg_col, seg_row, first_row):
    scores = lax.dot_general(query, key, (((1,), (1,)), ((), ())), preferred_element_type=F32)
    rows = lax.broadcasted_iota(jnp.int32, scores.shape, 0) + first_row
    columns = lax.broadcasted_iota(jnp.int32, scores.shape, 1)
    allowed = (seg_col == seg_row) & (rows >= columns)
    return jnp.where(allowed, scores, -1e30)


def attend_kernel(
    size, first_ref, weight_ref, cos_ref, sin_ref, segc_ref, segr_ref, near_ref, gate_ref,
    q_ref, k_ref, v_ref, o_ref, next_ref, gates_ref, oh_ref, zc_ref, szc, rzc, *shared,
):
    bulk = SharedGather(size, gate_ref, gates_ref, *shared, 0)
    bulk.load()
    take_near(size, zc_ref, near_ref, 1)
    greet(row_size=size, col_size=size, dp_size=2)
    bulk.start()
    line = ColGather(size, zc_ref, szc, rzc, 1, 2)
    line.event(1)
    heads, length, _ = q_ref.shape
    kvs = k_ref.shape[0]
    group = heads // kvs
    query_cols = heads * HEAD
    key_cols = (weight_ref.shape[1] - query_cols) // 2
    block = 256

    @pl.loop(0, length // block)
    def _(i):
        rows = pl.ds(pl.multiple_of(i * block, block), block)
        low = low_columns(block)
        cosine, sine = cos_ref[rows], sin_ref[rows]
        whole = jnp.dot(first_ref[rows], weight_ref[...], preferred_element_type=F32)
        for ref, count, start, factor in ((q_ref, heads, 0, HEAD ** (-0.5)), (k_ref, kvs, query_cols, 1.0)):
            for j in range((count + 1) // 2):
                part = whole[:, start + 128 * j : start + 128 * (j + 1)]
                part = ((part * cosine + turn(part, low) * sine) * factor).astype(BF16)
                for side in range(min(2, count - 2 * j)):
                    ref[2 * j + side, rows] = part[:, side * HEAD : (side + 1) * HEAD]
        for j in range(kvs):
            at = query_cols + key_cols + j * HEAD
            v_ref[j, rows] = whole[:, at : at + HEAD].astype(BF16)

    @pl.loop(0, heads)
    def _(head):
        kv = lax.div(head, group)
        for i in range(length // block):
            rows, extent = slice(i * block, (i + 1) * block), (i + 1) * block
            scores = masked_scores(q_ref[head, rows], k_ref[kv, :extent], segc_ref[rows], segr_ref[:, :extent], i * block)
            top = jnp.max(scores, axis=1, keepdims=True)
            weights = jnp.exp(scores - top)
            total = jnp.sum(weights, axis=1, keepdims=True)
            mixed = jnp.dot(weights.astype(BF16), v_ref[kv, :extent], preferred_element_type=F32)
            oh_ref[head, rows] = (mixed / total).astype(BF16)

    for head in range(heads):
        o_ref[:, head * HEAD : (head + 1) * HEAD] = oh_ref[head]
    for step in range(bulk.gather.bits):
        bulk.event(step)
    line.event(2)
    keep_near(size, zc_ref, next_ref, 2)
    line.finish()
    bulk.finish()


def attend_call(first, weight, cosine, sine, segc, segr, near, gate, heads, kvs):
    size = lax.axis_size("row")
    length = first.shape[0]
    dma = pltpu.SemaphoreType.DMA
    return pl.pallas_call(
        functools.partial(attend_kernel, size),
        out_shape=(
            jax.ShapeDtypeStruct((heads, length, HEAD), BF16),
            jax.ShapeDtypeStruct((kvs, length, HEAD), BF16),
            jax.ShapeDtypeStruct((kvs, length, HEAD), BF16),
            jax.ShapeDtypeStruct((length, heads * HEAD), BF16),
            jax.ShapeDtypeStruct(near.shape, BF16),
            jax.ShapeDtypeStruct((size,) + gate.shape, BF16),
        ),
        in_specs=[VM] * 8,
        out_specs=(VM,) * 5 + (pl.BlockSpec(memory_space=pl.ANY),),
        scratch_shapes=[
            pltpu.VMEM((heads, length, HEAD), BF16),
            pltpu.VMEM((size,) + near.shape[1:], BF16),
            dma((2 * (size - 1),)), dma((2 * (size - 1),)),
        ]
        + SharedGather.scratch(size, 1),
        compiler_params=params(6),
        cost_estimate=cost(45),
    )(first, weight, cosine, sine, segc, segr, near, gate)


class swap_halves:
    def __init__(self, part, other, sends, recvs):
        core = lax.axis_index("dp")
        share = part.shape[1] // 2
        self.move = remote(
            part.at[:, pl.ds(pl.multiple_of((1 - core) * share, 16), share)], other, sends, recvs, 0, {"dp": 1 - core}
        )

    def start(self):
        self.move.start()

    def wait(self):
        self.move.wait()


def add_halves(part, other, share):
    rows = pl.ds(pl.multiple_of(lax.axis_index("dp") * share.shape[1], 16), share.shape[1])
    for j in range(part.shape[0]):
        share[j] = (part[j, rows].astype(F32) + other[j].astype(F32)).astype(BF16)


def row_moves(size, source, target, sends, recvs, first, begin):
    row = lax.axis_index("row")
    if begin:
        target[row] = source[row]
    for mask in range(1, size):
        move = remote(source.at[row ^ mask], target.at[row], sends, recvs, first + mask - 1, {"row": row ^ mask})
        if begin:
            move.start()
        else:
            move.wait()


def cost(micros):
    return pl.CostEstimate(flops=int(micros * 1e9), bytes_accessed=1 << 20, transcendentals=0)


def attend_back_kernel(
    dmid_ref, weight_ref, q_ref, k_ref, v_ref, cos_ref, sin_ref, segc_ref, segr_ref,
    attn_ref, down_ref, mid_ref, upshare_ref, gateshare_ref,
    dqkv_ref, inner_ref, blk_ref, line_ref, gup_ref, ggate_ref, do_ref, dq_ref, dk_ref, dv_ref,
    recv_ref, part_ref, other_ref, share_ref, urecv_ref, drecv_ref, ustage_ref, dstage_ref,
    s1, r1, score, rcore, srow, rrow, su, ru, sd, rd, copied, sf, rf,
):
    row, core = lax.axis_index("row"), lax.axis_index("dp")
    cols_n = down_ref.shape[0]
    heads, length, _ = q_ref.shape
    kvs = k_ref.shape[0]
    group = heads // kvs
    query_cols = heads * HEAD
    key_cols = (dqkv_ref.shape[1] - query_cols) // 2
    block = 256
    parts, _, width = weight_ref.shape
    greet(row_size=parts, col_size=cols_n, dp_size=2)
    line = ColScatter(cols_n, down_ref, recv_ref, s1, r1)
    line.event(0)
    sums = [
        (RowScatter(parts, upshare_ref, urecv_ref, su, ru), ustage_ref, gup_ref),
        (RowScatter(parts, gateshare_ref, drecv_ref, sd, rd), dstage_ref, ggate_ref),
    ]
    for scatter, _, _ in sums:
        scatter.start()
    for j in range(parts):
        part_ref[j] = lax.dot_general(
            attn_ref[...], dmid_ref[:, j * width : (j + 1) * width], (((0,), (0,)), ((), ())), preferred_element_type=F32
        ).astype(BF16)
    cross = swap_halves(part_ref, other_ref, score, rcore)
    cross.start()
    dk_ref[...] = jnp.zeros_like(dk_ref)
    dv_ref[...] = jnp.zeros_like(dv_ref)
    inner_ref[...] = jnp.zeros_like(inner_ref)

    @pl.loop(0, length // block)
    def _(i):
        rows = pl.ds(pl.multiple_of(i * block, block), block)
        total = jnp.zeros((block, query_cols), F32)
        for j in range(parts):
            total += lax.dot_general(
                dmid_ref[rows, j * width : (j + 1) * width], weight_ref[j], (((1,), (1,)), ((), ())), preferred_element_type=F32
            )
        for head in range(heads):
            do_ref[head, rows] = total[:, head * HEAD : (head + 1) * HEAD].astype(BF16)

    @pl.loop(0, heads)
    def _(head):
        @pl.when(head == min(1, heads - 1))
        def _():
            cross.wait()
            add_halves(part_ref, other_ref, share_ref)
            row_moves(parts, share_ref, line_ref, srow, rrow, 0, True)

        @pl.when(head == heads // 2)
        def _():
            line.event(1)

        kv = lax.div(head, group)
        for i in range(length // block):
            rows, extent = slice(i * block, (i + 1) * block), (i + 1) * block
            query, keys, grads = q_ref[head, rows], k_ref[kv, :extent], do_ref[head, rows]
            scores = masked_scores(query, keys, segc_ref[rows], segr_ref[:, :extent], i * block)
            top = jnp.max(scores, axis=1, keepdims=True)
            weights = jnp.exp(scores - top)
            weights = weights * (1.0 / jnp.sum(weights, axis=1, keepdims=True))
            back = lax.dot_general(grads, v_ref[kv, :extent], (((1,), (1,)), ((), ())), preferred_element_type=F32)
            dv_ref[kv, :extent] += lax.dot_general(
                weights.astype(BF16), grads, (((0,), (0,)), ((), ())), preferred_element_type=F32
            )
            ds = (weights * (back - jnp.sum(weights * back, axis=1, keepdims=True))).astype(BF16)
            dq = jnp.dot(ds, keys, preferred_element_type=F32)
            inner_ref[rows] += jnp.sum(dq * query.astype(F32), axis=1, keepdims=True)
            for side in range(2):

                @pl.when(lax.rem(head, 2) == side)
                def _():
                    dq_ref[lax.div(head, 2), rows, side * HEAD : (side + 1) * HEAD] = dq

            dk_ref[kv, :extent] += lax.dot_general(ds, query, (((0,), (0,)), ((), ())), preferred_element_type=F32)

    @pl.loop(0, length // block)
    def _(i):
        rows = pl.ds(pl.multiple_of(i * block, block), block)
        low = low_columns(block)
        cosine, sine = cos_ref[rows], sin_ref[rows]
        for ref, count, start, factor in ((dq_ref, heads, 0, HEAD ** (-0.5)), (dk_ref, kvs, query_cols, 1.0), (dv_ref, kvs, query_cols + key_cols, None)):
            for j in range((count + 1) // 2):
                if ref is dq_ref:
                    part = dq_ref[j, rows]
                else:
                    sides = [ref[2 * j + side, rows] if 2 * j + side < count else jnp.zeros((block, HEAD), F32) for side in range(2)]
                    part = jnp.concatenate(sides, axis=1)
                if factor is not None:
                    part = (part * cosine - turn(part * sine, low)) * factor
                dqkv_ref[rows, start + 128 * j : start + 128 * (j + 1)] = part.astype(BF16)
        more = jnp.zeros((block, 1), F32)
        for kv in range(kvs):
            more += jnp.sum(dk_ref[kv, rows] * k_ref[kv, rows].astype(F32) + dv_ref[kv, rows] * v_ref[kv, rows].astype(F32), axis=1, keepdims=True)
        inner_ref[rows] += more

    def finish(stage):
        def act(rows, total):
            stage[rows] = total

        return act

    if cols_n > 2:
        line.event(2)
    bits = sums[0][0].bits
    for step in range(bits - 1):
        for scatter, stage, _ in sums:
            scatter.event(step, finish(stage))
    for time in range(3, line.times):
        line.event(time)
    results = []
    for k, (scatter, stage, out) in enumerate(sums):
        scatter.event(bits - 1, finish(stage))
        moves = settle(stage, out, core, copied, sf, rf, k)
        for move in moves:
            move.start()
        results += moves
        scatter.close()

    @pl.loop(0, mid_ref.shape[0] // 64)
    def _(i):
        rows = pl.ds(pl.multiple_of(i * 64, 16), 64)
        total = mid_ref[rows] + line.total(rows)
        for j in range(parts):
            blk_ref[j, rows] = total[:, j * width : (j + 1) * width].astype(BF16)

    row_moves(parts, share_ref, line_ref, srow, rrow, 0, False)
    for move in results:
        move.wait()


def attend_back_call(dmid, weight, q, k, v, cosine, sine, segc, segr, columns, attn, down, middle, upshare, gateshare):
    rows_n, cols_n = lax.axis_size("row"), lax.axis_size("col")
    _, heads_cols, width = weight.shape
    quarter = middle.shape[0]
    dma = pltpu.SemaphoreType.DMA
    heads, length, _ = q.shape
    kvs = k.shape[0]
    return pl.pallas_call(
        attend_back_kernel,
        out_shape=(
            jax.ShapeDtypeStruct((length, columns), BF16),
            jax.ShapeDtypeStruct((length, 1), F32),
            jax.ShapeDtypeStruct((rows_n, quarter, width), BF16),
            jax.ShapeDtypeStruct((rows_n, heads_cols // 2, width), BF16),
            jax.ShapeDtypeStruct((2 * upshare.shape[1], upshare.shape[2]), F32),
            jax.ShapeDtypeStruct((2 * gateshare.shape[1], gateshare.shape[2]), F32),
        ),
        in_specs=[VM] * 14,
        out_specs=(VM,) * 4 + (pl.BlockSpec(memory_space=pl.ANY),) * 2,
        scratch_shapes=[
            pltpu.VMEM((heads, length, HEAD), BF16),
            pltpu.VMEM(((heads + 1) // 2, length, 2 * HEAD), F32),
            pltpu.VMEM((kvs, length, HEAD), F32),
            pltpu.VMEM((kvs, length, HEAD), F32),
            pltpu.VMEM((down.shape[0] + 1,) + down.shape[1:], BF16),
            pltpu.VMEM(weight.shape, BF16),
            pltpu.VMEM((rows_n, heads_cols // 2, width), BF16),
            pltpu.VMEM((rows_n, heads_cols // 2, width), BF16),
            pltpu.VMEM((rows_n - 1,) + upshare.shape[1:], BF16),
            pltpu.VMEM((rows_n - 1,) + gateshare.shape[1:], BF16),
            pltpu.VMEM(upshare.shape[1:], F32),
            pltpu.VMEM(gateshare.shape[1:], F32),
            dma((2,)), dma((2 * cols_n,)), dma((1,)), dma((1,)), dma((rows_n - 1,)), dma((rows_n - 1,)),
        ]
        + [dma((2 * (rows_n - 1),))] * 4
        + [dma((2,))] * 3
        + [
        ],
        compiler_params=params(5),
        cost_estimate=cost(80),
    )(dmid, weight, q, k, v, cosine, sine, segc, segr, attn, down, middle, upshare, gateshare)


def middle_kernel(
    rows_n, cols_n, attn_ref, weight_ref, x_ref, gain_ref, tok_ref, near_ref, next_ref, up_ref, down_ref,
    mid_ref, second_ref, cot_ref, ups_ref, downs_ref, part_ref, recv0_ref, recv1_ref, s0, r0, s1, r1, s2, r2, szc, rzc, *shared,
):
    row, col = lax.axis_index("row"), lax.axis_index("col")
    quarter, features = mid_ref.shape
    width = features // rows_n
    bulks = [SharedGather(rows_n, up_ref, ups_ref, *shared, 0), SharedGather(rows_n, down_ref, downs_ref, *shared, 1)]
    for bulk in bulks:
        bulk.load()
    cot_ref[col] = tok_ref[...]
    take_near(cols_n, cot_ref, near_ref, 1)
    take_near(cols_n, cot_ref, next_ref, 2)
    greet(row_size=rows_n, col_size=cols_n, dp_size=2)
    rest = ColGather(cols_n, cot_ref, szc, rzc, 2)
    rest.event(2)

    @pl.loop(0, rows_n)
    def _(i):
        own = attn_ref[pl.ds(pl.multiple_of(i * quarter, 16), quarter)]
        for j in range(rows_n):
            part_ref[i, :, j * width : (j + 1) * width] = jnp.dot(own, weight_ref[j], preferred_element_type=F32).astype(BF16)

    half = quarter // 2

    def finish(k):
        def act(rows, total):
            here = pl.ds(pl.multiple_of(k * half + rows.start, 16), rows.size)
            own = pl.ds(pl.multiple_of(row * quarter + k * half + rows.start, 16), rows.size)
            squares = jnp.zeros((rows.size, 1), F32)
            for j in range(rows_n):
                columns = slice(j * width, (j + 1) * width)
                value = total[:, columns] + x_ref[j, own].astype(F32)
                mid_ref[here, columns] = value
                squares += jnp.sum(value * value, axis=1, keepdims=True)
            inverse = lax.rsqrt(squares / features + EPSILON)
            second_ref[col, here] = (mid_ref[here] * inverse * gain_ref[...]).astype(BF16)

        return act

    scatters = [
        RowScatter(rows_n, part_ref, recv0_ref, s0, r0, 0),
        RowScatter(rows_n, part_ref, recv1_ref, s1, r1, half),
    ]
    lines = [
        ColGather(cols_n, second_ref, s2, r2, 0, None, pl.ds(k * half, half), k * 2 * (cols_n - 1)) for k in range(2)
    ]
    bits = scatters[0].bits
    scatters[0].start()
    scatters[0].event(0, finish(0))
    scatters[1].start()
    for step in range(1, bits):
        scatters[0].event(step, finish(0))
    lines[0].event(0)
    for step in range(bits - 1):
        scatters[1].event(step, finish(1))
    for bulk in bulks:
        bulk.start()
    scatters[1].event(bits - 1, finish(1))
    lines[1].event(0)
    for step in range(3, cols_n):
        rest.event(step)
    rest.finish()
    lines[0].event(1)
    lines[0].event(2)
    lines[1].event(1)
    for step in range(3, cols_n):
        lines[0].event(step)
        lines[1].event(step - 1)
    for bulk in bulks:
        bulk.event(0)
    lines[1].event(cols_n - 1)
    for step in range(1, bits):
        for bulk in bulks:
            bulk.event(step)
    for bulk in bulks:
        bulk.finish()
    for scatter in scatters:
        scatter.close()
    for line in lines:
        line.finish()


def middle_call(attn, weight, x, gain, tok, near, following, up, down):
    rows_n, cols_n = lax.axis_size("row"), lax.axis_size("col")
    length, features = attn.shape[0], weight.shape[0] * weight.shape[2]
    quarter = length // rows_n
    dma = pltpu.SemaphoreType.DMA
    anywhere = pl.BlockSpec(memory_space=pl.ANY)
    return pl.pallas_call(
        functools.partial(middle_kernel, rows_n, cols_n),
        out_shape=(
            jax.ShapeDtypeStruct((quarter, features), F32),
            jax.ShapeDtypeStruct((cols_n, quarter, features), BF16),
            jax.ShapeDtypeStruct((cols_n, quarter, features), BF16),
            jax.ShapeDtypeStruct((rows_n,) + up.shape, BF16),
            jax.ShapeDtypeStruct((rows_n,) + down.shape, BF16),
        ),
        in_specs=[VM] * 9,
        out_specs=(VM, VM, VM, anywhere, anywhere),
        scratch_shapes=[
            pltpu.VMEM((rows_n, quarter, features), BF16),
            pltpu.VMEM((rows_n - 1, quarter // 2, features), BF16),
            pltpu.VMEM((rows_n - 1, quarter // 2, features), BF16),
        ]
        + [dma((2 * (rows_n - 1),))] * 4
        + [dma((4 * (cols_n - 1),))] * 2
        + [dma((2 * (cols_n - 1),))] * 2
        + SharedGather.scratch(rows_n, 2),
        compiler_params=params(2),
        cost_estimate=cost(130),
    )(attn, weight, x, gain, tok, near, following, up, down)


def settle(stage, out, core, copied, sends, recvs, place):
    rows = pl.ds(pl.multiple_of(core * stage.shape[0], 8), stage.shape[0])
    return (
        pltpu.make_async_copy(stage, out.at[rows], copied.at[place]),
        remote(stage, out.at[rows], sends, recvs, place, {"dp": 1 - core}),
    )


def back_kernel(
    rows_n, cols_n, dgate_ref, dup_ref, gate_ref, up_ref, mid_ref, tok_ref, gain_ref, second_ref, down_ref,
    dmid_ref, grad_ref, gdown_ref, share0_ref, share1_ref,
    w0_ref, w1_ref, part_ref, recv_ref, other_ref, drecv_ref, stage_ref,
    loads, s1, r1, s2, r2, sg, rg, score, rcore, copied, sf, rf, free,
):
    row, col, core = lax.axis_index("row"), lax.axis_index("col"), lax.axis_index("dp")
    quarter, features = mid_ref.shape
    width = features // rows_n
    hidden = dgate_ref.shape[1]
    share = width // 2
    moves = [pltpu.make_async_copy(ref, kept, loads.at[k]) for k, (ref, kept) in enumerate(((gate_ref, w0_ref), (up_ref, w1_ref)))]
    for move in moves:
        move.start()
    greet(row_size=rows_n, col_size=cols_n, dp_size=2)
    for move in moves:
        move.wait()

    def prepare(target):
        rows = pl.ds(pl.multiple_of(target * quarter, 16), quarter)

        @pl.loop(0, rows_n)
        def _(i):
            columns = pl.ds(pl.multiple_of(i * width, 128), width)
            value = lax.dot_general(dgate_ref[rows], w0_ref[i], (((1,), (1,)), ((), ())), preferred_element_type=F32)
            value += lax.dot_general(dup_ref[rows], w1_ref[i], (((1,), (1,)), ((), ())), preferred_element_type=F32)
            part_ref[target, :, columns] = value.astype(BF16)

    tile = min(512, hidden)

    def product(right, kept):
        @pl.loop(0, rows_n)
        def _(i):
            for t in range(hidden // tile):
                columns = slice(t * tile, (t + 1) * tile)
                kept[i, :, columns] = lax.dot_general(
                    second_ref[:, pl.ds(pl.multiple_of(i * width, 128), width)], right[:, columns], (((0,), (0,)), ((), ())),
                    preferred_element_type=F32,
                ).astype(BF16)

    def add(kept):
        chunk = min(64, share)
        chunks = share // chunk

        @pl.loop(0, rows_n * chunks)
        def _(i):
            block, start = lax.div(i, chunks), lax.rem(i, chunks) * chunk
            rows = pl.ds(pl.multiple_of(core * share + start, 16), chunk)
            other = other_ref[block, pl.ds(pl.multiple_of(start, 16), chunk)]
            kept[block, rows] = (kept[block, rows].astype(F32) + other.astype(F32)).astype(BF16)

    half = quarter // 2
    lines = [ColScatter(cols_n, part_ref, recv_ref, s1, r1, k * half, half, k) for k in range(2)]
    gathers = [RowGather(rows_n, dmid_ref, s2, r2, k * half, half, k * 2 * (rows_n - 1)) for k in range(2)]
    scatter = RowScatter(rows_n, down_ref, drecv_ref, sg, rg)
    cross = [
        remote(kept.at[:, pl.ds(pl.multiple_of((1 - core) * share, 16), share)], other_ref, score, rcore, k, {"dp": 1 - core})
        for k, kept in enumerate((w0_ref, w1_ref))
    ]
    keeps = [
        pltpu.make_async_copy(kept.at[:, pl.ds(pl.multiple_of(core * share, 16), share)], out, copied.at[1 + k])
        for k, (kept, out) in enumerate(((w0_ref, share0_ref), (w1_ref, share1_ref)))
    ]

    def finish(rows, total):
        stage_ref[rows] = total

    def norm_back(k):
        @pl.loop(0, half // 32)
        def _(i):
            rows = pl.ds(pl.multiple_of(k * half + i * 32, 32), 32)
            got = lines[k].total(rows)
            middle = mid_ref[rows]
            inverse = lax.rsqrt(jnp.sum(middle * middle, axis=1, keepdims=True) / features + EPSILON)
            weighted = got * gain_ref[...]
            inner = jnp.sum(middle * weighted, axis=1, keepdims=True) / features
            grad_ref[...] += jnp.sum(got * middle * inverse, axis=0, keepdims=True)
            value = tok_ref[rows].astype(F32) + inverse * weighted - middle * (inverse * inverse * inverse * inner)
            dmid_ref[row, rows] = value.astype(BF16)

    grad_ref[...] = jnp.zeros_like(grad_ref)
    scatter.start()
    for time in range(cols_n):
        lines[0].event(time, prepare)
        if time == cols_n - 2:
            for step in range(scatter.bits - 1):
                scatter.event(step, finish)
    lines[1].event(0)
    norm_back(0)
    gathers[0].start()
    scatter.event(scatter.bits - 1, finish)
    results = settle(stage_ref, gdown_ref, core, copied, sf, rf, 0)
    for move in results:
        move.start()
    product(dgate_ref, w0_ref)
    cross[0].start()
    lines[1].event(1)
    gathers[0].event(0)
    product(dup_ref, w1_ref)
    for time in range(2, cols_n - 1):
        lines[1].event(time)
    for step in range(1, gathers[0].bits):
        gathers[0].event(step)
    cross[0].wait()
    add(w0_ref)
    keeps[0].start()
    pl.semaphore_signal(free, inc=1, device_id={"dp": 1 - core}, device_id_type=MESH)
    pl.semaphore_wait(free, 1)
    cross[1].start()
    lines[1].event(cols_n - 1)
    norm_back(1)
    gathers[1].start()
    cross[1].wait()
    add(w1_ref)
    keeps[1].start()
    gathers[1].run()
    gathers[0].finish()
    scatter.close()
    for move in keeps:
        move.wait()
    for move in results:
        move.wait()


def back_call(dgate, dup, gate, up, middle, tok, gain, second, down_share):
    rows_n, cols_n = lax.axis_size("row"), lax.axis_size("col")
    quarter, features = middle.shape
    hidden = dgate.shape[1]
    width = features // rows_n
    dma = pltpu.SemaphoreType.DMA
    anywhere = pl.BlockSpec(memory_space=pl.ANY)
    line = 2 * (rows_n - 1)
    half = (rows_n, width // 2, hidden)
    return pl.pallas_call(
        functools.partial(back_kernel, rows_n, cols_n),
        out_shape=(
            jax.ShapeDtypeStruct((rows_n, quarter, features), BF16),
            jax.ShapeDtypeStruct((1, features), F32),
            jax.ShapeDtypeStruct((2 * down_share.shape[1], width), F32),
            jax.ShapeDtypeStruct(half, BF16),
            jax.ShapeDtypeStruct(half, BF16),
        ),
        in_specs=[VM, VM, anywhere, anywhere, VM, VM, VM, VM, VM],
        out_specs=(VM, VM, anywhere, anywhere, anywhere),
        scratch_shapes=[
            pltpu.VMEM((rows_n, width, hidden), BF16),
            pltpu.VMEM((rows_n, width, hidden), BF16),
            pltpu.VMEM((cols_n, quarter, features), BF16),
            pltpu.VMEM((cols_n + 1, quarter, features), BF16),
            pltpu.VMEM(half, BF16),
            pltpu.VMEM((rows_n - 1,) + down_share.shape[1:], BF16),
            pltpu.VMEM(down_share.shape[1:], F32),
            dma((2,)), dma((4,)), dma((4 * cols_n,)),
            dma((2 * line,)), dma((2 * line,)), dma((line,)), dma((line,)),
            dma((2,)), dma((2,)), dma((3,)), dma((1,)), dma((1,)), pltpu.SemaphoreType.REGULAR,
        ],
        compiler_params=params(3),
        cost_estimate=cost(130),
    )(dgate, dup, gate, up, middle, tok, gain, second, down_share)


def last_kernel(
    size, dqkv_ref, weight_ref, first_ref, outline_ref, blk_ref, inner_ref, act_ref, inv_ref, grad2_ref,
    out_ref, block_ref, inners_ref, gains_ref, gqkv_ref, gout_ref,
    part_ref, recv_ref, qpart_ref, qother_ref, qshare_ref, qline_ref, qrecv_ref, orecv_ref, rgain_ref, pair_ref, pairs_ref,
    s1, r1, sblk, rblk, sinn, rinn, score, rcore, srow, rrow, so, ro, sq, rq, sg, rg, sp, rp, sf, rf,
):
    row, col, core = lax.axis_index("row"), lax.axis_index("col"), lax.axis_index("dp")
    length, width = act_ref.shape
    quarter = length // size
    barrier = pltpu.get_barrier_semaphore()
    peers = [{"row": row ^ mask} for mask in range(1, size)]
    others = [{"col": lax.rem(col + k, size)} for k in range(1, size)]
    others += [{"col": lax.rem(col + k, size), "dp": 1 - core} for k in range(size)]
    for peer in peers + others:
        pl.semaphore_signal(barrier, inc=1, device_id=peer, device_id_type=MESH)
    pl.semaphore_wait(barrier, len(peers) + len(others))

    scatter = RowScatter(size, part_ref, recv_ref, s1, r1)
    inners_ref[row] = inner_ref[...]
    rgain_ref[row] = grad2_ref[row]
    small = []
    for mask in range(1, size):
        small.append(remote(inner_ref, inners_ref.at[row], sinn, rinn, mask - 1, {"row": row ^ mask}))
        small.append(remote(grad2_ref.at[row ^ mask], rgain_ref.at[row], sg, rg, mask - 1, {"row": row ^ mask}))
    for move in small:
        move.start()
    block_ref[pl.ds(pl.multiple_of(row * quarter, 16), quarter)] = blk_ref[row]
    for mask in range(1, size):
        remote(
            blk_ref.at[row ^ mask], block_ref.at[pl.ds(pl.multiple_of(row * quarter, 16), quarter)], sblk, rblk, mask - 1, {"row": row ^ mask}
        ).start()
    oline = ColScatter(size, outline_ref, orecv_ref, so, ro)
    oline.event(0)

    @pl.loop(0, size)
    def _(j):
        columns = pl.ds(pl.multiple_of(j * width, 128), width)
        qpart_ref[j] = lax.dot_general(
            first_ref[:, columns], dqkv_ref[...], (((0,), (0,)), ((), ())), preferred_element_type=F32
        ).astype(BF16)

    cross = swap_halves(qpart_ref, qother_ref, score, rcore)
    cross.start()
    oline.event(1)

    @pl.loop(0, size)
    def _(j):
        part_ref[j] = lax.dot_general(dqkv_ref[...], weight_ref[j], (((1,), (1,)), ((), ())), preferred_element_type=F32).astype(BF16)

    cross.wait()
    add_halves(qpart_ref, qother_ref, qshare_ref)
    row_moves(size, qshare_ref, qline_ref, srow, rrow, 0, True)
    for time in range(2, oline.times):
        oline.event(time)
    share_o = outline_ref.shape[1]
    share_q = qline_ref.shape[1]

    def across(ref, share, which):
        piece = ref.at[pl.ds(pl.multiple_of(core * share, 8), share)]
        return remote(piece, piece, sf, rf, which, {"dp": 1 - core})

    gout_ref[pl.ds(pl.multiple_of(core * share_o, 8), share_o)] = oline.total(slice(None))
    across(gout_ref, share_o, 0).start()

    row_moves(size, qshare_ref, qline_ref, srow, rrow, 0, False)
    scatter.start()
    qline = ColScatter(size, qline_ref, qrecv_ref, sq, rq)
    qline.event(0)
    pair_ref[0] = jnp.zeros_like(pair_ref[0])

    def finish(rows, total):
        out_ref[rows] = total
        pair_ref[0] += jnp.sum(total * act_ref[rows].astype(F32) * inv_ref[rows], axis=0, keepdims=True)

    for step in range(scatter.bits - 1):
        scatter.event(step, finish)
    for time in range(1, min(3, qline.times)):
        qline.event(time)
    scatter.event(scatter.bits - 1, finish)
    scatter.close()
    for move in small:
        move.wait()
    pair_ref[1] = jnp.sum(rgain_ref[...], axis=0)
    own = core * size + col
    pairs_ref[own] = pair_ref[...]
    for k, peer in enumerate(others):
        remote(pair_ref, pairs_ref.at[own], sp, rp, k, peer).start()
    for time in range(3, qline.times):
        qline.event(time)
    gqkv_ref[pl.ds(pl.multiple_of(core * share_q, 8), share_q)] = qline.total(slice(None))
    across(gqkv_ref, share_q, 1).start()
    for k, peer in enumerate(others):
        remote(pair_ref, pairs_ref.at[own], sp, rp, k, peer).wait()
    gains_ref[...] = jnp.sum(pairs_ref[...], axis=0)
    for mask in range(1, size):
        remote(
            blk_ref.at[row ^ mask], block_ref.at[pl.ds(pl.multiple_of(row * quarter, 16), quarter)], sblk, rblk, mask - 1, {"row": row ^ mask}
        ).wait()
    across(gout_ref, share_o, 0).wait()
    across(gqkv_ref, share_q, 1).wait()


def last_call(dqkv, weight, first, outline, blk, inner, activations, inv1, grad2):
    size = lax.axis_size("row")
    length, width = activations.shape
    columns = weight.shape[1]
    heads_cols = 2 * outline.shape[1]
    dma = pltpu.SemaphoreType.DMA
    count = 2 * size - 1
    return pl.pallas_call(
        functools.partial(last_kernel, size),
        out_shape=(
            jax.ShapeDtypeStruct((length, width), F32),
            jax.ShapeDtypeStruct((length, width), BF16),
            jax.ShapeDtypeStruct((size,) + inner.shape, F32),
            jax.ShapeDtypeStruct((2, 1, width), F32),
            jax.ShapeDtypeStruct((width, columns), F32),
            jax.ShapeDtypeStruct((heads_cols, width), F32),
        ),
        in_specs=[VM] * 9,
        out_specs=(VM,) * 6,
        scratch_shapes=[
            pltpu.VMEM((size, length, width), BF16),
            pltpu.VMEM((size - 1, length, width), BF16),
            pltpu.VMEM((size, width, columns), BF16),
            pltpu.VMEM((size, width // 2, columns), BF16),
            pltpu.VMEM((size, width // 2, columns), BF16),
            pltpu.VMEM((size, width // 2, columns), BF16),
            pltpu.VMEM((size + 1, width // 2, columns), BF16),
            pltpu.VMEM((size + 1, heads_cols // 2, width), BF16),
            pltpu.VMEM((size, 1, width), F32),
            pltpu.VMEM((2, 1, width), F32),
            pltpu.VMEM((2 * size, 2, 1, width), F32),
        ]
        + [dma((2 * (size - 1),))] * 2
        + [dma((size - 1,))] * 2
        + [dma((size - 1,))] * 2
        + [dma((1,))] * 2
        + [dma((size - 1,))] * 2
        + [dma((2,)), dma((2 * size,))] * 2
        + [dma((size - 1,))] * 2
        + [dma((count,))] * 2
        + [dma((2,))] * 2,
        compiler_params=params(4),
        cost_estimate=cost(80),
    )(dqkv, weight.reshape(size, width, columns), first, outline, blk, inner, activations, inv1, grad2.reshape(size, 1, width))


def feed_kernel(
    second_ref, cot_ref, gate_ref, up_ref, down_ref, dgate_ref, dup_ref, own_ref, part_ref,
    hidden_ref, keep_ref, send_ref, other_ref, sends, recvs,
):
    core = lax.axis_index("dp")
    step = pl.program_id(0)
    rows_n, tile, width = down_ref.shape
    tokens = second_ref.shape[0]
    tiles = hidden_ref.shape[0]
    block = min(512, tokens)
    mine = tiles // 2

    def place(t):
        return pl.ds(pl.multiple_of(lax.rem(t, mine) * tile, tile), tile)

    def give(t):
        return remote(send_ref.at[:, place(t)], other_ref.at[:, place(t)], sends, recvs, lax.rem(t, mine), {"dp": 1 - core})

    @pl.when(step == 0)
    def _():
        greet(dp_size=2)

    @pl.when(step < tiles)
    def _():
        keep_ref[step] = down_ref[...]

        @pl.loop(0, tokens // block)
        def _(i):
            rows = pl.ds(pl.multiple_of(i * block, block), block)
            gate = jnp.dot(second_ref[rows], gate_ref[...], preferred_element_type=F32)
            up = jnp.dot(second_ref[rows], up_ref[...], preferred_element_type=F32)
            back = jnp.zeros((block, tile), F32)
            for j in range(rows_n):
                back += lax.dot_general(
                    cot_ref[rows, j * width : (j + 1) * width], down_ref[j], (((1,), (1,)), ((), ())), preferred_element_type=F32
                )
            sigma = jax.nn.sigmoid(gate)
            swish = gate * sigma
            hidden_ref[step, rows] = (swish * up).astype(BF16)
            dgate_ref[rows] = (back * up * (sigma * (1.0 + gate * (1.0 - sigma)))).astype(BF16)
            dup_ref[rows] = (back * swish).astype(BF16)

        for j in range(rows_n):
            value = lax.dot_general(
                hidden_ref[step], cot_ref[:, j * width : (j + 1) * width], (((0,), (0,)), ((), ())), preferred_element_type=F32
            ).astype(BF16)

            @pl.when(lax.div(step, mine) == core)
            def _():
                own_ref[j, place(step)] = value

            @pl.when(lax.div(step, mine) != core)
            def _():
                send_ref[j, place(step)] = value

        @pl.when(lax.div(step, mine) != core)
        def _():
            give(step).start()

    @pl.when(step >= tiles)
    def _():
        quarter = part_ref.shape[1]
        rows = pl.ds(pl.multiple_of((step - tiles) * quarter, quarter), quarter)
        for j in range(rows_n):
            total = jnp.zeros((quarter, width), F32)
            for t in range(tiles):
                total += jnp.dot(hidden_ref[t, rows], keep_ref[t, j], preferred_element_type=F32)
            part_ref[0, :, j * width : (j + 1) * width] = total.astype(BF16)

    @pl.when(step == pl.num_programs(0) - 1)
    def _():
        for t in range(mine):
            give(t).wait()
            for j in range(rows_n):
                own_ref[j, place(t)] = (own_ref[j, place(t)].astype(F32) + other_ref[j, place(t)].astype(F32)).astype(BF16)


def feed_call(second, cot, gate, up, down):
    rows_n, hidden, width = down.shape
    cols_n = lax.axis_size("col")
    tokens, features = second.shape
    tile = 512
    tiles = hidden // tile
    half = (rows_n, hidden // 2, width)

    def place(i):
        return jnp.minimum(i, tiles - 1)

    return pl.pallas_call(
        feed_kernel,
        grid=(tiles + cols_n,),
        out_shape=(
            jax.ShapeDtypeStruct((tokens, hidden), BF16),
            jax.ShapeDtypeStruct((tokens, hidden), BF16),
            jax.ShapeDtypeStruct(half, BF16),
            jax.ShapeDtypeStruct((cols_n, tokens // cols_n, features), BF16),
        ),
        in_specs=[
            VM,
            VM,
            pl.BlockSpec((features, tile), lambda i: (0, place(i))),
            pl.BlockSpec((features, tile), lambda i: (0, place(i))),
            pl.BlockSpec((rows_n, tile, width), lambda i: (0, place(i), 0)),
        ],
        out_specs=(
            pl.BlockSpec((tokens, tile), lambda i: (0, place(i))),
            pl.BlockSpec((tokens, tile), lambda i: (0, place(i))),
            VM,
            pl.BlockSpec((1, tokens // cols_n, features), lambda i: (jnp.maximum(i - tiles, 0), 0, 0)),
        ),
        scratch_shapes=[
            pltpu.VMEM((tiles, tokens, tile), BF16),
            pltpu.VMEM((tiles, rows_n, tile, width), BF16),
            pltpu.VMEM(half, BF16),
            pltpu.VMEM(half, BF16),
            pltpu.SemaphoreType.DMA((tiles // 2,)),
            pltpu.SemaphoreType.DMA((tiles // 2,)),
        ],
        compiler_params=params(7),
        cost_estimate=cost(50),
    )(second, cot, gate, up, down)


def rotary_tables(positions):
    exponent = jnp.arange(0, HEAD, 2).astype(F32) / HEAD
    inverse = jnp.power(F32(THETA), -exponent)
    phase = positions[:, None] * inverse[None, :]
    phase = jnp.concatenate([phase] * (2 * 128 // HEAD), axis=1)
    return (jnp.cos(phase), jnp.sin(phase))


def local(
    activations, segments, positions, first_gain, query_weight, key_weight, value_weight, out_weight,
    second_gain, gate_weight, up_weight, down_weight, cotangent,
):
    rows = lax.axis_size("row")
    row, col = lax.axis_index("row"), lax.axis_index("col")
    length, width = activations.shape
    features = rows * width
    query_cols, key_cols = query_weight.shape[1], key_weight.shape[1]
    heads, kvs = query_cols // HEAD, key_cols // HEAD
    hidden_cols = gate_weight.shape[1]
    spare = jnp.zeros((width, -key_cols % 128), BF16)
    key_span = key_cols + spare.shape[1]
    qkv_cols = query_cols + 2 * key_span

    small = jnp.concatenate([segments.astype(F32), positions.astype(F32), first_gain, second_gain]).reshape(-1, 128)
    qkv_weight = jnp.concatenate([query_weight, key_weight, spare, value_weight, spare], axis=1)
    x_blocks, first, inv1, cot_tok, smalls, qkv_all, out_all_w, near = first_call(activations, cotangent, small, qkv_weight, out_weight)
    qkv_all = qkv_all.reshape(features, qkv_cols)
    smalls = smalls.reshape(rows, -1)
    own = lax.dynamic_slice_in_dim(smalls, col, 1, 0)[0]
    segment_own, position_own = own[:length], own[length : 2 * length]
    gain2 = smalls[:, 2 * length + width :].reshape(1, features)

    cosine, sine = rotary_tables(position_own)
    segc, segr = segment_own[:, None], segment_own[None]
    q, k, v, attn, following, gate_all = attend_call(first, qkv_all, cosine, sine, segc, segr, near, gate_weight, heads, kvs)
    middle, second_all, cot_all, up_all, down_all = middle_call(
        attn, out_all_w, x_blocks, gain2, cot_tok, near, following, up_weight, down_weight
    )
    gate_all, up_all = gate_all.reshape(features, hidden_cols), up_all.reshape(features, hidden_cols)
    second_all, cot_all = second_all.reshape(-1, features), cot_all.reshape(-1, features)
    dgate, dup, down_share, down_part = feed_call(second_all, cot_all, gate_all, up_all, down_all)
    dmid_all, gain2_grad, down_grad, gate_share, up_share = back_call(
        dgate, dup, gate_all.reshape(rows, width, hidden_cols), up_all.reshape(rows, width, hidden_cols), middle, cot_tok, gain2, second_all,
        down_share,
    )
    dmid_all = dmid_all.reshape(length, features)

    dqkv, inner1, blk, outline, up_grad, gate_grad = attend_back_call(
        dmid_all, out_all_w, q, k, v, cosine, sine, segc, segr, qkv_cols, attn, down_part, middle, up_share, gate_share
    )
    dfirst, block_out, inner1, gains, qkv_grad, out_grad = last_call(
        dqkv, qkv_all, first, outline, blk, inner1.reshape(-1, 128), activations, inv1, gain2_grad
    )
    inner1 = jnp.sum(inner1, axis=0).reshape(length, 1) / (inv1 * features)
    own_x = activations.astype(F32)
    dmid_own = lax.dynamic_slice_in_dim(dmid_all, row * width, width, 1).astype(F32)
    input_grad = dmid_own + inv1 * first_gain[None] * dfirst - own_x * (inv1 * inv1 * inv1 * inner1)

    return (
        block_out,
        input_grad,
        gains[0, 0],
        qkv_grad[:, :query_cols],
        qkv_grad[:, query_cols : query_cols + key_cols],
        qkv_grad[:, query_cols + key_span : query_cols + key_span + key_cols],
        out_grad,
        gains[1, 0],
        gate_grad,
        up_grad,
        down_grad,
    )


def solution(mesh):
    tokens, block, swapped = P(("dp", "col"), "row"), P("row", "col"), P("col", "row")
    return jax.shard_map(
        local,
        mesh=mesh,
        in_specs=(
            tokens, P(("dp", "row")), P(("dp", "row")), P("row"), block, block, block, swapped,
            P("row"), block, block, swapped, tokens,
        ),
        out_specs=(tokens, tokens, P("row"), block, block, block, swapped, P("row"), block, block, swapped),
        check_vma=False,
    )
```
